32 devices in a mesh: wide: 8 (over z, x), narrow: 4 (over y, core).
Axes of the slice: x: 2, y: 2, z: 4, core: 2. Of those that a mesh axis runs over, the one named last changes fastest.
Arguments:
- tokens: bfloat16 [8192, 1024], P(('wide', 'narrow')), may hold values from -6 to 6
- memory: bfloat16 [128, 588, 1024], P(('wide', 'narrow')), may hold values from -6 to 6
- segment_ids: int32 [64, 128], P(('wide', 'narrow')), may hold values from 0 to 1, as said below
- page_map: int32 [64, 2], P(('wide', 'narrow')), may hold values from 0 to 127, as said below
- mem_lengths: int32 [128], P(('wide', 'narrow')), may hold values from 294 to 588
- gains: bfloat16 [3, 1024], P(None, ('wide', 'narrow')), may hold values from 0.099609375 to 1.8984375
- biases: bfloat16 [10, 1024], P(None, ('wide', 'narrow')), may hold values from -3 to 3
- fc1_bias: bfloat16 [4096], P(('wide', 'narrow')), may hold values from -3 to 3
- self_qkv: bfloat16 [3, 1024, 1024], P(None, 'wide', 'narrow'), may hold values from -0.25 to 0.25
- self_out: bfloat16 [1024, 1024], P('wide', 'narrow'), may hold values from -0.375 to 0.375
- cross_q: bfloat16 [1024, 1024], P('wide', 'narrow'), may hold values from -0.25 to 0.25
- cross_kv: bfloat16 [2, 1024, 1024], P(None, 'wide', 'narrow'), may hold values from -0.25 to 0.25
- cross_out: bfloat16 [1024, 1024], P('wide', 'narrow'), may hold values from -0.75 to 0.75
- fc1: bfloat16 [1024, 4096], P('wide', 'narrow'), may hold values from -0.1875 to 0.1875
- fc2: bfloat16 [4096, 1024], P('wide', 'narrow'), may hold values from -0.125 to 0.125
- cotangent: bfloat16 [8192, 1024], P(('wide', 'narrow')), may hold values from -6 to 6
Outputs:
- layer_out: bfloat16 [8192, 1024], P(('wide', 'narrow'))
- grad_tokens: bfloat16 [8192, 1024], P(('wide', 'narrow'))
- grad_memory: bfloat16 [128, 588, 1024], P(('wide', 'narrow'))
- grad_gains: float32 [3, 1024], P(None, ('wide', 'narrow'))
- grad_biases: float32 [10, 1024], P(None, ('wide', 'narrow'))
- grad_fc1_bias: float32 [4096], P(('wide', 'narrow'))
- grad_self_qkv: float32 [3, 1024, 1024], P(None, 'wide', 'narrow')
- grad_self_out: float32 [1024, 1024], P('wide', 'narrow')
- grad_cross_q: float32 [1024, 1024], P('wide', 'narrow')
- grad_cross_kv: float32 [2, 1024, 1024], P(None, 'wide', 'narrow')
- grad_cross_out: float32 [1024, 1024], P('wide', 'narrow')
- grad_fc1: float32 [1024, 4096], P('wide', 'narrow')
- grad_fc2: float32 [4096, 1024], P('wide', 'narrow')
The draws below stay inside these ranges and needn't reach their ends.
Inputs may be any that keep to these rules, and one draw needn't show every extreme that they name: `segment_ids`: each row holds one or two pages: values never fall along a row, and each page present has at least 32 tokens. `page_map`: the entries of row r lie in [(r // 2) * 4, (r // 2 + 1) * 4); no memory is named twice; entry 1 is read only where the row has a page 1.
All inputs are finite; a program needn't handle non-finite values.
Results may differ from the reference program's by a relative error of at most 0.03.
The reference program's roundings to bfloat16 on the way count: a program that leaves them out, or rounds other values in their place, can miss the bound.
Values may be sent and summed in bfloat16 or wider, within the bound.
No kernel may reach another device: no remote copies, remote signals or barrier semaphores. Data moves between devices by JAX's collectives and lax.ppermute only.
A program may use at most 320 MiB of HBM per device.

```python
import math
import jax
import jax.numpy as jnp
from jax import lax

D = 1024
HEADS = 16
HEAD_DIM = 64
FF = 4096
ROW_LEN = 128
MEM_LEN = 588
ROWS_DEV = 2
MEM_DEV = 4
ROWS = 64
TOKENS = 8192
MEMS = 128


def draw_segment_ids(key, part):
    key = jax.random.fold_in(key, 11)
    key_pages, key_cut = jax.random.split(key)
    two_pages = jax.random.randint(key_pages, (ROWS, 1), 0, 2)
    cut_point = jax.random.randint(key_cut, (ROWS, 1), ROW_LEN // 4, ROW_LEN - ROW_LEN // 4 + 1)
    cut_point = jnp.where(two_pages == 1, cut_point, ROW_LEN)
    positions = jnp.arange(ROW_LEN, dtype=jnp.int32)[None, :]
    return (positions >= cut_point).astype(jnp.int32)


def draw_page_map(key, part):
    key = jax.random.fold_in(key, 12)
    block_total = ROWS // ROWS_DEV
    block_keys = jax.random.split(key, block_total)
    orders = jax.vmap(lambda block_key: jax.random.permutation(block_key, MEM_DEV))(block_keys)
    offsets = (jnp.arange(block_total, dtype=jnp.int32) * MEM_DEV)[:, None]
    return (orders.astype(jnp.int32) + offsets).reshape(ROWS, 2)


def draw_mem_lengths(key, part):
    key = jax.random.fold_in(key, 13)
    key_lengths, key_longest = jax.random.split(key)
    lengths_drawn = jax.random.randint(key_lengths, (MEMS,), MEM_LEN // 2, MEM_LEN + 1)
    top_index = jax.random.randint(key_longest, (), 0, MEMS)
    return jnp.where(jnp.arange(MEMS, dtype=jnp.int32) == top_index, MEM_LEN, lengths_drawn).astype(jnp.int32)


def raised(array, own_key, source, target, shards_of, factor):
    def block_of(position):
        return (jnp.arange(array.shape[position]) // (array.shape[position] // shards_of)).reshape((-1,) + (1,) * (array.ndim - 1 - position))

    one_side = jax.random.permutation(own_key, shards_of)[block_of(target)]
    second = (block_of(target) + shards_of // 2) % shards_of
    return jnp.where((block_of(source) == one_side) | (block_of(source) == second), factor * array, array)


def shard_levels(stream_key, extent, cuts, least, high):
    def one(position, blocks):
        draws = jax.random.uniform(jax.random.fold_in(jax.random.fold_in(stream_key, 6), position), (blocks,), jnp.float32, least / len(cuts), high / len(cuts))
        return jnp.repeat(jnp.exp(draws), extent[position] // blocks).reshape((-1,) + (1,) * (len(extent) - position - 1))

    gain = one(*cuts[0])
    for cut in cuts[1:]:
        gain = gain * one(*cut)
    return gain


def centred(own_key, dims, scale, reach, pieces=(), held_as=jnp.bfloat16):
    values = scale * jax.random.normal(own_key, dims, jnp.float32)
    if pieces:
        values = values * shard_levels(own_key, dims, pieces, -0.22, 0.18)
    return jnp.clip(values, -reach, reach).astype(held_as)


def bell_draw_with(own_key, dims, width, reach, shards, heavy, held_as=jnp.bfloat16):
    result = width * jax.random.normal(own_key, dims, jnp.float32)
    if shards:
        result = result * shard_levels(own_key, dims, shards, -0.22, 0.18)
    return jnp.clip(raised(result, jax.random.fold_in(own_key, 3), *heavy), -reach, reach).astype(held_as)


def setup_inputs(seed: int = 0) -> dict:
    streams_of = jax.random.split(jax.random.key(seed), 17)
    tokens = centred(streams_of[0], (TOKENS, D), 1.0, 6.0, ((0, 32),))
    memory = centred(streams_of[1], (MEMS, MEM_LEN, D), 1.0, 6.0, ((0, 32),))
    segment_ids = draw_segment_ids(jax.random.fold_in(streams_of[16], 71), 0)
    page_map = draw_page_map(jax.random.fold_in(streams_of[16], 71), 0)
    mem_lengths = draw_mem_lengths(jax.random.fold_in(streams_of[16], 71), 0)
    gains = jnp.clip(1.0 + 0.18 * jax.random.normal(streams_of[5], (3, D), jnp.float32), 0.099609375, 1.8984375).astype(jnp.bfloat16)
    biases = centred(streams_of[6], (10, D), 0.5, 3.0, ((1, 32),))
    fc1_bias = centred(streams_of[7], (FF,), 0.5, 3.0, ((0, 32),))
    self_qkv = centred(streams_of[8], (3, D, D), (D // 2) ** -0.5, 0.25, ((1, 8), (2, 4)))
    self_out = centred(streams_of[9], (D, D), (D // 4) ** -0.5, 0.375, ((0, 8), (1, 4)))
    cross_q = centred(streams_of[10], (D, D), (D // 2) ** -0.5, 0.25, ((0, 8), (1, 4)))
    cross_kv = centred(streams_of[11], (2, D, D), (D // 2) ** -0.5, 0.25, ((1, 8), (2, 4)))
    cross_out = centred(streams_of[12], (D, D), (D // 16) ** -0.5, 0.75, ((0, 8), (1, 4)))
    fc1 = centred(streams_of[13], (D, FF), D ** -0.5, 0.1875, ((0, 8), (1, 4)))
    fc2 = centred(streams_of[14], (FF, D), (FF // 2) ** -0.5, 0.125, ((0, 8), (1, 4)))
    cotangent = bell_draw_with(streams_of[15], (TOKENS, D), 1.0, 6.0, ((0, 32),), (0, 1, 32, 2.75))
    return dict(tokens=tokens, memory=memory, segment_ids=segment_ids, page_map=page_map, mem_lengths=mem_lengths, gains=gains, biases=biases, fc1_bias=fc1_bias, self_qkv=self_qkv, self_out=self_out, cross_q=cross_q, cross_kv=cross_kv, cross_out=cross_out, fc1=fc1, fc2=fc2, cotangent=cotangent)


EPSILON = 1e-05
NEG_FILL = -1e+30
PRECISE = lax.Precision.HIGHEST

@jax.custom_vjp
def low(v):
    return lax.optimization_barrier(v.astype(jnp.bfloat16)).astype(jnp.float32)

@jax.custom_vjp
def low_back(v):
    return v

def low_keep(v):
    return (low(v), None)

def low_pass(kept, grad):
    return (grad,)

def back_keep(v):
    return (v, None)

def back_low(kept, grad):
    return (low(grad),)
low.defvjp(low_keep, low_pass)
low_back.defvjp(back_keep, back_low)

def layer_norm(values, gain_row, bias_row):
    centre = values - lax.optimization_barrier(jnp.mean(values, axis=-1, keepdims=True))
    spread = lax.optimization_barrier(jnp.mean(centre * centre, axis=-1, keepdims=True))
    return centre * lax.rsqrt(spread + EPSILON) * gain_row + bias_row

def attend(queries, keys, values, allowed):
    head_scale = 1.0 / math.sqrt(queries.shape[-1])
    raw_scores = jnp.einsum('bthd,bshd->bhts', queries, keys, precision=PRECISE) * head_scale
    scores = low_back(raw_scores)
    soft_weights = jax.nn.softmax(jnp.where(allowed[:, None], scores, NEG_FILL), axis=-1)
    mixed_heads = jnp.einsum('bhts,bshd->bthd', low(soft_weights), values, precision=PRECISE)
    return low_back(low(mixed_heads.reshape(-1, queries.shape[2] * queries.shape[3])))

def block_forward(params, block_data):
    gains, biases, fc1_bias, self_qkv, self_out, cross_q, cross_kv, cross_out, fc1, fc2 = params
    tokens, memory, segment_ids, page_map, mem_lengths, block_index = block_data
    rows_here = segment_ids.shape[0]
    row_len = segment_ids.shape[1]
    token_count = rows_here * row_len
    mem_count = memory.shape[0]
    mem_len = memory.shape[1]
    normed_one = low(layer_norm(tokens, gains[0], biases[0]))
    self_queries = low_back(low(jnp.dot(normed_one, self_qkv[0], precision=PRECISE) + biases[1]))
    self_keys = low_back(low(jnp.dot(normed_one, self_qkv[1], precision=PRECISE)))
    self_values = low_back(low(jnp.dot(normed_one, self_qkv[2], precision=PRECISE) + biases[2]))
    seg_flat = segment_ids.reshape(-1)
    positions = jnp.arange(token_count, dtype=jnp.int32)
    row_of = positions // row_len
    self_allowed = ((row_of[:, None] == row_of[None, :]) & (seg_flat[:, None] == seg_flat[None, :]) & (positions[None, :] <= positions[:, None]))[None]
    head_shape = (1, token_count, HEADS, HEAD_DIM)
    self_mixed = attend(self_queries.reshape(head_shape), self_keys.reshape(head_shape), self_values.reshape(head_shape), self_allowed)
    after_self = tokens + low_back(jnp.dot(self_mixed, self_out, precision=PRECISE) + biases[3])
    normed_two = low(layer_norm(after_self, gains[1], biases[4]))
    cross_queries = low_back(low(jnp.dot(normed_two, cross_q, precision=PRECISE) + biases[5]))
    mem_keys = low_back(low(jnp.einsum('mld,de->mle', memory, cross_kv[0], precision=PRECISE)))
    mem_values = low_back(low(jnp.einsum('mld,de->mle', memory, cross_kv[1], precision=PRECISE) + biases[6]))
    local_map = (page_map - block_index * mem_count).astype(jnp.int32)
    row_keys = mem_keys[local_map].reshape(rows_here, 2 * mem_len, HEADS, HEAD_DIM)
    row_values = mem_values[local_map].reshape(rows_here, 2 * mem_len, HEADS, HEAD_DIM)
    row_lengths = mem_lengths[local_map]
    key_positions = jnp.arange(2 * mem_len, dtype=jnp.int32)
    part_of = key_positions // mem_len
    index_of = key_positions % mem_len
    length_of = jnp.where(part_of[None, :] == 0, row_lengths[:, 0:1], row_lengths[:, 1:2])
    cross_allowed = (segment_ids[:, :, None] == part_of[None, None, :]) & (index_of[None, None, :] < length_of[:, None, :])
    cross_mixed = attend(cross_queries.reshape(rows_here, row_len, HEADS, HEAD_DIM), row_keys, row_values, cross_allowed)
    after_cross = after_self + low_back(jnp.dot(cross_mixed, cross_out, precision=PRECISE) + biases[7])
    normed_three = low(layer_norm(after_cross, gains[2], biases[8]))
    pre_act = low_back(jnp.dot(normed_three, fc1, precision=PRECISE) + fc1_bias)
    activated = low(jax.nn.gelu(pre_act, approximate=False))
    return after_cross + low_back(jnp.dot(activated, fc2, precision=PRECISE) + biases[9])

def reference(tokens, memory, segment_ids, page_map, mem_lengths, gains, biases, fc1_bias, self_qkv, self_out, cross_q, cross_kv, cross_out, fc1, fc2, cotangent):
    block_total = ROWS // ROWS_DEV
    block_tokens = ROWS_DEV * ROW_LEN
    params = tuple((weight.astype(jnp.float32) for weight in (gains, biases, fc1_bias, self_qkv, self_out, cross_q, cross_kv, cross_out, fc1, fc2)))
    token_blocks = tokens.astype(jnp.float32).reshape(block_total, block_tokens, D)
    memory_blocks = memory.astype(jnp.float32).reshape(block_total, MEM_DEV, MEM_LEN, D)
    integer_blocks = (segment_ids.reshape(block_total, ROWS_DEV, ROW_LEN), page_map.reshape(block_total, ROWS_DEV, 2), mem_lengths.reshape(block_total, MEM_DEV), jnp.arange(block_total, dtype=jnp.int32))
    stepper = jax.checkpoint(block_forward)

    def forward(token_part, memory_part, param_part):

        def visit_block(carried, block_items):
            return (carried, stepper(param_part, block_items))
        unused, outputs = lax.scan(visit_block, jnp.zeros((), jnp.float32), (token_part, memory_part) + integer_blocks)
        return outputs
    outputs, pullback = jax.vjp(forward, token_blocks, memory_blocks, params)
    grad_token_blocks, grad_memory_blocks, grad_params = pullback(cotangent.astype(jnp.float32).reshape(block_total, block_tokens, D))
    grad_gains, grad_biases, grad_fc1_bias, grad_self_qkv, grad_self_out, grad_cross_q, grad_cross_kv, grad_cross_out, grad_fc1, grad_fc2 = grad_params
    return (outputs.reshape(TOKENS, D).astype(jnp.bfloat16), grad_token_blocks.reshape(TOKENS, D).astype(jnp.bfloat16), grad_memory_blocks.reshape(MEMS, MEM_LEN, D).astype(jnp.bfloat16), grad_gains, grad_biases, grad_fc1_bias, grad_self_qkv, grad_self_out, grad_cross_q, grad_cross_kv, grad_cross_out, grad_fc1, grad_fc2)
```

```python
import functools
import math

import jax
import jax.numpy as jnp
from jax import lax
from jax.experimental import pallas as pl
from jax.experimental.pallas import tpu as pltpu
from jax.sharding import PartitionSpec as P

D = 1024
HEADS = 16
HEAD_DIM = 64
PAIRS = HEADS // 2

EPSILON = 1e-05
NEG_FILL = -1e30
LOG2E = math.log2(math.e)
SCALE = 1.0 / math.sqrt(HEAD_DIM)
AXES = ("wide", "narrow")

F32 = jnp.float32
BF16 = jnp.bfloat16


def layer_norm(values, gain_row, bias_row):
    centre = values - jnp.mean(values, axis=-1, keepdims=True)
    spread = jnp.mean(centre * centre, axis=-1, keepdims=True)
    return centre * lax.rsqrt(spread + EPSILON) * gain_row + bias_row


def gelu_exact(values):
    return jax.nn.gelu(values, approximate=False)


def dot_nt(a, b):
    return lax.dot_general(a, b, (((1,), (1,)), ((), ())), preferred_element_type=F32)


def dot_nn(a, b):
    return lax.dot_general(a, b, (((1,), (0,)), ((), ())), preferred_element_type=F32)


def dot_tn(a, b):
    return lax.dot_general(a, b, (((0,), (0,)), ((), ())), preferred_element_type=F32)


def two_heads(block):
    lane = lax.broadcasted_iota(jnp.int32, block.shape, 1)
    zero = jnp.zeros_like(block)
    return jnp.concatenate(
        (jnp.where(lane < HEAD_DIM, block, zero), jnp.where(lane < HEAD_DIM, zero, block)), axis=0
    )


def join_heads(both):
    half = both.shape[0] // 2
    lane = lax.broadcasted_iota(jnp.int32, (half, both.shape[1]), 1)
    return jnp.where(lane < HEAD_DIM, both[:half], both[half:])


def pair_forward(q2, k2, v2, valid):
    scores = dot_nt(k2, two_heads(q2)) * (SCALE * LOG2E)
    scores = jnp.where(valid, scores, NEG_FILL)
    top = jnp.max(scores, axis=0, keepdims=True)
    expo = jnp.exp2(scores - top)
    total = jnp.sum(expo, axis=0, keepdims=True)
    weights = (expo * (1.0 / total)).astype(BF16)
    mixed = join_heads(dot_tn(weights, v2)).astype(BF16)
    return mixed, top + jnp.log2(total)


def pair_backward(q2, k2, v2, do2, lse, valid):
    qq = two_heads(q2)
    dd = two_heads(do2)
    scores = dot_nt(k2, qq) * (SCALE * LOG2E)
    weights = jnp.where(valid, jnp.exp2(scores - lse), 0.0)
    grad_weights = dot_nt(v2, dd)
    inner = jnp.sum(weights * grad_weights, axis=0, keepdims=True)
    grad_scores = (weights * (grad_weights - inner)).astype(BF16)
    grad_v = dot_nn(weights.astype(BF16), dd).astype(BF16)
    grad_k = (dot_nn(grad_scores, qq) * SCALE).astype(BF16)
    grad_q = (join_heads(dot_tn(grad_scores, k2)) * SCALE).astype(BF16)
    return grad_q, grad_k, grad_v


def self_valid(seg_row, seg_col):
    length = seg_row.shape[-1]
    key = lax.broadcasted_iota(jnp.int32, (length, length), 0)
    tok = lax.broadcasted_iota(jnp.int32, (length, length), 1)
    one = (key <= tok) & (seg_row == seg_col)
    return jnp.concatenate((one, one), axis=1)


def self_fwd_kernel(seg_row, seg_col, q_ref, k_ref, v_ref, o_ref, lse_ref):
    valid = self_valid(seg_row[0], seg_col[0])
    for h in range(PAIRS):
        cut = slice(128 * h, 128 * h + 128)
        mixed, lse = pair_forward(q_ref[:, cut], k_ref[:, cut], v_ref[:, cut], valid)
        o_ref[:, cut] = mixed
        lse_ref[0, h : h + 1, :] = lse


def self_bwd_kernel(seg_row, seg_col, q_ref, k_ref, v_ref, do_ref, lse_ref, dq_ref, dk_ref, dv_ref):
    valid = self_valid(seg_row[0], seg_col[0])
    for h in range(PAIRS):
        cut = slice(128 * h, 128 * h + 128)
        gq, gk, gv = pair_backward(
            q_ref[:, cut], k_ref[:, cut], v_ref[:, cut], do_ref[:, cut],
            lse_ref[0, h : h + 1, :], valid,
        )
        dq_ref[:, cut] = gq
        dk_ref[:, cut] = gk
        dv_ref[:, cut] = gv


def self_specs(row_len):
    seg = [
        pl.BlockSpec((1, 1, row_len), lambda r: (r, 0, 0)),
        pl.BlockSpec((1, row_len, 1), lambda r: (r, 0, 0)),
    ]
    row = pl.BlockSpec((row_len, D), lambda r: (r, 0))
    lse = pl.BlockSpec((1, PAIRS, 2 * row_len), lambda r: (r, 0, 0))
    return seg, row, lse


def self_forward(seg, queries, keys, values):
    rows, row_len = seg.shape
    seg_specs, row, lse = self_specs(row_len)
    return pl.pallas_call(
        self_fwd_kernel,
        grid=(rows,),
        in_specs=seg_specs + [row] * 3,
        out_specs=[row, lse],
        out_shape=[
            jax.ShapeDtypeStruct(queries.shape, BF16),
            jax.ShapeDtypeStruct((rows, PAIRS, 2 * row_len), F32),
        ],
        cost_estimate=pl.CostEstimate(flops=rows * 2 * 10**8, bytes_accessed=2 * 10**6, transcendentals=rows * 3 * 10**5),
        name="self_forward",
    )(seg[:, None, :], seg[:, :, None], queries, keys, values)


def self_backward(seg, queries, keys, values, grad_mixed, lse_rows):
    rows, row_len = seg.shape
    seg_specs, row, lse = self_specs(row_len)
    return pl.pallas_call(
        self_bwd_kernel,
        grid=(rows,),
        in_specs=seg_specs + [row] * 4 + [lse],
        out_specs=[row] * 3,
        out_shape=[jax.ShapeDtypeStruct(queries.shape, BF16)] * 3,
        cost_estimate=pl.CostEstimate(flops=rows * 5 * 10**8, bytes_accessed=4 * 10**6, transcendentals=rows * 3 * 10**5),
        name="self_backward",
    )(seg[:, None, :], seg[:, :, None], queries, keys, values, grad_mixed, lse_rows)


def cross_fwd_kernel(map_ref, len_ref, seg_row, seg_col, q_ref, k_ref, v_ref, o_ref, lse_ref):
    r, page = pl.program_id(0), pl.program_id(1)
    keys, toks = k_ref.shape[1], q_ref.shape[0]
    valid = lax.broadcasted_iota(jnp.int32, (keys, 2 * toks), 0) < len_ref[r * 2 + page]
    mine_col = (seg_col[0] == page) | (page == 0)
    mine_row = (seg_row[0] == page) | (page == 0)
    mine_row = jnp.concatenate((mine_row, mine_row), axis=1)
    for h in range(PAIRS):
        cut = slice(128 * h, 128 * h + 128)
        mixed, lse = pair_forward(q_ref[:, cut], k_ref[0, :, cut], v_ref[0, :, cut], valid)
        o_ref[:, cut] = jnp.where(mine_col, mixed, o_ref[:, cut])
        lse_ref[0, h : h + 1, :] = jnp.where(mine_row, lse, lse_ref[0, h : h + 1, :])


def cross_bwd_kernel(
    map_ref, len_ref, seg_row, seg_col, q_ref, k_ref, v_ref, do_ref, lse_ref, dq_ref, dk_ref, dv_ref
):
    r, page = pl.program_id(0), pl.program_id(1)
    keys, toks = k_ref.shape[1], q_ref.shape[0]
    valid = lax.broadcasted_iota(jnp.int32, (keys, 2 * toks), 0) < len_ref[r * 2 + page]
    mine_col = (seg_col[0] == page) | (page == 0)
    mine_row = seg_row[0] == page
    mine_row = jnp.concatenate((mine_row, mine_row), axis=1)
    for h in range(PAIRS):
        cut = slice(128 * h, 128 * h + 128)
        lse = jnp.where(mine_row, lse_ref[0, h : h + 1, :], -NEG_FILL)
        gq, gk, gv = pair_backward(
            q_ref[:, cut], k_ref[0, :, cut], v_ref[0, :, cut], do_ref[:, cut], lse, valid
        )
        dq_ref[:, cut] = jnp.where(mine_col, gq, dq_ref[:, cut])
        dk_ref[0, :, cut] = gk
        dv_ref[0, :, cut] = gv


def cross_specs(row_len, mem_len):
    seg = [
        pl.BlockSpec((1, 1, row_len), lambda r, p, *_: (r, 0, 0)),
        pl.BlockSpec((1, row_len, 1), lambda r, p, *_: (r, 0, 0)),
    ]
    row = pl.BlockSpec((row_len, D), lambda r, p, *_: (r, 0))
    mem = pl.BlockSpec((1, mem_len, D), lambda r, p, mp, ln: (mp[r * 2 + p], 0, 0))
    lse = pl.BlockSpec((1, PAIRS, 2 * row_len), lambda r, p, *_: (r, 0, 0))
    return seg, row, mem, lse


CROSS_PARAMS = pltpu.CompilerParams(
    dimension_semantics=("arbitrary", "arbitrary"), vmem_limit_bytes=40 * 2**20
)


def cross_forward(local_map, lengths, seg, queries, keys, values):
    rows, row_len = seg.shape
    mem_len = keys.shape[1]
    seg_specs, row, mem, lse = cross_specs(row_len, mem_len)
    return pl.pallas_call(
        cross_fwd_kernel,
        grid_spec=pltpu.PrefetchScalarGridSpec(
            num_scalar_prefetch=2,
            grid=(rows, 2),
            in_specs=seg_specs + [row, mem, mem],
            out_specs=[row, lse],
        ),
        out_shape=[
            jax.ShapeDtypeStruct(queries.shape, BF16),
            jax.ShapeDtypeStruct((rows, PAIRS, 2 * row_len), F32),
        ],
        compiler_params=CROSS_PARAMS,
        cost_estimate=pl.CostEstimate(flops=5 * 10**9, bytes_accessed=11 * 10**6, transcendentals=5 * 10**6),
        name="cross_forward",
    )(local_map, lengths, seg[:, None, :], seg[:, :, None], queries, keys, values)


def cross_backward(local_map, lengths, seg, queries, keys, values, grad_mixed, lse_rows):
    rows, row_len = seg.shape
    mem_len = keys.shape[1]
    seg_specs, row, mem, lse = cross_specs(row_len, mem_len)
    return pl.pallas_call(
        cross_bwd_kernel,
        grid_spec=pltpu.PrefetchScalarGridSpec(
            num_scalar_prefetch=2,
            grid=(rows, 2),
            in_specs=seg_specs + [row, mem, mem, row, lse],
            out_specs=[row, mem, mem],
        ),
        out_shape=[
            jax.ShapeDtypeStruct(queries.shape, BF16),
            jax.ShapeDtypeStruct(keys.shape, BF16),
            jax.ShapeDtypeStruct(values.shape, BF16),
        ],
        compiler_params=CROSS_PARAMS,
        cost_estimate=pl.CostEstimate(flops=12 * 10**9, bytes_accessed=22 * 10**6, transcendentals=5 * 10**6),
        name="cross_backward",
    )(local_map, lengths, seg[:, None, :], seg[:, :, None], queries, keys, values, grad_mixed, lse_rows)


class Grid:
    def __init__(self, wide, narrow):
        self.wide, self.narrow, self.ring = wide, narrow, wide // 2
        moves = {
            "z": lambda w, n: ((w + 2) % wide, n),
            "x": lambda w, n: (w ^ 1, n),
            "y": lambda w, n: (w, n ^ 2),
            "c": lambda w, n: (w, n ^ 1),
        }
        self.perms = {}
        for name, move in moves.items():
            pairs = []
            for w in range(wide):
                for n in range(narrow):
                    w2, n2 = move(w, n)
                    pairs.append((w * narrow + n, w2 * narrow + n2))
            self.perms[name] = pairs

    def send(self, name, array):
        return lax.ppermute(array, AXES, self.perms[name])


def assemble_kernel(labels, ring, place, *refs):
    pieces, whole, sems = refs[:-2], refs[-2], refs[-1]
    z, x, y, c = place[0], place[1], place[2], place[3]
    cols = pieces[0].shape[-1]
    copies = []
    for piece, piece_labels in zip(pieces, labels):
        for i, (dz, dx, dy, dc) in enumerate(piece_labels):
            row = 2 * lax.rem(z + (ring - dz), ring) + (x + dx - 2 * x * dx)
            col = 2 * (y + dy - 2 * y * dy) + (c + dc - 2 * c * dc)
            copies.append(
                pltpu.make_async_copy(
                    piece.at[i],
                    whole.at[:, row, :, pl.ds(pl.multiple_of(col * cols, 128), cols)],
                    sems.at[len(copies)],
                )
            )
    for copy in copies:
        copy.start()
    for copy in copies:
        copy.wait()


def gather_whole(grid, place, shard, order):
    g, rows, cols = shard.shape
    parts = [([(0, 0, 0, 0)], shard[None])]
    for stage in order + "c":
        if stage == "z":
            if len(parts) > 1:
                labels = [label for ls, _ in parts for label in ls]
                parts = [(labels, jnp.concatenate([a for _, a in parts], axis=0))]
            (labels, array), = parts
            ring = [(labels, array)]
            for step in range(1, grid.ring):
                array = grid.send("z", array)
                ring.append(([(step, dx, dy, dc) for _, dx, dy, dc in labels], array))
            if order[0] == "z":
                ring = [([l for ls, _ in ring for l in ls], jnp.concatenate([a for _, a in ring], axis=0))]
            parts = ring
        else:
            axis = "zxyc".index(stage)
            new = []
            for labels, array in parts:
                far = [tuple(1 if i == axis else v for i, v in enumerate(l)) for l in labels]
                new.append((far, grid.send(stage, array)))
            parts = parts + new
    n_blocks = grid.wide * grid.narrow
    whole = pl.pallas_call(
        functools.partial(assemble_kernel, [labels for labels, _ in parts], grid.ring),
        in_specs=[pl.BlockSpec(memory_space=pltpu.SMEM)] + [pl.BlockSpec(memory_space=pl.ANY)] * len(parts),
        out_specs=pl.BlockSpec(memory_space=pltpu.VMEM),
        out_shape=jax.ShapeDtypeStruct((g, grid.wide, rows, grid.narrow * cols), shard.dtype),
        compiler_params=pltpu.CompilerParams(vmem_limit_bytes=32 * 2**20),
        scratch_shapes=[pltpu.SemaphoreType.DMA((n_blocks,))],
        cost_estimate=pl.CostEstimate(flops=0, bytes_accessed=2 * n_blocks * shard.size * 2, transcendentals=0),
        name="assemble",
    )(place, *[array for _, array in parts])
    return whole.reshape(g, grid.wide * rows, grid.narrow * cols)


def reduce_to_owner(grid, place, columns, rows, order):
    z, x, y, c = place[0], place[1], place[2], place[3]

    def split(term):
        g, _, cols = term.shape
        return term.reshape(g, grid.ring, 2, rows, cols)

    def row_half(term, index):
        return lax.dynamic_index_in_dim(term, index, 2, keepdims=False)

    here, there = 2 * y + c, 2 * (1 - y) + c
    far = [columns(2 * y + (1 - c)).astype(BF16), columns(2 * (1 - y) + (1 - c)).astype(BF16)]
    from_c = [grid.send("c", f) for f in far]
    keep = columns(here) + from_c[0].astype(F32)
    other = columns(there) + from_c[1].astype(F32)
    if order == "yx":
        keep = keep + grid.send("y", other.astype(BF16)).astype(F32)
        keep = split(keep)
        from_x = grid.send("x", row_half(keep, 1 - x).astype(BF16))
        mine = row_half(keep, x) + from_x.astype(F32)
    else:
        keep, other = split(keep), split(other)
        from_x = grid.send(
            "x", jnp.stack((row_half(keep, 1 - x), row_half(other, 1 - x))).astype(BF16)
        ).astype(F32)
        mine = row_half(keep, x) + from_x[0]
        other = row_half(other, x) + from_x[1]
        mine = mine + grid.send("y", other.astype(BF16)).astype(F32)

    def chunk(step):
        index = lax.rem(z + (grid.ring - step), grid.ring)
        return lax.dynamic_index_in_dim(mine, index, 1, keepdims=False)

    total = chunk(1)
    for step in range(2, grid.ring + 1):
        total = chunk(step % grid.ring) + grid.send("z", total.astype(BF16)).astype(F32)
    return total


def reduce_small(grid, place, terms):
    z, x, y, c = place[0], place[1], place[2], place[3]
    mine = terms.reshape(grid.ring, 2, 2, 2, -1)
    for name, axis, at in (("c", 3, c), ("y", 2, y), ("x", 1, x)):
        far = lax.dynamic_index_in_dim(mine, 1 - at, axis, keepdims=False)
        mine = lax.dynamic_index_in_dim(mine, at, axis, keepdims=False) + grid.send(name, far)

    def chunk(step):
        return lax.dynamic_index_in_dim(mine, lax.rem(z + (grid.ring - step), grid.ring), 0, keepdims=False)

    total = chunk(1)
    for step in range(2, grid.ring + 1):
        total = chunk(step % grid.ring) + grid.send("z", total)
    return total


def columns_of(a, d, spec, grid):
    cols = d.shape[-1] // grid.narrow

    def term(n):
        cut = lax.dynamic_slice_in_dim(d, n * cols, cols, axis=d.ndim - 1)
        out = jnp.einsum(spec, a, cut, preferred_element_type=F32)
        return out if out.ndim == 3 else out[None]

    return term


def local(
    grid,
    tokens,
    memory,
    segment_ids,
    page_map,
    mem_lengths,
    gains,
    biases,
    fc1_bias,
    self_qkv,
    self_out,
    cross_q,
    cross_kv,
    cross_out,
    fc1,
    fc2,
    cotangent,
):
    wide_at, narrow_at = lax.axis_index("wide"), lax.axis_index("narrow")
    place = jnp.stack((wide_at // 2, wide_at % 2, narrow_at // 2, narrow_at % 2)).astype(jnp.int32)
    devices = grid.wide * grid.narrow
    token_count = tokens.shape[0]
    mem_count = memory.shape[0]

    small = jnp.concatenate((gains.reshape(-1), biases.reshape(-1), fc1_bias))
    small_all = lax.all_gather(small[None, None], AXES, axis=1, tiled=True)[0].astype(F32)
    n_gain, n_bias = gains.size, biases.size
    gain_full = small_all[:, :n_gain].reshape(devices, 3, -1).transpose(1, 0, 2).reshape(3, D)
    bias_full = (
        small_all[:, n_gain : n_gain + n_bias].reshape(devices, 10, -1).transpose(1, 0, 2).reshape(10, D)
    )
    fc1_bias_full = small_all[:, n_gain + n_bias :].reshape(-1)

    gather = functools.partial(gather_whole, grid, place)
    w_qkv = gather(self_qkv, "zyx")
    w_ckv = gather(cross_kv, "xyz")
    w_so = gather(self_out[None], "yxz")[0]
    w_cq = gather(cross_q[None], "yxz")[0]
    w_co = gather(cross_out[None], "zxy")[0]
    w_fc1 = gather(fc1[None], "zxy")[0]
    w_fc2 = gather(fc2[None], "zyx")[0]

    token_full = tokens.astype(F32)
    hidden_one, norm_one_back = jax.vjp(layer_norm, token_full, gain_full[0], bias_full[0])
    normed_one = hidden_one.astype(BF16)
    projected = jnp.einsum("td,kde->kte", normed_one, w_qkv, preferred_element_type=F32)
    self_queries = (projected[0] + bias_full[1]).astype(BF16)
    self_keys = projected[1].astype(BF16)
    self_values = (projected[2] + bias_full[2]).astype(BF16)
    self_mixed, self_lse = self_forward(segment_ids, self_queries, self_keys, self_values)
    after_self = token_full + jnp.dot(self_mixed, w_so, preferred_element_type=F32) + bias_full[3]

    hidden_two, norm_two_back = jax.vjp(layer_norm, after_self, gain_full[1], bias_full[4])
    normed_two = hidden_two.astype(BF16)
    cross_queries = (
        jnp.dot(normed_two, w_cq, preferred_element_type=F32) + bias_full[5]
    ).astype(BF16)
    mem_keys = jnp.einsum("mld,de->mle", memory, w_ckv[0], preferred_element_type=F32).astype(BF16)
    mem_values = (
        jnp.einsum("mld,de->mle", memory, w_ckv[1], preferred_element_type=F32) + bias_full[6]
    ).astype(BF16)
    first_mem = lax.axis_index(AXES) * mem_count
    local_map = (page_map - first_mem).reshape(-1).astype(jnp.int32)
    picks = local_map[:, None] == jnp.arange(mem_count, dtype=jnp.int32)[None, :]
    row_lengths = jnp.sum(jnp.where(picks, mem_lengths[None, :], 0), axis=-1).astype(jnp.int32)
    cross_mixed, cross_lse = cross_forward(
        local_map, row_lengths, segment_ids, cross_queries, mem_keys, mem_values
    )
    after_cross = (
        after_self + jnp.dot(cross_mixed, w_co, preferred_element_type=F32) + bias_full[7]
    )

    hidden_three, norm_three_back = jax.vjp(layer_norm, after_cross, gain_full[2], bias_full[8])
    normed_three = hidden_three.astype(BF16)
    pre_act = jnp.dot(normed_three, w_fc1, preferred_element_type=F32) + fc1_bias_full
    activated_full, gelu_back = jax.vjp(gelu_exact, pre_act)
    activated = activated_full.astype(BF16)
    layer_out = (
        after_cross + jnp.dot(activated, w_fc2, preferred_element_type=F32) + bias_full[9]
    ).astype(BF16)

    settle = functools.partial(reduce_to_owner, grid, place)
    grad_out = cotangent.astype(F32)
    fc2_shard = settle(
        columns_of(activated, cotangent, "tf,td->fd", grid), fc2.shape[0], "yx"
    )
    grad_bias_nine = jnp.sum(grad_out, axis=0)
    grad_act = jnp.einsum("td,fd->tf", cotangent, w_fc2, preferred_element_type=F32)
    grad_pre = gelu_back(grad_act)[0].astype(BF16)
    fc1_shard = settle(
        columns_of(normed_three, grad_pre, "td,tf->df", grid), fc1.shape[0], "xy"
    )
    grad_fc1_bias = jnp.sum(grad_pre, axis=0, dtype=F32)
    grad_normed_three = jnp.einsum("tf,df->td", grad_pre, w_fc1, preferred_element_type=F32)
    grad_from_three, grad_gain_three, grad_bias_eight = norm_three_back(grad_normed_three)
    grad_after_cross = grad_out + grad_from_three

    grad_branch_two = grad_after_cross.astype(BF16)
    cross_out_shard = settle(
        columns_of(cross_mixed, grad_branch_two, "td,te->de", grid), cross_out.shape[0], "yx"
    )
    grad_bias_seven = jnp.sum(grad_branch_two, axis=0, dtype=F32)
    grad_cross_mixed = jnp.einsum(
        "te,de->td", grad_branch_two, w_co, preferred_element_type=F32
    ).astype(BF16)
    grad_cq, grad_ck, grad_cv = cross_backward(
        local_map, row_lengths, segment_ids, cross_queries, mem_keys, mem_values,
        grad_cross_mixed, cross_lse,
    )
    grad_bias_five = jnp.sum(grad_cq, axis=0, dtype=F32)
    grad_bias_six = jnp.sum(grad_cv, axis=(0, 1), dtype=F32)
    cross_q_shard = settle(
        columns_of(normed_two, grad_cq, "td,te->de", grid), cross_q.shape[0], "yx"
    )
    cross_k_shard = settle(
        columns_of(memory, grad_ck, "mld,mle->de", grid), cross_q.shape[0], "xy"
    )
    cross_v_shard = settle(
        columns_of(memory, grad_cv, "mld,mle->de", grid), cross_q.shape[0], "yx"
    )
    grad_normed_two = jnp.einsum("te,de->td", grad_cq, w_cq, preferred_element_type=F32)
    grad_from_two, grad_gain_two, grad_bias_four = norm_two_back(grad_normed_two)
    grad_after_self = grad_after_cross + grad_from_two

    grad_branch_one = grad_after_self.astype(BF16)
    self_out_shard = settle(
        columns_of(self_mixed, grad_branch_one, "td,te->de", grid), self_out.shape[0], "yx"
    )
    grad_bias_three = jnp.sum(grad_branch_one, axis=0, dtype=F32)
    grad_self_mixed = jnp.einsum(
        "te,de->td", grad_branch_one, w_so, preferred_element_type=F32
    ).astype(BF16)
    grad_proj = self_backward(
        segment_ids, self_queries, self_keys, self_values, grad_self_mixed, self_lse
    )
    grad_proj = jnp.stack(grad_proj)
    qkv_shard = settle(
        columns_of(normed_one, grad_proj, "td,kte->kde", grid), self_qkv.shape[1], "xy"
    )
    grad_bias_one = jnp.sum(grad_proj[0], axis=0, dtype=F32)
    grad_bias_two = jnp.sum(grad_proj[2], axis=0, dtype=F32)
    grad_normed_one = jnp.einsum("kte,kde->td", grad_proj, w_qkv, preferred_element_type=F32)
    grad_from_one, grad_gain_one, grad_bias_zero = norm_one_back(grad_normed_one)
    grad_tokens = (grad_after_self + grad_from_one).astype(BF16)

    grad_memory = (
        jnp.einsum("mle,de->mld", grad_ck, w_ckv[0], preferred_element_type=F32)
        + jnp.einsum("mle,de->mld", grad_cv, w_ckv[1], preferred_element_type=F32)
    ).astype(BF16)

    def by_device(rows):
        array = jnp.stack(rows)
        return array.reshape(len(rows), devices, -1).transpose(1, 0, 2).reshape(devices, -1)

    small_grads = jnp.concatenate(
        (
            by_device((grad_gain_one, grad_gain_two, grad_gain_three)),
            by_device(
                (
                    grad_bias_zero,
                    grad_bias_one,
                    grad_bias_two,
                    grad_bias_three,
                    grad_bias_four,
                    grad_bias_five,
                    grad_bias_six,
                    grad_bias_seven,
                    grad_bias_eight,
                    grad_bias_nine,
                )
            ),
            by_device((grad_fc1_bias,)),
        ),
        axis=1,
    )
    small_shard = reduce_small(grid, place, small_grads)
    return (
        layer_out,
        grad_tokens,
        grad_memory,
        small_shard[:n_gain].reshape(gains.shape),
        small_shard[n_gain : n_gain + n_bias].reshape(biases.shape),
        small_shard[n_gain + n_bias :],
        qkv_shard,
        self_out_shard[0],
        cross_q_shard[0],
        jnp.concatenate((cross_k_shard, cross_v_shard), axis=0),
        cross_out_shard[0],
        fc1_shard[0],
        fc2_shard[0],
    )


def solution(mesh):
    grid = Grid(mesh.shape["wide"], mesh.shape["narrow"])
    in_specs = (
        P(AXES, None),
        P(AXES, None, None),
        P(AXES, None),
        P(AXES, None),
        P(AXES),
        P(None, AXES),
        P(None, AXES),
        P(AXES),
        P(None, "wide", "narrow"),
        P("wide", "narrow"),
        P("wide", "narrow"),
        P(None, "wide", "narrow"),
        P("wide", "narrow"),
        P("wide", "narrow"),
        P("wide", "narrow"),
        P(AXES, None),
    )
    out_specs = (
        P(AXES, None),
        P(AXES, None),
        P(AXES, None, None),
        P(None, AXES),
        P(None, AXES),
        P(AXES),
        P(None, "wide", "narrow"),
        P("wide", "narrow"),
        P("wide", "narrow"),
        P(None, "wide", "narrow"),
        P("wide", "narrow"),
        P("wide", "narrow"),
        P("wide", "narrow"),
    )
    return jax.shard_map(
        functools.partial(local, grid), mesh=mesh, in_specs=in_specs, out_specs=out_specs, check_vma=False
    )
```

```python
import functools
import math

import jax
import jax.numpy as jnp
from jax import lax
from jax.experimental import pallas as pl
from jax.experimental.pallas import tpu as pltpu
from jax.sharding import PartitionSpec as P

D = 1024
HEADS = 16
HEAD_DIM = 64
PAIRS = HEADS // 2

EPSILON = 1e-05
NEG_FILL = -1e30
LOG2E = math.log2(math.e)
SCALE = 1.0 / math.sqrt(HEAD_DIM)
AXES = ("wide", "narrow")

F32 = jnp.float32
BF16 = jnp.bfloat16


def dot_nt(a, b):
    return lax.dot_general(a, b, (((1,), (1,)), ((), ())), preferred_element_type=F32)


def dot_nn(a, b):
    return lax.dot_general(a, b, (((1,), (0,)), ((), ())), preferred_element_type=F32)


def dot_tn(a, b):
    return lax.dot_general(a, b, (((0,), (0,)), ((), ())), preferred_element_type=F32)


def two_heads(block):
    lane = lax.broadcasted_iota(jnp.int32, block.shape, 1)
    zero = jnp.zeros_like(block)
    return jnp.concatenate(
        (jnp.where(lane < HEAD_DIM, block, zero), jnp.where(lane < HEAD_DIM, zero, block)), axis=0
    )


def join_heads(both):
    half = both.shape[0] // 2
    lane = lax.broadcasted_iota(jnp.int32, (half, both.shape[1]), 1)
    return jnp.where(lane < HEAD_DIM, both[:half], both[half:])


def pair_forward(q2, k2, v2, valid):
    scores = dot_nt(k2, two_heads(q2)) * (SCALE * LOG2E)
    scores = jnp.where(valid, scores, NEG_FILL)
    top = jnp.max(scores, axis=0, keepdims=True)
    expo = jnp.exp2(scores - top)
    total = jnp.sum(expo, axis=0, keepdims=True)
    weights = (expo * (1.0 / total)).astype(BF16)
    mixed = join_heads(dot_tn(weights, v2)).astype(BF16)
    return mixed, top + jnp.log2(total)


def pair_backward(q2, k2, v2, do2, lse, valid):
    qq = two_heads(q2)
    dd = two_heads(do2)
    scores = dot_nt(k2, qq) * (SCALE * LOG2E)
    weights = jnp.where(valid, jnp.exp2(scores - lse), 0.0)
    grad_weights = dot_nt(v2, dd)
    inner = jnp.sum(weights * grad_weights, axis=0, keepdims=True)
    grad_scores = (weights * (grad_weights - inner)).astype(BF16)
    grad_v = dot_nn(weights.astype(BF16), dd).astype(BF16)
    grad_k = (dot_nn(grad_scores, qq) * SCALE).astype(BF16)
    grad_q = (join_heads(dot_tn(grad_scores, k2)) * SCALE).astype(BF16)
    return grad_q, grad_k, grad_v


def self_valid(seg_row, seg_col):
    length = seg_row.shape[-1]
    key = lax.broadcasted_iota(jnp.int32, (length, length), 0)
    tok = lax.broadcasted_iota(jnp.int32, (length, length), 1)
    one = (key <= tok) & (seg_row == seg_col)
    return jnp.concatenate((one, one), axis=1)


def self_fwd_kernel(seg_row, seg_col, q_ref, k_ref, v_ref, o_ref, lse_ref):
    valid = self_valid(seg_row[0], seg_col[0])
    for h in range(PAIRS):
        cut = slice(128 * h, 128 * h + 128)
        mixed, lse = pair_forward(q_ref[:, cut], k_ref[:, cut], v_ref[:, cut], valid)
        o_ref[:, cut] = mixed
        lse_ref[0, h : h + 1, :] = lse


def self_bwd_kernel(seg_row, seg_col, q_ref, k_ref, v_ref, do_ref, lse_ref, dq_ref, dk_ref, dv_ref):
    valid = self_valid(seg_row[0], seg_col[0])
    for h in range(PAIRS):
        cut = slice(128 * h, 128 * h + 128)
        gq, gk, gv = pair_backward(
            q_ref[:, cut], k_ref[:, cut], v_ref[:, cut], do_ref[:, cut],
            lse_ref[0, h : h + 1, :], valid,
        )
        dq_ref[:, cut] = gq
        dk_ref[:, cut] = gk
        dv_ref[:, cut] = gv


def self_specs(row_len):
    seg = [
        pl.BlockSpec((1, 1, row_len), lambda r: (r, 0, 0)),
        pl.BlockSpec((1, row_len, 1), lambda r: (r, 0, 0)),
    ]
    row = pl.BlockSpec((row_len, D), lambda r: (r, 0))
    lse = pl.BlockSpec((1, PAIRS, 2 * row_len), lambda r: (r, 0, 0))
    return seg, row, lse


def self_forward(seg, queries, keys, values):
    rows, row_len = seg.shape
    seg_specs, row, lse = self_specs(row_len)
    return pl.pallas_call(
        self_fwd_kernel,
        grid=(rows,),
        in_specs=seg_specs + [row] * 3,
        out_specs=[row, lse],
        out_shape=[
            jax.ShapeDtypeStruct(queries.shape, BF16),
            jax.ShapeDtypeStruct((rows, PAIRS, 2 * row_len), F32),
        ],
        cost_estimate=pl.CostEstimate(flops=rows * 2 * 10**8, bytes_accessed=2 * 10**6, transcendentals=rows * 3 * 10**5),
        name="self_forward",
    )(seg[:, None, :], seg[:, :, None], queries, keys, values)


def self_backward(seg, queries, keys, values, grad_mixed, lse_rows):
    rows, row_len = seg.shape
    seg_specs, row, lse = self_specs(row_len)
    return pl.pallas_call(
        self_bwd_kernel,
        grid=(rows,),
        in_specs=seg_specs + [row] * 4 + [lse],
        out_specs=[row] * 3,
        out_shape=[jax.ShapeDtypeStruct(queries.shape, BF16)] * 3,
        cost_estimate=pl.CostEstimate(flops=rows * 5 * 10**8, bytes_accessed=4 * 10**6, transcendentals=rows * 3 * 10**5),
        name="self_backward",
    )(seg[:, None, :], seg[:, :, None], queries, keys, values, grad_mixed, lse_rows)


def cross_fwd_kernel(map_ref, len_ref, seg_row, seg_col, q_ref, k_ref, v_ref, o_ref, lse_ref):
    r, page = pl.program_id(0), pl.program_id(1)
    keys, toks = k_ref.shape[1], q_ref.shape[0]
    valid = lax.broadcasted_iota(jnp.int32, (keys, 2 * toks), 0) < len_ref[r * 2 + page]
    mine_col = (seg_col[0] == page) | (page == 0)
    mine_row = (seg_row[0] == page) | (page == 0)
    mine_row = jnp.concatenate((mine_row, mine_row), axis=1)
    for h in range(PAIRS):
        cut = slice(128 * h, 128 * h + 128)
        mixed, lse = pair_forward(q_ref[:, cut], k_ref[0, :, cut], v_ref[0, :, cut], valid)
        o_ref[:, cut] = jnp.where(mine_col, mixed, o_ref[:, cut])
        lse_ref[0, h : h + 1, :] = jnp.where(mine_row, lse, lse_ref[0, h : h + 1, :])


def cross_bwd_kernel(
    map_ref, len_ref, seg_row, seg_col, q_ref, k_ref, v_ref, do_ref, lse_ref, dq_ref, dk_ref, dv_ref
):
    r, page = pl.program_id(0), pl.program_id(1)
    keys, toks = k_ref.shape[1], q_ref.shape[0]
    valid = lax.broadcasted_iota(jnp.int32, (keys, 2 * toks), 0) < len_ref[r * 2 + page]
    mine_col = (seg_col[0] == page) | (page == 0)
    mine_row = seg_row[0] == page
    mine_row = jnp.concatenate((mine_row, mine_row), axis=1)
    for h in range(PAIRS):
        cut = slice(128 * h, 128 * h + 128)
        lse = jnp.where(mine_row, lse_ref[0, h : h + 1, :], -NEG_FILL)
        gq, gk, gv = pair_backward(
            q_ref[:, cut], k_ref[0, :, cut], v_ref[0, :, cut], do_ref[:, cut], lse, valid
        )
        dq_ref[:, cut] = jnp.where(mine_col, gq, dq_ref[:, cut])
        dk_ref[0, :, cut] = gk
        dv_ref[0, :, cut] = gv


def cross_specs(row_len, mem_len):
    seg = [
        pl.BlockSpec((1, 1, row_len), lambda r, p, *_: (r, 0, 0)),
        pl.BlockSpec((1, row_len, 1), lambda r, p, *_: (r, 0, 0)),
    ]
    row = pl.BlockSpec((row_len, D), lambda r, p, *_: (r, 0))
    mem = pl.BlockSpec((1, mem_len, D), lambda r, p, mp, ln: (mp[r * 2 + p], 0, 0))
    lse = pl.BlockSpec((1, PAIRS, 2 * row_len), lambda r, p, *_: (r, 0, 0))
    return seg, row, mem, lse


CROSS_PARAMS = pltpu.CompilerParams(
    dimension_semantics=("arbitrary", "arbitrary"), vmem_limit_bytes=40 * 2**20
)


def cross_forward(local_map, lengths, seg, queries, keys, values):
    rows, row_len = seg.shape
    mem_len = keys.shape[1]
    seg_specs, row, mem, lse = cross_specs(row_len, mem_len)
    return pl.pallas_call(
        cross_fwd_kernel,
        grid_spec=pltpu.PrefetchScalarGridSpec(
            num_scalar_prefetch=2,
            grid=(rows, 2),
            in_specs=seg_specs + [row, mem, mem],
            out_specs=[row, lse],
        ),
        out_shape=[
            jax.ShapeDtypeStruct(queries.shape, BF16),
            jax.ShapeDtypeStruct((rows, PAIRS, 2 * row_len), F32),
        ],
        compiler_params=CROSS_PARAMS,
        cost_estimate=pl.CostEstimate(flops=5 * 10**9, bytes_accessed=11 * 10**6, transcendentals=5 * 10**6),
        name="cross_forward",
    )(local_map, lengths, seg[:, None, :], seg[:, :, None], queries, keys, values)


def cross_backward(local_map, lengths, seg, queries, keys, values, grad_mixed, lse_rows):
    rows, row_len = seg.shape
    mem_len = keys.shape[1]
    seg_specs, row, mem, lse = cross_specs(row_len, mem_len)
    return pl.pallas_call(
        cross_bwd_kernel,
        grid_spec=pltpu.PrefetchScalarGridSpec(
            num_scalar_prefetch=2,
            grid=(rows, 2),
            in_specs=seg_specs + [row, mem, mem, row, lse],
            out_specs=[row, mem, mem],
        ),
        out_shape=[
            jax.ShapeDtypeStruct(queries.shape, BF16),
            jax.ShapeDtypeStruct(keys.shape, BF16),
            jax.ShapeDtypeStruct(values.shape, BF16),
        ],
        compiler_params=CROSS_PARAMS,
        cost_estimate=pl.CostEstimate(flops=12 * 10**9, bytes_accessed=22 * 10**6, transcendentals=5 * 10**6),
        name="cross_backward",
    )(local_map, lengths, seg[:, None, :], seg[:, :, None], queries, keys, values, grad_mixed, lse_rows)


SMALL_ROWS = 16


def tie(values, *after):
    return lax.optimization_barrier((values, after))[0]


class Clock:
    def __init__(self):
        self.last = ()

    def now(self, values):
        return tie(values, *self.last) if self.last else values

    def tick(self, *arrays):
        self.last = arrays


class Grid:
    def __init__(self, wide, narrow):
        self.wide, self.narrow, self.ring = wide, narrow, wide // 2
        self.devices = wide * narrow
        moves = {
            "z": lambda w, n: ((w + 2) % wide, n),
            "x": lambda w, n: (w ^ 1, n),
            "y": lambda w, n: (w, n ^ 2),
            "c": lambda w, n: (w, n ^ 1),
        }
        self.perms = {}
        for name, move in moves.items():
            pairs = []
            for w in range(wide):
                for n in range(narrow):
                    w2, n2 = move(w, n)
                    pairs.append((w * narrow + n, w2 * narrow + n2))
            self.perms[name] = pairs
        self.clock = Clock()

    def send(self, name, array):
        return lax.ppermute(self.clock.now(array), AXES, self.perms[name])


CHEAP = pl.CostEstimate(flops=10**6, bytes_accessed=10**5, transcendentals=0)
BIG_VMEM = pltpu.CompilerParams(vmem_limit_bytes=48 * 2**20)


def half_kernel(labels, ring, wide, g, rows, place, *refs):
    n = len(labels)
    pieces, (out, sems) = refs[:n], refs[n:]
    z, x, y = place[0], place[1], place[2]
    height = wide * rows
    copies = []

    def copy(src, dst):
        copies.append(pltpu.make_async_copy(src, dst, sems.at[len(copies)]))

    for piece, piece_labels in zip(pieces, labels):
        for i, (dz, dx, dy) in enumerate(piece_labels):
            row = 2 * lax.rem(z + (ring - dz), ring) + (x + dx - 2 * x * dx)
            col = y + dy - 2 * y * dy
            for k in range(g):
                first = pl.multiple_of(row * rows, 16)
                copy(piece.at[i, pl.ds(k * rows, rows)], out.at[col, pl.ds(k * height + first, rows)])
            if piece.shape[1] > g * rows:
                first = pl.multiple_of(g * height + row * SMALL_ROWS, 16)
                copy(piece.at[i, pl.ds(g * rows, SMALL_ROWS)], out.at[col, pl.ds(first, SMALL_ROWS)])
    for one in copies:
        one.start()
    for one in copies:
        one.wait()


def anywhere(count):
    return [pl.BlockSpec(memory_space=pl.ANY)] * count


PLACE = pl.BlockSpec(memory_space=pltpu.SMEM)


class Gather:
    def __init__(self, grid, place, shard, g, small=False):
        self.grid, self.place, self.g, self.small, self.shard = grid, place, g, small, shard
        self.rows = (shard.shape[0] - (SMALL_ROWS if small else 0)) // g
        self.parts = [([(0, 0, 0)], shard[None])]

    def set_ring(self, arrays):
        labels = self.parts[0][0]
        self.parts = [([(step, dx, dy) for _, dx, dy in labels], a) for step, a in enumerate(arrays)]

    def join(self):
        labels = [l for ls, _ in self.parts for l in ls]
        self.parts = [(labels, jnp.concatenate([a for _, a in self.parts], axis=0))]
        return self.parts[0][1]

    def array(self):
        return self.parts[0][1]

    def pairs(self):
        labels, array = self.parts[0]
        self.from_x, self.from_y = self.grid.send("x", array), self.grid.send("y", array)
        self.parts.append(([(dz, 1, dy) for dz, _, dy in labels], self.from_x))
        self.parts.append(([(dz, dx, 1) for dz, dx, _ in labels], self.from_y))
        return self.from_x, self.from_y

    def corner(self):
        labels, array = self.parts[0]
        cut = self.corner_cut(array.shape[1])
        over_x = self.grid.send("x", self.from_y[:, :cut])
        over_y = self.grid.send("y", self.from_x[:, cut:])
        self.corner_parts = ([(dz, 1, 1) for dz, _, _ in labels], cut, over_x, over_y)
        return over_x, over_y

    def corner_cut(self, height):
        return height // 32 * 16

    def close(self):
        labels, cut, over_x, over_y = self.corner_parts
        self.parts.append((labels, jnp.concatenate((over_x, over_y), axis=1)))

    def half(self):
        grid, g, rows = self.grid, self.g, self.rows
        height, cols = self.shard.shape
        n = (g + (height > g * rows)) * grid.devices // 2
        self.own = pl.pallas_call(
            functools.partial(half_kernel, [l for l, _ in self.parts], grid.ring, grid.wide, g, rows),
            in_specs=[PLACE] + anywhere(len(self.parts)),
            out_specs=pl.BlockSpec(memory_space=pltpu.VMEM),
            out_shape=jax.ShapeDtypeStruct((2, grid.wide * height, cols), self.shard.dtype),
            scratch_shapes=[pltpu.SemaphoreType.DMA((n,))],
            compiler_params=BIG_VMEM,
            cost_estimate=CHEAP,
            name="half_weights",
        )(self.place, *[array for _, array in self.parts])
        return self.own

    def swap(self):
        self.other = self.grid.send("c", self.own)
        return self.other

    def small_rows(self):
        own, other = (a[:, self.g * self.grid.wide * self.rows :] for a in (self.own, self.other))
        both = jnp.where(self.place[3] == 0, jnp.stack((own, other)), jnp.stack((other, own)))
        both = both.reshape(2, 2, self.grid.wide, -1)
        return both.transpose(2, 1, 0, 3).reshape(self.grid.devices, -1)


def corners(place):
    y, c = place[2], place[3]
    return (2 * y + 1 - c, 2 * (1 - y) + 1 - c), (2 * y + c, 2 * (1 - y) + c)


def column(ref, n, cols):
    return ref[:, pl.ds(pl.multiple_of(n * cols, 128), cols)]


def far_kernel(place, *refs):
    out = refs[-1]
    cols = out.shape[-1]
    for i in range(out.shape[0]):
        a, d = refs[2 * i], refs[2 * i + 1]
        for j, n in enumerate(corners(place)[0]):
            out[i, j] = dot_tn(a[...], column(d, n, cols)).astype(BF16)


def put_quadrants(x, scratch, k, i, here, outs):
    dx, dy, qx, qy, own = outs
    rows = own.shape[2]
    if here:
        own[i, k] = scratch[k, x]
        qx[i, k] = scratch[k, 1 - x]
    else:
        qy[i, k] = scratch[k, x]
        dx[i, k] = scratch[k, 1 - x, pl.ds(0, rows // 2)].astype(BF16)
        dy[i, k] = scratch[k, 1 - x, pl.ds(rows // 2, rows // 2)].astype(BF16)


def near_kernel(place, *refs):
    from_c, *outs, scratch = refs[-7:]
    units, zs, rows, cols = outs[-1].shape
    for i in range(units):
        a, d = refs[2 * i], refs[2 * i + 1]
        for j, n in enumerate(corners(place)[1]):
            term = dot_tn(a[...], column(d, n, cols)) + from_c[i, j].astype(F32)
            scratch[...] = term.reshape(scratch.shape)
            for k in range(zs):
                put_quadrants(place[1], scratch, k, i, j == 0, outs)


def quadrant_shapes(units, ring, rows, cols):
    return [jax.ShapeDtypeStruct((units, ring, rows // 2, cols), BF16)] * 2 + [
        jax.ShapeDtypeStruct((units, ring, rows, cols), F32)
    ] * 3


def quadrant_specs(units, zs, rows, cols, stepped):
    def at(s, *_):
        return (0, s if stepped else 0, 0, 0)

    half = pl.BlockSpec((units, zs, rows // 2, cols), at)
    full = pl.BlockSpec((units, zs, rows, cols), at)
    return [half] * 2 + [full] * 3


def token_terms(grid, place, pairs, rows, cols, from_c=None):
    units, tokens = len(pairs), pairs[0][0].shape[0]
    height = grid.wide * rows
    zs = max(1, 128 // (2 * rows))
    if 2 * rows >= 128 and height // (2 * rows) > 1 and rows * cols <= 128 * 256:
        zs = min(grid.ring, 2)
    tall = zs * 2 * rows
    in_specs, args = [], []
    for a, d in pairs:
        in_specs += [
            pl.BlockSpec((tokens, tall), lambda s, *_: (0, s)),
            pl.BlockSpec(d.shape, lambda s, *_: (0, 0)),
        ]
        args += [a, d]
    block = pl.BlockSpec((units, 2, tall, cols), lambda s, *_: (0, 0, s, 0))
    scratch = []
    if from_c is None:
        kernel, out_specs = far_kernel, block
        out_shape = jax.ShapeDtypeStruct((units, 2, height, cols), BF16)
    else:
        in_specs.append(block)
        args.append(from_c)
        kernel = near_kernel
        out_specs = quadrant_specs(units, zs, rows, cols, True)
        out_shape = quadrant_shapes(units, grid.ring, rows, cols)
        scratch = [pltpu.VMEM((zs, 2, rows, cols), F32)]
    return pl.pallas_call(
        kernel,
        grid_spec=pltpu.PrefetchScalarGridSpec(
            num_scalar_prefetch=1,
            grid=(height // tall,),
            in_specs=in_specs,
            out_specs=out_specs,
            scratch_shapes=scratch,
        ),
        out_shape=out_shape,
        compiler_params=BIG_VMEM,
        cost_estimate=CHEAP,
        name="weight_terms",
    )(place, *args)


def memory_terms_kernel(near, place, mem, *refs):
    if near:
        *ds, from_c, dx, dy, qx, qy, own, acc = refs
    else:
        *ds, out, acc = refs
    cols = acc.shape[-1]
    m = pl.program_id(0)

    @pl.when(m == 0)
    def _():
        acc[...] = from_c[...].astype(F32).reshape(acc.shape) if near else jnp.zeros_like(acc)

    for i, d in enumerate(ds):
        for j, n in enumerate(corners(place)[1 if near else 0]):
            term = dot_tn(mem[0], d[0, :, pl.ds(pl.multiple_of(n * cols, 128), cols)])
            acc[i, j] += term.reshape(acc.shape[2:])

    @pl.when(m == pl.num_programs(0) - 1)
    def _():
        if near:
            x = place[1]
            zs, rows = own.shape[1], own.shape[2]
            for i in range(len(ds)):
                for j in range(2):
                    for k in range(zs):
                        put_quadrants(x, acc.at[i, j], k, i, j == 0, (dx, dy, qx, qy, own))
        else:
            out[...] = acc[...].reshape(out.shape).astype(BF16)


def memory_terms(grid, place, memory, grads, rows, cols, from_c=None):
    units, (mems, length, wide_cols) = len(grads), memory.shape
    height = grid.wide * rows
    near = from_c is not None
    one = pl.BlockSpec((1, length, wide_cols), lambda m, *_: (m, 0, 0))
    term = pl.BlockSpec((units, 2, height, cols), lambda m, *_: (0, 0, 0, 0))
    return pl.pallas_call(
        functools.partial(memory_terms_kernel, near),
        grid_spec=pltpu.PrefetchScalarGridSpec(
            num_scalar_prefetch=1,
            grid=(mems,),
            in_specs=[one] * (1 + units) + ([term] if near else []),
            out_specs=quadrant_specs(units, grid.ring, rows, cols, False) if near else term,
            scratch_shapes=[pltpu.VMEM((units, 2, grid.ring, 2, rows, cols), F32)],
        ),
        out_shape=quadrant_shapes(units, grid.ring, rows, cols)
        if near
        else jax.ShapeDtypeStruct((units, 2, height, cols), BF16),
        compiler_params=BIG_VMEM,
        cost_estimate=CHEAP,
        name="memory_terms",
    )(place, memory, *grads, *([from_c] if near else []))


def add_corners_kernel(qx, qy, from_x, from_y, sx, sy):
    half = from_x.shape[2]
    first, second = pl.ds(0, half), pl.ds(half, half)
    sx[0, 0, first] = qx[0, 0, first].astype(BF16)
    sx[0, 0, second] = (qx[0, 0, second] + from_y[0, 0].astype(F32)).astype(BF16)
    sy[0, 0, first] = (qy[0, 0, first] + from_x[0, 0].astype(F32)).astype(BF16)
    sy[0, 0, second] = qy[0, 0, second].astype(BF16)


def add_corners(qx, qy, from_x, from_y):
    units, ring, rows, cols = qx.shape
    full = pl.BlockSpec((1, 1, rows, cols), lambda i, k: (i, k, 0, 0))
    half = pl.BlockSpec((1, 1, rows // 2, cols), lambda i, k: (i, k, 0, 0))
    return pl.pallas_call(
        add_corners_kernel,
        grid=(units, ring),
        in_specs=[full, full, half, half],
        out_specs=[full, full],
        out_shape=[jax.ShapeDtypeStruct(qx.shape, BF16)] * 2,
        compiler_params=BIG_VMEM,
        cost_estimate=CHEAP,
        name="add_corners",
    )(qx, qy, from_x, from_y)


class Reduce:
    def __init__(self, grid, place, terms, rows):
        self.grid, self.place, self.terms, self.rows = grid, place, terms, rows

    def far(self):
        self.out = self.terms(None)
        return self.out

    def swap(self):
        self.from_c = self.grid.send("c", self.out)
        return self.from_c

    def near(self):
        self.dx, self.dy, self.qx, self.qy, self.own = self.terms(self.grid.clock.now(self.from_c))
        return self.dx

    def across(self):
        self.from_x, self.from_y = self.grid.send("x", self.dx), self.grid.send("y", self.dy)
        return self.from_x, self.from_y

    def add(self):
        from_x = self.grid.clock.now(self.from_x)
        self.sx, self.sy = add_corners(self.qx, self.qy, from_x, self.from_y)
        return self.sx

    def pairs(self):
        self.back_x, self.back_y = self.grid.send("x", self.sx), self.grid.send("y", self.sy)
        return self.back_x, self.back_y

    def chunk(self, step):
        index = lax.rem(self.place[0] + (self.grid.ring - step), self.grid.ring)
        parts = [
            lax.dynamic_index_in_dim(a, index, 1, keepdims=False) for a in (self.own, self.back_x, self.back_y)
        ]
        return parts[0] + parts[1].astype(F32) + parts[2].astype(F32)


class RingSum:
    def __init__(self, grid, reduces):
        self.grid, self.reduces, self.done, self.came = grid, reduces, 0, None

    def step(self):
        self.done += 1
        total = jnp.concatenate([r.chunk(self.done % self.grid.ring) for r in self.reduces], axis=0)
        if self.came is not None:
            total = total + self.came.astype(F32)
        if self.done == self.grid.ring:
            self.came = total
        else:
            self.came = self.grid.send("z", total.astype(BF16))
        return self.came


class SmallSum:
    def __init__(self, grid, place, terms):
        self.grid, self.place, self.done = grid, place, 0
        self.mine = terms.reshape(grid.ring, 2, 2, 2, -1)

    def step(self):
        grid, place = self.grid, self.place
        if self.done < 3:
            name, axis, at = ("c", "y", "x")[self.done], 3 - self.done, place[3 - self.done]
            far = lax.dynamic_index_in_dim(self.mine, 1 - at, axis, keepdims=False)
            near = lax.dynamic_index_in_dim(self.mine, at, axis, keepdims=False)
            self.mine = near + grid.send(name, far)
        else:
            index = lax.rem(place[0] + (grid.ring - (self.done - 2)), grid.ring)
            total = lax.dynamic_index_in_dim(self.mine, index, 0, keepdims=False)
            self.came = grid.send("z", total if self.done == 3 else total + self.came)
        self.done += 1
        return self.mine if self.done <= 3 else self.came

    def result(self):
        return lax.dynamic_index_in_dim(self.mine, self.place[0], 0, keepdims=False) + self.came


def halves(place, own, other):
    c = place[3]
    return [(2 * y + core, y, half) for half, core in ((own, c), (other, 1 - c)) for y in range(2)]


def at_block(n, cols):
    return pl.ds(pl.multiple_of(n * cols, 128), cols)


def times_t(place, d, own, other):
    cols = own.shape[-1]
    return sum(dot_nt(d[:, at_block(n, cols)], half[y]) for n, y, half in halves(place, own, other))


def norm_parts(values):
    centre = values - jnp.mean(values, axis=-1, keepdims=True)
    scale = lax.rsqrt(jnp.mean(centre * centre, axis=-1, keepdims=True) + EPSILON)
    return centre * scale, scale


def norm_back(normed, scale, gain, grad):
    inner = grad * gain
    back = scale * (
        inner
        - jnp.mean(inner, axis=-1, keepdims=True)
        - normed * jnp.mean(inner * normed, axis=-1, keepdims=True)
    )
    return back, jnp.sum(grad * normed, axis=0, keepdims=True), jnp.sum(grad, axis=0, keepdims=True)


def column_sum(values):
    return jnp.sum(values.astype(F32), axis=0, keepdims=True)


GAIN, BIAS = 0, 3


def row(vectors, i):
    return vectors[i : i + 1, :]


def memory_kernel(place, mem, vectors, k_own, k_other, v_own, v_other, keys, values):
    cols = k_own.shape[-1]
    for n, y, half in halves(place, k_own, k_other):
        keys[0, :, at_block(n, cols)] = dot_nn(mem[0], half[y]).astype(BF16)
    for n, y, half in halves(place, v_own, v_other):
        bias = vectors[BIAS + 6 : BIAS + 7, at_block(n, cols)]
        values[0, :, at_block(n, cols)] = (dot_nn(mem[0], half[y]) + bias).astype(BF16)


def qkv_kernel(place, tokens, vectors, *refs):
    weights, (normed, q, k, v) = refs[:6], refs[6:]
    n, _ = norm_parts(tokens[...].astype(F32))
    normed[...] = (n * row(vectors, GAIN) + row(vectors, BIAS)).astype(BF16)
    cols = weights[0].shape[-1]
    for i, (out, bias_at) in enumerate(((q, 1), (k, None), (v, 2))):
        for n, y, half in halves(place, weights[2 * i], weights[2 * i + 1]):
            term = dot_nn(normed[...], half[y])
            if bias_at is not None:
                term = term + vectors[BIAS + bias_at : BIAS + bias_at + 1, at_block(n, cols)]
            out[:, at_block(n, cols)] = term.astype(BF16)


def middle_kernel(place, tokens, mixed, vectors, so_own, so_other, cq_own, cq_other, after, normed, queries):
    cols = so_own.shape[-1]
    for n, y, half in halves(place, so_own, so_other):
        at = at_block(n, cols)
        after[:, at] = tokens[:, at].astype(F32) + dot_nn(mixed[...], half[y]) + vectors[BIAS + 3 : BIAS + 4, at]
    n, _ = norm_parts(after[...])
    normed[...] = (n * row(vectors, GAIN + 1) + row(vectors, BIAS + 4)).astype(BF16)
    for n, y, half in halves(place, cq_own, cq_other):
        at = at_block(n, cols)
        queries[:, at] = (dot_nn(normed[...], half[y]) + vectors[BIAS + 5 : BIAS + 6, at]).astype(BF16)


def cross_out_kernel(place, before, mixed, vectors, own, other, after, normed):
    cols = own.shape[-1]
    for n, y, half in halves(place, own, other):
        at = at_block(n, cols)
        after[:, at] = before[:, at] + dot_nn(mixed[...], half[y]) + vectors[BIAS + 7 : BIAS + 8, at]
    n, _ = norm_parts(after[...])
    normed[...] = (n * row(vectors, GAIN + 2) + row(vectors, BIAS + 8)).astype(BF16)


def up_kernel(place, normed, bias, own, other, act, slope):
    c = place[3]
    cols = own.shape[-1]

    def block(n, half):
        at = at_block(n, cols)
        u = dot_nn(normed[...], half[0]) + bias[:, at]
        below = 0.5 * (1.0 + lax.erf(u * (1.0 / math.sqrt(2.0))))
        act[:, at] = (u * below).astype(BF16)
        slope[:, at] = below + u * jnp.exp(-0.5 * u * u) * (1.0 / math.sqrt(2.0 * math.pi))

    y = pl.program_id(0)
    block(2 * y + c, own)
    block(2 * y + 1 - c, other)


def down_kernel(place, after, act, vectors, own, other, out):
    c, y = place[3], pl.program_id(0)
    cols = own.shape[-1]
    for n, half in ((2 * y + c, own), (2 * y + 1 - c, other)):
        at = at_block(n, cols)
        total = after[:, at] + dot_nn(act[...], half[0]) + vectors[BIAS + 9 : BIAS + 10, at]
        out[:, at] = total.astype(BF16)


def down_back_kernel(place, grad, slope, own, other, grad_pre, bias_grad):
    back = (times_t(place, grad, own, other) * slope[...]).astype(BF16)
    grad_pre[...] = back
    bias_grad[...] = column_sum(back)


def up_back_kernel(
    place, grad_pre, grad_out, after, vectors, own, other, co_own, co_other,
    grad, branch, mixed, gain_grad, shift_grad, out_grad, last_grad, total,
):
    c, y = place[3], pl.program_id(0)
    cols = own.shape[-1]
    term = dot_nt(grad_pre[:, at_block(2 * y + c, cols)], own[0])
    term = term + dot_nt(grad_pre[:, at_block(2 * y + 1 - c, cols)], other[0])

    @pl.when(y == 0)
    def _():
        total[...] = term

    @pl.when(y == 1)
    def _():
        n, scale = norm_parts(after[...])
        back, gain_grad[...], shift_grad[...] = norm_back(n, scale, row(vectors, GAIN + 2), total[...] + term)
        out = grad_out[...].astype(F32) + back
        grad[...] = out
        branch[...] = out.astype(BF16)
        out_grad[...] = column_sum(branch[...])
        last_grad[...] = column_sum(grad_out[...])
        mixed[...] = times_t(place, branch, co_own, co_other).astype(BF16)


def middle_back_kernel(
    place, grad_queries, grad_after, after, vectors, cq_own, cq_other, so_own, so_other,
    grad, branch, mixed, gain_grad, shift_grad, out_grad, query_grad,
):
    n, scale = norm_parts(after[...])
    dense = times_t(place, grad_queries, cq_own, cq_other)
    back, gain_grad[...], shift_grad[...] = norm_back(n, scale, row(vectors, GAIN + 1), dense)
    out = grad_after[...] + back
    grad[...] = out
    branch[...] = out.astype(BF16)
    out_grad[...] = column_sum(branch[...])
    query_grad[...] = column_sum(grad_queries[...])
    mixed[...] = times_t(place, branch, so_own, so_other).astype(BF16)


def first_back_kernel(place, tokens, grad_after, gq, gk, gv, vectors, *refs):
    weights, (grad, gain_grad, shift_grad, query_grad, value_grad) = refs[:6], refs[6:]
    n, scale = norm_parts(tokens[...].astype(F32))
    dense = sum(
        times_t(place, d, weights[2 * i], weights[2 * i + 1]) for i, d in enumerate((gq, gk, gv))
    )
    back, gain_grad[...], shift_grad[...] = norm_back(n, scale, row(vectors, GAIN), dense)
    grad[...] = (grad_after[...] + back).astype(BF16)
    query_grad[...] = column_sum(gq[...])
    value_grad[...] = column_sum(gv[...])


def memory_back_kernel(place, gk, gv, k_own, k_other, v_own, v_other, grad, value_grad):
    total = times_t(place, gk.at[0], k_own, k_other) + times_t(place, gv.at[0], v_own, v_other)
    grad[0] = total.astype(BF16)

    @pl.when(pl.program_id(0) == 0)
    def _():
        value_grad[...] = jnp.zeros_like(value_grad)

    value_grad[...] += column_sum(gv[0])


def dense_call(kernel, name, place, ins, outs, grid=(1,), scratch=()):
    def spec(array, block, index):
        block = block or array.shape
        zeros = (0,) * len(block)
        return pl.BlockSpec(block, index or (lambda *_: zeros))

    return pl.pallas_call(
        kernel,
        grid_spec=pltpu.PrefetchScalarGridSpec(
            num_scalar_prefetch=1,
            grid=grid,
            in_specs=[spec(*one) for one in ins],
            out_specs=[spec(*one) for one in outs],
            scratch_shapes=scratch,
        ),
        out_shape=[one[0] for one in outs],
        compiler_params=BIG_VMEM,
        cost_estimate=CHEAP,
        name=name,
    )(place, *[one[0] for one in ins])


def full(array):
    return (array, None, None)


def result(shape, dtype):
    return (jax.ShapeDtypeStruct(shape, dtype), None, None)


def matrix(gathered, i, height=D):
    block = (2, height, gathered.own.shape[-1])
    return [(half, block, lambda *_: (0, i, 0)) for half in (gathered.own, gathered.other)]


def by_y(gathered):
    block = (1,) + gathered.own.shape[1:]
    return [(half, block, lambda y, *_: (y, 0, 0)) for half in (gathered.own, gathered.other)]


def by_rows(gathered, rows):
    block = (2, rows, gathered.own.shape[-1])
    return [(half, block, lambda s, *_: (0, s, 0)) for half in (gathered.own, gathered.other)]


def local(
    shape,
    tokens,
    memory,
    segment_ids,
    page_map,
    mem_lengths,
    gains,
    biases,
    fc1_bias,
    self_qkv,
    self_out,
    cross_q,
    cross_kv,
    cross_out,
    fc1,
    fc2,
    cotangent,
):
    grid = Grid(*shape)
    wide_at, narrow_at = lax.axis_index("wide"), lax.axis_index("narrow")
    place = jnp.stack((wide_at // 2, wide_at % 2, narrow_at // 2, narrow_at % 2)).astype(jnp.int32)
    devices = grid.devices
    mem_count, token_count = memory.shape[0], tokens.shape[0]
    rows, cols = self_out.shape

    small = jnp.concatenate((gains.reshape(-1), biases.reshape(-1), fc1_bias))
    small = jnp.pad(small, (0, SMALL_ROWS * cols - small.size)).reshape(SMALL_ROWS, cols)
    n_gain, n_bias, n_fc1 = gains.size, biases.size, fc1_bias.size
    gather = functools.partial(Gather, grid, place)
    g_ckv = gather(jnp.concatenate((cross_kv[0], cross_kv[1], small), axis=0), 2, True)
    g_qkv = gather(self_qkv.reshape(3 * rows, cols), 3)
    g_mix = gather(jnp.concatenate((self_out, cross_q, cross_out), axis=0), 3)
    g_fc1 = gather(fc1, 1)
    g_fc2 = gather(fc2, 1)
    send, clock = grid.send, grid.clock
    now, tick = clock.now, clock.tick
    steps = grid.ring - 1

    ring_ckv = [g_ckv.array()]
    ring_ckv.append(send("z", ring_ckv[-1]))
    tick(ring_ckv[-1], *g_fc2.pairs())
    ring_ckv.append(send("z", ring_ckv[-1]))
    tick(ring_ckv[-1], *g_fc2.corner())
    for _ in range(steps - 2):
        ring_ckv.append(send("z", ring_ckv[-1]))
        tick(ring_ckv[-1])
    g_fc2.close()
    fc2_all = g_fc2.join()
    fc2_cut = fc2_all.shape[1] // 2
    g_ckv.set_ring(ring_ckv)
    g_ckv.join()

    ring_two = [jnp.concatenate((g_qkv.array(), g_mix.array()), axis=1)]
    ring_two.append(send("z", ring_two[-1]))
    tick(ring_two[-1], *g_ckv.pairs())
    ring_two.append(send("z", ring_two[-1]))
    tick(ring_two[-1], *g_ckv.corner())
    g_ckv.close()
    for _ in range(steps - 2):
        ring_two.append(send("z", ring_two[-1]))
        tick(ring_two[-1], g_ckv.half())
    cut = 3 * rows
    g_qkv.set_ring([a[:, :cut] for a in ring_two])
    g_mix.set_ring([a[:, cut:] for a in ring_two])
    g_qkv.join()
    g_mix.join()

    ring_fc1 = [g_fc1.array()]
    for _ in range(steps - 1):
        ring_fc1.append(send("z", ring_fc1[-1]))
    tick(ring_fc1[-1], g_ckv.swap(), *g_qkv.pairs())

    ring_fc1.append(send("z", ring_fc1[-1]))
    small_all = g_ckv.small_rows().astype(F32)
    vectors = small_all[:, : n_gain + n_bias].reshape(devices, 13, -1).transpose(1, 0, 2).reshape(13, D)
    up_bias = small_all[:, n_gain + n_bias : n_gain + n_bias + n_fc1].reshape(1, -1)
    mem_block = (1,) + memory.shape[1:]
    mem_shape = jax.ShapeDtypeStruct(memory.shape, BF16)

    def by_memory(array):
        return (array, mem_block, lambda m, *_: (m, 0, 0))

    mem_keys, mem_values = dense_call(
        memory_kernel, "memory_keys_values", place,
        [by_memory(now(memory)), full(vectors)] + matrix(g_ckv, 0) + matrix(g_ckv, 1),
        [by_memory(mem_shape), by_memory(mem_shape)], grid=(mem_count,),
    )
    tick(ring_fc1[-1], mem_keys, *g_qkv.corner())
    g_qkv.close()
    g_fc1.set_ring(ring_fc1)
    g_fc1.join()

    ring_a, ring_b = [fc2_all[:, :fc2_cut]], [fc2_all[:, fc2_cut:]]
    ring_a.append(send("z", ring_a[-1]))
    tick(ring_a[-1], g_qkv.half(), *g_mix.pairs())
    ring_b.append(send("z", ring_b[-1]))
    tick(g_qkv.swap(), ring_b[-1], *g_mix.corner())
    g_mix.close()

    ring_a.append(send("z", ring_a[-1]))
    ring_b.append(send("z", ring_b[-1]))
    wide_row = (token_count, D)
    normed_one, self_queries, self_keys, self_values = dense_call(
        qkv_kernel, "self_qkv", place,
        [full(now(tokens)), full(vectors)] + matrix(g_qkv, 0) + matrix(g_qkv, 1) + matrix(g_qkv, 2),
        [result(wide_row, BF16)] * 4,
    )
    self_mixed, self_lse = self_forward(segment_ids, self_queries, self_keys, self_values)
    g_mix.half()
    tick(ring_a[-1], ring_b[-1], self_mixed, g_mix.swap(), *g_fc1.pairs())

    for _ in range(steps - 2):
        ring_a.append(send("z", ring_a[-1]))
    after_self, normed_two, cross_queries = dense_call(
        middle_kernel, "self_out_cross_q", place,
        [full(tokens), full(now(self_mixed)), full(vectors)] + matrix(g_mix, 0) + matrix(g_mix, 1),
        [result(wide_row, F32), result(wide_row, BF16), result(wide_row, BF16)],
    )
    first_mem = lax.axis_index(AXES) * mem_count
    local_map = (page_map - first_mem).reshape(-1).astype(jnp.int32)
    picks = local_map[:, None] == jnp.arange(mem_count, dtype=jnp.int32)[None, :]
    row_lengths = jnp.sum(jnp.where(picks, mem_lengths[None, :], 0), axis=-1).astype(jnp.int32)
    cross_mixed, cross_lse = cross_forward(
        local_map, row_lengths, segment_ids, cross_queries, mem_keys, mem_values
    )
    tick(cross_mixed, ring_a[-1], *g_fc1.corner())
    g_fc1.close()
    after_cross, normed_three = dense_call(
        cross_out_kernel, "cross_out", place,
        [full(after_self), full(now(cross_mixed)), full(vectors)] + matrix(g_mix, 2),
        [result(wide_row, F32), result(wide_row, BF16)],
    )

    g_fc1.half()
    for _ in range(steps - 2):
        ring_b.append(send("z", ring_b[-1]))
    tick(g_fc1.swap(), normed_three, ring_b[-1])
    g_fc2.set_ring([jnp.concatenate(ab, axis=1) for ab in zip(ring_a, ring_b)])
    g_fc2.half()
    hidden = up_bias.shape[1]
    activated, slope = dense_call(
        up_kernel, "fc1_gelu", place,
        [full(now(normed_three)), full(up_bias)] + by_y(g_fc1),
        [result((token_count, hidden), BF16), result((token_count, hidden), F32)], grid=(2,),
    )
    tick(activated, g_fc2.swap())

    def settle(pairs, shard):
        part_rows, part_cols = shard.shape
        return Reduce(
            grid, place,
            lambda from_c: token_terms(grid, place, pairs, part_rows, part_cols, from_c),
            part_rows,
        )

    one_row = result((1, D), F32)
    r_fc2 = settle([(now(activated), cotangent)], fc2)
    tick(r_fc2.far())
    slab = hidden // 4
    some = lambda array: (array, (token_count, slab), lambda s, *_: (0, s))
    grad_pre, grad_up_bias = dense_call(
        down_back_kernel, "fc2_gelu_back", place,
        [full(now(cotangent)), some(slope)] + by_rows(g_fc2, slab),
        [
            some(jax.ShapeDtypeStruct((token_count, hidden), BF16)),
            (jax.ShapeDtypeStruct((1, hidden), F32), (1, slab), lambda s, *_: (0, s)),
        ],
        grid=(4,),
    )
    tick(r_fc2.swap(), grad_pre)
    grad_pre = now(grad_pre)
    r_fc1 = settle([(normed_three, grad_pre)], fc1)
    tick(r_fc2.near(), r_fc1.far())
    (
        grad_after_cross, grad_branch_two, grad_cross_mixed,
        grad_gain_three, grad_bias_eight, grad_bias_seven, grad_bias_nine,
    ) = dense_call(
        up_back_kernel, "fc1_norm_back", place,
        [full(now(grad_pre)), full(cotangent), full(after_cross), full(vectors)]
        + by_y(g_fc1) + matrix(g_mix, 2),
        [result(wide_row, F32), result(wide_row, BF16), result(wide_row, BF16)] + [one_row] * 4,
        grid=(2,), scratch=[pltpu.VMEM(wide_row, F32)],
    )
    tick(r_fc1.swap(), grad_cross_mixed, *r_fc2.across())
    tick(r_fc1.near(), r_fc2.add())

    grad_cq, grad_ck, grad_cv = cross_backward(
        local_map, row_lengths, segment_ids, cross_queries, mem_keys, mem_values,
        now(grad_cross_mixed), cross_lse,
    )
    tick(grad_cq, *r_fc2.pairs())
    ring_fc2 = RingSum(grid, [r_fc2])
    grad_cq = now(grad_cq)
    r_mem = Reduce(
        grid, place,
        lambda from_c: memory_terms(grid, place, memory, now((grad_ck, grad_cv)), rows, cols, from_c),
        rows,
    )
    r_cross = settle([(cross_mixed, grad_branch_two), (normed_two, grad_cq)], cross_q)
    tick(ring_fc2.step(), r_cross.far(), r_mem.far(), *r_fc1.across())
    tick(r_fc1.add())

    ring_fc2.step()
    (
        grad_after_self, grad_branch_one, grad_self_mixed,
        grad_gain_two, grad_bias_four, grad_bias_three, grad_bias_five,
    ) = dense_call(
        middle_back_kernel, "cross_q_norm_back", place,
        [full(now(grad_cq)), full(grad_after_cross), full(after_self), full(vectors)]
        + matrix(g_mix, 1) + matrix(g_mix, 0),
        [result(wide_row, F32), result(wide_row, BF16), result(wide_row, BF16)] + [one_row] * 4,
    )
    grad_sq, grad_sk, grad_sv = self_backward(
        segment_ids, self_queries, self_keys, self_values, grad_self_mixed, self_lse
    )
    r_self = settle(
        [(normed_one, grad_sq), (normed_one, grad_sk), (normed_one, grad_sv), (self_mixed, grad_branch_one)],
        cross_q,
    )
    tick(r_cross.swap(), r_mem.swap(), r_self.far(), ring_fc2.step(), *r_fc1.pairs())
    ring_fc2.step()
    ring_fc1 = RingSum(grid, [r_fc1])
    tick(r_cross.near(), r_mem.near())
    grad_tokens, grad_gain_one, grad_bias_zero, grad_bias_one, grad_bias_two = dense_call(
        first_back_kernel, "self_qkv_norm_back", place,
        [full(tokens), full(grad_after_self)] + [full(d) for d in now((grad_sq, grad_sk, grad_sv))]
        + [full(vectors)] + matrix(g_qkv, 0) + matrix(g_qkv, 1) + matrix(g_qkv, 2),
        [result(wide_row, BF16)] + [one_row] * 4,
    )
    tick(r_self.swap(), ring_fc1.step(), grad_tokens, *r_cross.across(), *r_mem.across())
    tick(r_cross.add(), r_mem.add(), r_self.near())
    ring_fc1.step()
    grad_memory, grad_bias_six = dense_call(
        memory_back_kernel, "memory_back", place,
        [by_memory(a) for a in now((grad_ck, grad_cv))] + matrix(g_ckv, 0) + matrix(g_ckv, 1),
        [by_memory(mem_shape), one_row], grid=(mem_count,),
    )
    tick(ring_fc1.step(), grad_memory, *r_cross.pairs(), *r_mem.pairs())
    ring_fc1.step()
    ring_cross = RingSum(grid, [r_cross, r_mem])

    def by_device(array):
        return array.reshape(array.shape[0], devices, -1).transpose(1, 0, 2).reshape(devices, -1)

    small_grads = jnp.concatenate(
        (
            by_device(
                jnp.concatenate(
                    (
                        grad_gain_one, grad_gain_two, grad_gain_three,
                        grad_bias_zero, grad_bias_one, grad_bias_two, grad_bias_three, grad_bias_four,
                        grad_bias_five, grad_bias_six, grad_bias_seven, grad_bias_eight, grad_bias_nine,
                    ),
                    axis=0,
                )
            ),
            by_device(grad_up_bias),
        ),
        axis=1,
    )
    small_sum = SmallSum(grid, place, now(small_grads))
    (layer_out,) = dense_call(
        down_kernel, "fc2", place,
        [full(after_cross), full(now(activated)), full(vectors)] + by_y(g_fc2),
        [result(wide_row, BF16)], grid=(2,),
    )
    tick(ring_cross.step(), layer_out, small_sum.step(), *r_self.across())
    tick(r_self.add())
    ring_cross.step()
    tick(ring_cross.step(), small_sum.step(), *r_self.pairs())
    for _ in range(steps - 3):
        ring_cross.step()
    ring_cross.step()
    ring_self = RingSum(grid, [r_self])
    for _ in range(steps):
        tick(ring_self.step(), small_sum.step())
    ring_self.step()
    while small_sum.done < steps + 3:
        tick(small_sum.step())
    for ring in (ring_fc2, ring_fc1):
        while ring.done < grid.ring:
            ring.step()
    small_shard = small_sum.result()
    came_cross, came_self = ring_cross.came, ring_self.came
    return (
        layer_out,
        grad_tokens,
        grad_memory,
        small_shard[:n_gain].reshape(gains.shape),
        small_shard[n_gain : n_gain + n_bias].reshape(biases.shape),
        small_shard[n_gain + n_bias :],
        came_self[:3],
        came_self[3],
        came_cross[1],
        came_cross[2:],
        came_cross[0],
        ring_fc1.came[0],
        ring_fc2.came[0],
    )


def solution(mesh):
    shape = (mesh.shape["wide"], mesh.shape["narrow"])
    in_specs = (
        P(AXES, None),
        P(AXES, None, None),
        P(AXES, None),
        P(AXES, None),
        P(AXES),
        P(None, AXES),
        P(None, AXES),
        P(AXES),
        P(None, "wide", "narrow"),
        P("wide", "narrow"),
        P("wide", "narrow"),
        P(None, "wide", "narrow"),
        P("wide", "narrow"),
        P("wide", "narrow"),
        P("wide", "narrow"),
        P(AXES, None),
    )
    out_specs = (
        P(AXES, None),
        P(AXES, None),
        P(AXES, None, None),
        P(None, AXES),
        P(None, AXES),
        P(AXES),
        P(None, "wide", "narrow"),
        P("wide", "narrow"),
        P("wide", "narrow"),
        P(None, "wide", "narrow"),
        P("wide", "narrow"),
        P("wide", "narrow"),
        P("wide", "narrow"),
    )
    return jax.shard_map(
        functools.partial(local, shape), mesh=mesh, in_specs=in_specs, out_specs=out_specs, check_vma=False
    )
```

```python
import functools
import math

import jax
import jax.numpy as jnp
from jax import lax
from jax.experimental import pallas as pl
from jax.experimental.pallas import tpu as pltpu
from jax.sharding import PartitionSpec as P

D = 1024
HEADS = 16
HEAD_DIM = 64
PAIRS = HEADS // 2

EPSILON = 1e-05
NEG_FILL = -1e30
LOG2E = math.log2(math.e)
SCALE = 1.0 / math.sqrt(HEAD_DIM)
AXES = ("wide", "narrow")

F32 = jnp.float32
BF16 = jnp.bfloat16
VMEM = 24 * 2**20
CHEAP = pl.CostEstimate(flops=10**6, bytes_accessed=10**5, transcendentals=0)
BIG_VMEM = pltpu.CompilerParams(vmem_limit_bytes=VMEM)
FULL_VMEM = pltpu.CompilerParams(vmem_limit_bytes=60 * 2**20)


def dot_nt(a, b):
    return lax.dot_general(a, b, (((1,), (1,)), ((), ())), preferred_element_type=F32)


def dot_nn(a, b):
    return lax.dot_general(a, b, (((1,), (0,)), ((), ())), preferred_element_type=F32)


def dot_tn(a, b):
    return lax.dot_general(a, b, (((0,), (0,)), ((), ())), preferred_element_type=F32)


def two_heads(block):
    lane = lax.broadcasted_iota(jnp.int32, block.shape, 1)
    zero = jnp.zeros_like(block)
    return jnp.concatenate(
        (jnp.where(lane < HEAD_DIM, block, zero), jnp.where(lane < HEAD_DIM, zero, block)), axis=0
    )


def own_heads(both):
    half = both.shape[1] // 2
    line = lax.broadcasted_iota(jnp.int32, (both.shape[0], half), 0)
    return jnp.transpose(jnp.where(line < HEAD_DIM, both[:, :half], both[:, half:]))


CUTS = [slice(128 * h, 128 * h + 128) for h in range(PAIRS)]


def heads_forward(q_ref, k_ref, v_ref, valid, put):
    scores = [dot_nt(k_ref(cut), two_heads(q_ref(cut))) for cut in CUTS]
    weights, lses = [], []
    for one in scores:
        one = jnp.where(valid, one * (SCALE * LOG2E), NEG_FILL)
        top = jnp.max(one, axis=0, keepdims=True)
        expo = jnp.exp2(one - top)
        total = jnp.sum(expo, axis=0, keepdims=True)
        weights.append((expo * (1.0 / total)).astype(BF16))
        lses.append(top + jnp.log2(total))
    for h, cut in enumerate(CUTS):
        put(h, own_heads(dot_tn(v_ref(cut), weights[h])).astype(BF16), lses[h])


def heads_backward(q_ref, k_ref, v_ref, do_ref, lse_of, valid, put, group=4):
    for first in range(0, PAIRS, group):
        hs = range(first, first + group)
        qs = [two_heads(q_ref(CUTS[h])) for h in hs]
        ds = [two_heads(do_ref(CUTS[h])) for h in hs]
        scores = [dot_nt(k_ref(CUTS[h]), q) for h, q in zip(hs, qs)]
        grads = [dot_nt(v_ref(CUTS[h]), d) for h, d in zip(hs, ds)]
        weights, grad_scores = [], []
        for h, one, grad in zip(hs, scores, grads):
            weight = jnp.where(valid, jnp.exp2(one * (SCALE * LOG2E) - lse_of(h)), 0.0)
            inner = jnp.sum(weight * grad, axis=0, keepdims=True)
            grad_scores.append((weight * (grad - inner)).astype(BF16))
            weights.append(weight.astype(BF16))
        for h, q, d, weight, grad in zip(hs, qs, ds, weights, grad_scores):
            grad_q = (own_heads(dot_tn(k_ref(CUTS[h]), grad)) * SCALE).astype(BF16)
            grad_k = (dot_nn(grad, q) * SCALE).astype(BF16)
            put(h, grad_q, grad_k, dot_nn(weight, d).astype(BF16))


def columns_in(ref):
    return lambda cut: ref[:, cut]


def memory_columns(ref):
    return lambda cut: ref[0, :, cut]


def self_valid(seg_row, seg_col):
    length = seg_row.shape[-1]
    key = lax.broadcasted_iota(jnp.int32, (length, length), 0)
    tok = lax.broadcasted_iota(jnp.int32, (length, length), 1)
    one = (key <= tok) & (seg_row == seg_col)
    return jnp.concatenate((one, one), axis=1)


def self_fwd_kernel(seg_row, seg_col, q_ref, k_ref, v_ref, o_ref, lse_ref):
    def put(h, mixed, lse):
        o_ref[:, CUTS[h]] = mixed
        lse_ref[0, h : h + 1, :] = lse

    heads_forward(
        columns_in(q_ref), columns_in(k_ref), columns_in(v_ref), self_valid(seg_row[0], seg_col[0]), put
    )


def self_bwd_kernel(seg_row, seg_col, q_ref, k_ref, v_ref, do_ref, lse_ref, dq_ref, dk_ref, dv_ref):
    def put(h, grad_q, grad_k, grad_v):
        dq_ref[:, CUTS[h]] = grad_q
        dk_ref[:, CUTS[h]] = grad_k
        dv_ref[:, CUTS[h]] = grad_v

    heads_backward(
        columns_in(q_ref), columns_in(k_ref), columns_in(v_ref), columns_in(do_ref),
        lambda h: lse_ref[0, h : h + 1, :], self_valid(seg_row[0], seg_col[0]), put, PAIRS,
    )


def self_specs(row_len):
    seg = [
        pl.BlockSpec((1, 1, row_len), lambda r: (r, 0, 0)),
        pl.BlockSpec((1, row_len, 1), lambda r: (r, 0, 0)),
    ]
    row = pl.BlockSpec((row_len, D), lambda r: (r, 0))
    lse = pl.BlockSpec((1, PAIRS, 2 * row_len), lambda r: (r, 0, 0))
    return seg, row, lse


def self_forward(seg, queries, keys, values):
    rows, row_len = seg.shape
    seg_specs, row, lse = self_specs(row_len)
    return pl.pallas_call(
        self_fwd_kernel,
        grid=(rows,),
        in_specs=seg_specs + [row] * 3,
        out_specs=[row, lse],
        out_shape=[
            jax.ShapeDtypeStruct(queries.shape, BF16),
            jax.ShapeDtypeStruct((rows, PAIRS, 2 * row_len), F32),
        ],
        compiler_params=BIG_VMEM,
        cost_estimate=CHEAP,
        name="self_forward",
    )(seg[:, None, :], seg[:, :, None], queries, keys, values)


def self_backward(seg, queries, keys, values, grad_mixed, lse_rows):
    rows, row_len = seg.shape
    seg_specs, row, lse = self_specs(row_len)
    return pl.pallas_call(
        self_bwd_kernel,
        grid=(rows,),
        in_specs=seg_specs + [row] * 4 + [lse],
        out_specs=[row] * 3,
        out_shape=[jax.ShapeDtypeStruct(queries.shape, BF16)] * 3,
        compiler_params=FULL_VMEM,
        cost_estimate=CHEAP,
        name="self_backward",
    )(seg[:, None, :], seg[:, :, None], queries, keys, values, grad_mixed, lse_rows)


def cross_fwd_kernel(map_ref, len_ref, seg_row, seg_col, q_ref, k_ref, v_ref, o_ref, lse_ref):
    r, page = pl.program_id(0), pl.program_id(1)
    keys, toks = k_ref.shape[1], q_ref.shape[0]
    valid = lax.broadcasted_iota(jnp.int32, (keys, 2 * toks), 0) < len_ref[r * 2 + page]
    mine_col = (seg_col[0] == page) | (page == 0)
    mine_row = (seg_row[0] == page) | (page == 0)
    mine_row = jnp.concatenate((mine_row, mine_row), axis=1)

    def put(h, mixed, lse):
        o_ref[:, CUTS[h]] = jnp.where(mine_col, mixed, o_ref[:, CUTS[h]])
        lse_ref[0, h : h + 1, :] = jnp.where(mine_row, lse, lse_ref[0, h : h + 1, :])

    heads_forward(columns_in(q_ref), memory_columns(k_ref), memory_columns(v_ref), valid, put)


def cross_bwd_kernel(
    map_ref, len_ref, seg_row, seg_col, q_ref, k_ref, v_ref, do_ref, lse_ref,
    dq_ref, dk_ref, dv_ref, sum_ref,
):
    r, page = pl.program_id(0), pl.program_id(1)
    keys, toks = k_ref.shape[1], q_ref.shape[0]
    valid = lax.broadcasted_iota(jnp.int32, (keys, 2 * toks), 0) < len_ref[r * 2 + page]
    mine_col = (seg_col[0] == page) | (page == 0)
    mine_row = seg_row[0] == page
    mine_row = jnp.concatenate((mine_row, mine_row), axis=1)

    def put(h, grad_q, grad_k, grad_v):
        cut = CUTS[h]
        dq_ref[:, cut] = jnp.where(mine_col, grad_q, dq_ref[:, cut])
        dk_ref[0, :, cut] = grad_k
        dv_ref[0, :, cut] = grad_v
        before = jnp.where(r + page == 0, jnp.zeros((1, 128), F32), sum_ref[:, cut])
        sum_ref[:, cut] = before + jnp.sum(grad_v.astype(F32), axis=0, keepdims=True)

    heads_backward(
        columns_in(q_ref), memory_columns(k_ref), memory_columns(v_ref), columns_in(do_ref),
        lambda h: jnp.where(mine_row, lse_ref[0, h : h + 1, :], -NEG_FILL), valid, put,
    )


def cross_specs(row_len, mem_len):
    seg = [
        pl.BlockSpec((1, 1, row_len), lambda r, p, *_: (r, 0, 0)),
        pl.BlockSpec((1, row_len, 1), lambda r, p, *_: (r, 0, 0)),
    ]
    row = pl.BlockSpec((row_len, D), lambda r, p, *_: (r, 0))
    mem = pl.BlockSpec((1, mem_len, D), lambda r, p, mp, ln: (mp[r * 2 + p], 0, 0))
    lse = pl.BlockSpec((1, PAIRS, 2 * row_len), lambda r, p, *_: (r, 0, 0))
    return seg, row, mem, lse


def cross_forward(local_map, lengths, seg, queries, keys, values):
    rows, row_len = seg.shape
    mem_len = keys.shape[1]
    seg_specs, row, mem, lse = cross_specs(row_len, mem_len)
    return pl.pallas_call(
        cross_fwd_kernel,
        grid_spec=pltpu.PrefetchScalarGridSpec(
            num_scalar_prefetch=2,
            grid=(rows, 2),
            in_specs=seg_specs + [row, mem, mem],
            out_specs=[row, lse],
        ),
        out_shape=[
            jax.ShapeDtypeStruct(queries.shape, BF16),
            jax.ShapeDtypeStruct((rows, PAIRS, 2 * row_len), F32),
        ],
        compiler_params=FULL_VMEM,
        cost_estimate=CHEAP,
        name="cross_forward",
    )(local_map, lengths, seg[:, None, :], seg[:, :, None], queries, keys, values)


def cross_backward(local_map, lengths, seg, queries, keys, values, grad_mixed, lse_rows):
    rows, row_len = seg.shape
    mem_len = keys.shape[1]
    seg_specs, row, mem, lse = cross_specs(row_len, mem_len)
    return pl.pallas_call(
        cross_bwd_kernel,
        grid_spec=pltpu.PrefetchScalarGridSpec(
            num_scalar_prefetch=2,
            grid=(rows, 2),
            in_specs=seg_specs + [row, mem, mem, row, lse],
            out_specs=[row, mem, mem, pl.BlockSpec((1, D), lambda r, p, *_: (0, 0))],
        ),
        out_shape=[
            jax.ShapeDtypeStruct(queries.shape, BF16),
            jax.ShapeDtypeStruct(keys.shape, BF16),
            jax.ShapeDtypeStruct(values.shape, BF16),
            jax.ShapeDtypeStruct((1, D), F32),
        ],
        compiler_params=FULL_VMEM,
        cost_estimate=CHEAP,
        name="cross_backward",
    )(local_map, lengths, seg[:, None, :], seg[:, :, None], queries, keys, values, grad_mixed, lse_rows)


SMALL_ROWS = 16


def tie(values, *after):
    return lax.optimization_barrier((values, after))[0]


class Clock:
    def __init__(self):
        self.last = ()

    def now(self, values):
        return tie(values, *self.last) if self.last else values

    def tick(self, *arrays):
        self.last = arrays


class Grid:
    def __init__(self, wide, narrow):
        self.wide, self.narrow, self.ring = wide, narrow, wide // 2
        self.devices = wide * narrow
        moves = {
            "z": lambda w, n: ((w + 2) % wide, n),
            "x": lambda w, n: (w ^ 1, n),
            "y": lambda w, n: (w, n ^ 2),
            "c": lambda w, n: (w, n ^ 1),
        }
        self.perms = {}
        for name, move in moves.items():
            pairs = []
            for w in range(wide):
                for n in range(narrow):
                    w2, n2 = move(w, n)
                    pairs.append((w * narrow + n, w2 * narrow + n2))
            self.perms[name] = pairs
        self.clock = Clock()

    def send(self, name, array):
        return lax.ppermute(self.clock.now(array), AXES, self.perms[name])


def segments(first, height, g, rows):
    out, at, end = [], first, first + height
    while at < end:
        k = min(at // rows, g)
        stop = min(end, (k + 1) * rows) if k < g else end
        out.append((k, at - k * rows, at - first, stop - at))
        at = stop
    return out


def half_kernel(parts, ring, wide, g, rows, place, *refs):
    arrays, (out, sems) = refs[:-2], refs[-2:]
    z, x, y = place[0], place[1], place[2]
    height, cols = wide * rows, out.shape[-1]
    copies = []

    def copy(src, dst):
        copies.append(pltpu.make_async_copy(src, dst, sems.at[len(copies)]))

    for which, first_row, count, offset, labels in parts:
        piece = arrays[which]
        for i, (dz, dx, dy) in enumerate(labels):
            row = 2 * lax.rem(z + (ring - dz), ring) + (x + dx - 2 * x * dx)
            col = y + dy - 2 * y * dy
            pieces = segments(offset, count, g, rows)
            if pieces[0][3] == rows and len([p for p in pieces if p[0] < g]) == g:
                copy(
                    piece.at[i, pl.ds(first_row, g * rows)].reshape(g, rows, cols),
                    out.at[col, pl.ds(0, g * height)].reshape(g, wide, rows, cols).at[:, row],
                )
                pieces = [p for p in pieces if p[0] == g]
            for k, matrix_row, at, n in pieces:
                each = rows if k < g else SMALL_ROWS
                first = pl.multiple_of(k * height + row * each + matrix_row, 16)
                copy(piece.at[i, pl.ds(first_row + at, n)], out.at[col, pl.ds(first, n)])
    for one in copies:
        one.start()
    for one in copies:
        one.wait()


def anywhere(count):
    return [pl.BlockSpec(memory_space=pl.ANY)] * count


PLACE = pl.BlockSpec(memory_space=pltpu.SMEM)


def rearrange_kernel(moves, n_in, *refs):
    ins, outs, sems = refs[:n_in], refs[n_in:-1], refs[-1]
    copies = []
    for i, bi, ri, ci, rows, o, bo, ro in moves:
        src = ins[i].at[bi, pl.ds(ri, rows), pl.ds(ci, outs[o].shape[-1])]
        copies.append(pltpu.make_async_copy(src, outs[o].at[bo, pl.ds(ro, rows)], sems.at[len(copies)]))
    for one in copies:
        one.start()
    for one in copies:
        one.wait()


class Rearrange:
    def __init__(self):
        self.ins, self.shapes, self.moves = [], [], []

    def source(self, array):
        for i, known in enumerate(self.ins):
            if known is array:
                return i
        self.ins.append(array)
        return len(self.ins) - 1

    def out(self, blocks, rows, cols):
        self.shapes.append((blocks, rows, cols))
        return len(self.shapes) - 1

    def move(self, out, block, row, array, from_block, first, rows, column=0):
        self.moves.append((self.source(array), from_block, first, column, rows, out, block, row))

    def run(self, clock):
        outs = pl.pallas_call(
            functools.partial(rearrange_kernel, self.moves, len(self.ins)),
            in_specs=anywhere(len(self.ins)),
            out_specs=[pl.BlockSpec(memory_space=pltpu.VMEM)] * len(self.shapes),
            out_shape=[jax.ShapeDtypeStruct(shape, BF16) for shape in self.shapes],
            scratch_shapes=[pltpu.SemaphoreType.DMA((len(self.moves),))],
            compiler_params=BIG_VMEM,
            cost_estimate=CHEAP,
            name="rearrange",
        )(*clock.now(self.ins))
        return list(outs)


class Gather:
    def __init__(self, grid, place, g, height, cols, small=False):
        self.grid, self.place, self.g, self.height, self.cols = grid, place, g, height, cols
        self.rows = (height - (SMALL_ROWS if small else 0)) // g
        self.parts = []

    def put(self, labels, array, first_row, count, offset):
        self.parts.append((labels, array, first_row, count, offset))

    def half(self, *after):
        grid, arrays, parts, n = self.grid, [], [], 0
        for labels, array, first_row, count, offset in self.parts:
            which = [i for i, known in enumerate(arrays) if known is array]
            if not which:
                arrays.append(array)
                which = [len(arrays) - 1]
            parts.append((which[0], first_row, count, offset, labels))
            n += len(labels) * len(segments(offset, count, self.g, self.rows))
        self.own = pl.pallas_call(
            functools.partial(half_kernel, parts, grid.ring, grid.wide, self.g, self.rows),
            in_specs=[PLACE] + anywhere(len(arrays)),
            out_specs=pl.BlockSpec(memory_space=pltpu.VMEM),
            out_shape=jax.ShapeDtypeStruct((2, grid.wide * self.height, self.cols), BF16),
            scratch_shapes=[pltpu.SemaphoreType.DMA((n,))],
            compiler_params=BIG_VMEM,
            cost_estimate=CHEAP,
            name="half_weights",
        )(self.place, *tie(grid.clock.now(arrays), *after))
        return self.own

    def swap(self):
        self.other = self.grid.send("c", self.own)
        return self.other

    def small_rows(self):
        first = self.g * self.grid.wide * self.rows
        own, other = self.grid.clock.now((self.own[:, first:], self.other[:, first:]))
        flip = self.place[3] == 0
        both = jnp.stack((jnp.where(flip, own, other), jnp.where(flip, other, own)))
        return both.reshape(2, 2, self.grid.wide, SMALL_ROWS, -1).astype(F32)


class Square:
    def __init__(self, gather, blocks, height, offset=0):
        self.gather, self.blocks, self.height, self.offset = gather, blocks, height, offset
        self.cut = height // 32 * 16

    def labels(self, dx, dy):
        return [(dz, dx, dy) for dz in range(len(self.blocks))]


def exchange(grid, before, after):
    make = Rearrange()
    cols = (before or after).gather.cols
    depth = len((before or after).blocks)
    heights = [0, 0]
    if before:
        heights = [before.cut, before.height - before.cut]
    total = [h + (after.height if after else 0) for h in heights]
    outs = [make.out(depth, h, cols) for h in total]
    if before:
        (near_x, x_first), (near_y, y_first) = before.near
        for k in range(depth):
            make.move(outs[0], k, 0, near_y, k, y_first, heights[0])
            make.move(outs[1], k, 0, near_x, k, x_first + before.cut, heights[1])
    if after:
        for out, first in zip(outs, heights):
            for k, pieces in enumerate(after.blocks):
                at = first
                for array, block, row, count, column in pieces:
                    make.move(out, k, at, array, block, row, count, column)
                    at += count
    send_x, send_y = make.run(grid.clock)
    from_x, from_y = grid.send("x", send_x), grid.send("y", send_y)
    if before:
        before.gather.put(before.labels(1, 1), from_x, 0, heights[0], before.offset)
        before.gather.put(before.labels(1, 1), from_y, 0, heights[1], before.offset + before.cut)
    if after:
        after.near = ((from_x, heights[0]), (from_y, heights[1]))
        put = after.gather.put
        put(after.labels(0, 0), send_x, heights[0], after.height, after.offset)
        put(after.labels(1, 0), from_x, heights[0], after.height, after.offset)
        put(after.labels(0, 1), from_y, heights[1], after.height, after.offset)
    return from_x, from_y


def unfold(small, count, start, width):
    part = small[:, :, :, :count, start : start + width]
    return part.transpose(3, 2, 1, 0, 4).reshape(count, -1)


def corners(place):
    y, c = place[2], place[3]
    return (2 * y + 1 - c, 2 * (1 - y) + 1 - c), (2 * y + c, 2 * (1 - y) + c)


def column(ref, n, cols):
    return ref[:, pl.ds(pl.multiple_of(n * cols, 128), cols)]


def both_columns(ref, blocks, cols):
    return jnp.concatenate([column(ref, n, cols) for n in blocks], axis=1)


def far_kernel(place, *refs):
    out = refs[-1]
    cols = out.shape[-1]
    for i in range(out.shape[0]):
        a, d = refs[2 * i], refs[2 * i + 1]
        term = dot_tn(a[...], both_columns(d, corners(place)[0], cols))
        for j in range(2):
            out[i, j] = term[:, j * cols : (j + 1) * cols].astype(BF16)


def put_quadrants(x, scratch, k, i, here, outs):
    dx, dy, qx, qy, own = outs
    rows = own.shape[2]
    if here:
        own[i, k] = scratch[k, x]
        qx[i, k] = scratch[k, 1 - x].astype(BF16)
    else:
        qy[i, k] = scratch[k, x].astype(BF16)
        dx[i, k] = scratch[k, 1 - x, pl.ds(0, rows // 2)].astype(BF16)
        dy[i, k] = scratch[k, 1 - x, pl.ds(rows // 2, rows // 2)].astype(BF16)


def near_kernel(place, *refs):
    from_c, *outs, scratch = refs[-7:]
    units, zs, rows, cols = outs[-1].shape
    for i in range(units):
        a, d = refs[2 * i], refs[2 * i + 1]
        term = dot_tn(a[...], both_columns(d, corners(place)[1], cols))
        for j in range(2):
            part = term[:, j * cols : (j + 1) * cols] + from_c[i, j].astype(F32)
            scratch[...] = part.reshape(scratch.shape)
            for k in range(zs):
                put_quadrants(place[1], scratch, k, i, j == 0, outs)


def quadrant_shapes(units, ring, rows, cols):
    half, full = (units, ring, rows // 2, cols), (units, ring, rows, cols)
    return [jax.ShapeDtypeStruct(half, BF16)] * 2 + [
        jax.ShapeDtypeStruct(full, BF16), jax.ShapeDtypeStruct(full, BF16), jax.ShapeDtypeStruct(full, F32)
    ]


def quadrant_specs(units, zs, rows, cols, stepped):
    def at(s, *_):
        return (0, s if stepped else 0, 0, 0)

    half = pl.BlockSpec((units, zs, rows // 2, cols), at)
    full = pl.BlockSpec((units, zs, rows, cols), at)
    return [half] * 2 + [full] * 3


def token_terms(grid, place, pairs, rows, cols, from_c=None):
    units, tokens = len(pairs), pairs[0][0].shape[0]
    height = grid.wide * rows
    zs = max(1, 128 // (2 * rows))
    if 2 * rows >= 128 and height // (2 * rows) > 1 and rows * cols <= 128 * 256:
        zs = min(grid.ring, 2)
    tall = zs * 2 * rows
    in_specs, args = [], []
    for a, d in pairs:
        in_specs += [
            pl.BlockSpec((tokens, tall), lambda s, *_: (0, s)),
            pl.BlockSpec(d.shape, lambda s, *_: (0, 0)),
        ]
        args += [a, d]
    block = pl.BlockSpec((units, 2, tall, cols), lambda s, *_: (0, 0, s, 0))
    scratch = []
    if from_c is None:
        kernel, out_specs = far_kernel, block
        out_shape = jax.ShapeDtypeStruct((units, 2, height, cols), BF16)
    else:
        in_specs.append(block)
        args.append(from_c)
        kernel = near_kernel
        out_specs = quadrant_specs(units, zs, rows, cols, True)
        out_shape = quadrant_shapes(units, grid.ring, rows, cols)
        scratch = [pltpu.VMEM((zs, 2, rows, cols), F32)]
    return pl.pallas_call(
        kernel,
        grid_spec=pltpu.PrefetchScalarGridSpec(
            num_scalar_prefetch=1,
            grid=(height // tall,),
            in_specs=in_specs,
            out_specs=out_specs,
            scratch_shapes=scratch,
        ),
        out_shape=out_shape,
        compiler_params=FULL_VMEM,
        cost_estimate=CHEAP,
        name="weight_terms",
    )(place, *args)


def memory_terms_kernel(near, pairs, place, mem, dk, dv, *refs):
    tokens, refs = refs[: 2 * pairs], refs[2 * pairs :]
    if near:
        from_c, dx, dy, qx, qy, own, acc = refs
    else:
        out, acc = refs
    cols = acc.shape[-1]
    m = pl.program_id(0)
    blocks = corners(place)[1 if near else 0]

    @pl.when(m == 0)
    def _():
        for i in range(pairs):
            term = dot_tn(tokens[2 * i][...], both_columns(tokens[2 * i + 1], blocks, cols))
            for j in range(2):
                acc[i, j] = term[:, j * cols : (j + 1) * cols].reshape(acc.shape[2:])
        acc[pairs:] = jnp.zeros_like(acc[pairs:])
        if near:
            acc[...] += from_c[...].astype(F32).reshape(acc.shape)

    grads = jnp.concatenate([both_columns(d.at[0], blocks, cols) for d in (dk, dv)], axis=1)
    term = dot_tn(mem[0], grads)
    for q in range(4):
        part = term[:, q * cols : (q + 1) * cols].reshape(acc.shape[2:])
        acc[pairs + q // 2, q % 2] += part

    @pl.when(m == pl.num_programs(0) - 1)
    def _():
        if near:
            x = place[1]
            for i in range(pairs + 2):
                for j in range(2):
                    for k in range(own.shape[1]):
                        put_quadrants(x, acc.at[i, j], k, i, j == 0, (dx, dy, qx, qy, own))
        else:
            out[...] = acc[...].reshape(out.shape).astype(BF16)


def memory_terms(grid, place, memory, grads, pairs, rows, cols, from_c=None):
    units, (mems, length, wide_cols) = len(pairs) + 2, memory.shape
    height = grid.wide * rows
    near = from_c is not None
    one = pl.BlockSpec((1, length, wide_cols), lambda m, *_: (m, 0, 0))
    term = pl.BlockSpec((units, 2, height, cols), lambda m, *_: (0, 0, 0, 0))
    tokens = [array for pair in pairs for array in pair]
    return pl.pallas_call(
        functools.partial(memory_terms_kernel, near, len(pairs)),
        grid_spec=pltpu.PrefetchScalarGridSpec(
            num_scalar_prefetch=1,
            grid=(mems,),
            in_specs=[one] * 3
            + [pl.BlockSpec(a.shape, lambda m, *_: (0, 0)) for a in tokens]
            + ([term] if near else []),
            out_specs=quadrant_specs(units, grid.ring, rows, cols, False) if near else term,
            scratch_shapes=[pltpu.VMEM((units, 2, grid.ring, 2, rows, cols), F32)],
        ),
        out_shape=quadrant_shapes(units, grid.ring, rows, cols)
        if near
        else jax.ShapeDtypeStruct((units, 2, height, cols), BF16),
        compiler_params=FULL_VMEM,
        cost_estimate=CHEAP,
        name="memory_terms",
    )(place, memory, *grads, *tokens, *([from_c] if near else []))


def add_corners_kernel(qx, qy, from_x, from_y, sx, sy):
    half = from_x.shape[2]
    first, second = pl.ds(0, half), pl.ds(half, half)
    sx[0, :, first] = qx[0, :, first]
    sx[0, :, second] = (qx[0, :, second].astype(F32) + from_y[0].astype(F32)).astype(BF16)
    sy[0, :, first] = (qy[0, :, first].astype(F32) + from_x[0].astype(F32)).astype(BF16)
    sy[0, :, second] = qy[0, :, second]


def add_corners(qx, qy, from_x, from_y):
    units, ring, rows, cols = qx.shape
    zs = ring if units > 1 else 1
    full = pl.BlockSpec((1, zs, rows, cols), lambda i, k: (i, k, 0, 0))
    half = pl.BlockSpec((1, zs, rows // 2, cols), lambda i, k: (i, k, 0, 0))
    return pl.pallas_call(
        add_corners_kernel,
        grid=(units, ring // zs),
        in_specs=[full, full, half, half],
        out_specs=[full, full],
        out_shape=[jax.ShapeDtypeStruct(qx.shape, BF16)] * 2,
        compiler_params=FULL_VMEM,
        cost_estimate=CHEAP,
        name="add_corners",
    )(qx, qy, from_x, from_y)


class Reduce:
    def __init__(self, grid, place, terms, rows):
        self.grid, self.place, self.terms, self.rows = grid, place, terms, rows

    def far(self):
        self.out = self.terms(None)
        return self.out

    def swap(self):
        self.from_c = self.grid.send("c", self.out)
        return self.from_c

    def near(self):
        self.dx, self.dy, self.qx, self.qy, self.own = self.terms(self.grid.clock.now(self.from_c))
        return self.dx

    def across(self):
        self.from_x, self.from_y = self.grid.send("x", self.dx), self.grid.send("y", self.dy)
        return self.from_x, self.from_y

    def add(self):
        from_x = self.grid.clock.now(self.from_x)
        self.sx, self.sy = add_corners(self.qx, self.qy, from_x, self.from_y)
        return self.sx

    def pairs(self):
        self.back_x, self.back_y = self.grid.send("x", self.sx), self.grid.send("y", self.sy)
        return self.back_x, self.back_y

    def chunk(self, step):
        index = lax.rem(self.place[0] + (self.grid.ring - step), self.grid.ring)
        parts = [
            lax.dynamic_index_in_dim(a, index, 1, keepdims=False) for a in (self.own, self.back_x, self.back_y)
        ]
        return parts[0] + parts[1].astype(F32) + parts[2].astype(F32)


class RingSum:
    def __init__(self, grid, reduces):
        self.grid, self.reduces, self.done, self.came = grid, reduces, 0, None

    def step(self, *after):
        self.done += 1
        total = jnp.concatenate([r.chunk(self.done % self.grid.ring) for r in self.reduces], axis=0)
        if self.came is not None:
            total = total + tie(self.grid.clock.now(self.came), *after).astype(F32)
        if self.done == self.grid.ring:
            self.came = total
        else:
            self.came = self.grid.send("z", total.astype(BF16))
        return self.came


class SmallSum:
    def __init__(self, grid, place, terms):
        self.grid, self.place, self.done = grid, place, 0
        self.mine = terms.reshape(grid.ring, 2, 2, 2, -1)

    def step(self):
        grid, place = self.grid, self.place
        if self.done < 3:
            name, axis, at = ("c", "y", "x")[self.done], 3 - self.done, place[3 - self.done]
            far = lax.dynamic_index_in_dim(self.mine, 1 - at, axis, keepdims=False)
            near = lax.dynamic_index_in_dim(self.mine, at, axis, keepdims=False)
            self.mine = near + grid.send(name, far)
        else:
            index = lax.rem(place[0] + (grid.ring - (self.done - 2)), grid.ring)
            total = lax.dynamic_index_in_dim(self.mine, index, 0, keepdims=False)
            self.came = grid.send("z", total if self.done == 3 else total + self.came)
        self.done += 1
        return self.mine if self.done <= 3 else self.came

    def result(self):
        return lax.dynamic_index_in_dim(self.mine, self.place[0], 0, keepdims=False) + self.came


def halves(place, own, other):
    c = place[3]
    return [(2 * y + core, y, half) for half, core in ((own, c), (other, 1 - c)) for y in range(2)]


def at_block(n, cols):
    return pl.ds(pl.multiple_of(n * cols, 128), cols)


def times_t(place, d, own, other):
    cols = own.shape[-1]
    return sum(dot_nt(d[:, at_block(n, cols)], half[y]) for n, y, half in halves(place, own, other))


def norm_parts(values):
    centre = values - jnp.mean(values, axis=-1, keepdims=True)
    scale = lax.rsqrt(jnp.mean(centre * centre, axis=-1, keepdims=True) + EPSILON)
    return centre * scale, scale


def norm_back(normed, scale, gain, grad):
    inner = grad * gain
    back = scale * (
        inner
        - jnp.mean(inner, axis=-1, keepdims=True)
        - normed * jnp.mean(inner * normed, axis=-1, keepdims=True)
    )
    return back, jnp.sum(grad * normed, axis=0, keepdims=True), jnp.sum(grad, axis=0, keepdims=True)


def column_sum(values):
    return jnp.sum(values.astype(F32), axis=0, keepdims=True)


GAIN, BIAS = 0, 3


def row(vectors, i):
    return vectors[i : i + 1, :]


def memory_kernel(place, mem, vectors, k_own, k_other, v_own, v_other, keys, values):
    cols = k_own.shape[-1]
    for n, y, half in halves(place, k_own, k_other):
        keys[0, :, at_block(n, cols)] = dot_nn(mem[0], half[y]).astype(BF16)
    for n, y, half in halves(place, v_own, v_other):
        bias = vectors[BIAS + 6 : BIAS + 7, at_block(n, cols)]
        values[0, :, at_block(n, cols)] = (dot_nn(mem[0], half[y]) + bias).astype(BF16)


def qkv_kernel(place, tokens, vectors, *refs):
    weights, (normed, q, k, v) = refs[:6], refs[6:]
    n, _ = norm_parts(tokens[...].astype(F32))
    normed[...] = (n * row(vectors, GAIN) + row(vectors, BIAS)).astype(BF16)
    cols = weights[0].shape[-1]
    for i, (out, bias_at) in enumerate(((q, 1), (k, None), (v, 2))):
        for n, y, half in halves(place, weights[2 * i], weights[2 * i + 1]):
            term = dot_nn(normed[...], half[y])
            if bias_at is not None:
                term = term + vectors[BIAS + bias_at : BIAS + bias_at + 1, at_block(n, cols)]
            out[:, at_block(n, cols)] = term.astype(BF16)


def middle_kernel(place, tokens, mixed, vectors, so_own, so_other, cq_own, cq_other, after, normed, queries):
    cols = so_own.shape[-1]
    for n, y, half in halves(place, so_own, so_other):
        at = at_block(n, cols)
        after[:, at] = tokens[:, at].astype(F32) + dot_nn(mixed[...], half[y]) + vectors[BIAS + 3 : BIAS + 4, at]
    n, _ = norm_parts(after[...])
    normed[...] = (n * row(vectors, GAIN + 1) + row(vectors, BIAS + 4)).astype(BF16)
    for n, y, half in halves(place, cq_own, cq_other):
        at = at_block(n, cols)
        queries[:, at] = (dot_nn(normed[...], half[y]) + vectors[BIAS + 5 : BIAS + 6, at]).astype(BF16)


def cross_out_kernel(place, before, mixed, vectors, own, other, after, normed):
    cols = own.shape[-1]
    for n, y, half in halves(place, own, other):
        at = at_block(n, cols)
        after[:, at] = before[:, at] + dot_nn(mixed[...], half[y]) + vectors[BIAS + 7 : BIAS + 8, at]
    n, _ = norm_parts(after[...])
    normed[...] = (n * row(vectors, GAIN + 2) + row(vectors, BIAS + 8)).astype(BF16)


def up_kernel(place, normed, bias, own, other, act, slope):
    c, cols = place[3], own.shape[-1]
    y = pl.program_id(0)
    for n, half in ((2 * y + c, own), (2 * y + 1 - c, other)):
        for j in range(4):
            at = at_block(4 * n + j, cols)
            u = dot_nn(normed[...], half[0, j * D : (j + 1) * D]) + bias[:, at]
            below = 0.5 * (1.0 + lax.erf(u * (1.0 / math.sqrt(2.0))))
            act[:, at] = (u * below).astype(BF16)
            slope[:, at] = (below + u * jnp.exp(-0.5 * u * u) * (1.0 / math.sqrt(2.0 * math.pi))).astype(BF16)


def down_kernel(place, after, act, vectors, own, other, out):
    c, y = place[3], pl.program_id(0)
    cols = own.shape[-1]
    for n, half in ((2 * y + c, own), (2 * y + 1 - c, other)):
        at = at_block(n, cols)
        total = after[:, at] + dot_nn(act[...], half[0]) + vectors[BIAS + 9 : BIAS + 10, at]
        out[:, at] = total.astype(BF16)


def down_back_kernel(place, grad, slope, own, other, grad_pre, bias_grad):
    back = (times_t(place, grad, own, other) * slope[...].astype(F32)).astype(BF16)
    grad_pre[...] = back
    bias_grad[...] = column_sum(back)


def up_back_kernel(
    place, grad_pre, grad_out, after, vectors, own, other, co_own, co_other,
    grad, branch, mixed, gain_grad, shift_grad, out_grad, last_grad, total,
):
    c, y = place[3], pl.program_id(0)
    cols = own.shape[-1]
    term = sum(
        dot_nt(grad_pre[:, at_block(4 * n + j, cols)], half[0, j * D : (j + 1) * D])
        for n, half in ((2 * y + c, own), (2 * y + 1 - c, other))
        for j in range(4)
    )

    @pl.when(y == 0)
    def _():
        total[...] = term

    @pl.when(y == 1)
    def _():
        n, scale = norm_parts(after[...])
        back, gain_grad[...], shift_grad[...] = norm_back(n, scale, row(vectors, GAIN + 2), total[...] + term)
        out = grad_out[...].astype(F32) + back
        grad[...] = out
        branch[...] = out.astype(BF16)
        out_grad[...] = column_sum(branch[...])
        last_grad[...] = column_sum(grad_out[...])
        mixed[...] = times_t(place, branch, co_own, co_other).astype(BF16)


def middle_back_kernel(
    place, grad_queries, grad_after, after, vectors, cq_own, cq_other, so_own, so_other,
    grad, branch, mixed, gain_grad, shift_grad, out_grad, query_grad,
):
    n, scale = norm_parts(after[...])
    dense = times_t(place, grad_queries, cq_own, cq_other)
    back, gain_grad[...], shift_grad[...] = norm_back(n, scale, row(vectors, GAIN + 1), dense)
    out = grad_after[...] + back
    grad[...] = out
    branch[...] = out.astype(BF16)
    out_grad[...] = column_sum(branch[...])
    query_grad[...] = column_sum(grad_queries[...])
    mixed[...] = times_t(place, branch, so_own, so_other).astype(BF16)


def first_back_kernel(place, tokens, grad_after, gq, gk, gv, vectors, *refs):
    weights, (grad, gain_grad, shift_grad, query_grad, value_grad) = refs[:6], refs[6:]
    n, scale = norm_parts(tokens[...].astype(F32))
    dense = sum(
        times_t(place, d, weights[2 * i], weights[2 * i + 1]) for i, d in enumerate((gq, gk, gv))
    )
    back, gain_grad[...], shift_grad[...] = norm_back(n, scale, row(vectors, GAIN), dense)
    grad[...] = (grad_after[...] + back).astype(BF16)
    query_grad[...] = column_sum(gq[...])
    value_grad[...] = column_sum(gv[...])


def memory_back_kernel(place, gk, gv, k_own, k_other, v_own, v_other, grad):
    total = times_t(place, gk.at[0], k_own, k_other) + times_t(place, gv.at[0], v_own, v_other)
    grad[0] = total.astype(BF16)


def in_place(array):
    return pl.pallas_call(
        lambda _, out: None,
        in_specs=anywhere(1),
        out_specs=pl.BlockSpec(memory_space=pl.ANY),
        out_shape=jax.ShapeDtypeStruct(array.shape, array.dtype),
        input_output_aliases={0: 0},
        compiler_params=BIG_VMEM,
        cost_estimate=CHEAP,
        name="in_place",
    )(array)


def dense_call(kernel, name, place, ins, outs, grid=(1,), scratch=(), params=BIG_VMEM):
    def spec(array, block, index):
        block = block or array.shape
        zeros = (0,) * len(block)
        return pl.BlockSpec(block, index or (lambda *_: zeros))

    return pl.pallas_call(
        kernel,
        grid_spec=pltpu.PrefetchScalarGridSpec(
            num_scalar_prefetch=1,
            grid=grid,
            in_specs=[spec(*one) for one in ins],
            out_specs=[spec(*one) for one in outs],
            scratch_shapes=scratch,
        ),
        out_shape=[one[0] for one in outs],
        compiler_params=params,
        cost_estimate=CHEAP,
        name=name,
    )(place, *[one[0] for one in ins])


def full(array):
    return (array, None, None)


def result(shape, dtype):
    return (jax.ShapeDtypeStruct(shape, dtype), None, None)


def matrix(gathered, i, height=D):
    block = (2, height, gathered.own.shape[-1])
    return [(half, block, lambda *_: (0, i, 0)) for half in (gathered.own, gathered.other)]


def by_y(gathered):
    block = (1,) + gathered.own.shape[1:]
    return [(half, block, lambda y, *_: (y, 0, 0)) for half in (gathered.own, gathered.other)]


def by_rows(gathered, rows):
    block = (2, rows, gathered.own.shape[-1])
    return [(half, block, lambda s, *_: (0, s, 0)) for half in (gathered.own, gathered.other)]


def local(
    shape,
    tokens,
    memory,
    segment_ids,
    page_map,
    mem_lengths,
    gains,
    biases,
    fc1_bias,
    self_qkv,
    self_out,
    cross_q,
    cross_kv,
    cross_out,
    fc1,
    fc2,
    cotangent,
):
    grid = Grid(*shape)
    wide_at, narrow_at = lax.axis_index("wide"), lax.axis_index("narrow")
    place = jnp.stack((wide_at // 2, wide_at % 2, narrow_at // 2, narrow_at % 2)).astype(jnp.int32)
    devices = grid.devices
    mem_count, token_count = memory.shape[0], tokens.shape[0]
    rows, cols = self_out.shape

    each, up_each = gains.shape[1], fc1_bias.size
    n_gain, n_bias = gains.size, biases.size
    small = jnp.pad(
        jnp.concatenate((gains, biases), axis=0), ((0, SMALL_ROWS - 13), (0, cols - each))
    )
    small = lax.dynamic_update_slice(small, fc1_bias[None], (0, 128))
    send, clock = grid.send, grid.clock
    now, tick = clock.now, clock.tick
    steps = grid.ring - 1
    gather = functools.partial(Gather, grid, place)
    ckv_height = 2 * rows + SMALL_ROWS
    fc2_rows = fc2.shape[0]
    part = fc2_rows // 2
    g_ckv = gather(2, ckv_height, cols, True)
    g_qkv = gather(3, 3 * rows, cols)
    g_mix = gather(3, 3 * rows, cols)
    g_fc1 = gather(4, 4 * rows, cols)
    g_fc2 = gather(1, fc2_rows, cols)

    start = Rearrange()
    out = start.out(1, 5 * rows, cols)
    for k, (array, i) in enumerate(((cross_kv, 0), (cross_kv, 1), (self_qkv, 0), (self_qkv, 1), (self_qkv, 2))):
        start.move(out, 0, k * rows, array, i, 0, rows)
    ring_one = start.run(clock)
    ring_one.append(send("z", ring_one[-1]))
    top = Square(g_fc2, [[(fc2[None], 0, 0, part, 0)]], part)
    memory = in_place(memory)
    more = Rearrange()
    out = more.out(1, 3 * rows, cols)
    for k, array in enumerate((self_out, cross_q, cross_out)):
        more.move(out, 0, k * rows, array[None], 0, 0, rows)
    out = more.out(1, 4 * rows + part, cols)
    for k in range(4):
        more.move(out, 0, k * rows, fc1[None], 0, 0, rows, k * cols)
    more.move(out, 0, 4 * rows, fc2[None], 0, part, part)
    ring_mix, ring_up = [[array] for array in more.run(clock)]
    tick(ring_one[-1], memory, ring_mix[0], ring_up[0], *exchange(grid, None, top))
    ring_one.append(send("z", ring_one[-1]))
    ring_small = [small[None]]
    ring_small.append(send("z", ring_small[-1]))
    tick(ring_one[-1], ring_small[-1], *exchange(grid, top, None))
    for _ in range(steps - 2):
        ring_one.append(send("z", ring_one[-1]))
        ring_small.append(send("z", ring_small[-1]))
        tick(ring_one[-1], ring_small[-1])
    ring_small.append(send("z", ring_small[-1]))

    def from_ring(arrays, first, count):
        return [[(array, 0, first, count, 0)] for array in arrays]

    ckv = Square(
        g_ckv, [a + b for a, b in zip(from_ring(ring_one, 0, 2 * rows), from_ring(ring_small, 0, SMALL_ROWS))],
        ckv_height,
    )
    qkv = Square(g_qkv, from_ring(ring_one, 2 * rows, 3 * rows), 3 * rows)
    ring_mix.append(send("z", ring_mix[-1]))
    ring_up.append(send("z", ring_up[-1]))
    tick(ring_mix[-1], ring_up[-1], *exchange(grid, None, ckv))

    make = Rearrange()
    out = make.out(4, part, cols)
    (_, own, own_at, _, _), (_, by_x, x_at, _, _), (_, by_y_, y_at, _, _), (_, low, _, _, _), (_, high, _, _, _) = g_fc2.parts
    g_fc2.parts = []
    for k, (array, at) in enumerate(((own, own_at), (by_x, x_at), (by_y_, y_at))):
        make.move(out, k, 0, array, 0, at, part)
    make.move(out, 3, 0, low, 0, 0, top.cut)
    make.move(out, 3, top.cut, high, 0, 0, part - top.cut)
    came = exchange(grid, ckv, qkv)
    ring_top = make.run(clock)
    ring_up.append(send("z", ring_up[-1]))
    for _ in range(steps - 1):
        ring_mix.append(send("z", ring_mix[-1]))
    tick(ring_mix[-1], ring_up[-1], ring_top[-1], *came)

    mix = Square(g_mix, from_ring(ring_mix, 0, 3 * rows), 3 * rows)
    came = exchange(grid, qkv, mix)
    for _ in range(steps - 2):
        ring_up.append(send("z", ring_up[-1]))
    g_ckv.half(g_mix.parts[0][1])
    g_ckv.swap()
    small_all = g_ckv.small_rows()
    vectors = unfold(small_all, 13, 0, each)
    up_bias = unfold(small_all, 1, 128, up_each)
    mem_block = (1,) + memory.shape[1:]
    mem_shape = jax.ShapeDtypeStruct(memory.shape, BF16)

    def by_memory(array):
        return (array, mem_block, lambda m, *_: (m, 0, 0))

    mem_keys, mem_values = dense_call(
        memory_kernel, "memory_keys_values", place,
        [by_memory(now(memory)), full(vectors)] + matrix(g_ckv, 0) + matrix(g_ckv, 1),
        [by_memory(mem_shape), by_memory(mem_shape)], grid=(mem_count,),
    )
    tick(ring_up[-1], mem_keys, *came)

    up = Square(g_fc1, from_ring(ring_up, 0, 4 * rows), 4 * rows)
    low = Square(g_fc2, from_ring(ring_up, 4 * rows, part), part, part)
    came = exchange(grid, mix, up)
    ring_top.append(send("z", ring_top[-1]))
    g_qkv.half(g_fc1.parts[0][1])
    g_qkv.swap()
    wide_row = (token_count, D)
    normed_one, self_queries, self_keys, self_values = dense_call(
        qkv_kernel, "self_qkv", place,
        [full(now(tokens)), full(vectors)] + matrix(g_qkv, 0) + matrix(g_qkv, 1) + matrix(g_qkv, 2),
        [result(wide_row, BF16)] * 4,
    )
    self_mixed, self_lse = self_forward(segment_ids, self_queries, self_keys, self_values)
    tick(self_mixed, ring_top[-1], *came)

    came = exchange(grid, up, low)
    g_mix.half(g_fc2.parts[0][1])
    g_mix.swap()
    ring_top.append(send("z", ring_top[-1]))
    after_self, normed_two, cross_queries = dense_call(
        middle_kernel, "self_out_cross_q", place,
        [full(tokens), full(now(self_mixed)), full(vectors)] + matrix(g_mix, 0) + matrix(g_mix, 1),
        [result(wide_row, F32), result(wide_row, BF16), result(wide_row, BF16)],
    )
    first_mem = lax.axis_index(AXES) * mem_count
    local_map = (page_map - first_mem).reshape(-1).astype(jnp.int32)
    picks = local_map[:, None] == jnp.arange(mem_count, dtype=jnp.int32)[None, :]
    row_lengths = jnp.sum(jnp.where(picks, mem_lengths[None, :], 0), axis=-1).astype(jnp.int32)
    cross_mixed, cross_lse = cross_forward(
        local_map, row_lengths, segment_ids, cross_queries, mem_keys, mem_values
    )
    tick(cross_mixed, ring_top[-1], *came)

    came = exchange(grid, low, None)
    for _ in range(steps - 2):
        ring_top.append(send("z", ring_top[-1]))
    g_fc1.half()
    g_fc1.swap()
    after_cross, normed_three = dense_call(
        cross_out_kernel, "cross_out", place,
        [full(after_self), full(now(cross_mixed)), full(vectors)] + matrix(g_mix, 2),
        [result(wide_row, F32), result(wide_row, BF16)],
    )
    hidden = up_bias.shape[1]
    activated, slope = dense_call(
        up_kernel, "fc1_gelu", place,
        [full(normed_three), full(up_bias)] + by_y(g_fc1),
        [result((token_count, hidden), BF16)] * 2, grid=(2,),
    )
    tick(activated, ring_top[-1], *came)
    spread = [(0, 0), (1, 0), (0, 1), (1, 1)]
    for step, array in enumerate(ring_top):
        g_fc2.put([(step, dx, dy) for dx, dy in spread], array, 0, part, 0)

    def settle(pairs, shard):
        part_rows, part_cols = shard.shape
        return Reduce(
            grid, place,
            lambda from_c: token_terms(grid, place, pairs, part_rows, part_cols, from_c),
            part_rows,
        )

    one_row = result((1, D), F32)
    r_fc2 = settle([(now(activated), cotangent)], fc2)
    r_fc2.far()
    r_fc2.swap()
    g_fc2.half()
    g_fc2.swap()
    tick(r_fc2.near(), g_fc2.other)
    slab = hidden // 4
    some = lambda array: (array, (token_count, slab), lambda s, *_: (0, s))
    grad_pre, grad_up_bias = dense_call(
        down_back_kernel, "fc2_gelu_back", place,
        [full(now(cotangent)), some(slope)] + by_rows(g_fc2, slab),
        [
            some(jax.ShapeDtypeStruct((token_count, hidden), BF16)),
            (jax.ShapeDtypeStruct((1, hidden), F32), (1, slab), lambda s, *_: (0, s)),
        ],
        grid=(4,), params=FULL_VMEM,
    )
    r_fc1 = settle([(normed_three, grad_pre)], fc1)
    tick(r_fc1.far(), *r_fc2.across())
    r_fc2.add()
    r_fc1.swap()
    (
        grad_after_cross, grad_branch_two, grad_cross_mixed,
        grad_gain_three, grad_bias_eight, grad_bias_seven, grad_bias_nine,
    ) = dense_call(
        up_back_kernel, "fc1_norm_back", place,
        [full(now(grad_pre)), full(cotangent), full(after_cross), full(vectors)]
        + by_y(g_fc1) + matrix(g_mix, 2),
        [result(wide_row, F32), result(wide_row, BF16), result(wide_row, BF16)] + [one_row] * 4,
        grid=(2,), scratch=[pltpu.VMEM(wide_row, F32)], params=FULL_VMEM,
    )
    tick(r_fc1.near(), grad_cross_mixed, *r_fc2.pairs())
    ring_fc2 = RingSum(grid, [r_fc2])

    grad_cq, grad_ck, grad_cv, grad_bias_six = cross_backward(
        local_map, row_lengths, segment_ids, cross_queries, mem_keys, mem_values,
        now(grad_cross_mixed), cross_lse,
    )
    tick(grad_cq, ring_fc2.step(), *r_fc1.across())
    r_fc1.add()
    grad_cq = now(grad_cq)
    cross_pairs = [(cross_mixed, grad_branch_two), (normed_two, grad_cq)]
    r_cross = Reduce(
        grid, place,
        lambda from_c: memory_terms(
            grid, place, memory, (grad_ck, grad_cv), cross_pairs, rows, cols, from_c
        ),
        rows,
    )
    r_cross.far()
    r_cross.swap()
    (
        grad_after_self, grad_branch_one, grad_self_mixed,
        grad_gain_two, grad_bias_four, grad_bias_three, grad_bias_five,
    ) = dense_call(
        middle_back_kernel, "cross_q_norm_back", place,
        [full(grad_cq), full(grad_after_cross), full(after_self), full(vectors)]
        + matrix(g_mix, 1) + matrix(g_mix, 0),
        [result(wide_row, F32), result(wide_row, BF16), result(wide_row, BF16)] + [one_row] * 4,
        params=FULL_VMEM,
    )
    tick(r_cross.near(), grad_self_mixed, ring_fc2.step(), *r_fc1.pairs())
    ring_fc1 = RingSum(grid, [r_fc1])

    grad_sq, grad_sk, grad_sv = self_backward(
        segment_ids, self_queries, self_keys, self_values, now(grad_self_mixed), self_lse
    )
    r_self = settle(
        [(normed_one, grad_sq), (normed_one, grad_sk), (normed_one, grad_sv), (self_mixed, grad_branch_one)],
        cross_q,
    )
    tick(r_self.far(), ring_fc2.step(), *r_cross.across())
    ring_fc2.step()
    r_cross.add()
    r_self.swap()
    grad_tokens, grad_gain_one, grad_bias_zero, grad_bias_one, grad_bias_two = dense_call(
        first_back_kernel, "self_qkv_norm_back", place,
        [full(tokens), full(grad_after_self)] + [full(d) for d in now((grad_sq, grad_sk, grad_sv))]
        + [full(vectors)] + matrix(g_qkv, 0) + matrix(g_qkv, 1) + matrix(g_qkv, 2),
        [result(wide_row, BF16)] + [one_row] * 4,
        params=FULL_VMEM,
    )
    ring_fc1.step()
    ring_fc1.step(grad_tokens)
    tick(r_self.near(), grad_tokens, ring_fc1.came, *r_cross.pairs())
    ring_cross = RingSum(grid, [r_cross])

    def by_device(array):
        return array.reshape(array.shape[0], devices, -1).transpose(1, 0, 2).reshape(devices, -1)

    small_grads = jnp.concatenate(
        (
            by_device(
                jnp.concatenate(
                    (
                        grad_gain_one, grad_gain_two, grad_gain_three,
                        grad_bias_zero, grad_bias_one, grad_bias_two, grad_bias_three, grad_bias_four,
                        grad_bias_five, grad_bias_six, grad_bias_seven, grad_bias_eight, grad_bias_nine,
                    ),
                    axis=0,
                )
            ),
            by_device(grad_up_bias),
        ),
        axis=1,
    )
    small_sum = SmallSum(grid, place, now(small_grads))
    (grad_memory,) = dense_call(
        memory_back_kernel, "memory_back", place,
        [by_memory(a) for a in now((grad_ck, grad_cv))] + matrix(g_ckv, 0) + matrix(g_ckv, 1),
        [by_memory(mem_shape)], grid=(mem_count,), params=FULL_VMEM,
    )
    ring_fc1.step()
    tick(grad_memory, ring_fc1.came, ring_cross.step(), small_sum.step(), *r_self.across())
    r_self.add()
    (layer_out,) = dense_call(
        down_kernel, "fc2", place,
        [full(after_cross), full(now(activated)), full(vectors)] + by_y(g_fc2),
        [result(wide_row, BF16)], grid=(2,), params=FULL_VMEM,
    )
    ring_cross.step()
    ring_cross.step(layer_out)
    tick(layer_out, ring_cross.came, small_sum.step(), *r_self.pairs())
    ring_fc1.step()
    ring_self = RingSum(grid, [r_self])
    for _ in range(steps):
        tick(ring_self.step(), small_sum.step())
    for ring in (ring_fc2, ring_fc1, ring_cross, ring_self):
        while ring.done < grid.ring:
            ring.step()
    while small_sum.done < steps + 3:
        tick(small_sum.step())
    small_shard = small_sum.result()
    came_cross, came_self = ring_cross.came, ring_self.came
    return (
        layer_out,
        grad_tokens,
        grad_memory,
        small_shard[:n_gain].reshape(gains.shape),
        small_shard[n_gain : n_gain + n_bias].reshape(biases.shape),
        small_shard[n_gain + n_bias :],
        came_self[:3],
        came_self[3],
        came_cross[1],
        came_cross[2:],
        came_cross[0],
        ring_fc1.came[0],
        ring_fc2.came[0],
    )


def solution(mesh):
    shape = (mesh.shape["wide"], mesh.shape["narrow"])
    in_specs = (
        P(AXES, None),
        P(AXES, None, None),
        P(AXES, None),
        P(AXES, None),
        P(AXES),
        P(None, AXES),
        P(None, AXES),
        P(AXES),
        P(None, "wide", "narrow"),
        P("wide", "narrow"),
        P("wide", "narrow"),
        P(None, "wide", "narrow"),
        P("wide", "narrow"),
        P("wide", "narrow"),
        P("wide", "narrow"),
        P(AXES, None),
    )
    out_specs = (
        P(AXES, None),
        P(AXES, None),
        P(AXES, None, None),
        P(None, AXES),
        P(None, AXES),
        P(AXES),
        P(None, "wide", "narrow"),
        P("wide", "narrow"),
        P("wide", "narrow"),
        P(None, "wide", "narrow"),
        P("wide", "narrow"),
        P("wide", "narrow"),
        P("wide", "narrow"),
    )
    return jax.shard_map(
        functools.partial(local, shape), mesh=mesh, in_specs=in_specs, out_specs=out_specs, check_vma=False
    )
```

```python
import functools
import math

import jax
import jax.numpy as jnp
from jax import lax
from jax.experimental import pallas as pl
from jax.experimental.pallas import tpu as pltpu
from jax.sharding import PartitionSpec as P

D = 1024
HEADS = 16
HEAD_DIM = 64
PAIRS = HEADS // 2

EPSILON = 1e-05
NEG_FILL = -1e30
LOG2E = math.log2(math.e)
SCALE = 1.0 / math.sqrt(HEAD_DIM)
AXES = ("wide", "narrow")

F32 = jnp.float32
BF16 = jnp.bfloat16
VMEM = 24 * 2**20
CHEAP = pl.CostEstimate(flops=10**6, bytes_accessed=10**5, transcendentals=0)
BIG_VMEM = pltpu.CompilerParams(vmem_limit_bytes=VMEM)
FULL_VMEM = pltpu.CompilerParams(vmem_limit_bytes=60 * 2**20)


def dot_nt(a, b):
    return lax.dot_general(a, b, (((1,), (1,)), ((), ())), preferred_element_type=F32)


def dot_nn(a, b):
    return lax.dot_general(a, b, (((1,), (0,)), ((), ())), preferred_element_type=F32)


def dot_tn(a, b):
    return lax.dot_general(a, b, (((0,), (0,)), ((), ())), preferred_element_type=F32)


def two_heads(block):
    lane = lax.broadcasted_iota(jnp.int32, block.shape, 1)
    zero = jnp.zeros_like(block)
    return jnp.concatenate(
        (jnp.where(lane < HEAD_DIM, block, zero), jnp.where(lane < HEAD_DIM, zero, block)), axis=0
    )


def own_heads(both):
    half = both.shape[1] // 2
    line = lax.broadcasted_iota(jnp.int32, (both.shape[0], half), 0)
    return jnp.transpose(jnp.where(line < HEAD_DIM, both[:, :half], both[:, half:]))


CUTS = [slice(128 * h, 128 * h + 128) for h in range(PAIRS)]


def heads_forward(q_ref, k_ref, v_ref, valid, put):
    scores = [dot_nt(k_ref(cut), two_heads(q_ref(cut))) for cut in CUTS]
    weights, lses = [], []
    for one in scores:
        one = jnp.where(valid, one * (SCALE * LOG2E), NEG_FILL)
        top = jnp.max(one, axis=0, keepdims=True)
        expo = jnp.exp2(one - top)
        total = jnp.sum(expo, axis=0, keepdims=True)
        weights.append((expo * (1.0 / total)).astype(BF16))
        lses.append(top + jnp.log2(total))
    for h, cut in enumerate(CUTS):
        put(h, own_heads(dot_tn(v_ref(cut), weights[h])).astype(BF16), lses[h])


def heads_backward(q_ref, k_ref, v_ref, do_ref, lse_of, valid, put, group=4):
    for first in range(0, PAIRS, group):
        hs = range(first, first + group)
        qs = [two_heads(q_ref(CUTS[h])) for h in hs]
        ds = [two_heads(do_ref(CUTS[h])) for h in hs]
        scores = [dot_nt(k_ref(CUTS[h]), q) for h, q in zip(hs, qs)]
        grads = [dot_nt(v_ref(CUTS[h]), d) for h, d in zip(hs, ds)]
        weights, grad_scores = [], []
        for h, one, grad in zip(hs, scores, grads):
            weight = jnp.where(valid, jnp.exp2(one * (SCALE * LOG2E) - lse_of(h)), 0.0)
            inner = jnp.sum(weight * grad, axis=0, keepdims=True)
            grad_scores.append((weight * (grad - inner)).astype(BF16))
            weights.append(weight.astype(BF16))
        for h, q, d, weight, grad in zip(hs, qs, ds, weights, grad_scores):
            grad_q = (own_heads(dot_tn(k_ref(CUTS[h]), grad)) * SCALE).astype(BF16)
            grad_k = (dot_nn(grad, q) * SCALE).astype(BF16)
            put(h, grad_q, grad_k, dot_nn(weight, d).astype(BF16))


def columns_in(ref):
    return lambda cut: ref[:, cut]


def memory_columns(ref):
    return lambda cut: ref[0, :, cut]


def self_valid(seg_row, seg_col):
    length = seg_row.shape[-1]
    key = lax.broadcasted_iota(jnp.int32, (length, length), 0)
    tok = lax.broadcasted_iota(jnp.int32, (length, length), 1)
    one = (key <= tok) & (seg_row == seg_col)
    return jnp.concatenate((one, one), axis=1)


def self_fwd_kernel(seg_row, seg_col, q_ref, k_ref, v_ref, o_ref, lse_ref):
    def put(h, mixed, lse):
        o_ref[:, CUTS[h]] = mixed
        lse_ref[0, h : h + 1, :] = lse

    heads_forward(
        columns_in(q_ref), columns_in(k_ref), columns_in(v_ref), self_valid(seg_row[0], seg_col[0]), put
    )


def self_bwd_kernel(seg_row, seg_col, q_ref, k_ref, v_ref, do_ref, lse_ref, dq_ref, dk_ref, dv_ref):
    def put(h, grad_q, grad_k, grad_v):
        dq_ref[:, CUTS[h]] = grad_q
        dk_ref[:, CUTS[h]] = grad_k
        dv_ref[:, CUTS[h]] = grad_v

    heads_backward(
        columns_in(q_ref), columns_in(k_ref), columns_in(v_ref), columns_in(do_ref),
        lambda h: lse_ref[0, h : h + 1, :], self_valid(seg_row[0], seg_col[0]), put, PAIRS,
    )


def self_specs(row_len):
    seg = [
        pl.BlockSpec((1, 1, row_len), lambda r: (r, 0, 0)),
        pl.BlockSpec((1, row_len, 1), lambda r: (r, 0, 0)),
    ]
    row = pl.BlockSpec((row_len, D), lambda r: (r, 0))
    lse = pl.BlockSpec((1, PAIRS, 2 * row_len), lambda r: (r, 0, 0))
    return seg, row, lse


def self_forward(seg, queries, keys, values):
    rows, row_len = seg.shape
    seg_specs, row, lse = self_specs(row_len)
    return pl.pallas_call(
        self_fwd_kernel,
        grid=(rows,),
        in_specs=seg_specs + [row] * 3,
        out_specs=[row, lse],
        out_shape=[
            jax.ShapeDtypeStruct(queries.shape, BF16),
            jax.ShapeDtypeStruct((rows, PAIRS, 2 * row_len), F32),
        ],
        compiler_params=BIG_VMEM,
        cost_estimate=CHEAP,
        name="self_forward",
    )(seg[:, None, :], seg[:, :, None], queries, keys, values)


def self_backward(seg, queries, keys, values, grad_mixed, lse_rows):
    rows, row_len = seg.shape
    seg_specs, row, lse = self_specs(row_len)
    return pl.pallas_call(
        self_bwd_kernel,
        grid=(rows,),
        in_specs=seg_specs + [row] * 4 + [lse],
        out_specs=[row] * 3,
        out_shape=[jax.ShapeDtypeStruct(queries.shape, BF16)] * 3,
        compiler_params=FULL_VMEM,
        cost_estimate=CHEAP,
        name="self_backward",
    )(seg[:, None, :], seg[:, :, None], queries, keys, values, grad_mixed, lse_rows)


def cross_fwd_kernel(map_ref, len_ref, seg_row, seg_col, q_ref, k_ref, v_ref, o_ref, lse_ref):
    r, page = pl.program_id(0), pl.program_id(1)
    keys, toks = k_ref.shape[1], q_ref.shape[0]
    valid = lax.broadcasted_iota(jnp.int32, (keys, 2 * toks), 0) < len_ref[r * 2 + page]
    mine_col = (seg_col[0] == page) | (page == 0)
    mine_row = (seg_row[0] == page) | (page == 0)
    mine_row = jnp.concatenate((mine_row, mine_row), axis=1)

    def put(h, mixed, lse):
        o_ref[:, CUTS[h]] = jnp.where(mine_col, mixed, o_ref[:, CUTS[h]])
        lse_ref[0, h : h + 1, :] = jnp.where(mine_row, lse, lse_ref[0, h : h + 1, :])

    heads_forward(columns_in(q_ref), memory_columns(k_ref), memory_columns(v_ref), valid, put)


def cross_bwd_kernel(
    map_ref, len_ref, seg_row, seg_col, q_ref, k_ref, v_ref, do_ref, lse_ref,
    dq_ref, dk_ref, dv_ref, sum_ref,
):
    r, page = pl.program_id(0), pl.program_id(1)
    keys, toks = k_ref.shape[1], q_ref.shape[0]
    valid = lax.broadcasted_iota(jnp.int32, (keys, 2 * toks), 0) < len_ref[r * 2 + page]
    mine_col = (seg_col[0] == page) | (page == 0)
    mine_row = seg_row[0] == page
    mine_row = jnp.concatenate((mine_row, mine_row), axis=1)

    def put(h, grad_q, grad_k, grad_v):
        cut = CUTS[h]
        dq_ref[:, cut] = jnp.where(mine_col, grad_q, dq_ref[:, cut])
        dk_ref[0, :, cut] = grad_k
        dv_ref[0, :, cut] = grad_v
        before = jnp.where(r + page == 0, jnp.zeros((1, 128), F32), sum_ref[:, cut])
        sum_ref[:, cut] = before + jnp.sum(grad_v.astype(F32), axis=0, keepdims=True)

    heads_backward(
        columns_in(q_ref), memory_columns(k_ref), memory_columns(v_ref), columns_in(do_ref),
        lambda h: jnp.where(mine_row, lse_ref[0, h : h + 1, :], -NEG_FILL), valid, put,
    )


def cross_specs(row_len, mem_len):
    seg = [
        pl.BlockSpec((1, 1, row_len), lambda r, p, *_: (r, 0, 0)),
        pl.BlockSpec((1, row_len, 1), lambda r, p, *_: (r, 0, 0)),
    ]
    row = pl.BlockSpec((row_len, D), lambda r, p, *_: (r, 0))
    mem = pl.BlockSpec((1, mem_len, D), lambda r, p, mp, ln: (mp[r * 2 + p], 0, 0))
    lse = pl.BlockSpec((1, PAIRS, 2 * row_len), lambda r, p, *_: (r, 0, 0))
    return seg, row, mem, lse


def cross_forward(local_map, lengths, seg, queries, keys, values):
    rows, row_len = seg.shape
    mem_len = keys.shape[1]
    seg_specs, row, mem, lse = cross_specs(row_len, mem_len)
    return pl.pallas_call(
        cross_fwd_kernel,
        grid_spec=pltpu.PrefetchScalarGridSpec(
            num_scalar_prefetch=2,
            grid=(rows, 2),
            in_specs=seg_specs + [row, mem, mem],
            out_specs=[row, lse],
        ),
        out_shape=[
            jax.ShapeDtypeStruct(queries.shape, BF16),
            jax.ShapeDtypeStruct((rows, PAIRS, 2 * row_len), F32),
        ],
        compiler_params=FULL_VMEM,
        cost_estimate=CHEAP,
        name="cross_forward",
    )(local_map, lengths, seg[:, None, :], seg[:, :, None], queries, keys, values)


def cross_backward(local_map, lengths, seg, queries, keys, values, grad_mixed, lse_rows):
    rows, row_len = seg.shape
    mem_len = keys.shape[1]
    seg_specs, row, mem, lse = cross_specs(row_len, mem_len)
    return pl.pallas_call(
        cross_bwd_kernel,
        grid_spec=pltpu.PrefetchScalarGridSpec(
            num_scalar_prefetch=2,
            grid=(rows, 2),
            in_specs=seg_specs + [row, mem, mem, row, lse],
            out_specs=[row, mem, mem, pl.BlockSpec((1, D), lambda r, p, *_: (0, 0))],
        ),
        out_shape=[
            jax.ShapeDtypeStruct(queries.shape, BF16),
            jax.ShapeDtypeStruct(keys.shape, BF16),
            jax.ShapeDtypeStruct(values.shape, BF16),
            jax.ShapeDtypeStruct((1, D), F32),
        ],
        compiler_params=FULL_VMEM,
        cost_estimate=CHEAP,
        name="cross_backward",
    )(local_map, lengths, seg[:, None, :], seg[:, :, None], queries, keys, values, grad_mixed, lse_rows)


SMALL_ROWS = 16


def tie(values, *after):
    return lax.optimization_barrier((values, after))[0]


class Clock:
    def __init__(self):
        self.last = ()

    def now(self, values):
        return tie(values, *self.last) if self.last else values

    def tick(self, *arrays):
        self.last = arrays


class Grid:
    def __init__(self, wide, narrow):
        self.wide, self.narrow, self.ring = wide, narrow, wide // 2
        self.devices = wide * narrow
        moves = {
            "z": lambda w, n: ((w + 2) % wide, n),
            "x": lambda w, n: (w ^ 1, n),
            "y": lambda w, n: (w, n ^ 2),
            "c": lambda w, n: (w, n ^ 1),
        }
        self.perms = {}
        for name, move in moves.items():
            pairs = []
            for w in range(wide):
                for n in range(narrow):
                    w2, n2 = move(w, n)
                    pairs.append((w * narrow + n, w2 * narrow + n2))
            self.perms[name] = pairs
        self.clock = Clock()

    def send(self, name, array):
        return lax.ppermute(self.clock.now(array), AXES, self.perms[name])


def segments(first, height, g, rows):
    out, at, end = [], first, first + height
    while at < end:
        k = min(at // rows, g)
        stop = min(end, (k + 1) * rows) if k < g else end
        out.append((k, at - k * rows, at - first, stop - at))
        at = stop
    return out


def half_kernel(parts, ring, wide, g, rows, place, *refs):
    arrays, (out, sems) = refs[:-2], refs[-2:]
    z, x, y = place[0], place[1], place[2]
    height, cols = wide * rows, out.shape[-1]
    copies = []

    def copy(src, dst):
        copies.append(pltpu.make_async_copy(src, dst, sems.at[len(copies)]))

    for which, first_row, count, offset, labels in parts:
        piece = arrays[which]
        for i, (dz, dx, dy) in enumerate(labels):
            row = 2 * lax.rem(z + (ring - dz), ring) + (x + dx - 2 * x * dx)
            col = y + dy - 2 * y * dy
            pieces = segments(offset, count, g, rows)
            if pieces[0][3] == rows and len([p for p in pieces if p[0] < g]) == g:
                copy(
                    piece.at[i, pl.ds(first_row, g * rows)].reshape(g, rows, cols),
                    out.at[col, pl.ds(0, g * height)].reshape(g, wide, rows, cols).at[:, row],
                )
                pieces = [p for p in pieces if p[0] == g]
            for k, matrix_row, at, n in pieces:
                each = rows if k < g else SMALL_ROWS
                first = pl.multiple_of(k * height + row * each + matrix_row, 16)
                copy(piece.at[i, pl.ds(first_row + at, n)], out.at[col, pl.ds(first, n)])
    for one in copies:
        one.start()
    for one in copies:
        one.wait()


def anywhere(count):
    return [pl.BlockSpec(memory_space=pl.ANY)] * count


PLACE = pl.BlockSpec(memory_space=pltpu.SMEM)


def rearrange_kernel(moves, n_in, *refs):
    ins, outs, sems = refs[:n_in], refs[n_in:-1], refs[-1]
    copies = []
    for i, bi, ri, ci, rows, o, bo, ro in moves:
        src = ins[i].at[bi, pl.ds(ri, rows), pl.ds(ci, outs[o].shape[-1])]
        copies.append(pltpu.make_async_copy(src, outs[o].at[bo, pl.ds(ro, rows)], sems.at[len(copies)]))
    for one in copies:
        one.start()
    for one in copies:
        one.wait()


class Rearrange:
    def __init__(self):
        self.ins, self.shapes, self.moves = [], [], []

    def source(self, array):
        for i, known in enumerate(self.ins):
            if known is array:
                return i
        self.ins.append(array)
        return len(self.ins) - 1

    def out(self, blocks, rows, cols):
        self.shapes.append((blocks, rows, cols))
        return len(self.shapes) - 1

    def move(self, out, block, row, array, from_block, first, rows, column=0):
        self.moves.append((self.source(array), from_block, first, column, rows, out, block, row))

    def run(self, clock):
        outs = pl.pallas_call(
            functools.partial(rearrange_kernel, self.moves, len(self.ins)),
            in_specs=anywhere(len(self.ins)),
            out_specs=[pl.BlockSpec(memory_space=pltpu.VMEM)] * len(self.shapes),
            out_shape=[jax.ShapeDtypeStruct(shape, BF16) for shape in self.shapes],
            scratch_shapes=[pltpu.SemaphoreType.DMA((len(self.moves),))],
            compiler_params=BIG_VMEM,
            cost_estimate=CHEAP,
            name="rearrange",
        )(*clock.now(self.ins))
        return list(outs)


class Gather:
    def __init__(self, grid, place, g, height, cols, small=False):
        self.grid, self.place, self.g, self.height, self.cols = grid, place, g, height, cols
        self.rows = (height - (SMALL_ROWS if small else 0)) // g
        self.parts = []

    def put(self, labels, array, first_row, count, offset):
        self.parts.append((labels, array, first_row, count, offset))

    def half(self, *after):
        grid, arrays, parts, n = self.grid, [], [], 0
        for labels, array, first_row, count, offset in self.parts:
            which = [i for i, known in enumerate(arrays) if known is array]
            if not which:
                arrays.append(array)
                which = [len(arrays) - 1]
            parts.append((which[0], first_row, count, offset, labels))
            n += len(labels) * len(segments(offset, count, self.g, self.rows))
        self.own = pl.pallas_call(
            functools.partial(half_kernel, parts, grid.ring, grid.wide, self.g, self.rows),
            in_specs=[PLACE] + anywhere(len(arrays)),
            out_specs=pl.BlockSpec(memory_space=pltpu.VMEM),
            out_shape=jax.ShapeDtypeStruct((2, grid.wide * self.height, self.cols), BF16),
            scratch_shapes=[pltpu.SemaphoreType.DMA((n,))],
            compiler_params=BIG_VMEM,
            cost_estimate=CHEAP,
            name="half_weights",
        )(self.place, *tie(grid.clock.now(arrays), *after))
        return self.own

    def swap(self):
        self.other = self.grid.send("c", self.own)
        return self.other

    def small_rows(self):
        first = self.g * self.grid.wide * self.rows
        own, other = self.grid.clock.now((self.own[:, first:], self.other[:, first:]))
        flip = self.place[3] == 0
        both = jnp.stack((jnp.where(flip, own, other), jnp.where(flip, other, own)))
        return both.reshape(2, 2, self.grid.wide, SMALL_ROWS, -1).astype(F32)


class Square:
    def __init__(self, gather, blocks, height, offset=0):
        self.gather, self.blocks, self.height, self.offset = gather, blocks, height, offset
        self.cut = height // 32 * 16

    def labels(self, dx, dy):
        return [(dz, dx, dy) for dz in range(len(self.blocks))]


def exchange(grid, before, after):
    make = Rearrange()
    cols = (before or after).gather.cols
    depth = len((before or after).blocks)
    heights = [0, 0]
    if before:
        heights = [before.cut, before.height - before.cut]
    total = [h + (after.height if after else 0) for h in heights]
    outs = [make.out(depth, h, cols) for h in total]
    if before:
        (near_x, x_first), (near_y, y_first) = before.near
        for k in range(depth):
            make.move(outs[0], k, 0, near_y, k, y_first, heights[0])
            make.move(outs[1], k, 0, near_x, k, x_first + before.cut, heights[1])
    if after:
        for out, first in zip(outs, heights):
            for k, pieces in enumerate(after.blocks):
                at = first
                for array, block, row, count, column in pieces:
                    make.move(out, k, at, array, block, row, count, column)
                    at += count
    send_x, send_y = make.run(grid.clock)
    from_x, from_y = grid.send("x", send_x), grid.send("y", send_y)
    if before:
        before.gather.put(before.labels(1, 1), from_x, 0, heights[0], before.offset)
        before.gather.put(before.labels(1, 1), from_y, 0, heights[1], before.offset + before.cut)
    if after:
        after.near = ((from_x, heights[0]), (from_y, heights[1]))
        put = after.gather.put
        put(after.labels(0, 0), send_x, heights[0], after.height, after.offset)
        put(after.labels(1, 0), from_x, heights[0], after.height, after.offset)
        put(after.labels(0, 1), from_y, heights[1], after.height, after.offset)
    return from_x, from_y


def unfold(small, count, start, width):
    part = small[:, :, :, :count, start : start + width]
    return part.transpose(3, 2, 1, 0, 4).reshape(count, -1)


def corners(place):
    y, c = place[2], place[3]
    return (2 * y + 1 - c, 2 * (1 - y) + 1 - c), (2 * y + c, 2 * (1 - y) + c)


def column(ref, n, cols):
    return ref[:, pl.ds(pl.multiple_of(n * cols, 128), cols)]


def both_columns(ref, blocks, cols):
    return jnp.concatenate([column(ref, n, cols) for n in blocks], axis=1)


def far_kernel(place, *refs):
    out = refs[-1]
    cols = out.shape[-1]
    for i in range(out.shape[0]):
        a, d = refs[2 * i], refs[2 * i + 1]
        term = dot_tn(a[...], both_columns(d, corners(place)[0], cols))
        for j in range(2):
            out[i, j] = term[:, j * cols : (j + 1) * cols].astype(BF16)


def put_quadrants(x, scratch, k, i, here, outs):
    dx, dy, qx, qy, own = outs
    rows = own.shape[2]
    if here:
        own[k, i] = scratch[k, x]
        qx[k, i] = scratch[k, 1 - x].astype(BF16)
    else:
        qy[k, i] = scratch[k, x].astype(BF16)
        dx[k, i] = scratch[k, 1 - x, pl.ds(0, rows // 2)].astype(BF16)
        dy[k, i] = scratch[k, 1 - x, pl.ds(rows // 2, rows // 2)].astype(BF16)


def near_kernel(place, *refs):
    from_c, *outs, scratch = refs[-7:]
    zs, units, rows, cols = outs[-1].shape
    for i in range(units):
        a, d = refs[2 * i], refs[2 * i + 1]
        term = dot_tn(a[...], both_columns(d, corners(place)[1], cols))
        for j in range(2):
            part = term[:, j * cols : (j + 1) * cols] + from_c[i, j].astype(F32)
            scratch[...] = part.reshape(scratch.shape)
            for k in range(zs):
                put_quadrants(place[1], scratch, k, i, j == 0, outs)


def quadrant_shapes(units, ring, rows, cols):
    half, full = (ring, units, rows // 2, cols), (ring, units, rows, cols)
    return [jax.ShapeDtypeStruct(half, BF16)] * 2 + [
        jax.ShapeDtypeStruct(full, BF16), jax.ShapeDtypeStruct(full, BF16), jax.ShapeDtypeStruct(full, F32)
    ]


def quadrant_specs(units, zs, rows, cols, stepped):
    def at(s, *_):
        return (s if stepped else 0, 0, 0, 0)

    half = pl.BlockSpec((zs, units, rows // 2, cols), at)
    full = pl.BlockSpec((zs, units, rows, cols), at)
    return [half] * 2 + [full] * 3


def token_terms(grid, place, pairs, rows, cols, from_c=None, params=FULL_VMEM):
    units, tokens = len(pairs), pairs[0][0].shape[0]
    height = grid.wide * rows
    zs = max(1, 128 // (2 * rows))
    if 2 * rows >= 128 and height // (2 * rows) > 1 and rows * cols <= 128 * 256:
        zs = min(grid.ring, 2)
    tall = zs * 2 * rows
    in_specs, args = [], []
    for a, d in pairs:
        in_specs += [
            pl.BlockSpec((tokens, tall), lambda s, *_: (0, s)),
            pl.BlockSpec(d.shape, lambda s, *_: (0, 0)),
        ]
        args += [a, d]
    block = pl.BlockSpec((units, 2, tall, cols), lambda s, *_: (0, 0, s, 0))
    scratch = []
    if from_c is None:
        kernel, out_specs = far_kernel, block
        out_shape = jax.ShapeDtypeStruct((units, 2, height, cols), BF16)
    else:
        in_specs.append(block)
        args.append(from_c)
        kernel = near_kernel
        out_specs = quadrant_specs(units, zs, rows, cols, True)
        out_shape = quadrant_shapes(units, grid.ring, rows, cols)
        scratch = [pltpu.VMEM((zs, 2, rows, cols), F32)]
    return pl.pallas_call(
        kernel,
        grid_spec=pltpu.PrefetchScalarGridSpec(
            num_scalar_prefetch=1,
            grid=(height // tall,),
            in_specs=in_specs,
            out_specs=out_specs,
            scratch_shapes=scratch,
        ),
        out_shape=out_shape,
        compiler_params=params,
        cost_estimate=CHEAP,
        name="weight_terms",
    )(place, *args)


def memory_terms_kernel(near, pairs, place, mem, dk, dv, *refs):
    tokens, refs = refs[: 2 * pairs], refs[2 * pairs :]
    if near:
        from_c, dx, dy, qx, qy, own, acc = refs
    else:
        out, acc = refs
    cols = acc.shape[-1]
    m = pl.program_id(0)
    blocks = corners(place)[1 if near else 0]

    @pl.when(m == 0)
    def _():
        for i in range(pairs):
            term = dot_tn(tokens[2 * i][...], both_columns(tokens[2 * i + 1], blocks, cols))
            for j in range(2):
                acc[i, j] = term[:, j * cols : (j + 1) * cols].reshape(acc.shape[2:])
        acc[pairs:] = jnp.zeros_like(acc[pairs:])
        if near:
            acc[...] += from_c[...].astype(F32).reshape(acc.shape)

    grads = jnp.concatenate([both_columns(d.at[0], blocks, cols) for d in (dk, dv)], axis=1)
    term = dot_tn(mem[0], grads)
    for q in range(4):
        part = term[:, q * cols : (q + 1) * cols].reshape(acc.shape[2:])
        acc[pairs + q // 2, q % 2] += part

    @pl.when(m == pl.num_programs(0) - 1)
    def _():
        if near:
            x = place[1]
            for i in range(pairs + 2):
                for j in range(2):
                    for k in range(own.shape[0]):
                        put_quadrants(x, acc.at[i, j], k, i, j == 0, (dx, dy, qx, qy, own))
        else:
            out[...] = acc[...].reshape(out.shape).astype(BF16)


def memory_terms(grid, place, memory, grads, pairs, rows, cols, from_c=None):
    units, (mems, length, wide_cols) = len(pairs) + 2, memory.shape
    height = grid.wide * rows
    near = from_c is not None
    one = pl.BlockSpec((1, length, wide_cols), lambda m, *_: (m, 0, 0))
    term = pl.BlockSpec((units, 2, height, cols), lambda m, *_: (0, 0, 0, 0))
    tokens = [array for pair in pairs for array in pair]
    return pl.pallas_call(
        functools.partial(memory_terms_kernel, near, len(pairs)),
        grid_spec=pltpu.PrefetchScalarGridSpec(
            num_scalar_prefetch=1,
            grid=(mems,),
            in_specs=[one] * 3
            + [pl.BlockSpec(a.shape, lambda m, *_: (0, 0)) for a in tokens]
            + ([term] if near else []),
            out_specs=quadrant_specs(units, grid.ring, rows, cols, False) if near else term,
            scratch_shapes=[pltpu.VMEM((units, 2, grid.ring, 2, rows, cols), F32)],
        ),
        out_shape=quadrant_shapes(units, grid.ring, rows, cols)
        if near
        else jax.ShapeDtypeStruct((units, 2, height, cols), BF16),
        compiler_params=FULL_VMEM,
        cost_estimate=CHEAP,
        name="memory_terms",
    )(place, memory, *grads, *tokens, *([from_c] if near else []))


def add_corners_kernel(qx, qy, from_x, from_y, sx, sy):
    half = from_x.shape[2]
    first, second = pl.ds(0, half), pl.ds(half, half)
    sx[0, :, first] = qx[0, :, first]
    sx[0, :, second] = (qx[0, :, second].astype(F32) + from_y[0].astype(F32)).astype(BF16)
    sy[0, :, first] = (qy[0, :, first].astype(F32) + from_x[0].astype(F32)).astype(BF16)
    sy[0, :, second] = qy[0, :, second]


def add_corners(qx, qy, from_x, from_y):
    ring, units, rows, cols = qx.shape
    full = pl.BlockSpec((1, units, rows, cols), lambda k: (k, 0, 0, 0))
    half = pl.BlockSpec((1, units, rows // 2, cols), lambda k: (k, 0, 0, 0))
    return pl.pallas_call(
        add_corners_kernel,
        grid=(ring,),
        in_specs=[full, full, half, half],
        out_specs=[full, full],
        out_shape=[jax.ShapeDtypeStruct(qx.shape, BF16)] * 2,
        compiler_params=FULL_VMEM,
        cost_estimate=CHEAP,
        name="add_corners",
    )(qx, qy, from_x, from_y)


class Reduce:
    def __init__(self, grid, place, terms, rows):
        self.grid, self.place, self.terms, self.rows = grid, place, terms, rows

    def far(self):
        self.out = self.terms(None)
        return self.out

    def swap(self):
        self.from_c = self.grid.send("c", self.out)
        return self.from_c

    def near(self):
        self.dx, self.dy, self.qx, self.qy, self.own = self.terms(self.grid.clock.now(self.from_c))
        return self.dx

    def across(self):
        self.from_x, self.from_y = self.grid.send("x", self.dx), self.grid.send("y", self.dy)
        return self.from_x, self.from_y

    def add(self):
        from_x = self.grid.clock.now(self.from_x)
        self.sx, self.sy = add_corners(self.qx, self.qy, from_x, self.from_y)
        return self.sx

    def pairs(self):
        self.back_x, self.back_y = self.grid.send("x", self.sx), self.grid.send("y", self.sy)
        return self.back_x, self.back_y

    def chunk(self, step):
        index = lax.rem(self.place[0] + (self.grid.ring - step), self.grid.ring)
        parts = [
            lax.dynamic_index_in_dim(a, index, 0, keepdims=False)
            for a in self.grid.clock.now((self.own, self.back_x, self.back_y))
        ]
        return parts[0] + parts[1].astype(F32) + parts[2].astype(F32)


class RingSum:
    def __init__(self, grid, reduces):
        self.grid, self.reduces, self.done, self.came = grid, reduces, 0, None

    def step(self, *after):
        self.done += 1
        total = jnp.concatenate([r.chunk(self.done % self.grid.ring) for r in self.reduces], axis=0)
        if self.came is not None:
            total = total + tie(self.grid.clock.now(self.came), *after).astype(F32)
        if self.done == self.grid.ring:
            self.came = total
        else:
            self.came = self.grid.send("z", total.astype(BF16))
        return self.came


class SmallSum:
    def __init__(self, grid, place, terms):
        self.grid, self.place, self.done, self.came = grid, place, 0, None
        self.mine = terms.reshape(grid.ring, 2, 2, 2, -1)
        self.steps = grid.ring + 2

    def pair(self, name, axis, at):
        far = lax.dynamic_index_in_dim(self.mine, 1 - at, axis, keepdims=False)
        self.came = self.grid.send(name, far)
        self.near = lax.dynamic_index_in_dim(self.mine, at, axis, keepdims=False)

    def settle(self, *after):
        if self.came is not None:
            came = tie(self.came, *after) if after else self.came
            self.mine = self.near + came

    def step(self, *after):
        grid, place = self.grid, self.place
        if self.done == 0:
            self.pair("c", 3, place[3])
        elif self.done < grid.ring:
            if self.done == 1:
                self.settle(*after)
            index = lax.rem(place[0] + (grid.ring - self.done), grid.ring)
            total = lax.dynamic_index_in_dim(self.mine, index, 0, keepdims=False)
            if self.done > 1:
                total = total + (tie(self.came, *after) if after else self.came)
            self.came = grid.send("z", total)
            self.near = lax.dynamic_index_in_dim(self.mine, place[0], 0, keepdims=False)
        else:
            self.settle(*after)
            if self.done == grid.ring:
                self.pair("y", 1, place[2])
            else:
                self.pair("x", 0, place[1])
        self.done += 1
        return self.came

    def result(self):
        return self.near + self.came


def halves(place, own, other):
    c = place[3]
    return [(2 * y + core, y, half) for half, core in ((own, c), (other, 1 - c)) for y in range(2)]


def at_block(n, cols):
    return pl.ds(pl.multiple_of(n * cols, 128), cols)


def times_t(place, d, own, other):
    cols = own.shape[-1]
    return sum(dot_nt(d[:, at_block(n, cols)], half[y]) for n, y, half in halves(place, own, other))


def norm_parts(values):
    centre = values - jnp.mean(values, axis=-1, keepdims=True)
    scale = lax.rsqrt(jnp.mean(centre * centre, axis=-1, keepdims=True) + EPSILON)
    return centre * scale, scale


def norm_back(normed, scale, gain, grad):
    inner = grad * gain
    back = scale * (
        inner
        - jnp.mean(inner, axis=-1, keepdims=True)
        - normed * jnp.mean(inner * normed, axis=-1, keepdims=True)
    )
    return back, jnp.sum(grad * normed, axis=0, keepdims=True), jnp.sum(grad, axis=0, keepdims=True)


def column_sum(values):
    return jnp.sum(values.astype(F32), axis=0, keepdims=True)


GAIN, BIAS = 0, 3


def row(vectors, i):
    return vectors[i : i + 1, :]


def memory_kernel(place, mem, vectors, k_own, k_other, v_own, v_other, keys, values):
    cols = k_own.shape[-1]
    for n, y, half in halves(place, k_own, k_other):
        keys[0, :, at_block(n, cols)] = dot_nn(mem[0], half[y]).astype(BF16)
    for n, y, half in halves(place, v_own, v_other):
        bias = vectors[BIAS + 6 : BIAS + 7, at_block(n, cols)]
        values[0, :, at_block(n, cols)] = (dot_nn(mem[0], half[y]) + bias).astype(BF16)


def qkv_kernel(place, tokens, vectors, *refs):
    weights, (normed, q, k, v) = refs[:6], refs[6:]
    n, _ = norm_parts(tokens[...].astype(F32))
    normed[...] = (n * row(vectors, GAIN) + row(vectors, BIAS)).astype(BF16)
    cols = weights[0].shape[-1]
    for i, (out, bias_at) in enumerate(((q, 1), (k, None), (v, 2))):
        for n, y, half in halves(place, weights[2 * i], weights[2 * i + 1]):
            term = dot_nn(normed[...], half[y])
            if bias_at is not None:
                term = term + vectors[BIAS + bias_at : BIAS + bias_at + 1, at_block(n, cols)]
            out[:, at_block(n, cols)] = term.astype(BF16)


def middle_kernel(place, tokens, mixed, vectors, so_own, so_other, cq_own, cq_other, after, normed, queries):
    cols = so_own.shape[-1]
    for n, y, half in halves(place, so_own, so_other):
        at = at_block(n, cols)
        after[:, at] = tokens[:, at].astype(F32) + dot_nn(mixed[...], half[y]) + vectors[BIAS + 3 : BIAS + 4, at]
    n, _ = norm_parts(after[...])
    normed[...] = (n * row(vectors, GAIN + 1) + row(vectors, BIAS + 4)).astype(BF16)
    for n, y, half in halves(place, cq_own, cq_other):
        at = at_block(n, cols)
        queries[:, at] = (dot_nn(normed[...], half[y]) + vectors[BIAS + 5 : BIAS + 6, at]).astype(BF16)


def cross_out_kernel(place, before, mixed, vectors, own, other, after, normed):
    cols = own.shape[-1]
    for n, y, half in halves(place, own, other):
        at = at_block(n, cols)
        after[:, at] = before[:, at] + dot_nn(mixed[...], half[y]) + vectors[BIAS + 7 : BIAS + 8, at]
    n, _ = norm_parts(after[...])
    normed[...] = (n * row(vectors, GAIN + 2) + row(vectors, BIAS + 8)).astype(BF16)


def up_kernel(place, normed, bias, own, other, act, slope):
    c, cols = place[3], own.shape[-1]
    y = pl.program_id(0)
    for n, half in ((2 * y + c, own), (2 * y + 1 - c, other)):
        for j in range(4):
            at = at_block(4 * n + j, cols)
            u = dot_nn(normed[...], half[0, j * D : (j + 1) * D]) + bias[:, at]
            below = 0.5 * (1.0 + lax.erf(u * (1.0 / math.sqrt(2.0))))
            act[:, at] = (u * below).astype(BF16)
            slope[:, at] = (below + u * jnp.exp(-0.5 * u * u) * (1.0 / math.sqrt(2.0 * math.pi))).astype(BF16)


def down_kernel(place, after, act, vectors, own, other, out):
    c, y = place[3], pl.program_id(0)
    cols = own.shape[-1]
    for n, half in ((2 * y + c, own), (2 * y + 1 - c, other)):
        at = at_block(n, cols)
        total = after[:, at] + dot_nn(act[...], half[0]) + vectors[BIAS + 9 : BIAS + 10, at]
        out[:, at] = total.astype(BF16)


def down_back_kernel(place, grad, slope, own, other, grad_pre, bias_grad):
    back = (times_t(place, grad, own, other) * slope[...].astype(F32)).astype(BF16)
    grad_pre[...] = back
    bias_grad[...] = column_sum(back)


def up_back_kernel(
    place, grad_pre, grad_out, after, vectors, own, other, co_own, co_other,
    grad, branch, mixed, gain_grad, shift_grad, out_grad, last_grad, total,
):
    c, y = place[3], pl.program_id(0)
    cols = own.shape[-1]
    term = sum(
        dot_nt(grad_pre[:, at_block(4 * n + j, cols)], half[0, j * D : (j + 1) * D])
        for n, half in ((2 * y + c, own), (2 * y + 1 - c, other))
        for j in range(4)
    )

    @pl.when(y == 0)
    def _():
        total[...] = term

    @pl.when(y == 1)
    def _():
        n, scale = norm_parts(after[...])
        back, gain_grad[...], shift_grad[...] = norm_back(n, scale, row(vectors, GAIN + 2), total[...] + term)
        out = grad_out[...].astype(F32) + back
        grad[...] = out
        branch[...] = out.astype(BF16)
        out_grad[...] = column_sum(branch[...])
        last_grad[...] = column_sum(grad_out[...])
        mixed[...] = times_t(place, branch, co_own, co_other).astype(BF16)


def middle_back_kernel(
    place, grad_queries, grad_after, after, vectors, cq_own, cq_other, so_own, so_other,
    grad, branch, mixed, gain_grad, shift_grad, out_grad, query_grad,
):
    n, scale = norm_parts(after[...])
    dense = times_t(place, grad_queries, cq_own, cq_other)
    back, gain_grad[...], shift_grad[...] = norm_back(n, scale, row(vectors, GAIN + 1), dense)
    out = grad_after[...] + back
    grad[...] = out
    branch[...] = out.astype(BF16)
    out_grad[...] = column_sum(branch[...])
    query_grad[...] = column_sum(grad_queries[...])
    mixed[...] = times_t(place, branch, so_own, so_other).astype(BF16)


def first_back_kernel(place, tokens, grad_after, gq, gk, gv, vectors, *refs):
    weights, (grad, gain_grad, shift_grad, query_grad, value_grad) = refs[:6], refs[6:]
    n, scale = norm_parts(tokens[...].astype(F32))
    dense = sum(
        times_t(place, d, weights[2 * i], weights[2 * i + 1]) for i, d in enumerate((gq, gk, gv))
    )
    back, gain_grad[...], shift_grad[...] = norm_back(n, scale, row(vectors, GAIN), dense)
    grad[...] = (grad_after[...] + back).astype(BF16)
    query_grad[...] = column_sum(gq[...])
    value_grad[...] = column_sum(gv[...])


def memory_back_kernel(place, gk, gv, k_own, k_other, v_own, v_other, grad):
    total = times_t(place, gk.at[0], k_own, k_other) + times_t(place, gv.at[0], v_own, v_other)
    grad[0] = total.astype(BF16)


def in_place(array):
    return pl.pallas_call(
        lambda _, out: None,
        in_specs=anywhere(1),
        out_specs=pl.BlockSpec(memory_space=pl.ANY),
        out_shape=jax.ShapeDtypeStruct(array.shape, array.dtype),
        input_output_aliases={0: 0},
        compiler_params=BIG_VMEM,
        cost_estimate=CHEAP,
        name="in_place",
    )(array)


def dense_call(kernel, name, place, ins, outs, grid=(1,), scratch=(), params=BIG_VMEM):
    def spec(array, block, index):
        block = block or array.shape
        zeros = (0,) * len(block)
        return pl.BlockSpec(block, index or (lambda *_: zeros))

    return pl.pallas_call(
        kernel,
        grid_spec=pltpu.PrefetchScalarGridSpec(
            num_scalar_prefetch=1,
            grid=grid,
            in_specs=[spec(*one) for one in ins],
            out_specs=[spec(*one) for one in outs],
            scratch_shapes=scratch,
        ),
        out_shape=[one[0] for one in outs],
        compiler_params=params,
        cost_estimate=CHEAP,
        name=name,
    )(place, *[one[0] for one in ins])


def full(array):
    return (array, None, None)


def result(shape, dtype):
    return (jax.ShapeDtypeStruct(shape, dtype), None, None)


def matrix(gathered, i, height=D):
    block = (2, height, gathered.own.shape[-1])
    return [(half, block, lambda *_: (0, i, 0)) for half in (gathered.own, gathered.other)]


def by_y(gathered):
    block = (1,) + gathered.own.shape[1:]
    return [(half, block, lambda y, *_: (y, 0, 0)) for half in (gathered.own, gathered.other)]


def by_rows(gathered, rows):
    block = (2, rows, gathered.own.shape[-1])
    return [(half, block, lambda s, *_: (0, s, 0)) for half in (gathered.own, gathered.other)]


def local(
    shape,
    tokens,
    memory,
    segment_ids,
    page_map,
    mem_lengths,
    gains,
    biases,
    fc1_bias,
    self_qkv,
    self_out,
    cross_q,
    cross_kv,
    cross_out,
    fc1,
    fc2,
    cotangent,
):
    grid = Grid(*shape)
    wide_at, narrow_at = lax.axis_index("wide"), lax.axis_index("narrow")
    place = jnp.stack((wide_at // 2, wide_at % 2, narrow_at // 2, narrow_at % 2)).astype(jnp.int32)
    devices = grid.devices
    mem_count, token_count = memory.shape[0], tokens.shape[0]
    rows, cols = self_out.shape

    each, up_each = gains.shape[1], fc1_bias.size
    n_gain, n_bias = gains.size, biases.size
    small = jnp.pad(
        jnp.concatenate((gains, biases), axis=0), ((0, SMALL_ROWS - 13), (0, cols - each))
    )
    small = lax.dynamic_update_slice(small, fc1_bias[None], (0, 128))
    send, clock = grid.send, grid.clock
    now, tick = clock.now, clock.tick
    steps = grid.ring - 1
    gather = functools.partial(Gather, grid, place)
    ckv_height = 2 * rows + SMALL_ROWS
    fc2_rows = fc2.shape[0]
    part = fc2_rows // 2
    g_ckv = gather(2, ckv_height, cols, True)
    g_qkv = gather(3, 3 * rows, cols)
    g_mix = gather(3, 3 * rows, cols)
    g_fc1 = gather(4, 4 * rows, cols)
    g_fc2 = gather(1, fc2_rows, cols)

    start = Rearrange()
    out = start.out(1, 5 * rows, cols)
    for k, (array, i) in enumerate(((cross_kv, 0), (cross_kv, 1), (self_qkv, 0), (self_qkv, 1), (self_qkv, 2))):
        start.move(out, 0, k * rows, array, i, 0, rows)
    ring_one = start.run(clock)
    ring_one.append(send("z", ring_one[-1]))
    ring_small = [small[None]]
    ring_small.append(send("z", ring_small[-1]))
    top = Square(g_fc2, [[(fc2[None], 0, 0, part, 0)]], part)
    more = Rearrange()
    out = more.out(1, 3 * rows, cols)
    for k, array in enumerate((self_out, cross_q, cross_out)):
        more.move(out, 0, k * rows, array[None], 0, 0, rows)
    out = more.out(1, 4 * rows + part, cols)
    for k in range(4):
        more.move(out, 0, k * rows, fc1[None], 0, 0, rows, k * cols)
    more.move(out, 0, 4 * rows, fc2[None], 0, part, part)
    ring_mix, ring_up = [[array] for array in more.run(clock)]
    tick(ring_one[-1], ring_small[-1], ring_mix[0], ring_up[0], *exchange(grid, None, top))
    ring_one.append(send("z", ring_one[-1]))
    ring_small.append(send("z", ring_small[-1]))
    memory = in_place(now(memory))
    tick(ring_one[-1], ring_small[-1], memory, *exchange(grid, top, None))
    for _ in range(steps - 2):
        ring_one.append(send("z", ring_one[-1]))
        ring_small.append(send("z", ring_small[-1]))
        tick(ring_one[-1], ring_small[-1])

    def from_ring(arrays, first, count):
        return [[(array, 0, first, count, 0)] for array in arrays]

    ckv = Square(
        g_ckv, [a + b for a, b in zip(from_ring(ring_one, 0, 2 * rows), from_ring(ring_small, 0, SMALL_ROWS))],
        ckv_height,
    )
    qkv = Square(g_qkv, from_ring(ring_one, 2 * rows, 3 * rows), 3 * rows)
    ring_mix.append(send("z", ring_mix[-1]))
    ring_up.append(send("z", ring_up[-1]))
    tick(ring_mix[-1], ring_up[-1], *exchange(grid, None, ckv))

    make = Rearrange()
    out = make.out(4, part, cols)
    (_, own, own_at, _, _), (_, by_x, x_at, _, _), (_, by_y_, y_at, _, _), (_, low, _, _, _), (_, high, _, _, _) = g_fc2.parts
    g_fc2.parts = []
    for k, (array, at) in enumerate(((own, own_at), (by_x, x_at), (by_y_, y_at))):
        make.move(out, k, 0, array, 0, at, part)
    make.move(out, 3, 0, low, 0, 0, top.cut)
    make.move(out, 3, top.cut, high, 0, 0, part - top.cut)
    came = exchange(grid, ckv, qkv)
    ring_top = make.run(clock)
    ring_up.append(send("z", ring_up[-1]))
    for _ in range(steps - 1):
        ring_mix.append(send("z", ring_mix[-1]))
    tick(ring_mix[-1], ring_up[-1], ring_top[-1], *came)

    mix = Square(g_mix, from_ring(ring_mix, 0, 3 * rows), 3 * rows)
    came = exchange(grid, qkv, mix)
    for _ in range(steps - 2):
        ring_up.append(send("z", ring_up[-1]))
    g_ckv.half(g_mix.parts[0][1])
    g_ckv.swap()
    small_all = g_ckv.small_rows()
    vectors = unfold(small_all, 13, 0, each)
    up_bias = unfold(small_all, 1, 128, up_each)
    mem_block = (1,) + memory.shape[1:]
    mem_shape = jax.ShapeDtypeStruct(memory.shape, BF16)

    def by_memory(array):
        return (array, mem_block, lambda m, *_: (m, 0, 0))

    mem_keys, mem_values = dense_call(
        memory_kernel, "memory_keys_values", place,
        [by_memory(now(memory)), full(vectors)] + matrix(g_ckv, 0) + matrix(g_ckv, 1),
        [by_memory(mem_shape), by_memory(mem_shape)], grid=(mem_count,),
    )
    tick(ring_up[-1], mem_keys, *came)

    up = Square(g_fc1, from_ring(ring_up, 0, 4 * rows), 4 * rows)
    low = Square(g_fc2, from_ring(ring_up, 4 * rows, part), part, part)
    came = exchange(grid, mix, up)
    ring_top.append(send("z", ring_top[-1]))
    g_qkv.half(g_fc1.parts[0][1])
    g_qkv.swap()
    wide_row = (token_count, D)
    normed_one, self_queries, self_keys, self_values = dense_call(
        qkv_kernel, "self_qkv", place,
        [full(now(tokens)), full(vectors)] + matrix(g_qkv, 0) + matrix(g_qkv, 1) + matrix(g_qkv, 2),
        [result(wide_row, BF16)] * 4,
    )
    self_mixed, self_lse = self_forward(segment_ids, self_queries, self_keys, self_values)
    tick(self_mixed, ring_top[-1], *came)

    came = exchange(grid, up, low)
    g_mix.half(g_fc2.parts[0][1])
    g_mix.swap()
    ring_top.append(send("z", ring_top[-1]))
    after_self, normed_two, cross_queries = dense_call(
        middle_kernel, "self_out_cross_q", place,
        [full(tokens), full(now(self_mixed)), full(vectors)] + matrix(g_mix, 0) + matrix(g_mix, 1),
        [result(wide_row, F32), result(wide_row, BF16), result(wide_row, BF16)],
    )
    first_mem = lax.axis_index(AXES) * mem_count
    local_map = (page_map - first_mem).reshape(-1).astype(jnp.int32)
    picks = local_map[:, None] == jnp.arange(mem_count, dtype=jnp.int32)[None, :]
    row_lengths = jnp.sum(jnp.where(picks, mem_lengths[None, :], 0), axis=-1).astype(jnp.int32)
    cross_mixed, cross_lse = cross_forward(
        local_map, row_lengths, segment_ids, cross_queries, mem_keys, mem_values
    )
    tick(cross_mixed, ring_top[-1], *came)

    came = exchange(grid, low, None)
    for _ in range(steps - 2):
        ring_top.append(send("z", ring_top[-1]))
    g_fc1.half()
    g_fc1.swap()
    after_cross, normed_three = dense_call(
        cross_out_kernel, "cross_out", place,
        [full(after_self), full(now(cross_mixed)), full(vectors)] + matrix(g_mix, 2),
        [result(wide_row, F32), result(wide_row, BF16)],
    )
    hidden = up_bias.shape[1]
    activated, slope = dense_call(
        up_kernel, "fc1_gelu", place,
        [full(normed_three), full(up_bias)] + by_y(g_fc1),
        [result((token_count, hidden), BF16)] * 2, grid=(2,),
    )
    tick(activated, ring_top[-1], *came)
    spread = [(0, 0), (1, 0), (0, 1), (1, 1)]
    for step, array in enumerate(ring_top):
        g_fc2.put([(step, dx, dy) for dx, dy in spread], array, 0, part, 0)

    def settle(pairs, shard, params=FULL_VMEM):
        part_rows, part_cols = shard.shape
        return Reduce(
            grid, place,
            lambda from_c: token_terms(grid, place, pairs, part_rows, part_cols, from_c, params),
            part_rows,
        )

    one_row = result((1, D), F32)
    r_fc2 = settle([(now(activated), cotangent)], fc2, BIG_VMEM)
    r_fc2.far()
    r_fc2.swap()
    g_fc2.half()
    g_fc2.swap()
    tick(r_fc2.near(), g_fc2.other)
    slab = hidden // 4
    some = lambda array: (array, (token_count, slab), lambda s, *_: (0, s))
    grad_pre, grad_up_bias = dense_call(
        down_back_kernel, "fc2_gelu_back", place,
        [full(now(cotangent)), some(slope)] + by_rows(g_fc2, slab),
        [
            some(jax.ShapeDtypeStruct((token_count, hidden), BF16)),
            (jax.ShapeDtypeStruct((1, hidden), F32), (1, slab), lambda s, *_: (0, s)),
        ],
        grid=(4,), params=FULL_VMEM,
    )
    r_fc1 = settle([(normed_three, grad_pre)], fc1)
    tick(r_fc1.far(), *r_fc2.across())
    r_fc2.add()
    r_fc1.swap()
    (
        grad_after_cross, grad_branch_two, grad_cross_mixed,
        grad_gain_three, grad_bias_eight, grad_bias_seven, grad_bias_nine,
    ) = dense_call(
        up_back_kernel, "fc1_norm_back", place,
        [full(now(grad_pre)), full(cotangent), full(after_cross), full(vectors)]
        + by_y(g_fc1) + matrix(g_mix, 2),
        [result(wide_row, F32), result(wide_row, BF16), result(wide_row, BF16)] + [one_row] * 4,
        grid=(2,), scratch=[pltpu.VMEM(wide_row, F32)], params=FULL_VMEM,
    )
    tick(r_fc1.near(), r_fc2.sx, grad_cross_mixed)

    came = [*r_fc2.pairs(), *r_fc1.across()]
    grad_cq, grad_ck, grad_cv, grad_bias_six = cross_backward(
        local_map, row_lengths, segment_ids, cross_queries, mem_keys, mem_values,
        now(grad_cross_mixed), cross_lse,
    )
    r_mem = Reduce(
        grid, place,
        lambda from_c: memory_terms(grid, place, memory, (grad_ck, grad_cv), [], rows, cols, from_c),
        rows,
    )
    tick(grad_cq, r_mem.far(), *came)
    ring_fc2 = RingSum(grid, [r_fc2])
    r_fc1.add()
    r_mem.swap()
    ring_fc2.step()
    grad_cq = tie(now(grad_cq), r_fc1.sx)
    (
        grad_after_self, grad_branch_one, grad_self_mixed,
        grad_gain_two, grad_bias_four, grad_bias_three, grad_bias_five,
    ) = dense_call(
        middle_back_kernel, "cross_q_norm_back", place,
        [full(grad_cq), full(grad_after_cross), full(after_self), full(vectors)]
        + matrix(g_mix, 1) + matrix(g_mix, 0),
        [result(wide_row, F32), result(wide_row, BF16), result(wide_row, BF16)] + [one_row] * 4,
        params=FULL_VMEM,
    )
    grad_sq, grad_sk, grad_sv = self_backward(
        segment_ids, self_queries, self_keys, self_values, grad_self_mixed, self_lse
    )
    r_rest = settle(
        [
            (normed_one, grad_sq), (normed_one, grad_sk), (normed_one, grad_sv),
            (self_mixed, grad_branch_one), (normed_two, grad_cq), (cross_mixed, grad_branch_two),
        ],
        cross_q,
    )
    tick(r_rest.far(), r_mem.near(), ring_fc2.came, *r_fc1.pairs())
    ring_fc1 = RingSum(grid, [r_fc1])
    came = r_mem.across()
    r_rest.swap()
    ring_fc2.step()
    ring_fc1.step()
    grad_tokens, grad_gain_one, grad_bias_zero, grad_bias_one, grad_bias_two = dense_call(
        first_back_kernel, "self_qkv_norm_back", place,
        [full(tokens), full(grad_after_self)] + [full(d) for d in now((grad_sq, grad_sk, grad_sv))]
        + [full(vectors)] + matrix(g_qkv, 0) + matrix(g_qkv, 1) + matrix(g_qkv, 2),
        [result(wide_row, BF16)] + [one_row] * 4,
        params=FULL_VMEM,
    )
    tick(r_rest.near(), grad_tokens, ring_fc2.came, ring_fc1.came, *came)

    def by_device(array):
        return array.reshape(array.shape[0], devices, -1).transpose(1, 0, 2).reshape(devices, -1)

    small_grads = jnp.concatenate(
        (
            by_device(
                jnp.concatenate(
                    (
                        grad_gain_one, grad_gain_two, grad_gain_three,
                        grad_bias_zero, grad_bias_one, grad_bias_two, grad_bias_three, grad_bias_four,
                        grad_bias_five, grad_bias_six, grad_bias_seven, grad_bias_eight, grad_bias_nine,
                    ),
                    axis=0,
                )
            ),
            by_device(grad_up_bias),
        ),
        axis=1,
    )
    small_sum = SmallSum(grid, place, now(small_grads))
    r_mem.add()
    ring_fc2.step()
    (grad_memory,) = dense_call(
        memory_back_kernel, "memory_back", place,
        [by_memory(a) for a in tie(now((grad_ck, grad_cv)), r_mem.sx)] + matrix(g_ckv, 0) + matrix(g_ckv, 1),
        [by_memory(mem_shape)], grid=(mem_count,), params=FULL_VMEM,
    )
    (layer_out,) = dense_call(
        down_kernel, "fc2", place,
        [full(after_cross), full(tie(now(activated), r_mem.sx)), full(vectors)] + by_y(g_fc2),
        [result(wide_row, BF16)], grid=(2,), params=FULL_VMEM,
    )
    tick(grad_memory, layer_out, ring_fc2.came, *r_mem.pairs(), *r_rest.across())
    small_sum.step()
    ring_mem = RingSum(grid, [r_mem])
    r_rest.add()
    turned_memory = in_place(tie(now(grad_memory).transpose(1, 0, 2), r_rest.sx))
    grad_memory = turned_memory.transpose(1, 0, 2)
    ring_fc1.step()
    ring_mem.step()
    for _ in range(steps):
        small_sum.step()
    ring_fc1.step(turned_memory)
    tick(turned_memory, small_sum.came, ring_fc1.came, ring_mem.came, *r_rest.pairs())
    ring_fc2.step()
    ring_rest = RingSum(grid, [r_rest])
    ring_rest.step()
    ring_fc1.step()
    ring_mem.step()
    small_sum.step()
    tick(ring_rest.came, ring_mem.came, small_sum.came)
    for _ in range(steps - 1):
        ring_mem.step() if ring_mem.done < grid.ring else None
        small_sum.step() if small_sum.done < small_sum.steps else None
        tick(ring_rest.step(), ring_mem.came, small_sum.came)
    for ring in (ring_fc2, ring_fc1, ring_mem, ring_rest):
        while ring.done < grid.ring:
            ring.step()
    while small_sum.done < small_sum.steps:
        small_sum.step()
    came_mem, came_rest = ring_mem.came, ring_rest.came
    small_shard = small_sum.result()
    return (
        layer_out,
        grad_tokens,
        grad_memory,
        small_shard[:n_gain].reshape(gains.shape),
        small_shard[n_gain : n_gain + n_bias].reshape(biases.shape),
        small_shard[n_gain + n_bias :],
        came_rest[:3],
        came_rest[3],
        came_rest[4],
        came_mem,
        came_rest[5],
        ring_fc1.came[0],
        ring_fc2.came[0],
    )


def solution(mesh):
    shape = (mesh.shape["wide"], mesh.shape["narrow"])
    in_specs = (
        P(AXES, None),
        P(AXES, None, None),
        P(AXES, None),
        P(AXES, None),
        P(AXES),
        P(None, AXES),
        P(None, AXES),
        P(AXES),
        P(None, "wide", "narrow"),
        P("wide", "narrow"),
        P("wide", "narrow"),
        P(None, "wide", "narrow"),
        P("wide", "narrow"),
        P("wide", "narrow"),
        P("wide", "narrow"),
        P(AXES, None),
    )
    out_specs = (
        P(AXES, None),
        P(AXES, None),
        P(AXES, None, None),
        P(None, AXES),
        P(None, AXES),
        P(AXES),
        P(None, "wide", "narrow"),
        P("wide", "narrow"),
        P("wide", "narrow"),
        P(None, "wide", "narrow"),
        P("wide", "narrow"),
        P("wide", "narrow"),
        P("wide", "narrow"),
    )
    return jax.shard_map(
        functools.partial(local, shape), mesh=mesh, in_specs=in_specs, out_specs=out_specs, check_vma=False
    )
```

```python
import functools
import math

import jax
import jax.numpy as jnp
from jax import lax
from jax.experimental import pallas as pl
from jax.experimental.pallas import tpu as pltpu
from jax.sharding import PartitionSpec as P

D = 1024
HEADS = 16
HEAD_DIM = 64
PAIRS = HEADS // 2

EPSILON = 1e-05
NEG_FILL = -1e30
LOG2E = math.log2(math.e)
SCALE = 1.0 / math.sqrt(HEAD_DIM)
AXES = ("wide", "narrow")

F32 = jnp.float32
BF16 = jnp.bfloat16
VMEM = 24 * 2**20
CHEAP = pl.CostEstimate(flops=10**6, bytes_accessed=10**5, transcendentals=0)
BIG_VMEM = pltpu.CompilerParams(vmem_limit_bytes=VMEM)
FULL_VMEM = pltpu.CompilerParams(vmem_limit_bytes=60 * 2**20)


def dot_nt(a, b):
    return lax.dot_general(a, b, (((1,), (1,)), ((), ())), preferred_element_type=F32)


def dot_nn(a, b):
    return lax.dot_general(a, b, (((1,), (0,)), ((), ())), preferred_element_type=F32)


def dot_tn(a, b):
    return lax.dot_general(a, b, (((0,), (0,)), ((), ())), preferred_element_type=F32)


def two_heads(block):
    lane = lax.broadcasted_iota(jnp.int32, block.shape, 1)
    zero = jnp.zeros_like(block)
    return jnp.concatenate(
        (jnp.where(lane < HEAD_DIM, block, zero), jnp.where(lane < HEAD_DIM, zero, block)), axis=0
    )


def own_heads(both):
    half = both.shape[1] // 2
    line = lax.broadcasted_iota(jnp.int32, (both.shape[0], half), 0)
    return jnp.transpose(jnp.where(line < HEAD_DIM, both[:, :half], both[:, half:]))


CUTS = [slice(128 * h, 128 * h + 128) for h in range(PAIRS)]


def heads_forward(q_ref, k_ref, v_ref, valid, put):
    scores = [dot_nt(k_ref(cut), two_heads(q_ref(cut))) for cut in CUTS]
    weights, lses = [], []
    for one in scores:
        one = jnp.where(valid, one * (SCALE * LOG2E), NEG_FILL)
        top = jnp.max(one, axis=0, keepdims=True)
        expo = jnp.exp2(one - top)
        total = jnp.sum(expo, axis=0, keepdims=True)
        weights.append((expo * (1.0 / total)).astype(BF16))
        lses.append(top + jnp.log2(total))
    for h, cut in enumerate(CUTS):
        put(h, own_heads(dot_tn(v_ref(cut), weights[h])).astype(BF16), lses[h])


def heads_backward(q_ref, k_ref, v_ref, do_ref, lse_of, valid, put, group=4):
    for first in range(0, PAIRS, group):
        hs = range(first, first + group)
        qs = [two_heads(q_ref(CUTS[h])) for h in hs]
        ds = [two_heads(do_ref(CUTS[h])) for h in hs]
        scores = [dot_nt(k_ref(CUTS[h]), q) for h, q in zip(hs, qs)]
        grads = [dot_nt(v_ref(CUTS[h]), d) for h, d in zip(hs, ds)]
        weights, grad_scores = [], []
        for h, one, grad in zip(hs, scores, grads):
            weight = jnp.where(valid, jnp.exp2(one * (SCALE * LOG2E) - lse_of(h)), 0.0)
            inner = jnp.sum(weight * grad, axis=0, keepdims=True)
            grad_scores.append((weight * (grad - inner)).astype(BF16))
            weights.append(weight.astype(BF16))
        for h, q, d, weight, grad in zip(hs, qs, ds, weights, grad_scores):
            grad_q = (own_heads(dot_tn(k_ref(CUTS[h]), grad)) * SCALE).astype(BF16)
            grad_k = (dot_nn(grad, q) * SCALE).astype(BF16)
            put(h, grad_q, grad_k, dot_nn(weight, d).astype(BF16))


def columns_in(ref):
    return lambda cut: ref[:, cut]


def memory_columns(ref):
    return lambda cut: ref[0, :, cut]


def self_valid(seg_row, seg_col):
    length = seg_row.shape[-1]
    key = lax.broadcasted_iota(jnp.int32, (length, length), 0)
    tok = lax.broadcasted_iota(jnp.int32, (length, length), 1)
    one = (key <= tok) & (seg_row == seg_col)
    return jnp.concatenate((one, one), axis=1)


def self_fwd_kernel(seg_row, seg_col, q_ref, k_ref, v_ref, o_ref, lse_ref):
    def put(h, mixed, lse):
        o_ref[:, CUTS[h]] = mixed
        lse_ref[0, h : h + 1, :] = lse

    heads_forward(
        columns_in(q_ref), columns_in(k_ref), columns_in(v_ref), self_valid(seg_row[0], seg_col[0]), put
    )


def self_bwd_kernel(seg_row, seg_col, q_ref, k_ref, v_ref, do_ref, lse_ref, dq_ref, dk_ref, dv_ref):
    def put(h, grad_q, grad_k, grad_v):
        dq_ref[:, CUTS[h]] = grad_q
        dk_ref[:, CUTS[h]] = grad_k
        dv_ref[:, CUTS[h]] = grad_v

    heads_backward(
        columns_in(q_ref), columns_in(k_ref), columns_in(v_ref), columns_in(do_ref),
        lambda h: lse_ref[0, h : h + 1, :], self_valid(seg_row[0], seg_col[0]), put, PAIRS,
    )


def self_specs(row_len):
    seg = [
        pl.BlockSpec((1, 1, row_len), lambda r: (r, 0, 0)),
        pl.BlockSpec((1, row_len, 1), lambda r: (r, 0, 0)),
    ]
    row = pl.BlockSpec((row_len, D), lambda r: (r, 0))
    lse = pl.BlockSpec((1, PAIRS, 2 * row_len), lambda r: (r, 0, 0))
    return seg, row, lse


def self_forward(seg, queries, keys, values):
    rows, row_len = seg.shape
    seg_specs, row, lse = self_specs(row_len)
    return pl.pallas_call(
        self_fwd_kernel,
        grid=(rows,),
        in_specs=seg_specs + [row] * 3,
        out_specs=[row, lse],
        out_shape=[
            jax.ShapeDtypeStruct(queries.shape, BF16),
            jax.ShapeDtypeStruct((rows, PAIRS, 2 * row_len), F32),
        ],
        compiler_params=BIG_VMEM,
        cost_estimate=CHEAP,
        name="self_forward",
    )(seg[:, None, :], seg[:, :, None], queries, keys, values)


def self_backward(seg, queries, keys, values, grad_mixed, lse_rows):
    rows, row_len = seg.shape
    seg_specs, row, lse = self_specs(row_len)
    return pl.pallas_call(
        self_bwd_kernel,
        grid=(rows,),
        in_specs=seg_specs + [row] * 4 + [lse],
        out_specs=[row] * 3,
        out_shape=[jax.ShapeDtypeStruct(queries.shape, BF16)] * 3,
        compiler_params=FULL_VMEM,
        cost_estimate=CHEAP,
        name="self_backward",
    )(seg[:, None, :], seg[:, :, None], queries, keys, values, grad_mixed, lse_rows)


def cross_fwd_kernel(map_ref, len_ref, seg_row, seg_col, q_ref, k_ref, v_ref, o_ref, lse_ref):
    r, page = pl.program_id(0), pl.program_id(1)
    keys, toks = k_ref.shape[1], q_ref.shape[0]
    valid = lax.broadcasted_iota(jnp.int32, (keys, 2 * toks), 0) < len_ref[r * 2 + page]
    mine_col = (seg_col[0] == page) | (page == 0)
    mine_row = (seg_row[0] == page) | (page == 0)
    mine_row = jnp.concatenate((mine_row, mine_row), axis=1)

    def put(h, mixed, lse):
        o_ref[:, CUTS[h]] = jnp.where(mine_col, mixed, o_ref[:, CUTS[h]])
        lse_ref[0, h : h + 1, :] = jnp.where(mine_row, lse, lse_ref[0, h : h + 1, :])

    heads_forward(columns_in(q_ref), memory_columns(k_ref), memory_columns(v_ref), valid, put)


def cross_bwd_kernel(
    map_ref, len_ref, seg_row, seg_col, q_ref, k_ref, v_ref, do_ref, lse_ref,
    dq_ref, dk_ref, dv_ref, sum_ref,
):
    r, page = pl.program_id(0), pl.program_id(1)
    keys, toks = k_ref.shape[1], q_ref.shape[0]
    valid = lax.broadcasted_iota(jnp.int32, (keys, 2 * toks), 0) < len_ref[r * 2 + page]
    mine_col = (seg_col[0] == page) | (page == 0)
    mine_row = seg_row[0] == page
    mine_row = jnp.concatenate((mine_row, mine_row), axis=1)

    def put(h, grad_q, grad_k, grad_v):
        cut = CUTS[h]
        dq_ref[:, cut] = jnp.where(mine_col, grad_q, dq_ref[:, cut])
        dk_ref[0, :, cut] = grad_k
        dv_ref[0, :, cut] = grad_v
        before = jnp.where(r + page == 0, jnp.zeros((1, 128), F32), sum_ref[:, cut])
        sum_ref[:, cut] = before + jnp.sum(grad_v.astype(F32), axis=0, keepdims=True)

    heads_backward(
        columns_in(q_ref), memory_columns(k_ref), memory_columns(v_ref), columns_in(do_ref),
        lambda h: jnp.where(mine_row, lse_ref[0, h : h + 1, :], -NEG_FILL), valid, put,
    )


def cross_specs(row_len, mem_len):
    seg = [
        pl.BlockSpec((1, 1, row_len), lambda r, p, *_: (r, 0, 0)),
        pl.BlockSpec((1, row_len, 1), lambda r, p, *_: (r, 0, 0)),
    ]
    row = pl.BlockSpec((row_len, D), lambda r, p, *_: (r, 0))
    mem = pl.BlockSpec((1, mem_len, D), lambda r, p, mp, ln: (mp[r * 2 + p], 0, 0))
    lse = pl.BlockSpec((1, PAIRS, 2 * row_len), lambda r, p, *_: (r, 0, 0))
    return seg, row, mem, lse


def cross_forward(local_map, lengths, seg, queries, keys, values):
    rows, row_len = seg.shape
    mem_len = keys.shape[1]
    seg_specs, row, mem, lse = cross_specs(row_len, mem_len)
    return pl.pallas_call(
        cross_fwd_kernel,
        grid_spec=pltpu.PrefetchScalarGridSpec(
            num_scalar_prefetch=2,
            grid=(rows, 2),
            in_specs=seg_specs + [row, mem, mem],
            out_specs=[row, lse],
        ),
        out_shape=[
            jax.ShapeDtypeStruct(queries.shape, BF16),
            jax.ShapeDtypeStruct((rows, PAIRS, 2 * row_len), F32),
        ],
        compiler_params=FULL_VMEM,
        cost_estimate=CHEAP,
        name="cross_forward",
    )(local_map, lengths, seg[:, None, :], seg[:, :, None], queries, keys, values)


def cross_backward(local_map, lengths, seg, queries, keys, values, grad_mixed, lse_rows):
    rows, row_len = seg.shape
    mem_len = keys.shape[1]
    seg_specs, row, mem, lse = cross_specs(row_len, mem_len)
    return pl.pallas_call(
        cross_bwd_kernel,
        grid_spec=pltpu.PrefetchScalarGridSpec(
            num_scalar_prefetch=2,
            grid=(rows, 2),
            in_specs=seg_specs + [row, mem, mem, row, lse],
            out_specs=[row, mem, mem, pl.BlockSpec((1, D), lambda r, p, *_: (0, 0))],
        ),
        out_shape=[
            jax.ShapeDtypeStruct(queries.shape, BF16),
            jax.ShapeDtypeStruct(keys.shape, BF16),
            jax.ShapeDtypeStruct(values.shape, BF16),
            jax.ShapeDtypeStruct((1, D), F32),
        ],
        compiler_params=FULL_VMEM,
        cost_estimate=CHEAP,
        name="cross_backward",
    )(local_map, lengths, seg[:, None, :], seg[:, :, None], queries, keys, values, grad_mixed, lse_rows)


SMALL_ROWS = 16


def tie(values, *after):
    return lax.optimization_barrier((values, after))[0]


class Clock:
    def __init__(self):
        self.last = ()

    def now(self, values):
        return tie(values, *self.last) if self.last else values

    def tick(self, *arrays):
        self.last = arrays


class Grid:
    def __init__(self, wide, narrow):
        self.wide, self.narrow, self.ring = wide, narrow, wide // 2
        self.devices = wide * narrow
        moves = {
            "z": lambda w, n: ((w + 2) % wide, n),
            "x": lambda w, n: (w ^ 1, n),
            "y": lambda w, n: (w, n ^ 2),
            "c": lambda w, n: (w, n ^ 1),
        }
        self.perms = {}
        for name, move in moves.items():
            pairs = []
            for w in range(wide):
                for n in range(narrow):
                    w2, n2 = move(w, n)
                    pairs.append((w * narrow + n, w2 * narrow + n2))
            self.perms[name] = pairs
        self.clock = Clock()

    def send(self, name, array):
        return lax.ppermute(self.clock.now(array), AXES, self.perms[name])


def segments(first, height, g, rows):
    out, at, end = [], first, first + height
    while at < end:
        k = min(at // rows, g)
        stop = min(end, (k + 1) * rows) if k < g else end
        out.append((k, at - k * rows, at - first, stop - at))
        at = stop
    return out


def half_kernel(parts, ring, wide, g, rows, place, *refs):
    *arrays, out = refs
    z, x, y = place[0], place[1], place[2]
    height = wide * rows
    for which, first_row, count, offset, labels in parts:
        for i, (dz, dx, dy) in enumerate(labels):
            row = 2 * lax.rem(z + (ring - dz), ring) + (x + dx - 2 * x * dx)
            col = y + dy - 2 * y * dy
            for k, matrix_row, at, n in segments(offset, count, g, rows):
                each = rows if k < g else SMALL_ROWS
                first = pl.multiple_of(k * height + row * each + matrix_row, 16)
                out[col, pl.ds(first, n)] = arrays[which][i, pl.ds(first_row + at, n)]


def anywhere(count):
    return [pl.BlockSpec(memory_space=pl.ANY)] * count


PLACE = pl.BlockSpec(memory_space=pltpu.SMEM)


def rearrange_kernel(moves, n_in, *refs):
    ins, outs = refs[:n_in], refs[n_in:]
    for i, bi, ri, ci, rows, o, bo, ro in moves:
        cols = outs[o].shape[-1]
        outs[o][bo, pl.ds(ro, rows)] = ins[i][bi, pl.ds(ri, rows), pl.ds(ci, cols)]


class Rearrange:
    def __init__(self):
        self.ins, self.shapes, self.moves = [], [], []

    def source(self, array):
        for i, known in enumerate(self.ins):
            if known is array:
                return i
        self.ins.append(array)
        return len(self.ins) - 1

    def out(self, blocks, rows, cols):
        self.shapes.append((blocks, rows, cols))
        return len(self.shapes) - 1

    def move(self, out, block, row, array, from_block, first, rows, column=0):
        self.moves.append((self.source(array), from_block, first, column, rows, out, block, row))

    def run(self, clock):
        outs = pl.pallas_call(
            functools.partial(rearrange_kernel, self.moves, len(self.ins)),
            in_specs=[pl.BlockSpec(memory_space=pltpu.VMEM)] * len(self.ins),
            out_specs=[pl.BlockSpec(memory_space=pltpu.VMEM)] * len(self.shapes),
            out_shape=[jax.ShapeDtypeStruct(shape, BF16) for shape in self.shapes],
            compiler_params=BIG_VMEM,
            cost_estimate=CHEAP,
            name="rearrange",
        )(*clock.now(self.ins))
        return list(outs)


class Gather:
    def __init__(self, grid, place, g, height, cols, small=False):
        self.grid, self.place, self.g, self.height, self.cols = grid, place, g, height, cols
        self.rows = (height - (SMALL_ROWS if small else 0)) // g
        self.parts = []

    def put(self, labels, array, first_row, count, offset):
        self.parts.append((labels, array, first_row, count, offset))

    def half(self, *after):
        grid, arrays, parts = self.grid, [], []
        for labels, array, first_row, count, offset in self.parts:
            which = [i for i, known in enumerate(arrays) if known is array]
            if not which:
                arrays.append(array)
                which = [len(arrays) - 1]
            parts.append((which[0], first_row, count, offset, labels))
        self.own = pl.pallas_call(
            functools.partial(half_kernel, parts, grid.ring, grid.wide, self.g, self.rows),
            in_specs=[PLACE] + [pl.BlockSpec(memory_space=pltpu.VMEM)] * len(arrays),
            out_specs=pl.BlockSpec(memory_space=pltpu.VMEM),
            out_shape=jax.ShapeDtypeStruct((2, grid.wide * self.height, self.cols), BF16),
            compiler_params=BIG_VMEM,
            cost_estimate=CHEAP,
            name="half_weights",
        )(self.place, *tie(grid.clock.now(arrays), *after))
        return self.own

    def swap(self):
        self.other = self.grid.send("c", self.own)
        return self.other

    def small_rows(self):
        first = self.g * self.grid.wide * self.rows
        own, other = self.grid.clock.now((self.own[:, first:], self.other[:, first:]))
        flip = self.place[3] == 0
        both = jnp.stack((jnp.where(flip, own, other), jnp.where(flip, other, own)))
        return both.reshape(2, 2, self.grid.wide, SMALL_ROWS, -1).astype(F32)


class Square:
    def __init__(self, gather, blocks, height, offset=0):
        self.gather, self.blocks, self.height, self.offset = gather, blocks, height, offset
        self.cut = height // 32 * 16

    def labels(self, dx, dy):
        return [(dz, dx, dy) for dz in range(len(self.blocks))]


def exchange(grid, before, after):
    make = Rearrange()
    cols = (before or after).gather.cols
    depth = len((before or after).blocks)
    heights = [0, 0]
    if before:
        heights = [before.cut, before.height - before.cut]
    total = [h + (after.height if after else 0) for h in heights]
    outs = [make.out(depth, h, cols) for h in total]
    if before:
        (near_x, x_first), (near_y, y_first) = before.near
        for k in range(depth):
            make.move(outs[0], k, 0, near_y, k, y_first, heights[0])
            make.move(outs[1], k, 0, near_x, k, x_first + before.cut, heights[1])
    if after:
        for out, first in zip(outs, heights):
            for k, pieces in enumerate(after.blocks):
                at = first
                for array, block, row, count, column in pieces:
                    make.move(out, k, at, array, block, row, count, column)
                    at += count
    send_x, send_y = make.run(grid.clock)
    from_x, from_y = grid.send("x", send_x), grid.send("y", send_y)
    if before:
        before.gather.put(before.labels(1, 1), from_x, 0, heights[0], before.offset)
        before.gather.put(before.labels(1, 1), from_y, 0, heights[1], before.offset + before.cut)
    if after:
        after.near = ((from_x, heights[0]), (from_y, heights[1]))
        put = after.gather.put
        put(after.labels(0, 0), send_x, heights[0], after.height, after.offset)
        put(after.labels(1, 0), from_x, heights[0], after.height, after.offset)
        put(after.labels(0, 1), from_y, heights[1], after.height, after.offset)
    return from_x, from_y


def unfold(small, count, start, width):
    part = small[:, :, :, :count, start : start + width]
    return part.transpose(3, 2, 1, 0, 4).reshape(count, -1)


def corners(place):
    y, c = place[2], place[3]
    return (2 * y + 1 - c, 2 * (1 - y) + 1 - c), (2 * y + c, 2 * (1 - y) + c)


def column(ref, n, cols):
    return ref[:, pl.ds(pl.multiple_of(n * cols, 128), cols)]


def both_columns(ref, blocks, cols):
    return jnp.concatenate([column(ref, n, cols) for n in blocks], axis=1)


def far_kernel(place, *refs):
    out = refs[-1]
    cols = out.shape[-1]
    for i in range(out.shape[0]):
        a, d = refs[2 * i], refs[2 * i + 1]
        term = dot_tn(a[...], both_columns(d, corners(place)[0], cols))
        for j in range(2):
            out[i, j] = term[:, j * cols : (j + 1) * cols].astype(BF16)


def put_quadrants(x, scratch, k, i, here, outs):
    dx, dy, qx, qy, own = outs
    rows = own.shape[2]
    if here:
        own[k, i] = scratch[k, x]
        qx[k, i] = scratch[k, 1 - x].astype(BF16)
    else:
        qy[k, i] = scratch[k, x].astype(BF16)
        dx[k, i] = scratch[k, 1 - x, pl.ds(0, rows // 2)].astype(BF16)
        dy[k, i] = scratch[k, 1 - x, pl.ds(rows // 2, rows // 2)].astype(BF16)


def near_kernel(place, *refs):
    from_c, *outs, scratch = refs[-7:]
    zs, units, rows, cols = outs[-1].shape
    for i in range(units):
        a, d = refs[2 * i], refs[2 * i + 1]
        term = dot_tn(a[...], both_columns(d, corners(place)[1], cols))
        for j in range(2):
            part = term[:, j * cols : (j + 1) * cols] + from_c[i, j].astype(F32)
            scratch[...] = part.reshape(scratch.shape)
            for k in range(zs):
                put_quadrants(place[1], scratch, k, i, j == 0, outs)


def quadrant_shapes(units, ring, rows, cols):
    half, full = (ring, units, rows // 2, cols), (ring, units, rows, cols)
    return [jax.ShapeDtypeStruct(half, BF16)] * 2 + [
        jax.ShapeDtypeStruct(full, BF16), jax.ShapeDtypeStruct(full, BF16), jax.ShapeDtypeStruct(full, F32)
    ]


def quadrant_specs(units, zs, rows, cols, stepped):
    def at(s, *_):
        return (s if stepped else 0, 0, 0, 0)

    half = pl.BlockSpec((zs, units, rows // 2, cols), at)
    full = pl.BlockSpec((zs, units, rows, cols), at)
    return [half] * 2 + [full] * 3


def token_terms(grid, place, pairs, rows, cols, from_c=None, params=FULL_VMEM):
    units, tokens = len(pairs), pairs[0][0].shape[0]
    height = grid.wide * rows
    zs = max(1, 128 // (2 * rows))
    if 2 * rows >= 128 and height // (2 * rows) > 1 and rows * cols <= 128 * 256:
        zs = min(grid.ring, 2)
    tall = zs * 2 * rows
    in_specs, args = [], []
    for a, d in pairs:
        in_specs += [
            pl.BlockSpec((tokens, tall), lambda s, *_: (0, s)),
            pl.BlockSpec(d.shape, lambda s, *_: (0, 0)),
        ]
        args += [a, d]
    block = pl.BlockSpec((units, 2, tall, cols), lambda s, *_: (0, 0, s, 0))
    scratch = []
    if from_c is None:
        kernel, out_specs = far_kernel, block
        out_shape = jax.ShapeDtypeStruct((units, 2, height, cols), BF16)
    else:
        in_specs.append(block)
        args.append(from_c)
        kernel = near_kernel
        out_specs = quadrant_specs(units, zs, rows, cols, True)
        out_shape = quadrant_shapes(units, grid.ring, rows, cols)
        scratch = [pltpu.VMEM((zs, 2, rows, cols), F32)]
    return pl.pallas_call(
        kernel,
        grid_spec=pltpu.PrefetchScalarGridSpec(
            num_scalar_prefetch=1,
            grid=(height // tall,),
            in_specs=in_specs,
            out_specs=out_specs,
            scratch_shapes=scratch,
        ),
        out_shape=out_shape,
        compiler_params=params,
        cost_estimate=CHEAP,
        name="weight_terms",
    )(place, *args)


def memory_terms_kernel(near, pairs, place, mem, dk, dv, *refs):
    tokens, refs = refs[: 2 * pairs], refs[2 * pairs :]
    if near:
        from_c, dx, dy, qx, qy, own, acc = refs
    else:
        out, acc = refs
    cols = acc.shape[-1]
    m = pl.program_id(0)
    blocks = corners(place)[1 if near else 0]

    @pl.when(m == 0)
    def _():
        for i in range(pairs):
            term = dot_tn(tokens[2 * i][...], both_columns(tokens[2 * i + 1], blocks, cols))
            for j in range(2):
                acc[i, j] = term[:, j * cols : (j + 1) * cols].reshape(acc.shape[2:])
        acc[pairs:] = jnp.zeros_like(acc[pairs:])
        if near:
            acc[...] += from_c[...].astype(F32).reshape(acc.shape)

    grads = jnp.concatenate([both_columns(d.at[0], blocks, cols) for d in (dk, dv)], axis=1)
    term = dot_tn(mem[0], grads)
    for q in range(4):
        part = term[:, q * cols : (q + 1) * cols].reshape(acc.shape[2:])
        acc[pairs + q // 2, q % 2] += part

    @pl.when(m == pl.num_programs(0) - 1)
    def _():
        if near:
            x = place[1]
            for i in range(pairs + 2):
                for j in range(2):
                    for k in range(own.shape[0]):
                        put_quadrants(x, acc.at[i, j], k, i, j == 0, (dx, dy, qx, qy, own))
        else:
            out[...] = acc[...].reshape(out.shape).astype(BF16)


def memory_terms(grid, place, memory, grads, pairs, rows, cols, from_c=None):
    units, (mems, length, wide_cols) = len(pairs) + 2, memory.shape
    height = grid.wide * rows
    near = from_c is not None
    one = pl.BlockSpec((1, length, wide_cols), lambda m, *_: (m, 0, 0))
    term = pl.BlockSpec((units, 2, height, cols), lambda m, *_: (0, 0, 0, 0))
    tokens = [array for pair in pairs for array in pair]
    return pl.pallas_call(
        functools.partial(memory_terms_kernel, near, len(pairs)),
        grid_spec=pltpu.PrefetchScalarGridSpec(
            num_scalar_prefetch=1,
            grid=(mems,),
            in_specs=[one] * 3
            + [pl.BlockSpec(a.shape, lambda m, *_: (0, 0)) for a in tokens]
            + ([term] if near else []),
            out_specs=quadrant_specs(units, grid.ring, rows, cols, False) if near else term,
            scratch_shapes=[pltpu.VMEM((units, 2, grid.ring, 2, rows, cols), F32)],
        ),
        out_shape=quadrant_shapes(units, grid.ring, rows, cols)
        if near
        else jax.ShapeDtypeStruct((units, 2, height, cols), BF16),
        compiler_params=FULL_VMEM,
        cost_estimate=CHEAP,
        name="memory_terms",
    )(place, memory, *grads, *tokens, *([from_c] if near else []))


def add_corners_kernel(qx, qy, from_x, from_y, sx, sy):
    half = from_x.shape[2]
    first, second = pl.ds(0, half), pl.ds(half, half)
    sx[0, :, first] = qx[0, :, first]
    sx[0, :, second] = (qx[0, :, second].astype(F32) + from_y[0].astype(F32)).astype(BF16)
    sy[0, :, first] = (qy[0, :, first].astype(F32) + from_x[0].astype(F32)).astype(BF16)
    sy[0, :, second] = qy[0, :, second]


def add_corners(qx, qy, from_x, from_y):
    ring, units, rows, cols = qx.shape
    full = pl.BlockSpec((1, units, rows, cols), lambda k: (k, 0, 0, 0))
    half = pl.BlockSpec((1, units, rows // 2, cols), lambda k: (k, 0, 0, 0))
    return pl.pallas_call(
        add_corners_kernel,
        grid=(ring,),
        in_specs=[full, full, half, half],
        out_specs=[full, full],
        out_shape=[jax.ShapeDtypeStruct(qx.shape, BF16)] * 2,
        compiler_params=FULL_VMEM,
        cost_estimate=CHEAP,
        name="add_corners",
    )(qx, qy, from_x, from_y)


class Reduce:
    def __init__(self, grid, place, terms, rows):
        self.grid, self.place, self.terms, self.rows = grid, place, terms, rows

    def far(self):
        self.out = self.terms(None)
        return self.out

    def swap(self):
        self.from_c = self.grid.send("c", self.out)
        return self.from_c

    def near(self):
        self.dx, self.dy, self.qx, self.qy, self.own = self.terms(self.grid.clock.now(self.from_c))
        return self.dx

    def across(self):
        self.from_x, self.from_y = self.grid.send("x", self.dx), self.grid.send("y", self.dy)
        return self.from_x, self.from_y

    def add(self):
        from_x = self.grid.clock.now(self.from_x)
        self.sx, self.sy = add_corners(self.qx, self.qy, from_x, self.from_y)
        return self.sx

    def pairs(self):
        self.back_x, self.back_y = self.grid.send("x", self.sx), self.grid.send("y", self.sy)
        return self.back_x, self.back_y

    def chunk(self, step):
        index = lax.rem(self.place[0] + (self.grid.ring - step), self.grid.ring)
        parts = [
            lax.dynamic_index_in_dim(a, index, 0, keepdims=False)
            for a in self.grid.clock.now((self.own, self.back_x, self.back_y))
        ]
        return parts[0] + parts[1].astype(F32) + parts[2].astype(F32)


class RingSum:
    def __init__(self, grid, reduces):
        self.grid, self.reduces, self.done, self.came = grid, reduces, 0, None

    def step(self, *after):
        self.done += 1
        total = jnp.concatenate([r.chunk(self.done % self.grid.ring) for r in self.reduces], axis=0)
        if self.came is not None:
            total = total + tie(self.grid.clock.now(self.came), *after).astype(F32)
        if self.done == self.grid.ring:
            self.came = total
        else:
            self.came = self.grid.send("z", total.astype(BF16))
        return self.came


class SmallSum:
    def __init__(self, grid, place, terms):
        self.grid, self.place, self.done, self.came = grid, place, 0, None
        self.mine = terms.reshape(grid.ring, 2, 2, 2, -1)
        self.steps = grid.ring + 2

    def pair(self, name, axis, at):
        far = lax.dynamic_index_in_dim(self.mine, 1 - at, axis, keepdims=False)
        self.came = self.grid.send(name, far)
        self.near = lax.dynamic_index_in_dim(self.mine, at, axis, keepdims=False)

    def settle(self, *after):
        if self.came is not None:
            came = tie(self.came, *after) if after else self.came
            self.mine = self.near + came

    def step(self, *after):
        grid, place = self.grid, self.place
        if self.done == 0:
            self.pair("c", 3, place[3])
        elif self.done < grid.ring:
            if self.done == 1:
                self.settle(*after)
            index = lax.rem(place[0] + (grid.ring - self.done), grid.ring)
            total = lax.dynamic_index_in_dim(self.mine, index, 0, keepdims=False)
            if self.done > 1:
                total = total + (tie(self.came, *after) if after else self.came)
            self.came = grid.send("z", total)
            self.near = lax.dynamic_index_in_dim(self.mine, place[0], 0, keepdims=False)
        else:
            self.settle(*after)
            if self.done == grid.ring:
                self.pair("y", 1, place[2])
            else:
                self.pair("x", 0, place[1])
        self.done += 1
        return self.came

    def result(self):
        return self.near + self.came


def halves(place, own, other):
    c = place[3]
    return [(2 * y + core, y, half) for half, core in ((own, c), (other, 1 - c)) for y in range(2)]


def at_block(n, cols):
    return pl.ds(pl.multiple_of(n * cols, 128), cols)


def times_t(place, d, own, other):
    cols = own.shape[-1]
    return sum(dot_nt(d[:, at_block(n, cols)], half[y]) for n, y, half in halves(place, own, other))


def norm_parts(values):
    centre = values - jnp.mean(values, axis=-1, keepdims=True)
    scale = lax.rsqrt(jnp.mean(centre * centre, axis=-1, keepdims=True) + EPSILON)
    return centre * scale, scale


def norm_back(normed, scale, gain, grad):
    inner = grad * gain
    back = scale * (
        inner
        - jnp.mean(inner, axis=-1, keepdims=True)
        - normed * jnp.mean(inner * normed, axis=-1, keepdims=True)
    )
    return back, jnp.sum(grad * normed, axis=0, keepdims=True), jnp.sum(grad, axis=0, keepdims=True)


def column_sum(values):
    return jnp.sum(values.astype(F32), axis=0, keepdims=True)


GAIN, BIAS = 0, 3


def row(vectors, i):
    return vectors[i : i + 1, :]


def memory_kernel(place, mem, vectors, k_own, k_other, v_own, v_other, keys, values):
    cols = k_own.shape[-1]
    for n, y, half in halves(place, k_own, k_other):
        keys[0, :, at_block(n, cols)] = dot_nn(mem[0], half[y]).astype(BF16)
    for n, y, half in halves(place, v_own, v_other):
        bias = vectors[BIAS + 6 : BIAS + 7, at_block(n, cols)]
        values[0, :, at_block(n, cols)] = (dot_nn(mem[0], half[y]) + bias).astype(BF16)


def qkv_kernel(place, tokens, vectors, *refs):
    weights, (normed, q, k, v) = refs[:6], refs[6:]
    n, _ = norm_parts(tokens[...].astype(F32))
    normed[...] = (n * row(vectors, GAIN) + row(vectors, BIAS)).astype(BF16)
    cols = weights[0].shape[-1]
    for i, (out, bias_at) in enumerate(((q, 1), (k, None), (v, 2))):
        for n, y, half in halves(place, weights[2 * i], weights[2 * i + 1]):
            term = dot_nn(normed[...], half[y])
            if bias_at is not None:
                term = term + vectors[BIAS + bias_at : BIAS + bias_at + 1, at_block(n, cols)]
            out[:, at_block(n, cols)] = term.astype(BF16)


def middle_kernel(place, tokens, mixed, vectors, so_own, so_other, cq_own, cq_other, after, normed, queries):
    cols = so_own.shape[-1]
    for n, y, half in halves(place, so_own, so_other):
        at = at_block(n, cols)
        after[:, at] = tokens[:, at].astype(F32) + dot_nn(mixed[...], half[y]) + vectors[BIAS + 3 : BIAS + 4, at]
    n, _ = norm_parts(after[...])
    normed[...] = (n * row(vectors, GAIN + 1) + row(vectors, BIAS + 4)).astype(BF16)
    for n, y, half in halves(place, cq_own, cq_other):
        at = at_block(n, cols)
        queries[:, at] = (dot_nn(normed[...], half[y]) + vectors[BIAS + 5 : BIAS + 6, at]).astype(BF16)


def cross_out_kernel(place, before, mixed, vectors, own, other, after, normed):
    cols = own.shape[-1]
    for n, y, half in halves(place, own, other):
        at = at_block(n, cols)
        after[:, at] = before[:, at] + dot_nn(mixed[...], half[y]) + vectors[BIAS + 7 : BIAS + 8, at]
    n, _ = norm_parts(after[...])
    normed[...] = (n * row(vectors, GAIN + 2) + row(vectors, BIAS + 8)).astype(BF16)


def up_kernel(place, normed, bias, own, other, act, slope):
    c, cols = place[3], own.shape[-1]
    y = pl.program_id(0)
    for n, half in ((2 * y + c, own), (2 * y + 1 - c, other)):
        for j in range(4):
            at = at_block(4 * n + j, cols)
            u = dot_nn(normed[...], half[0, j * D : (j + 1) * D]) + bias[:, at]
            below = 0.5 * (1.0 + lax.erf(u * (1.0 / math.sqrt(2.0))))
            act[:, at] = (u * below).astype(BF16)
            slope[:, at] = (below + u * jnp.exp(-0.5 * u * u) * (1.0 / math.sqrt(2.0 * math.pi))).astype(BF16)


def down_kernel(place, after, act, vectors, own, other, out):
    c, y = place[3], pl.program_id(0)
    cols = own.shape[-1]
    for n, half in ((2 * y + c, own), (2 * y + 1 - c, other)):
        at = at_block(n, cols)
        total = after[:, at] + dot_nn(act[...], half[0]) + vectors[BIAS + 9 : BIAS + 10, at]
        out[:, at] = total.astype(BF16)


def down_back_kernel(place, grad, slope, normed, own, other, grad_pre, bias_grad, far):
    back = (times_t(place, grad, own, other) * slope[...].astype(F32)).astype(BF16)
    grad_pre[...] = back
    bias_grad[...] = column_sum(back)
    for i, n in enumerate(corners(place)[0]):

        @pl.when(pl.program_id(0) == n)
        def _():
            far[0, i] = dot_tn(normed[...], back).astype(BF16)


def up_back_kernel(
    place, grad_pre, grad_out, after, vectors, own, other, co_own, co_other,
    grad, branch, mixed, gain_grad, shift_grad, out_grad, last_grad, total,
):
    c, y = place[3], pl.program_id(0)
    cols = own.shape[-1]
    term = sum(
        dot_nt(grad_pre[:, at_block(4 * n + j, cols)], half[0, j * D : (j + 1) * D])
        for n, half in ((2 * y + c, own), (2 * y + 1 - c, other))
        for j in range(4)
    )

    @pl.when(y == 0)
    def _():
        total[...] = term

    @pl.when(y == 1)
    def _():
        n, scale = norm_parts(after[...])
        back, gain_grad[...], shift_grad[...] = norm_back(n, scale, row(vectors, GAIN + 2), total[...] + term)
        out = grad_out[...].astype(F32) + back
        grad[...] = out
        branch[...] = out.astype(BF16)
        out_grad[...] = column_sum(branch[...])
        last_grad[...] = column_sum(grad_out[...])
        mixed[...] = times_t(place, branch, co_own, co_other).astype(BF16)


def middle_back_kernel(
    place, grad_queries, grad_after, after, vectors, cq_own, cq_other, so_own, so_other,
    grad, branch, mixed, gain_grad, shift_grad, out_grad, query_grad,
):
    n, scale = norm_parts(after[...])
    dense = times_t(place, grad_queries, cq_own, cq_other)
    back, gain_grad[...], shift_grad[...] = norm_back(n, scale, row(vectors, GAIN + 1), dense)
    out = grad_after[...] + back
    grad[...] = out
    branch[...] = out.astype(BF16)
    out_grad[...] = column_sum(branch[...])
    query_grad[...] = column_sum(grad_queries[...])
    mixed[...] = times_t(place, branch, so_own, so_other).astype(BF16)


def first_back_kernel(place, tokens, grad_after, gq, gk, gv, vectors, *refs):
    weights, (grad, gain_grad, shift_grad, query_grad, value_grad) = refs[:6], refs[6:]
    n, scale = norm_parts(tokens[...].astype(F32))
    dense = sum(
        times_t(place, d, weights[2 * i], weights[2 * i + 1]) for i, d in enumerate((gq, gk, gv))
    )
    back, gain_grad[...], shift_grad[...] = norm_back(n, scale, row(vectors, GAIN), dense)
    grad[...] = (grad_after[...] + back).astype(BF16)
    query_grad[...] = column_sum(gq[...])
    value_grad[...] = column_sum(gv[...])


def memory_back_kernel(place, gk, gv, k_own, k_other, v_own, v_other, grad):
    total = times_t(place, gk.at[0], k_own, k_other) + times_t(place, gv.at[0], v_own, v_other)
    grad[0] = total.astype(BF16)


def in_place(array):
    return pl.pallas_call(
        lambda _, out: None,
        in_specs=anywhere(1),
        out_specs=pl.BlockSpec(memory_space=pl.ANY),
        out_shape=jax.ShapeDtypeStruct(array.shape, array.dtype),
        input_output_aliases={0: 0},
        compiler_params=BIG_VMEM,
        cost_estimate=CHEAP,
        name="in_place",
    )(array)


def dense_call(kernel, name, place, ins, outs, grid=(1,), scratch=(), params=BIG_VMEM):
    def spec(array, block, index):
        block = block or array.shape
        zeros = (0,) * len(block)
        return pl.BlockSpec(block, index or (lambda *_: zeros))

    return pl.pallas_call(
        kernel,
        grid_spec=pltpu.PrefetchScalarGridSpec(
            num_scalar_prefetch=1,
            grid=grid,
            in_specs=[spec(*one) for one in ins],
            out_specs=[spec(*one) for one in outs],
            scratch_shapes=scratch,
        ),
        out_shape=[one[0] for one in outs],
        compiler_params=params,
        cost_estimate=CHEAP,
        name=name,
    )(place, *[one[0] for one in ins])


def full(array):
    return (array, None, None)


def result(shape, dtype):
    return (jax.ShapeDtypeStruct(shape, dtype), None, None)


def matrix(gathered, i, height=D):
    block = (2, height, gathered.own.shape[-1])
    return [(half, block, lambda *_: (0, i, 0)) for half in (gathered.own, gathered.other)]


def by_y(gathered):
    block = (1,) + gathered.own.shape[1:]
    return [(half, block, lambda y, *_: (y, 0, 0)) for half in (gathered.own, gathered.other)]


def by_rows(gathered, rows):
    block = (2, rows, gathered.own.shape[-1])
    return [(half, block, lambda s, *_: (0, s, 0)) for half in (gathered.own, gathered.other)]


def local(
    shape,
    tokens,
    memory,
    segment_ids,
    page_map,
    mem_lengths,
    gains,
    biases,
    fc1_bias,
    self_qkv,
    self_out,
    cross_q,
    cross_kv,
    cross_out,
    fc1,
    fc2,
    cotangent,
):
    grid = Grid(*shape)
    wide_at, narrow_at = lax.axis_index("wide"), lax.axis_index("narrow")
    place = jnp.stack((wide_at // 2, wide_at % 2, narrow_at // 2, narrow_at % 2)).astype(jnp.int32)
    devices = grid.devices
    mem_count, token_count = memory.shape[0], tokens.shape[0]
    rows, cols = self_out.shape

    each, up_each = gains.shape[1], fc1_bias.size
    n_gain, n_bias = gains.size, biases.size
    small = jnp.pad(
        jnp.concatenate((gains, biases), axis=0), ((0, SMALL_ROWS - 13), (0, cols - each))
    )
    small = lax.dynamic_update_slice(small, fc1_bias[None], (0, 128))
    send, clock = grid.send, grid.clock
    now, tick = clock.now, clock.tick
    steps = grid.ring - 1
    gather = functools.partial(Gather, grid, place)
    ckv_height = 2 * rows + SMALL_ROWS
    fc2_rows = fc2.shape[0]
    part = fc2_rows // 2
    g_ckv = gather(2, ckv_height, cols, True)
    g_qkv = gather(3, 3 * rows, cols)
    g_mix = gather(3, 3 * rows, cols)
    g_fc1 = gather(4, 4 * rows, cols)
    g_fc2 = gather(1, fc2_rows, cols)

    start = Rearrange()
    out = start.out(1, 5 * rows, cols)
    for k, (array, i) in enumerate(((cross_kv, 0), (cross_kv, 1), (self_qkv, 0), (self_qkv, 1), (self_qkv, 2))):
        start.move(out, 0, k * rows, array, i, 0, rows)
    ring_one = start.run(clock)
    ring_one.append(send("z", ring_one[-1]))
    ring_small = [small[None]]
    ring_small.append(send("z", ring_small[-1]))
    top = Square(g_fc2, [[(fc2[None], 0, 0, part, 0)]], part)
    more = Rearrange()
    out = more.out(1, 3 * rows, cols)
    for k, array in enumerate((self_out, cross_q, cross_out)):
        more.move(out, 0, k * rows, array[None], 0, 0, rows)
    out = more.out(1, 4 * rows + part, cols)
    for k in range(4):
        more.move(out, 0, k * rows, fc1[None], 0, 0, rows, k * cols)
    more.move(out, 0, 4 * rows, fc2[None], 0, part, part)
    ring_mix, ring_up = [[array] for array in more.run(clock)]
    tick(ring_one[-1], ring_small[-1], ring_mix[0], ring_up[0], *exchange(grid, None, top))
    ring_one.append(send("z", ring_one[-1]))
    ring_small.append(send("z", ring_small[-1]))
    memory = in_place(now(memory))
    tick(ring_one[-1], ring_small[-1], memory, *exchange(grid, top, None))
    for _ in range(steps - 2):
        ring_one.append(send("z", ring_one[-1]))
        ring_small.append(send("z", ring_small[-1]))
        tick(ring_one[-1], ring_small[-1])

    def from_ring(arrays, first, count):
        return [[(array, 0, first, count, 0)] for array in arrays]

    ckv = Square(
        g_ckv, [a + b for a, b in zip(from_ring(ring_one, 0, 2 * rows), from_ring(ring_small, 0, SMALL_ROWS))],
        ckv_height,
    )
    qkv = Square(g_qkv, from_ring(ring_one, 2 * rows, 3 * rows), 3 * rows)
    ring_mix.append(send("z", ring_mix[-1]))
    ring_up.append(send("z", ring_up[-1]))
    tick(ring_mix[-1], ring_up[-1], *exchange(grid, None, ckv))

    make = Rearrange()
    out = make.out(4, part, cols)
    (_, own, own_at, _, _), (_, by_x, x_at, _, _), (_, by_y_, y_at, _, _), (_, low, _, _, _), (_, high, _, _, _) = g_fc2.parts
    g_fc2.parts = []
    for k, (array, at) in enumerate(((own, own_at), (by_x, x_at), (by_y_, y_at))):
        make.move(out, k, 0, array, 0, at, part)
    make.move(out, 3, 0, low, 0, 0, top.cut)
    make.move(out, 3, top.cut, high, 0, 0, part - top.cut)
    came = exchange(grid, ckv, qkv)
    ring_top = make.run(clock)
    ring_up.append(send("z", ring_up[-1]))
    for _ in range(steps - 1):
        ring_mix.append(send("z", ring_mix[-1]))
    tick(ring_mix[-1], ring_up[-1], ring_top[-1], *came)

    mix = Square(g_mix, from_ring(ring_mix, 0, 3 * rows), 3 * rows)
    came = exchange(grid, qkv, mix)
    for _ in range(steps - 2):
        ring_up.append(send("z", ring_up[-1]))
    g_ckv.half(g_mix.parts[0][1])
    g_ckv.swap()
    small_all = g_ckv.small_rows()
    vectors = unfold(small_all, 13, 0, each)
    up_bias = unfold(small_all, 1, 128, up_each)
    mem_block = (1,) + memory.shape[1:]
    mem_shape = jax.ShapeDtypeStruct(memory.shape, BF16)

    def by_memory(array):
        return (array, mem_block, lambda m, *_: (m, 0, 0))

    mem_keys, mem_values = dense_call(
        memory_kernel, "memory_keys_values", place,
        [by_memory(now(memory)), full(vectors)] + matrix(g_ckv, 0) + matrix(g_ckv, 1),
        [by_memory(mem_shape), by_memory(mem_shape)], grid=(mem_count,),
    )
    tick(ring_up[-1], mem_keys, *came)

    up = Square(g_fc1, from_ring(ring_up, 0, 4 * rows), 4 * rows)
    low = Square(g_fc2, from_ring(ring_up, 4 * rows, part), part, part)
    came = exchange(grid, mix, up)
    ring_top.append(send("z", ring_top[-1]))
    g_qkv.half(g_fc1.parts[0][1])
    g_qkv.swap()
    wide_row = (token_count, D)
    normed_one, self_queries, self_keys, self_values = dense_call(
        qkv_kernel, "self_qkv", place,
        [full(now(tokens)), full(vectors)] + matrix(g_qkv, 0) + matrix(g_qkv, 1) + matrix(g_qkv, 2),
        [result(wide_row, BF16)] * 4,
    )
    self_mixed, self_lse = self_forward(segment_ids, self_queries, self_keys, self_values)
    tick(self_mixed, ring_top[-1], *came)

    came = exchange(grid, up, low)
    g_mix.half(g_fc2.parts[0][1])
    g_mix.swap()
    ring_top.append(send("z", ring_top[-1]))
    after_self, normed_two, cross_queries = dense_call(
        middle_kernel, "self_out_cross_q", place,
        [full(tokens), full(now(self_mixed)), full(vectors)] + matrix(g_mix, 0) + matrix(g_mix, 1),
        [result(wide_row, F32), result(wide_row, BF16), result(wide_row, BF16)],
    )
    first_mem = lax.axis_index(AXES) * mem_count
    local_map = (page_map - first_mem).reshape(-1).astype(jnp.int32)
    picks = local_map[:, None] == jnp.arange(mem_count, dtype=jnp.int32)[None, :]
    row_lengths = jnp.sum(jnp.where(picks, mem_lengths[None, :], 0), axis=-1).astype(jnp.int32)
    cross_mixed, cross_lse = cross_forward(
        local_map, row_lengths, segment_ids, cross_queries, mem_keys, mem_values
    )
    tick(cross_mixed, ring_top[-1], *came)

    came = exchange(grid, low, None)
    for _ in range(steps - 2):
        ring_top.append(send("z", ring_top[-1]))
    g_fc1.half()
    g_fc1.swap()
    after_cross, normed_three = dense_call(
        cross_out_kernel, "cross_out", place,
        [full(after_self), full(now(cross_mixed)), full(vectors)] + matrix(g_mix, 2),
        [result(wide_row, F32), result(wide_row, BF16)],
    )
    hidden = up_bias.shape[1]
    activated, slope = dense_call(
        up_kernel, "fc1_gelu", place,
        [full(normed_three), full(up_bias)] + by_y(g_fc1),
        [result((token_count, hidden), BF16)] * 2, grid=(2,),
    )
    tick(activated, ring_top[-1], *came)
    spread = [(0, 0), (1, 0), (0, 1), (1, 1)]
    for step, array in enumerate(ring_top):
        g_fc2.put([(step, dx, dy) for dx, dy in spread], array, 0, part, 0)

    def settle(pairs, shard, params=FULL_VMEM):
        part_rows, part_cols = shard.shape
        return Reduce(
            grid, place,
            lambda from_c: token_terms(grid, place, pairs, part_rows, part_cols, from_c, params),
            part_rows,
        )

    one_row = result((1, D), F32)
    r_fc2 = settle([(now(activated), cotangent)], fc2, BIG_VMEM)
    r_fc2.far()
    r_fc2.swap()
    g_fc2.half()
    g_fc2.swap()
    tick(r_fc2.near())
    slab = hidden // 4
    some = lambda array: (array, (token_count, slab), lambda s, *_: (0, s))
    grad_pre, grad_up_bias, far_fc1 = dense_call(
        down_back_kernel, "fc2_gelu_back", place,
        [full(now(cotangent)), some(slope), full(normed_three)] + by_rows(g_fc2, slab),
        [
            some(jax.ShapeDtypeStruct((token_count, hidden), BF16)),
            (jax.ShapeDtypeStruct((1, hidden), F32), (1, slab), lambda s, *_: (0, s)),
            result((1, 2, D, slab), BF16),
        ],
        grid=(4,), params=FULL_VMEM,
    )
    r_fc1 = settle([(normed_three, grad_pre)], fc1)
    r_fc1.out = far_fc1
    tick(far_fc1, *r_fc2.across())
    r_fc2.add()
    r_fc1.swap()
    (
        grad_after_cross, grad_branch_two, grad_cross_mixed,
        grad_gain_three, grad_bias_eight, grad_bias_seven, grad_bias_nine,
    ) = dense_call(
        up_back_kernel, "fc1_norm_back", place,
        [full(now(grad_pre)), full(cotangent), full(after_cross), full(vectors)]
        + by_y(g_fc1) + matrix(g_mix, 2),
        [result(wide_row, F32), result(wide_row, BF16), result(wide_row, BF16)] + [one_row] * 4,
        grid=(2,), scratch=[pltpu.VMEM(wide_row, F32)], params=FULL_VMEM,
    )
    tick(r_fc1.near(), r_fc2.sx, grad_cross_mixed)

    came = [*r_fc2.pairs(), *r_fc1.across()]
    grad_cq, grad_ck, grad_cv, grad_bias_six = cross_backward(
        local_map, row_lengths, segment_ids, cross_queries, mem_keys, mem_values,
        now(grad_cross_mixed), cross_lse,
    )
    r_mem = Reduce(
        grid, place,
        lambda from_c: memory_terms(grid, place, memory, (grad_ck, grad_cv), [], rows, cols, from_c),
        rows,
    )
    tick(grad_cq, r_mem.far(), *came)
    ring_fc2 = RingSum(grid, [r_fc2])
    r_fc1.add()
    r_mem.swap()
    ring_fc2.step()
    grad_cq = tie(now(grad_cq), r_fc1.sx)
    (
        grad_after_self, grad_branch_one, grad_self_mixed,
        grad_gain_two, grad_bias_four, grad_bias_three, grad_bias_five,
    ) = dense_call(
        middle_back_kernel, "cross_q_norm_back", place,
        [full(grad_cq), full(grad_after_cross), full(after_self), full(vectors)]
        + matrix(g_mix, 1) + matrix(g_mix, 0),
        [result(wide_row, F32), result(wide_row, BF16), result(wide_row, BF16)] + [one_row] * 4,
        params=FULL_VMEM,
    )
    grad_sq, grad_sk, grad_sv = self_backward(
        segment_ids, self_queries, self_keys, self_values, grad_self_mixed, self_lse
    )
    r_rest = settle(
        [
            (normed_one, grad_sq), (normed_one, grad_sk), (normed_one, grad_sv),
            (self_mixed, grad_branch_one), (normed_two, grad_cq), (cross_mixed, grad_branch_two),
        ],
        cross_q,
    )
    tick(r_rest.far(), r_mem.near(), ring_fc2.came, *r_fc1.pairs())
    ring_fc1 = RingSum(grid, [r_fc1])
    came = r_mem.across()
    r_rest.swap()
    ring_fc2.step()
    ring_fc1.step()
    grad_tokens, grad_gain_one, grad_bias_zero, grad_bias_one, grad_bias_two = dense_call(
        first_back_kernel, "self_qkv_norm_back", place,
        [full(tokens), full(grad_after_self)] + [full(d) for d in now((grad_sq, grad_sk, grad_sv))]
        + [full(vectors)] + matrix(g_qkv, 0) + matrix(g_qkv, 1) + matrix(g_qkv, 2),
        [result(wide_row, BF16)] + [one_row] * 4,
        params=FULL_VMEM,
    )
    tick(r_rest.near(), grad_tokens, ring_fc2.came, ring_fc1.came, *came)

    def by_device(array):
        return array.reshape(array.shape[0], devices, -1).transpose(1, 0, 2).reshape(devices, -1)

    small_grads = jnp.concatenate(
        (
            by_device(
                jnp.concatenate(
                    (
                        grad_gain_one, grad_gain_two, grad_gain_three,
                        grad_bias_zero, grad_bias_one, grad_bias_two, grad_bias_three, grad_bias_four,
                        grad_bias_five, grad_bias_six, grad_bias_seven, grad_bias_eight, grad_bias_nine,
                    ),
                    axis=0,
                )
            ),
            by_device(grad_up_bias),
        ),
        axis=1,
    )
    small_sum = SmallSum(grid, place, now(small_grads))
    r_mem.add()
    ring_fc2.step()
    (grad_memory,) = dense_call(
        memory_back_kernel, "memory_back", place,
        [by_memory(a) for a in tie(now((grad_ck, grad_cv)), r_mem.sx)] + matrix(g_ckv, 0) + matrix(g_ckv, 1),
        [by_memory(mem_shape)], grid=(mem_count,), params=FULL_VMEM,
    )
    (layer_out,) = dense_call(
        down_kernel, "fc2", place,
        [full(after_cross), full(tie(now(activated), r_mem.sx)), full(vectors)] + by_y(g_fc2),
        [result(wide_row, BF16)], grid=(2,), params=FULL_VMEM,
    )
    tick(grad_memory, layer_out, ring_fc2.came, *r_mem.pairs(), *r_rest.across())
    small_sum.step()
    ring_mem = RingSum(grid, [r_mem])
    r_rest.add()
    turned_memory = in_place(tie(now(grad_memory).transpose(1, 0, 2), r_rest.sx))
    grad_memory = turned_memory.transpose(1, 0, 2)
    ring_fc1.step()
    ring_mem.step()
    for _ in range(steps):
        small_sum.step()
    ring_fc1.step(turned_memory)
    tick(turned_memory, small_sum.came, ring_fc1.came, ring_mem.came, *r_rest.pairs())
    ring_fc2.step()
    ring_rest = RingSum(grid, [r_rest])
    ring_rest.step()
    ring_fc1.step()
    ring_mem.step()
    small_sum.step()
    tick(ring_rest.came, ring_mem.came, small_sum.came)
    for _ in range(steps - 1):
        ring_mem.step() if ring_mem.done < grid.ring else None
        small_sum.step() if small_sum.done < small_sum.steps else None
        tick(ring_rest.step(), ring_mem.came, small_sum.came)
    for ring in (ring_fc2, ring_fc1, ring_mem, ring_rest):
        while ring.done < grid.ring:
            ring.step()
    while small_sum.done < small_sum.steps:
        small_sum.step()
    came_mem, came_rest = ring_mem.came, ring_rest.came
    small_shard = small_sum.result()
    return (
        layer_out,
        grad_tokens,
        grad_memory,
        small_shard[:n_gain].reshape(gains.shape),
        small_shard[n_gain : n_gain + n_bias].reshape(biases.shape),
        small_shard[n_gain + n_bias :],
        came_rest[:3],
        came_rest[3],
        came_rest[4],
        came_mem,
        came_rest[5],
        ring_fc1.came[0],
        ring_fc2.came[0],
    )


def solution(mesh):
    shape = (mesh.shape["wide"], mesh.shape["narrow"])
    in_specs = (
        P(AXES, None),
        P(AXES, None, None),
        P(AXES, None),
        P(AXES, None),
        P(AXES),
        P(None, AXES),
        P(None, AXES),
        P(AXES),
        P(None, "wide", "narrow"),
        P("wide", "narrow"),
        P("wide", "narrow"),
        P(None, "wide", "narrow"),
        P("wide", "narrow"),
        P("wide", "narrow"),
        P("wide", "narrow"),
        P(AXES, None),
    )
    out_specs = (
        P(AXES, None),
        P(AXES, None),
        P(AXES, None, None),
        P(None, AXES),
        P(None, AXES),
        P(AXES),
        P(None, "wide", "narrow"),
        P("wide", "narrow"),
        P("wide", "narrow"),
        P(None, "wide", "narrow"),
        P("wide", "narrow"),
        P("wide", "narrow"),
        P("wide", "narrow"),
    )
    return jax.shard_map(
        functools.partial(local, shape), mesh=mesh, in_specs=in_specs, out_specs=out_specs, check_vma=False
    )
```

```python
import functools
import math

import jax
import jax.numpy as jnp
from jax import lax
from jax.experimental import pallas as pl
from jax.experimental.pallas import tpu as pltpu
from jax.sharding import PartitionSpec as P

D = 1024
HEADS = 16
HEAD_DIM = 64
PAIRS = HEADS // 2

EPSILON = 1e-05
NEG_FILL = -1e30
LOG2E = math.log2(math.e)
SCALE = 1.0 / math.sqrt(HEAD_DIM)
AXES = ("wide", "narrow")

F32 = jnp.float32
BF16 = jnp.bfloat16
VMEM = 24 * 2**20
CHEAP = pl.CostEstimate(flops=10**6, bytes_accessed=10**5, transcendentals=0)
BIG_VMEM = pltpu.CompilerParams(vmem_limit_bytes=VMEM)
SMALL_VMEM = pltpu.CompilerParams(vmem_limit_bytes=16 * 2**20)
FULL_VMEM = pltpu.CompilerParams(vmem_limit_bytes=60 * 2**20)


def dot_nt(a, b):
    return lax.dot_general(a, b, (((1,), (1,)), ((), ())), preferred_element_type=F32)


def dot_nn(a, b):
    return lax.dot_general(a, b, (((1,), (0,)), ((), ())), preferred_element_type=F32)


def dot_tn(a, b):
    return lax.dot_general(a, b, (((0,), (0,)), ((), ())), preferred_element_type=F32)


def two_heads(block):
    lane = lax.broadcasted_iota(jnp.int32, block.shape, 1)
    zero = jnp.zeros_like(block)
    return jnp.concatenate(
        (jnp.where(lane < HEAD_DIM, block, zero), jnp.where(lane < HEAD_DIM, zero, block)), axis=0
    )


def own_heads(both):
    half = both.shape[1] // 2
    line = lax.broadcasted_iota(jnp.int32, (both.shape[0], half), 0)
    return jnp.transpose(jnp.where(line < HEAD_DIM, both[:, :half], both[:, half:]))


CUTS = [slice(128 * h, 128 * h + 128) for h in range(PAIRS)]


def heads_forward(q_ref, k_ref, v_ref, valid, put):
    scores = [dot_nt(k_ref(cut), two_heads(q_ref(cut))) for cut in CUTS]
    weights, lses = [], []
    for one in scores:
        one = jnp.where(valid, one * (SCALE * LOG2E), NEG_FILL)
        top = jnp.max(one, axis=0, keepdims=True)
        expo = jnp.exp2(one - top)
        total = jnp.sum(expo, axis=0, keepdims=True)
        weights.append((expo * (1.0 / total)).astype(BF16))
        lses.append(top + jnp.log2(total))
    for h, cut in enumerate(CUTS):
        put(h, own_heads(dot_tn(v_ref(cut), weights[h])).astype(BF16), lses[h])


def heads_backward(q_ref, k_ref, v_ref, do_ref, lse_of, valid, put, group=4):
    for first in range(0, PAIRS, group):
        hs = range(first, first + group)
        qs = [two_heads(q_ref(CUTS[h])) for h in hs]
        ds = [two_heads(do_ref(CUTS[h])) for h in hs]
        scores = [dot_nt(k_ref(CUTS[h]), q) for h, q in zip(hs, qs)]
        grads = [dot_nt(v_ref(CUTS[h]), d) for h, d in zip(hs, ds)]
        weights, grad_scores = [], []
        for h, one, grad in zip(hs, scores, grads):
            weight = jnp.where(valid, jnp.exp2(one * (SCALE * LOG2E) - lse_of(h)), 0.0)
            inner = jnp.sum(weight * grad, axis=0, keepdims=True)
            grad_scores.append((weight * (grad - inner)).astype(BF16))
            weights.append(weight.astype(BF16))
        for h, q, d, weight, grad in zip(hs, qs, ds, weights, grad_scores):
            grad_q = (own_heads(dot_tn(k_ref(CUTS[h]), grad)) * SCALE).astype(BF16)
            grad_k = (dot_nn(grad, q) * SCALE).astype(BF16)
            put(h, grad_q, grad_k, dot_nn(weight, d).astype(BF16))


def columns_in(ref):
    return lambda cut: ref[:, cut]


def memory_columns(ref):
    return lambda cut: ref[0, :, cut]


def self_valid(seg_row, seg_col):
    length = seg_row.shape[-1]
    key = lax.broadcasted_iota(jnp.int32, (length, length), 0)
    tok = lax.broadcasted_iota(jnp.int32, (length, length), 1)
    one = (key <= tok) & (seg_row == seg_col)
    return jnp.concatenate((one, one), axis=1)


def self_fwd_kernel(seg_row, seg_col, q_ref, k_ref, v_ref, o_ref, lse_ref):
    def put(h, mixed, lse):
        o_ref[:, CUTS[h]] = mixed
        lse_ref[0, h : h + 1, :] = lse

    heads_forward(
        columns_in(q_ref), columns_in(k_ref), columns_in(v_ref), self_valid(seg_row[0], seg_col[0]), put
    )


def self_bwd_kernel(seg_row, seg_col, q_ref, k_ref, v_ref, do_ref, lse_ref, dq_ref, dk_ref, dv_ref):
    def put(h, grad_q, grad_k, grad_v):
        dq_ref[:, CUTS[h]] = grad_q
        dk_ref[:, CUTS[h]] = grad_k
        dv_ref[:, CUTS[h]] = grad_v

    heads_backward(
        columns_in(q_ref), columns_in(k_ref), columns_in(v_ref), columns_in(do_ref),
        lambda h: lse_ref[0, h : h + 1, :], self_valid(seg_row[0], seg_col[0]), put, PAIRS,
    )


def self_specs(row_len):
    seg = [
        pl.BlockSpec((1, 1, row_len), lambda r: (r, 0, 0)),
        pl.BlockSpec((1, row_len, 1), lambda r: (r, 0, 0)),
    ]
    row = pl.BlockSpec((row_len, D), lambda r: (r, 0))
    lse = pl.BlockSpec((1, PAIRS, 2 * row_len), lambda r: (r, 0, 0))
    return seg, row, lse


def self_forward(seg, queries, keys, values):
    rows, row_len = seg.shape
    seg_specs, row, lse = self_specs(row_len)
    return pl.pallas_call(
        self_fwd_kernel,
        grid=(rows,),
        in_specs=seg_specs + [row] * 3,
        out_specs=[row, lse],
        out_shape=[
            jax.ShapeDtypeStruct(queries.shape, BF16),
            jax.ShapeDtypeStruct((rows, PAIRS, 2 * row_len), F32),
        ],
        compiler_params=BIG_VMEM,
        cost_estimate=CHEAP,
        name="self_forward",
    )(seg[:, None, :], seg[:, :, None], queries, keys, values)


def self_backward(seg, queries, keys, values, grad_mixed, lse_rows):
    rows, row_len = seg.shape
    seg_specs, row, lse = self_specs(row_len)
    return pl.pallas_call(
        self_bwd_kernel,
        grid=(rows,),
        in_specs=seg_specs + [row] * 4 + [lse],
        out_specs=[row] * 3,
        out_shape=[jax.ShapeDtypeStruct(queries.shape, BF16)] * 3,
        compiler_params=FULL_VMEM,
        cost_estimate=CHEAP,
        name="self_backward",
    )(seg[:, None, :], seg[:, :, None], queries, keys, values, grad_mixed, lse_rows)


def cross_fwd_kernel(map_ref, len_ref, seg_row, seg_col, q_ref, k_ref, v_ref, o_ref, lse_ref):
    r, page = pl.program_id(0), pl.program_id(1)
    keys, toks = k_ref.shape[1], q_ref.shape[0]
    valid = lax.broadcasted_iota(jnp.int32, (keys, 2 * toks), 0) < len_ref[r * 2 + page]
    mine_col = (seg_col[0] == page) | (page == 0)
    mine_row = (seg_row[0] == page) | (page == 0)
    mine_row = jnp.concatenate((mine_row, mine_row), axis=1)

    def put(h, mixed, lse):
        o_ref[:, CUTS[h]] = jnp.where(mine_col, mixed, o_ref[:, CUTS[h]])
        lse_ref[0, h : h + 1, :] = jnp.where(mine_row, lse, lse_ref[0, h : h + 1, :])

    heads_forward(columns_in(q_ref), memory_columns(k_ref), memory_columns(v_ref), valid, put)


def cross_bwd_kernel(
    map_ref, len_ref, seg_row, seg_col, q_ref, k_ref, v_ref, do_ref, lse_ref,
    dq_ref, dk_ref, dv_ref, sum_ref,
):
    r, page = pl.program_id(0), pl.program_id(1)
    keys, toks = k_ref.shape[1], q_ref.shape[0]
    valid = lax.broadcasted_iota(jnp.int32, (keys, 2 * toks), 0) < len_ref[r * 2 + page]
    mine_col = (seg_col[0] == page) | (page == 0)
    mine_row = seg_row[0] == page
    mine_row = jnp.concatenate((mine_row, mine_row), axis=1)

    def put(h, grad_q, grad_k, grad_v):
        cut = CUTS[h]
        dq_ref[:, cut] = jnp.where(mine_col, grad_q, dq_ref[:, cut])
        dk_ref[0, :, cut] = grad_k
        dv_ref[0, :, cut] = grad_v
        before = jnp.where(r + page == 0, jnp.zeros((1, 128), F32), sum_ref[:, cut])
        sum_ref[:, cut] = before + jnp.sum(grad_v.astype(F32), axis=0, keepdims=True)

    heads_backward(
        columns_in(q_ref), memory_columns(k_ref), memory_columns(v_ref), columns_in(do_ref),
        lambda h: jnp.where(mine_row, lse_ref[0, h : h + 1, :], -NEG_FILL), valid, put,
    )


def cross_specs(row_len, mem_len):
    seg = [
        pl.BlockSpec((1, 1, row_len), lambda r, p, *_: (r, 0, 0)),
        pl.BlockSpec((1, row_len, 1), lambda r, p, *_: (r, 0, 0)),
    ]
    row = pl.BlockSpec((row_len, D), lambda r, p, *_: (r, 0))
    mem = pl.BlockSpec((1, mem_len, D), lambda r, p, mp, ln: (mp[r * 2 + p], 0, 0))
    lse = pl.BlockSpec((1, PAIRS, 2 * row_len), lambda r, p, *_: (r, 0, 0))
    return seg, row, mem, lse


def cross_forward(local_map, lengths, seg, queries, keys, values):
    rows, row_len = seg.shape
    mem_len = keys.shape[1]
    seg_specs, row, mem, lse = cross_specs(row_len, mem_len)
    return pl.pallas_call(
        cross_fwd_kernel,
        grid_spec=pltpu.PrefetchScalarGridSpec(
            num_scalar_prefetch=2,
            grid=(rows, 2),
            in_specs=seg_specs + [row, mem, mem],
            out_specs=[row, lse],
        ),
        out_shape=[
            jax.ShapeDtypeStruct(queries.shape, BF16),
            jax.ShapeDtypeStruct((rows, PAIRS, 2 * row_len), F32),
        ],
        compiler_params=FULL_VMEM,
        cost_estimate=CHEAP,
        name="cross_forward",
    )(local_map, lengths, seg[:, None, :], seg[:, :, None], queries, keys, values)


def cross_backward(local_map, lengths, seg, queries, keys, values, grad_mixed, lse_rows):
    rows, row_len = seg.shape
    mem_len = keys.shape[1]
    seg_specs, row, mem, lse = cross_specs(row_len, mem_len)
    return pl.pallas_call(
        cross_bwd_kernel,
        grid_spec=pltpu.PrefetchScalarGridSpec(
            num_scalar_prefetch=2,
            grid=(rows, 2),
            in_specs=seg_specs + [row, mem, mem, row, lse],
            out_specs=[row, mem, mem, pl.BlockSpec((1, D), lambda r, p, *_: (0, 0))],
        ),
        out_shape=[
            jax.ShapeDtypeStruct(queries.shape, BF16),
            jax.ShapeDtypeStruct(keys.shape, BF16),
            jax.ShapeDtypeStruct(values.shape, BF16),
            jax.ShapeDtypeStruct((1, D), F32),
        ],
        compiler_params=FULL_VMEM,
        cost_estimate=CHEAP,
        name="cross_backward",
    )(local_map, lengths, seg[:, None, :], seg[:, :, None], queries, keys, values, grad_mixed, lse_rows)


SMALL_ROWS = 16


def tie(values, *after):
    return lax.optimization_barrier((values, after))[0]


class Clock:
    def __init__(self):
        self.last = ()

    def now(self, values):
        return tie(values, *self.last) if self.last else values

    def tick(self, *arrays):
        self.last = arrays


class Grid:
    def __init__(self, wide, narrow):
        self.wide, self.narrow, self.ring = wide, narrow, wide // 2
        self.devices = wide * narrow
        moves = {
            "z": lambda w, n: ((w + 2) % wide, n),
            "x": lambda w, n: (w ^ 1, n),
            "y": lambda w, n: (w, n ^ 2),
            "c": lambda w, n: (w, n ^ 1),
        }
        self.perms = {}
        for name, move in moves.items():
            pairs = []
            for w in range(wide):
                for n in range(narrow):
                    w2, n2 = move(w, n)
                    pairs.append((w * narrow + n, w2 * narrow + n2))
            self.perms[name] = pairs
        self.clock = Clock()

    def send(self, name, array):
        return lax.ppermute(self.clock.now(array), AXES, self.perms[name])


def segments(first, height, g, rows):
    out, at, end = [], first, first + height
    while at < end:
        k = min(at // rows, g)
        stop = min(end, (k + 1) * rows) if k < g else end
        out.append((k, at - k * rows, at - first, stop - at))
        at = stop
    return out


def half_kernel(parts, ring, wide, g, rows, place, *refs):
    *arrays, out = refs
    z, x, y = place[0], place[1], place[2]
    height = wide * rows
    for which, first_row, count, offset, labels in parts:
        for i, (dz, dx, dy) in enumerate(labels):
            row = 2 * lax.rem(z + (ring - dz), ring) + (x + dx - 2 * x * dx)
            col = y + dy - 2 * y * dy
            for k, matrix_row, at, n in segments(offset, count, g, rows):
                each = rows if k < g else SMALL_ROWS
                first = pl.multiple_of(k * height + row * each + matrix_row, 16)
                out[col, pl.ds(first, n)] = arrays[which][i, pl.ds(first_row + at, n)]


def anywhere(count):
    return [pl.BlockSpec(memory_space=pl.ANY)] * count


PLACE = pl.BlockSpec(memory_space=pltpu.SMEM)


def rearrange_kernel(moves, n_in, *refs):
    ins, outs = refs[:n_in], refs[n_in:]
    for i, bi, ri, ci, rows, o, bo, ro in moves:
        cols = outs[o].shape[-1]
        outs[o][bo, pl.ds(ro, rows)] = ins[i][bi, pl.ds(ri, rows), pl.ds(ci, cols)]


class Rearrange:
    def __init__(self):
        self.ins, self.shapes, self.moves = [], [], []

    def source(self, array):
        for i, known in enumerate(self.ins):
            if known is array:
                return i
        self.ins.append(array)
        return len(self.ins) - 1

    def out(self, blocks, rows, cols):
        self.shapes.append((blocks, rows, cols))
        return len(self.shapes) - 1

    def move(self, out, block, row, array, from_block, first, rows, column=0):
        self.moves.append((self.source(array), from_block, first, column, rows, out, block, row))

    def run(self, clock):
        outs = pl.pallas_call(
            functools.partial(rearrange_kernel, self.moves, len(self.ins)),
            in_specs=[pl.BlockSpec(memory_space=pltpu.VMEM)] * len(self.ins),
            out_specs=[pl.BlockSpec(memory_space=pltpu.VMEM)] * len(self.shapes),
            out_shape=[jax.ShapeDtypeStruct(shape, BF16) for shape in self.shapes],
            compiler_params=SMALL_VMEM,
            cost_estimate=CHEAP,
            name="rearrange",
        )(*clock.now(self.ins))
        return list(outs)


class Gather:
    def __init__(self, grid, place, g, height, cols, small=False):
        self.grid, self.place, self.g, self.height, self.cols = grid, place, g, height, cols
        self.rows = (height - (SMALL_ROWS if small else 0)) // g
        self.parts = []

    def put(self, labels, array, first_row, count, offset):
        self.parts.append((labels, array, first_row, count, offset))

    def half(self, *after):
        grid, arrays, parts = self.grid, [], []
        for labels, array, first_row, count, offset in self.parts:
            which = [i for i, known in enumerate(arrays) if known is array]
            if not which:
                arrays.append(array)
                which = [len(arrays) - 1]
            parts.append((which[0], first_row, count, offset, labels))
        self.own = pl.pallas_call(
            functools.partial(half_kernel, parts, grid.ring, grid.wide, self.g, self.rows),
            in_specs=[PLACE] + [pl.BlockSpec(memory_space=pltpu.VMEM)] * len(arrays),
            out_specs=pl.BlockSpec(memory_space=pltpu.VMEM),
            out_shape=jax.ShapeDtypeStruct((2, grid.wide * self.height, self.cols), BF16),
            compiler_params=SMALL_VMEM,
            cost_estimate=CHEAP,
            name="half_weights",
        )(self.place, *tie(grid.clock.now(arrays), *after))
        return self.own

    def swap(self):
        self.other = self.grid.send("c", self.own)
        return self.other

    def small_rows(self):
        first = self.g * self.grid.wide * self.rows
        own, other = self.grid.clock.now((self.own[:, first:], self.other[:, first:]))
        flip = self.place[3] == 0
        both = jnp.stack((jnp.where(flip, own, other), jnp.where(flip, other, own)))
        return both.reshape(2, 2, self.grid.wide, SMALL_ROWS, -1).astype(F32)


class Square:
    def __init__(self, gather, blocks, height, offset=0):
        self.gather, self.blocks, self.height, self.offset = gather, blocks, height, offset
        self.cut = height // 32 * 16

    def labels(self, dx, dy):
        return [(dz, dx, dy) for dz in range(len(self.blocks))]


def exchange(grid, before, after):
    make = Rearrange()
    cols = (before or after).gather.cols
    depth = len((before or after).blocks)
    heights = [0, 0]
    if before:
        heights = [before.cut, before.height - before.cut]
    total = [h + (after.height if after else 0) for h in heights]
    outs = [make.out(depth, h, cols) for h in total]
    if before:
        (near_x, x_first), (near_y, y_first) = before.near
        for k in range(depth):
            make.move(outs[0], k, 0, near_y, k, y_first, heights[0])
            make.move(outs[1], k, 0, near_x, k, x_first + before.cut, heights[1])
    if after:
        for out, first in zip(outs, heights):
            for k, pieces in enumerate(after.blocks):
                at = first
                for array, block, row, count, column in pieces:
                    make.move(out, k, at, array, block, row, count, column)
                    at += count
    send_x, send_y = make.run(grid.clock)
    from_x, from_y = grid.send("x", send_x), grid.send("y", send_y)
    if before:
        before.gather.put(before.labels(1, 1), from_x, 0, heights[0], before.offset)
        before.gather.put(before.labels(1, 1), from_y, 0, heights[1], before.offset + before.cut)
    if after:
        after.near = ((from_x, heights[0]), (from_y, heights[1]))
        put = after.gather.put
        put(after.labels(0, 0), send_x, heights[0], after.height, after.offset)
        put(after.labels(1, 0), from_x, heights[0], after.height, after.offset)
        put(after.labels(0, 1), from_y, heights[1], after.height, after.offset)
    return from_x, from_y


def unfold(small, count, start, width):
    part = small[:, :, :, :count, start : start + width]
    return part.transpose(3, 2, 1, 0, 4).reshape(count, -1)


def corners(place):
    y, c = place[2], place[3]
    return (2 * y + 1 - c, 2 * (1 - y) + 1 - c), (2 * y + c, 2 * (1 - y) + c)


def column(ref, n, cols):
    return ref[:, pl.ds(pl.multiple_of(n * cols, 128), cols)]


def both_columns(ref, blocks, cols):
    return jnp.concatenate([column(ref, n, cols) for n in blocks], axis=1)


def far_kernel(place, *refs):
    out = refs[-1]
    cols = out.shape[-1]
    for i in range(out.shape[0]):
        a, d = refs[2 * i], refs[2 * i + 1]
        term = dot_tn(a[...], both_columns(d, corners(place)[0], cols))
        for j in range(2):
            out[i, j] = term[:, j * cols : (j + 1) * cols].astype(BF16)


def put_quadrants(x, scratch, k, i, here, outs):
    dx, dy, qx, qy, own = outs
    rows = own.shape[2]
    if here:
        own[k, i] = scratch[k, x]
        qx[k, i] = scratch[k, 1 - x].astype(BF16)
    else:
        qy[k, i] = scratch[k, x].astype(BF16)
        dx[k, i] = scratch[k, 1 - x, pl.ds(0, rows // 2)].astype(BF16)
        dy[k, i] = scratch[k, 1 - x, pl.ds(rows // 2, rows // 2)].astype(BF16)


def near_kernel(place, *refs):
    from_c, *outs, scratch = refs[-7:]
    zs, units, rows, cols = outs[-1].shape
    for i in range(units):
        a, d = refs[2 * i], refs[2 * i + 1]
        term = dot_tn(a[...], both_columns(d, corners(place)[1], cols))
        for j in range(2):
            part = term[:, j * cols : (j + 1) * cols] + from_c[i, j].astype(F32)
            scratch[...] = part.reshape(scratch.shape)
            for k in range(zs):
                put_quadrants(place[1], scratch, k, i, j == 0, outs)


def quadrant_shapes(units, ring, rows, cols):
    half, full = (ring, units, rows // 2, cols), (ring, units, rows, cols)
    return [jax.ShapeDtypeStruct(half, BF16)] * 2 + [
        jax.ShapeDtypeStruct(full, BF16), jax.ShapeDtypeStruct(full, BF16), jax.ShapeDtypeStruct(full, F32)
    ]


def quadrant_specs(units, zs, rows, cols, stepped):
    def at(s, *_):
        return (s if stepped else 0, 0, 0, 0)

    half = pl.BlockSpec((zs, units, rows // 2, cols), at)
    full = pl.BlockSpec((zs, units, rows, cols), at)
    return [half] * 2 + [full] * 3


def token_terms(grid, place, pairs, rows, cols, from_c=None, params=FULL_VMEM):
    units, tokens = len(pairs), pairs[0][0].shape[0]
    height = grid.wide * rows
    zs = max(1, 128 // (2 * rows))
    if 2 * rows >= 128 and height // (2 * rows) > 1 and rows * cols <= 128 * 256:
        zs = min(grid.ring, 2)
    tall = zs * 2 * rows
    in_specs, args = [], []
    for a, d in pairs:
        in_specs += [
            pl.BlockSpec((tokens, tall), lambda s, *_: (0, s)),
            pl.BlockSpec(d.shape, lambda s, *_: (0, 0)),
        ]
        args += [a, d]
    block = pl.BlockSpec((units, 2, tall, cols), lambda s, *_: (0, 0, s, 0))
    scratch = []
    if from_c is None:
        kernel, out_specs = far_kernel, block
        out_shape = jax.ShapeDtypeStruct((units, 2, height, cols), BF16)
    else:
        in_specs.append(block)
        args.append(from_c)
        kernel = near_kernel
        out_specs = quadrant_specs(units, zs, rows, cols, True)
        out_shape = quadrant_shapes(units, grid.ring, rows, cols)
        scratch = [pltpu.VMEM((zs, 2, rows, cols), F32)]
    return pl.pallas_call(
        kernel,
        grid_spec=pltpu.PrefetchScalarGridSpec(
            num_scalar_prefetch=1,
            grid=(height // tall,),
            in_specs=in_specs,
            out_specs=out_specs,
            scratch_shapes=scratch,
        ),
        out_shape=out_shape,
        compiler_params=params,
        cost_estimate=CHEAP,
        name="weight_terms",
    )(place, *args)


def memory_terms_kernel(near, pairs, place, mem, dk, dv, *refs):
    tokens, refs = refs[: 2 * pairs], refs[2 * pairs :]
    if near:
        from_c, dx, dy, qx, qy, own, acc = refs
    else:
        out, acc = refs
    cols = acc.shape[-1]
    m = pl.program_id(0)
    blocks = corners(place)[1 if near else 0]

    @pl.when(m == 0)
    def _():
        for i in range(pairs):
            term = dot_tn(tokens[2 * i][...], both_columns(tokens[2 * i + 1], blocks, cols))
            for j in range(2):
                acc[i, j] = term[:, j * cols : (j + 1) * cols].reshape(acc.shape[2:])
        acc[pairs:] = jnp.zeros_like(acc[pairs:])
        if near:
            acc[...] += from_c[...].astype(F32).reshape(acc.shape)

    grads = jnp.concatenate([both_columns(d.at[0], blocks, cols) for d in (dk, dv)], axis=1)
    term = dot_tn(mem[0], grads)
    for q in range(4):
        part = term[:, q * cols : (q + 1) * cols].reshape(acc.shape[2:])
        acc[pairs + q // 2, q % 2] += part

    @pl.when(m == pl.num_programs(0) - 1)
    def _():
        if near:
            x = place[1]
            for i in range(pairs + 2):
                for j in range(2):
                    for k in range(own.shape[0]):
                        put_quadrants(x, acc.at[i, j], k, i, j == 0, (dx, dy, qx, qy, own))
        else:
            out[...] = acc[...].reshape(out.shape).astype(BF16)


def memory_terms(grid, place, memory, grads, pairs, rows, cols, from_c=None):
    units, (mems, length, wide_cols) = len(pairs) + 2, memory.shape
    height = grid.wide * rows
    near = from_c is not None
    one = pl.BlockSpec((1, length, wide_cols), lambda m, *_: (m, 0, 0))
    term = pl.BlockSpec((units, 2, height, cols), lambda m, *_: (0, 0, 0, 0))
    tokens = [array for pair in pairs for array in pair]
    return pl.pallas_call(
        functools.partial(memory_terms_kernel, near, len(pairs)),
        grid_spec=pltpu.PrefetchScalarGridSpec(
            num_scalar_prefetch=1,
            grid=(mems,),
            in_specs=[one] * 3
            + [pl.BlockSpec(a.shape, lambda m, *_: (0, 0)) for a in tokens]
            + ([term] if near else []),
            out_specs=quadrant_specs(units, grid.ring, rows, cols, False) if near else term,
            scratch_shapes=[pltpu.VMEM((units, 2, grid.ring, 2, rows, cols), F32)],
        ),
        out_shape=quadrant_shapes(units, grid.ring, rows, cols)
        if near
        else jax.ShapeDtypeStruct((units, 2, height, cols), BF16),
        compiler_params=FULL_VMEM,
        cost_estimate=CHEAP,
        name="memory_terms",
    )(place, memory, *grads, *tokens, *([from_c] if near else []))


def add_corners_kernel(qx, qy, from_x, from_y, sx, sy):
    half = from_x.shape[2]
    first, second = pl.ds(0, half), pl.ds(half, half)
    sx[0, :, first] = qx[0, :, first]
    sx[0, :, second] = (qx[0, :, second].astype(F32) + from_y[0].astype(F32)).astype(BF16)
    sy[0, :, first] = (qy[0, :, first].astype(F32) + from_x[0].astype(F32)).astype(BF16)
    sy[0, :, second] = qy[0, :, second]


def add_corners(qx, qy, from_x, from_y):
    ring, units, rows, cols = qx.shape
    full = pl.BlockSpec((1, units, rows, cols), lambda k: (k, 0, 0, 0))
    half = pl.BlockSpec((1, units, rows // 2, cols), lambda k: (k, 0, 0, 0))
    return pl.pallas_call(
        add_corners_kernel,
        grid=(ring,),
        in_specs=[full, full, half, half],
        out_specs=[full, full],
        out_shape=[jax.ShapeDtypeStruct(qx.shape, BF16)] * 2,
        compiler_params=FULL_VMEM,
        cost_estimate=CHEAP,
        name="add_corners",
    )(qx, qy, from_x, from_y)


class Reduce:
    def __init__(self, grid, place, terms, rows):
        self.grid, self.place, self.terms, self.rows = grid, place, terms, rows

    def far(self):
        self.out = self.terms(None)
        return self.out

    def swap(self):
        self.from_c = self.grid.send("c", self.out)
        return self.from_c

    def near(self):
        self.dx, self.dy, self.qx, self.qy, self.own = self.terms(self.grid.clock.now(self.from_c))
        return self.dx

    def across(self):
        self.from_x, self.from_y = self.grid.send("x", self.dx), self.grid.send("y", self.dy)
        return self.from_x, self.from_y

    def add(self):
        from_x = self.grid.clock.now(self.from_x)
        self.sx, self.sy = add_corners(self.qx, self.qy, from_x, self.from_y)
        return self.sx

    def pairs(self):
        self.back_x, self.back_y = self.grid.send("x", self.sx), self.grid.send("y", self.sy)
        return self.back_x, self.back_y

    def chunk(self, step):
        index = lax.rem(self.place[0] + (self.grid.ring - step), self.grid.ring)
        parts = [
            lax.dynamic_index_in_dim(a, index, 0, keepdims=False)
            for a in self.grid.clock.now((self.own, self.back_x, self.back_y))
        ]
        return parts[0] + parts[1].astype(F32) + parts[2].astype(F32)


class RingSum:
    def __init__(self, grid, reduces):
        self.grid, self.reduces, self.done, self.came = grid, reduces, 0, None

    def step(self, *after):
        self.done += 1
        total = jnp.concatenate([r.chunk(self.done % self.grid.ring) for r in self.reduces], axis=0)
        if self.came is not None:
            total = total + tie(self.grid.clock.now(self.came), *after).astype(F32)
        if self.done == self.grid.ring:
            self.came = total
        else:
            self.came = self.grid.send("z", total.astype(BF16))
        return self.came


class SmallSum:
    def __init__(self, grid, place, terms):
        self.grid, self.place, self.done, self.came = grid, place, 0, None
        self.mine = terms.reshape(grid.ring, 2, 2, 2, -1)
        self.steps = grid.ring + 2

    def pair(self, name, axis, at):
        far = lax.dynamic_index_in_dim(self.mine, 1 - at, axis, keepdims=False)
        self.came = self.grid.send(name, far)
        self.near = lax.dynamic_index_in_dim(self.mine, at, axis, keepdims=False)

    def settle(self, *after):
        if self.came is not None:
            came = tie(self.came, *after) if after else self.came
            self.mine = self.near + came

    def step(self, *after):
        grid, place = self.grid, self.place
        if self.done == 0:
            self.pair("c", 3, place[3])
        elif self.done < grid.ring:
            if self.done == 1:
                self.settle(*after)
            index = lax.rem(place[0] + (grid.ring - self.done), grid.ring)
            total = lax.dynamic_index_in_dim(self.mine, index, 0, keepdims=False)
            if self.done > 1:
                total = total + (tie(self.came, *after) if after else self.came)
            self.came = grid.send("z", total)
            self.near = lax.dynamic_index_in_dim(self.mine, place[0], 0, keepdims=False)
        else:
            self.settle(*after)
            if self.done == grid.ring:
                self.pair("y", 1, place[2])
            else:
                self.pair("x", 0, place[1])
        self.done += 1
        return self.came

    def result(self):
        return self.near + self.came


def halves(place, own, other):
    c = place[3]
    return [(2 * y + core, y, half) for half, core in ((own, c), (other, 1 - c)) for y in range(2)]


def at_block(n, cols):
    return pl.ds(pl.multiple_of(n * cols, 128), cols)


def times_t(place, d, own, other):
    cols = own.shape[-1]
    return sum(dot_nt(d[:, at_block(n, cols)], half[y]) for n, y, half in halves(place, own, other))


def norm_parts(values):
    centre = values - jnp.mean(values, axis=-1, keepdims=True)
    scale = lax.rsqrt(jnp.mean(centre * centre, axis=-1, keepdims=True) + EPSILON)
    return centre * scale, scale


def norm_back(normed, scale, gain, grad):
    inner = grad * gain
    back = scale * (
        inner
        - jnp.mean(inner, axis=-1, keepdims=True)
        - normed * jnp.mean(inner * normed, axis=-1, keepdims=True)
    )
    return back, jnp.sum(grad * normed, axis=0, keepdims=True), jnp.sum(grad, axis=0, keepdims=True)


def column_sum(values):
    return jnp.sum(values.astype(F32), axis=0, keepdims=True)


GAIN, BIAS = 0, 3


def row(vectors, i):
    return vectors[i : i + 1, :]


def memory_kernel(place, mem, vectors, k_own, k_other, v_own, v_other, keys, values):
    cols = k_own.shape[-1]
    for n, y, half in halves(place, k_own, k_other):
        keys[0, :, at_block(n, cols)] = dot_nn(mem[0], half[y]).astype(BF16)
    for n, y, half in halves(place, v_own, v_other):
        bias = vectors[BIAS + 6 : BIAS + 7, at_block(n, cols)]
        values[0, :, at_block(n, cols)] = (dot_nn(mem[0], half[y]) + bias).astype(BF16)


def qkv_kernel(place, tokens, vectors, *refs):
    weights, (normed, q, k, v) = refs[:6], refs[6:]
    n, _ = norm_parts(tokens[...].astype(F32))
    normed[...] = (n * row(vectors, GAIN) + row(vectors, BIAS)).astype(BF16)
    cols = weights[0].shape[-1]
    for i, (out, bias_at) in enumerate(((q, 1), (k, None), (v, 2))):
        for n, y, half in halves(place, weights[2 * i], weights[2 * i + 1]):
            term = dot_nn(normed[...], half[y])
            if bias_at is not None:
                term = term + vectors[BIAS + bias_at : BIAS + bias_at + 1, at_block(n, cols)]
            out[:, at_block(n, cols)] = term.astype(BF16)


def middle_kernel(place, tokens, mixed, vectors, so_own, so_other, cq_own, cq_other, after, normed, queries):
    cols = so_own.shape[-1]
    for n, y, half in halves(place, so_own, so_other):
        at = at_block(n, cols)
        after[:, at] = tokens[:, at].astype(F32) + dot_nn(mixed[...], half[y]) + vectors[BIAS + 3 : BIAS + 4, at]
    n, _ = norm_parts(after[...])
    normed[...] = (n * row(vectors, GAIN + 1) + row(vectors, BIAS + 4)).astype(BF16)
    for n, y, half in halves(place, cq_own, cq_other):
        at = at_block(n, cols)
        queries[:, at] = (dot_nn(normed[...], half[y]) + vectors[BIAS + 5 : BIAS + 6, at]).astype(BF16)


def cross_out_kernel(place, before, mixed, vectors, own, other, after, normed):
    cols = own.shape[-1]
    for n, y, half in halves(place, own, other):
        at = at_block(n, cols)
        after[:, at] = before[:, at] + dot_nn(mixed[...], half[y]) + vectors[BIAS + 7 : BIAS + 8, at]
    n, _ = norm_parts(after[...])
    normed[...] = (n * row(vectors, GAIN + 2) + row(vectors, BIAS + 8)).astype(BF16)


def up_kernel(place, normed, bias, own, other, act, slope):
    c, cols = place[3], own.shape[-1]
    y = pl.program_id(0)
    for n, half in ((2 * y + c, own), (2 * y + 1 - c, other)):
        for j in range(4):
            at = at_block(4 * n + j, cols)
            u = dot_nn(normed[...], half[0, j * D : (j + 1) * D]) + bias[:, at]
            below = 0.5 * (1.0 + lax.erf(u * (1.0 / math.sqrt(2.0))))
            act[:, at] = (u * below).astype(BF16)
            slope[:, at] = (below + u * jnp.exp(-0.5 * u * u) * (1.0 / math.sqrt(2.0 * math.pi))).astype(BF16)


def down_kernel(place, after, act, vectors, own, other, out):
    c, y = place[3], pl.program_id(0)
    cols = own.shape[-1]
    for n, half in ((2 * y + c, own), (2 * y + 1 - c, other)):
        at = at_block(n, cols)
        total = after[:, at] + dot_nn(act[...], half[0]) + vectors[BIAS + 9 : BIAS + 10, at]
        out[:, at] = total.astype(BF16)


def down_back_kernel(place, grad, slope, normed, own, other, grad_pre, bias_grad, far):
    back = (times_t(place, grad, own, other) * slope[...].astype(F32)).astype(BF16)
    grad_pre[...] = back
    bias_grad[...] = column_sum(back)
    for i, n in enumerate(corners(place)[0]):

        @pl.when(pl.program_id(0) == n)
        def _():
            far[0, i] = dot_tn(normed[...], back).astype(BF16)


def up_back_kernel(
    place, grad_pre, grad_out, after, vectors, own, other, co_own, co_other,
    grad, branch, mixed, gain_grad, shift_grad, out_grad, last_grad, total,
):
    c, y = place[3], pl.program_id(0)
    cols = own.shape[-1]
    term = sum(
        dot_nt(grad_pre[:, at_block(4 * n + j, cols)], half[0, j * D : (j + 1) * D])
        for n, half in ((2 * y + c, own), (2 * y + 1 - c, other))
        for j in range(4)
    )

    @pl.when(y == 0)
    def _():
        total[...] = term

    @pl.when(y == 1)
    def _():
        n, scale = norm_parts(after[...])
        back, gain_grad[...], shift_grad[...] = norm_back(n, scale, row(vectors, GAIN + 2), total[...] + term)
        out = grad_out[...].astype(F32) + back
        grad[...] = out
        branch[...] = out.astype(BF16)
        out_grad[...] = column_sum(branch[...])
        last_grad[...] = column_sum(grad_out[...])
        mixed[...] = times_t(place, branch, co_own, co_other).astype(BF16)


def middle_back_kernel(
    place, grad_queries, grad_after, after, vectors, cq_own, cq_other, so_own, so_other,
    grad, branch, mixed, gain_grad, shift_grad, out_grad, query_grad,
):
    n, scale = norm_parts(after[...])
    dense = times_t(place, grad_queries, cq_own, cq_other)
    back, gain_grad[...], shift_grad[...] = norm_back(n, scale, row(vectors, GAIN + 1), dense)
    out = grad_after[...] + back
    grad[...] = out
    branch[...] = out.astype(BF16)
    out_grad[...] = column_sum(branch[...])
    query_grad[...] = column_sum(grad_queries[...])
    mixed[...] = times_t(place, branch, so_own, so_other).astype(BF16)


def first_back_kernel(place, tokens, grad_after, gq, gk, gv, vectors, *refs):
    weights, (grad, gain_grad, shift_grad, query_grad, value_grad) = refs[:6], refs[6:]
    n, scale = norm_parts(tokens[...].astype(F32))
    dense = sum(
        times_t(place, d, weights[2 * i], weights[2 * i + 1]) for i, d in enumerate((gq, gk, gv))
    )
    back, gain_grad[...], shift_grad[...] = norm_back(n, scale, row(vectors, GAIN), dense)
    grad[...] = (grad_after[...] + back).astype(BF16)
    query_grad[...] = column_sum(gq[...])
    value_grad[...] = column_sum(gv[...])


def memory_back_kernel(place, gk, gv, k_own, k_other, v_own, v_other, grad):
    total = times_t(place, gk.at[0], k_own, k_other) + times_t(place, gv.at[0], v_own, v_other)
    grad[0] = total.astype(BF16)


def in_place(array):
    return pl.pallas_call(
        lambda _, out: None,
        in_specs=anywhere(1),
        out_specs=pl.BlockSpec(memory_space=pl.ANY),
        out_shape=jax.ShapeDtypeStruct(array.shape, array.dtype),
        input_output_aliases={0: 0},
        compiler_params=BIG_VMEM,
        cost_estimate=CHEAP,
        name="in_place",
    )(array)


def dense_call(kernel, name, place, ins, outs, grid=(1,), scratch=(), params=BIG_VMEM):
    def spec(array, block, index):
        block = block or array.shape
        zeros = (0,) * len(block)
        return pl.BlockSpec(block, index or (lambda *_: zeros))

    return pl.pallas_call(
        kernel,
        grid_spec=pltpu.PrefetchScalarGridSpec(
            num_scalar_prefetch=1,
            grid=grid,
            in_specs=[spec(*one) for one in ins],
            out_specs=[spec(*one) for one in outs],
            scratch_shapes=scratch,
        ),
        out_shape=[one[0] for one in outs],
        compiler_params=params,
        cost_estimate=CHEAP,
        name=name,
    )(place, *[one[0] for one in ins])


def full(array):
    return (array, None, None)


def result(shape, dtype):
    return (jax.ShapeDtypeStruct(shape, dtype), None, None)


def matrix(gathered, i, height=D):
    block = (2, height, gathered.own.shape[-1])
    return [(half, block, lambda *_: (0, i, 0)) for half in (gathered.own, gathered.other)]


def by_y(gathered):
    block = (1,) + gathered.own.shape[1:]
    return [(half, block, lambda y, *_: (y, 0, 0)) for half in (gathered.own, gathered.other)]


def by_rows(gathered, rows):
    block = (2, rows, gathered.own.shape[-1])
    return [(half, block, lambda s, *_: (0, s, 0)) for half in (gathered.own, gathered.other)]


def local(
    shape,
    tokens,
    memory,
    segment_ids,
    page_map,
    mem_lengths,
    gains,
    biases,
    fc1_bias,
    self_qkv,
    self_out,
    cross_q,
    cross_kv,
    cross_out,
    fc1,
    fc2,
    cotangent,
):
    grid = Grid(*shape)
    wide_at, narrow_at = lax.axis_index("wide"), lax.axis_index("narrow")
    place = jnp.stack((wide_at // 2, wide_at % 2, narrow_at // 2, narrow_at % 2)).astype(jnp.int32)
    devices = grid.devices
    mem_count, token_count = memory.shape[0], tokens.shape[0]
    rows, cols = self_out.shape

    each, up_each = gains.shape[1], fc1_bias.size
    n_gain, n_bias = gains.size, biases.size
    small = jnp.pad(
        jnp.concatenate((gains, biases), axis=0), ((0, SMALL_ROWS - 13), (0, cols - each))
    )
    small = lax.dynamic_update_slice(small, fc1_bias[None], (0, 128))
    send, clock = grid.send, grid.clock
    now, tick = clock.now, clock.tick
    steps = grid.ring - 1
    gather = functools.partial(Gather, grid, place)
    ckv_height = 2 * rows + SMALL_ROWS
    fc2_rows = fc2.shape[0]
    part = fc2_rows // 2
    g_ckv = gather(2, ckv_height, cols, True)
    g_qkv = gather(3, 3 * rows, cols)
    g_mix = gather(3, 3 * rows, cols)
    g_fc1 = gather(4, 4 * rows, cols)
    g_fc2 = gather(1, fc2_rows, cols)

    start = Rearrange()
    out = start.out(1, 5 * rows, cols)
    for k, (array, i) in enumerate(((cross_kv, 0), (cross_kv, 1), (self_qkv, 0), (self_qkv, 1), (self_qkv, 2))):
        start.move(out, 0, k * rows, array, i, 0, rows)
    ring_one = start.run(clock)
    ring_one.append(send("z", ring_one[-1]))
    ring_small = [small[None]]
    ring_small.append(send("z", ring_small[-1]))
    top = Square(g_fc2, [[(fc2[None], 0, 0, part, 0)]], part)
    more = Rearrange()
    out = more.out(1, 3 * rows, cols)
    for k, array in enumerate((self_out, cross_q, cross_out)):
        more.move(out, 0, k * rows, array[None], 0, 0, rows)
    out = more.out(1, 4 * rows + part, cols)
    for k in range(4):
        more.move(out, 0, k * rows, fc1[None], 0, 0, rows, k * cols)
    more.move(out, 0, 4 * rows, fc2[None], 0, part, part)
    ring_mix, ring_up = [[array] for array in more.run(clock)]
    came = exchange(grid, None, top)
    tick(ring_one[-1], ring_small[-1], ring_mix[0], ring_up[0])
    ring_one.append(send("z", ring_one[-1]))
    ring_small.append(send("z", ring_small[-1]))
    memory = in_place(now(memory))
    tick(ring_one[-1], ring_small[-1], memory, *came)
    came = exchange(grid, top, None)
    for _ in range(steps - 2):
        ring_one.append(send("z", ring_one[-1]))
        ring_small.append(send("z", ring_small[-1]))
        tick(ring_one[-1], ring_small[-1], *came)

    def from_ring(arrays, first, count):
        return [[(array, 0, first, count, 0)] for array in arrays]

    ckv = Square(
        g_ckv, [a + b for a, b in zip(from_ring(ring_one, 0, 2 * rows), from_ring(ring_small, 0, SMALL_ROWS))],
        ckv_height,
    )
    qkv = Square(g_qkv, from_ring(ring_one, 2 * rows, 3 * rows), 3 * rows)
    ring_mix.append(send("z", ring_mix[-1]))
    ring_up.append(send("z", ring_up[-1]))
    tick(ring_mix[-1], ring_up[-1], *exchange(grid, None, ckv))

    make = Rearrange()
    out = make.out(4, part, cols)
    (_, own, own_at, _, _), (_, by_x, x_at, _, _), (_, by_y_, y_at, _, _), (_, low, _, _, _), (_, high, _, _, _) = g_fc2.parts
    g_fc2.parts = []
    for k, (array, at) in enumerate(((own, own_at), (by_x, x_at), (by_y_, y_at))):
        make.move(out, k, 0, array, 0, at, part)
    make.move(out, 3, 0, low, 0, 0, top.cut)
    make.move(out, 3, top.cut, high, 0, 0, part - top.cut)
    came = exchange(grid, ckv, qkv)
    ring_top = make.run(clock)
    ring_up.append(send("z", ring_up[-1]))
    for _ in range(steps - 1):
        ring_mix.append(send("z", ring_mix[-1]))
    tick(ring_mix[-1], ring_up[-1], ring_top[-1], *came)

    mix = Square(g_mix, from_ring(ring_mix, 0, 3 * rows), 3 * rows)
    came = exchange(grid, qkv, mix)
    for _ in range(steps - 2):
        ring_up.append(send("z", ring_up[-1]))
    ring_top.append(send("z", ring_top[-1]))
    g_ckv.half(g_mix.parts[0][1])
    g_ckv.swap()
    small_all = g_ckv.small_rows()
    vectors = unfold(small_all, 13, 0, each)
    up_bias = unfold(small_all, 1, 128, up_each)
    mem_block = (1,) + memory.shape[1:]
    mem_shape = jax.ShapeDtypeStruct(memory.shape, BF16)

    def by_memory(array):
        return (array, mem_block, lambda m, *_: (m, 0, 0))

    mem_keys, mem_values = dense_call(
        memory_kernel, "memory_keys_values", place,
        [by_memory(now(memory)), full(vectors)] + matrix(g_ckv, 0) + matrix(g_ckv, 1),
        [by_memory(mem_shape), by_memory(mem_shape)], grid=(mem_count,),
    )
    tick(ring_up[-1], ring_top[-1], mem_keys, *came)

    up = Square(g_fc1, from_ring(ring_up, 0, 4 * rows), 4 * rows)
    low = Square(g_fc2, from_ring(ring_up, 4 * rows, part), part, part)
    came = exchange(grid, mix, up)
    ring_top.append(send("z", ring_top[-1]))
    g_qkv.half(g_fc1.parts[0][1])
    g_qkv.swap()
    wide_row = (token_count, D)
    normed_one, self_queries, self_keys, self_values = dense_call(
        qkv_kernel, "self_qkv", place,
        [full(now(tokens)), full(vectors)] + matrix(g_qkv, 0) + matrix(g_qkv, 1) + matrix(g_qkv, 2),
        [result(wide_row, BF16)] * 4,
    )
    self_mixed, self_lse = self_forward(segment_ids, self_queries, self_keys, self_values)
    tick(self_mixed, ring_top[-1], *came)

    came = exchange(grid, up, low)
    g_mix.half(g_fc2.parts[0][1])
    g_mix.swap()
    for _ in range(steps - 2):
        ring_top.append(send("z", ring_top[-1]))
    after_self, normed_two, cross_queries = dense_call(
        middle_kernel, "self_out_cross_q", place,
        [full(tokens), full(now(self_mixed)), full(vectors)] + matrix(g_mix, 0) + matrix(g_mix, 1),
        [result(wide_row, F32), result(wide_row, BF16), result(wide_row, BF16)],
    )
    first_mem = lax.axis_index(AXES) * mem_count
    local_map = (page_map - first_mem).reshape(-1).astype(jnp.int32)
    picks = local_map[:, None] == jnp.arange(mem_count, dtype=jnp.int32)[None, :]
    row_lengths = jnp.sum(jnp.where(picks, mem_lengths[None, :], 0), axis=-1).astype(jnp.int32)
    cross_mixed, cross_lse = cross_forward(
        local_map, row_lengths, segment_ids, cross_queries, mem_keys, mem_values
    )
    tick(cross_mixed, ring_top[-1], *came)

    came = exchange(grid, low, None)
    g_fc1.half()
    g_fc1.swap()
    after_cross, normed_three = dense_call(
        cross_out_kernel, "cross_out", place,
        [full(after_self), full(now(cross_mixed)), full(vectors)] + matrix(g_mix, 2),
        [result(wide_row, F32), result(wide_row, BF16)],
    )
    hidden = up_bias.shape[1]
    activated, slope = dense_call(
        up_kernel, "fc1_gelu", place,
        [full(normed_three), full(up_bias)] + by_y(g_fc1),
        [result((token_count, hidden), BF16)] * 2, grid=(2,),
    )
    tick(activated, *came)
    spread = [(0, 0), (1, 0), (0, 1), (1, 1)]
    for step, array in enumerate(ring_top):
        g_fc2.put([(step, dx, dy) for dx, dy in spread], array, 0, part, 0)

    def settle(pairs, shard, params=FULL_VMEM):
        part_rows, part_cols = shard.shape
        return Reduce(
            grid, place,
            lambda from_c: token_terms(grid, place, pairs, part_rows, part_cols, from_c, params),
            part_rows,
        )

    one_row = result((1, D), F32)
    r_fc2 = settle([(now(activated), cotangent)], fc2, BIG_VMEM)
    r_fc2.far()
    r_fc2.swap()
    g_fc2.half()
    g_fc2.swap()
    tick(r_fc2.near())
    slab = hidden // 4
    some = lambda array: (array, (token_count, slab), lambda s, *_: (0, s))
    grad_pre, grad_up_bias, far_fc1 = dense_call(
        down_back_kernel, "fc2_gelu_back", place,
        [full(now(cotangent)), some(slope), full(normed_three)] + by_rows(g_fc2, slab),
        [
            some(jax.ShapeDtypeStruct((token_count, hidden), BF16)),
            (jax.ShapeDtypeStruct((1, hidden), F32), (1, slab), lambda s, *_: (0, s)),
            result((1, 2, D, slab), BF16),
        ],
        grid=(4,), params=FULL_VMEM,
    )
    r_fc1 = settle([(normed_three, grad_pre)], fc1)
    r_fc1.out = far_fc1
    tick(far_fc1, *r_fc2.across())
    r_fc2.add()
    r_fc1.swap()
    (
        grad_after_cross, grad_branch_two, grad_cross_mixed,
        grad_gain_three, grad_bias_eight, grad_bias_seven, grad_bias_nine,
    ) = dense_call(
        up_back_kernel, "fc1_norm_back", place,
        [full(now(grad_pre)), full(cotangent), full(after_cross), full(vectors)]
        + by_y(g_fc1) + matrix(g_mix, 2),
        [result(wide_row, F32), result(wide_row, BF16), result(wide_row, BF16)] + [one_row] * 4,
        grid=(2,), scratch=[pltpu.VMEM(wide_row, F32)], params=FULL_VMEM,
    )
    tick(r_fc1.near(), r_fc2.sx, grad_cross_mixed)

    came = [*r_fc2.pairs(), *r_fc1.across()]
    grad_cq, grad_ck, grad_cv, grad_bias_six = cross_backward(
        local_map, row_lengths, segment_ids, cross_queries, mem_keys, mem_values,
        now(grad_cross_mixed), cross_lse,
    )
    r_mem = Reduce(
        grid, place,
        lambda from_c: memory_terms(grid, place, memory, (grad_ck, grad_cv), [], rows, cols, from_c),
        rows,
    )
    tick(grad_cq, r_mem.far(), *came)
    ring_fc2 = RingSum(grid, [r_fc2])
    r_fc1.add()
    r_mem.swap()
    ring_fc2.step()
    grad_cq = tie(now(grad_cq), r_fc1.sx)
    (
        grad_after_self, grad_branch_one, grad_self_mixed,
        grad_gain_two, grad_bias_four, grad_bias_three, grad_bias_five,
    ) = dense_call(
        middle_back_kernel, "cross_q_norm_back", place,
        [full(grad_cq), full(grad_after_cross), full(after_self), full(vectors)]
        + matrix(g_mix, 1) + matrix(g_mix, 0),
        [result(wide_row, F32), result(wide_row, BF16), result(wide_row, BF16)] + [one_row] * 4,
        params=FULL_VMEM,
    )
    grad_sq, grad_sk, grad_sv = self_backward(
        segment_ids, self_queries, self_keys, self_values, grad_self_mixed, self_lse
    )
    r_rest = settle(
        [
            (normed_one, grad_sq), (normed_one, grad_sk), (normed_one, grad_sv),
            (self_mixed, grad_branch_one), (normed_two, grad_cq), (cross_mixed, grad_branch_two),
        ],
        cross_q,
    )
    tick(r_rest.far(), r_mem.near(), ring_fc2.came, *r_fc1.pairs())
    ring_fc1 = RingSum(grid, [r_fc1])
    came = r_mem.across()
    r_rest.swap()
    ring_fc2.step()
    ring_fc1.step()
    grad_tokens, grad_gain_one, grad_bias_zero, grad_bias_one, grad_bias_two = dense_call(
        first_back_kernel, "self_qkv_norm_back", place,
        [full(tokens), full(grad_after_self)] + [full(d) for d in now((grad_sq, grad_sk, grad_sv))]
        + [full(vectors)] + matrix(g_qkv, 0) + matrix(g_qkv, 1) + matrix(g_qkv, 2),
        [result(wide_row, BF16)] + [one_row] * 4,
        params=FULL_VMEM,
    )
    tick(r_rest.near(), grad_tokens, ring_fc2.came, ring_fc1.came, *came)

    def by_device(array):
        return array.reshape(array.shape[0], devices, -1).transpose(1, 0, 2).reshape(devices, -1)

    small_grads = jnp.concatenate(
        (
            by_device(
                jnp.concatenate(
                    (
                        grad_gain_one, grad_gain_two, grad_gain_three,
                        grad_bias_zero, grad_bias_one, grad_bias_two, grad_bias_three, grad_bias_four,
                        grad_bias_five, grad_bias_six, grad_bias_seven, grad_bias_eight, grad_bias_nine,
                    ),
                    axis=0,
                )
            ),
            by_device(grad_up_bias),
        ),
        axis=1,
    )
    small_sum = SmallSum(grid, place, now(small_grads))
    r_mem.add()
    ring_fc2.step()
    (grad_memory,) = dense_call(
        memory_back_kernel, "memory_back", place,
        [by_memory(a) for a in tie(now((grad_ck, grad_cv)), r_mem.sx)] + matrix(g_ckv, 0) + matrix(g_ckv, 1),
        [by_memory(mem_shape)], grid=(mem_count,), params=FULL_VMEM,
    )
    (layer_out,) = dense_call(
        down_kernel, "fc2", place,
        [full(after_cross), full(tie(now(activated), r_mem.sx)), full(vectors)] + by_y(g_fc2),
        [result(wide_row, BF16)], grid=(2,), params=FULL_VMEM,
    )
    tick(grad_memory, layer_out, ring_fc2.came, *r_mem.pairs(), *r_rest.across())
    small_sum.step()
    ring_mem = RingSum(grid, [r_mem])
    r_rest.add()
    turned_memory = in_place(tie(now(grad_memory).transpose(1, 0, 2), r_rest.sx))
    grad_memory = turned_memory.transpose(1, 0, 2)
    ring_fc1.step()
    ring_mem.step()
    for _ in range(steps):
        small_sum.step()
    ring_fc1.step(turned_memory)
    tick(turned_memory, small_sum.came, ring_fc1.came, ring_mem.came, *r_rest.pairs())
    ring_fc2.step()
    ring_rest = RingSum(grid, [r_rest])
    ring_rest.step()
    ring_fc1.step()
    ring_mem.step()
    small_sum.step()
    tick(ring_rest.came, ring_mem.came, small_sum.came)
    for _ in range(steps - 1):
        ring_mem.step() if ring_mem.done < grid.ring else None
        small_sum.step() if small_sum.done < small_sum.steps else None
        tick(ring_rest.step(), ring_mem.came, small_sum.came)
    for ring in (ring_fc2, ring_fc1, ring_mem, ring_rest):
        while ring.done < grid.ring:
            ring.step()
    while small_sum.done < small_sum.steps:
        small_sum.step()
    came_mem, came_rest = ring_mem.came, ring_rest.came
    small_shard = small_sum.result()
    return (
        layer_out,
        grad_tokens,
        grad_memory,
        small_shard[:n_gain].reshape(gains.shape),
        small_shard[n_gain : n_gain + n_bias].reshape(biases.shape),
        small_shard[n_gain + n_bias :],
        came_rest[:3],
        came_rest[3],
        came_rest[4],
        came_mem,
        came_rest[5],
        ring_fc1.came[0],
        ring_fc2.came[0],
    )


def solution(mesh):
    shape = (mesh.shape["wide"], mesh.shape["narrow"])
    in_specs = (
        P(AXES, None),
        P(AXES, None, None),
        P(AXES, None),
        P(AXES, None),
        P(AXES),
        P(None, AXES),
        P(None, AXES),
        P(AXES),
        P(None, "wide", "narrow"),
        P("wide", "narrow"),
        P("wide", "narrow"),
        P(None, "wide", "narrow"),
        P("wide", "narrow"),
        P("wide", "narrow"),
        P("wide", "narrow"),
        P(AXES, None),
    )
    out_specs = (
        P(AXES, None),
        P(AXES, None),
        P(AXES, None, None),
        P(None, AXES),
        P(None, AXES),
        P(AXES),
        P(None, "wide", "narrow"),
        P("wide", "narrow"),
        P("wide", "narrow"),
        P(None, "wide", "narrow"),
        P("wide", "narrow"),
        P("wide", "narrow"),
        P("wide", "narrow"),
    )
    return jax.shard_map(
        functools.partial(local, shape), mesh=mesh, in_specs=in_specs, out_specs=out_specs, check_vma=False
    )
```

```python
import functools
import math

import jax
import jax.numpy as jnp
from jax import lax
from jax.experimental import pallas as pl
from jax.experimental.pallas import tpu as pltpu
from jax.sharding import PartitionSpec as P

D = 1024
HEADS = 16
HEAD_DIM = 64
PAIRS = HEADS // 2

EPSILON = 1e-05
NEG_FILL = -1e30
LOG2E = math.log2(math.e)
SCALE = 1.0 / math.sqrt(HEAD_DIM)
AXES = ("wide", "narrow")

F32 = jnp.float32
BF16 = jnp.bfloat16
VMEM = 24 * 2**20
CHEAP = pl.CostEstimate(flops=10**6, bytes_accessed=10**5, transcendentals=0)
BIG_VMEM = pltpu.CompilerParams(vmem_limit_bytes=VMEM)
SMALL_VMEM = pltpu.CompilerParams(vmem_limit_bytes=16 * 2**20)
FULL_VMEM = pltpu.CompilerParams(vmem_limit_bytes=44 * 2**20)


def dot_nt(a, b):
    return lax.dot_general(a, b, (((1,), (1,)), ((), ())), preferred_element_type=F32)


def dot_nn(a, b):
    return lax.dot_general(a, b, (((1,), (0,)), ((), ())), preferred_element_type=F32)


def dot_tn(a, b):
    return lax.dot_general(a, b, (((0,), (0,)), ((), ())), preferred_element_type=F32)


def two_heads(block):
    lane = lax.broadcasted_iota(jnp.int32, block.shape, 1)
    zero = jnp.zeros_like(block)
    return jnp.concatenate(
        (jnp.where(lane < HEAD_DIM, block, zero), jnp.where(lane < HEAD_DIM, zero, block)), axis=0
    )


def own_heads(both):
    half = both.shape[1] // 2
    line = lax.broadcasted_iota(jnp.int32, (both.shape[0], half), 0)
    return jnp.transpose(jnp.where(line < HEAD_DIM, both[:, :half], both[:, half:]))


CUTS = [slice(128 * h, 128 * h + 128) for h in range(PAIRS)]


def heads_forward(q_ref, k_ref, v_ref, valid, put):
    scores = [dot_nt(k_ref(cut), two_heads(q_ref(cut))) for cut in CUTS]
    weights, lses = [], []
    for one in scores:
        one = jnp.where(valid, one * (SCALE * LOG2E), NEG_FILL)
        top = jnp.max(one, axis=0, keepdims=True)
        expo = jnp.exp2(one - top)
        total = jnp.sum(expo, axis=0, keepdims=True)
        weights.append((expo * (1.0 / total)).astype(BF16))
        lses.append(top + jnp.log2(total))
    for h, cut in enumerate(CUTS):
        put(h, own_heads(dot_tn(v_ref(cut), weights[h])).astype(BF16), lses[h])


def heads_backward(q_ref, k_ref, v_ref, do_ref, lse_of, valid, put, group=4):
    for first in range(0, PAIRS, group):
        hs = range(first, first + group)
        qs = [two_heads(q_ref(CUTS[h])) for h in hs]
        ds = [two_heads(do_ref(CUTS[h])) for h in hs]
        scores = [dot_nt(k_ref(CUTS[h]), q) for h, q in zip(hs, qs)]
        grads = [dot_nt(v_ref(CUTS[h]), d) for h, d in zip(hs, ds)]
        weights, grad_scores = [], []
        for h, one, grad in zip(hs, scores, grads):
            weight = jnp.where(valid, jnp.exp2(one * (SCALE * LOG2E) - lse_of(h)), 0.0)
            inner = jnp.sum(weight * grad, axis=0, keepdims=True)
            grad_scores.append((weight * (grad - inner)).astype(BF16))
            weights.append(weight.astype(BF16))
        for h, q, d, weight, grad in zip(hs, qs, ds, weights, grad_scores):
            grad_q = (own_heads(dot_tn(k_ref(CUTS[h]), grad)) * SCALE).astype(BF16)
            grad_k = (dot_nn(grad, q) * SCALE).astype(BF16)
            put(h, grad_q, grad_k, dot_nn(weight, d).astype(BF16))


def columns_in(ref):
    return lambda cut: ref[:, cut]


def memory_columns(ref):
    return lambda cut: ref[0, :, cut]


def self_valid(seg_row, seg_col):
    length = seg_row.shape[-1]
    key = lax.broadcasted_iota(jnp.int32, (length, length), 0)
    tok = lax.broadcasted_iota(jnp.int32, (length, length), 1)
    one = (key <= tok) & (seg_row == seg_col)
    return jnp.concatenate((one, one), axis=1)


def self_fwd_kernel(seg_row, seg_col, q_ref, k_ref, v_ref, o_ref, lse_ref):
    def put(h, mixed, lse):
        o_ref[:, CUTS[h]] = mixed
        lse_ref[0, h : h + 1, :] = lse

    heads_forward(
        columns_in(q_ref), columns_in(k_ref), columns_in(v_ref), self_valid(seg_row[0], seg_col[0]), put
    )


def self_bwd_kernel(seg_row, seg_col, q_ref, k_ref, v_ref, do_ref, lse_ref, dq_ref, dk_ref, dv_ref):
    def put(h, grad_q, grad_k, grad_v):
        dq_ref[:, CUTS[h]] = grad_q
        dk_ref[:, CUTS[h]] = grad_k
        dv_ref[:, CUTS[h]] = grad_v

    heads_backward(
        columns_in(q_ref), columns_in(k_ref), columns_in(v_ref), columns_in(do_ref),
        lambda h: lse_ref[0, h : h + 1, :], self_valid(seg_row[0], seg_col[0]), put, PAIRS,
    )


def self_specs(row_len):
    seg = [
        pl.BlockSpec((1, 1, row_len), lambda r: (r, 0, 0)),
        pl.BlockSpec((1, row_len, 1), lambda r: (r, 0, 0)),
    ]
    row = pl.BlockSpec((row_len, D), lambda r: (r, 0))
    lse = pl.BlockSpec((1, PAIRS, 2 * row_len), lambda r: (r, 0, 0))
    return seg, row, lse


def self_forward(seg, queries, keys, values):
    rows, row_len = seg.shape
    seg_specs, row, lse = self_specs(row_len)
    return pl.pallas_call(
        self_fwd_kernel,
        grid=(rows,),
        in_specs=seg_specs + [row] * 3,
        out_specs=[row, lse],
        out_shape=[
            jax.ShapeDtypeStruct(queries.shape, BF16),
            jax.ShapeDtypeStruct((rows, PAIRS, 2 * row_len), F32),
        ],
        compiler_params=BIG_VMEM,
        cost_estimate=CHEAP,
        name="self_forward",
    )(seg[:, None, :], seg[:, :, None], queries, keys, values)


def self_backward(seg, queries, keys, values, grad_mixed, lse_rows):
    rows, row_len = seg.shape
    seg_specs, row, lse = self_specs(row_len)
    return pl.pallas_call(
        self_bwd_kernel,
        grid=(rows,),
        in_specs=seg_specs + [row] * 4 + [lse],
        out_specs=[row] * 3,
        out_shape=[jax.ShapeDtypeStruct(queries.shape, BF16)] * 3,
        compiler_params=FULL_VMEM,
        cost_estimate=CHEAP,
        name="self_backward",
    )(seg[:, None, :], seg[:, :, None], queries, keys, values, grad_mixed, lse_rows)


def cross_fwd_kernel(map_ref, len_ref, seg_row, seg_col, q_ref, k_ref, v_ref, o_ref, lse_ref):
    r, page = pl.program_id(0), pl.program_id(1)
    keys, toks = k_ref.shape[1], q_ref.shape[0]
    valid = lax.broadcasted_iota(jnp.int32, (keys, 2 * toks), 0) < len_ref[r * 2 + page]
    mine_col = (seg_col[0] == page) | (page == 0)
    mine_row = (seg_row[0] == page) | (page == 0)
    mine_row = jnp.concatenate((mine_row, mine_row), axis=1)

    def put(h, mixed, lse):
        o_ref[:, CUTS[h]] = jnp.where(mine_col, mixed, o_ref[:, CUTS[h]])
        lse_ref[0, h : h + 1, :] = jnp.where(mine_row, lse, lse_ref[0, h : h + 1, :])

    heads_forward(columns_in(q_ref), memory_columns(k_ref), memory_columns(v_ref), valid, put)


def cross_bwd_kernel(
    map_ref, len_ref, seg_row, seg_col, q_ref, k_ref, v_ref, do_ref, lse_ref,
    dq_ref, dk_ref, dv_ref, sum_ref,
):
    r, page = pl.program_id(0), pl.program_id(1)
    keys, toks = k_ref.shape[1], q_ref.shape[0]
    valid = lax.broadcasted_iota(jnp.int32, (keys, 2 * toks), 0) < len_ref[r * 2 + page]
    mine_col = (seg_col[0] == page) | (page == 0)
    mine_row = seg_row[0] == page
    mine_row = jnp.concatenate((mine_row, mine_row), axis=1)

    def put(h, grad_q, grad_k, grad_v):
        cut = CUTS[h]
        dq_ref[:, cut] = jnp.where(mine_col, grad_q, dq_ref[:, cut])
        dk_ref[0, :, cut] = grad_k
        dv_ref[0, :, cut] = grad_v
        before = jnp.where(r + page == 0, jnp.zeros((1, 128), F32), sum_ref[:, cut])
        sum_ref[:, cut] = before + jnp.sum(grad_v.astype(F32), axis=0, keepdims=True)

    heads_backward(
        columns_in(q_ref), memory_columns(k_ref), memory_columns(v_ref), columns_in(do_ref),
        lambda h: jnp.where(mine_row, lse_ref[0, h : h + 1, :], -NEG_FILL), valid, put,
    )


def cross_specs(row_len, mem_len):
    seg = [
        pl.BlockSpec((1, 1, row_len), lambda r, p, *_: (r, 0, 0)),
        pl.BlockSpec((1, row_len, 1), lambda r, p, *_: (r, 0, 0)),
    ]
    row = pl.BlockSpec((row_len, D), lambda r, p, *_: (r, 0))
    mem = pl.BlockSpec((1, mem_len, D), lambda r, p, mp, ln: (mp[r * 2 + p], 0, 0))
    lse = pl.BlockSpec((1, PAIRS, 2 * row_len), lambda r, p, *_: (r, 0, 0))
    return seg, row, mem, lse


def cross_forward(local_map, lengths, seg, queries, keys, values):
    rows, row_len = seg.shape
    mem_len = keys.shape[1]
    seg_specs, row, mem, lse = cross_specs(row_len, mem_len)
    return pl.pallas_call(
        cross_fwd_kernel,
        grid_spec=pltpu.PrefetchScalarGridSpec(
            num_scalar_prefetch=2,
            grid=(rows, 2),
            in_specs=seg_specs + [row, mem, mem],
            out_specs=[row, lse],
        ),
        out_shape=[
            jax.ShapeDtypeStruct(queries.shape, BF16),
            jax.ShapeDtypeStruct((rows, PAIRS, 2 * row_len), F32),
        ],
        compiler_params=FULL_VMEM,
        cost_estimate=CHEAP,
        name="cross_forward",
    )(local_map, lengths, seg[:, None, :], seg[:, :, None], queries, keys, values)


def cross_backward(local_map, lengths, seg, queries, keys, values, grad_mixed, lse_rows):
    rows, row_len = seg.shape
    mem_len = keys.shape[1]
    seg_specs, row, mem, lse = cross_specs(row_len, mem_len)
    return pl.pallas_call(
        cross_bwd_kernel,
        grid_spec=pltpu.PrefetchScalarGridSpec(
            num_scalar_prefetch=2,
            grid=(rows, 2),
            in_specs=seg_specs + [row, mem, mem, row, lse],
            out_specs=[row, mem, mem, pl.BlockSpec((1, D), lambda r, p, *_: (0, 0))],
        ),
        out_shape=[
            jax.ShapeDtypeStruct(queries.shape, BF16),
            jax.ShapeDtypeStruct(keys.shape, BF16),
            jax.ShapeDtypeStruct(values.shape, BF16),
            jax.ShapeDtypeStruct((1, D), F32),
        ],
        compiler_params=FULL_VMEM,
        cost_estimate=CHEAP,
        name="cross_backward",
    )(local_map, lengths, seg[:, None, :], seg[:, :, None], queries, keys, values, grad_mixed, lse_rows)


SMALL_ROWS = 16


def tie(values, *after):
    return lax.optimization_barrier((values, after))[0]


class Clock:
    def __init__(self):
        self.last = ()

    def now(self, values):
        return tie(values, *self.last) if self.last else values

    def tick(self, *arrays):
        self.last = arrays


class Grid:
    def __init__(self, wide, narrow):
        self.wide, self.narrow, self.ring = wide, narrow, wide // 2
        self.devices = wide * narrow
        moves = {
            "z": lambda w, n: ((w + 2) % wide, n),
            "x": lambda w, n: (w ^ 1, n),
            "y": lambda w, n: (w, n ^ 2),
            "c": lambda w, n: (w, n ^ 1),
        }
        self.perms = {}
        for name, move in moves.items():
            pairs = []
            for w in range(wide):
                for n in range(narrow):
                    w2, n2 = move(w, n)
                    pairs.append((w * narrow + n, w2 * narrow + n2))
            self.perms[name] = pairs
        self.clock = Clock()

    def send(self, name, array):
        return lax.ppermute(self.clock.now(array), AXES, self.perms[name])


def segments(first, height, g, rows):
    out, at, end = [], first, first + height
    while at < end:
        k = min(at // rows, g)
        stop = min(end, (k + 1) * rows) if k < g else end
        out.append((k, at - k * rows, at - first, stop - at))
        at = stop
    return out


def half_kernel(parts, ring, wide, g, rows, place, *refs):
    *arrays, out = refs
    z, x, y = place[0], place[1], place[2]
    height = wide * rows
    for which, first_row, count, offset, labels in parts:
        for i, (dz, dx, dy) in enumerate(labels):
            row = 2 * lax.rem(z + (ring - dz), ring) + (x + dx - 2 * x * dx)
            col = y + dy - 2 * y * dy
            for k, matrix_row, at, n in segments(offset, count, g, rows):
                each = rows if k < g else SMALL_ROWS
                first = pl.multiple_of(k * height + row * each + matrix_row, 16)
                out[col, pl.ds(first, n)] = arrays[which][i, pl.ds(first_row + at, n)]


def anywhere(count):
    return [pl.BlockSpec(memory_space=pl.ANY)] * count


PLACE = pl.BlockSpec(memory_space=pltpu.SMEM)


def rearrange_kernel(moves, n_in, *refs):
    ins, outs = refs[:n_in], refs[n_in:]
    for i, bi, ri, ci, rows, o, bo, ro in moves:
        cols = outs[o].shape[-1]
        outs[o][bo, pl.ds(ro, rows)] = ins[i][bi, pl.ds(ri, rows), pl.ds(ci, cols)]


class Rearrange:
    def __init__(self):
        self.ins, self.shapes, self.moves = [], [], []

    def source(self, array):
        for i, known in enumerate(self.ins):
            if known is array:
                return i
        self.ins.append(array)
        return len(self.ins) - 1

    def out(self, blocks, rows, cols):
        self.shapes.append((blocks, rows, cols))
        return len(self.shapes) - 1

    def move(self, out, block, row, array, from_block, first, rows, column=0):
        self.moves.append((self.source(array), from_block, first, column, rows, out, block, row))

    def run(self, clock):
        outs = pl.pallas_call(
            functools.partial(rearrange_kernel, self.moves, len(self.ins)),
            in_specs=[pl.BlockSpec(memory_space=pltpu.VMEM)] * len(self.ins),
            out_specs=[pl.BlockSpec(memory_space=pltpu.VMEM)] * len(self.shapes),
            out_shape=[jax.ShapeDtypeStruct(shape, BF16) for shape in self.shapes],
            compiler_params=SMALL_VMEM,
            cost_estimate=CHEAP,
            name="rearrange",
        )(*clock.now(self.ins))
        return list(outs)


class Gather:
    def __init__(self, grid, place, g, height, cols, small=False):
        self.grid, self.place, self.g, self.height, self.cols = grid, place, g, height, cols
        self.rows = (height - (SMALL_ROWS if small else 0)) // g
        self.parts = []

    def put(self, labels, array, first_row, count, offset):
        self.parts.append((labels, array, first_row, count, offset))

    def half(self, *after):
        grid, arrays, parts = self.grid, [], []
        for labels, array, first_row, count, offset in self.parts:
            which = [i for i, known in enumerate(arrays) if known is array]
            if not which:
                arrays.append(array)
                which = [len(arrays) - 1]
            parts.append((which[0], first_row, count, offset, labels))
        self.own = pl.pallas_call(
            functools.partial(half_kernel, parts, grid.ring, grid.wide, self.g, self.rows),
            in_specs=[PLACE] + [pl.BlockSpec(memory_space=pltpu.VMEM)] * len(arrays),
            out_specs=pl.BlockSpec(memory_space=pltpu.VMEM),
            out_shape=jax.ShapeDtypeStruct((2, grid.wide * self.height, self.cols), BF16),
            compiler_params=SMALL_VMEM,
            cost_estimate=CHEAP,
            name="half_weights",
        )(self.place, *tie(grid.clock.now(arrays), *after))
        return self.own

    def swap(self):
        self.other = self.grid.send("c", self.own)
        return self.other

    def small_rows(self):
        first = self.g * self.grid.wide * self.rows
        own, other = self.grid.clock.now((self.own[:, first:], self.other[:, first:]))
        flip = self.place[3] == 0
        both = jnp.stack((jnp.where(flip, own, other), jnp.where(flip, other, own)))
        return both.reshape(2, 2, self.grid.wide, SMALL_ROWS, -1).astype(F32)


class Square:
    def __init__(self, gather, blocks, height, offset=0):
        self.gather, self.blocks, self.height, self.offset = gather, blocks, height, offset
        self.cut = height // 32 * 16

    def labels(self, dx, dy):
        return [(dz, dx, dy) for dz in range(len(self.blocks))]


def exchange(grid, before, after):
    make = Rearrange()
    cols = (before or after).gather.cols
    depth = len((before or after).blocks)
    heights = [0, 0]
    if before:
        heights = [before.cut, before.height - before.cut]
    total = [h + (after.height if after else 0) for h in heights]
    outs = [make.out(depth, h, cols) for h in total]
    if before:
        (near_x, x_first), (near_y, y_first) = before.near
        for k in range(depth):
            make.move(outs[0], k, 0, near_y, k, y_first, heights[0])
            make.move(outs[1], k, 0, near_x, k, x_first + before.cut, heights[1])
    if after:
        for out, first in zip(outs, heights):
            for k, pieces in enumerate(after.blocks):
                at = first
                for array, block, row, count, column in pieces:
                    make.move(out, k, at, array, block, row, count, column)
                    at += count
    send_x, send_y = make.run(grid.clock)
    from_x, from_y = grid.send("x", send_x), grid.send("y", send_y)
    if before:
        before.gather.put(before.labels(1, 1), from_x, 0, heights[0], before.offset)
        before.gather.put(before.labels(1, 1), from_y, 0, heights[1], before.offset + before.cut)
    if after:
        after.near = ((from_x, heights[0]), (from_y, heights[1]))
        put = after.gather.put
        put(after.labels(0, 0), send_x, heights[0], after.height, after.offset)
        put(after.labels(1, 0), from_x, heights[0], after.height, after.offset)
        put(after.labels(0, 1), from_y, heights[1], after.height, after.offset)
    return from_x, from_y


def unfold(small, count, start, width):
    part = small[:, :, :, :count, start : start + width]
    return part.transpose(3, 2, 1, 0, 4).reshape(count, -1)


def corners(place):
    y, c = place[2], place[3]
    return (2 * y + 1 - c, 2 * (1 - y) + 1 - c), (2 * y + c, 2 * (1 - y) + c)


def column(ref, n, cols):
    return ref[:, pl.ds(pl.multiple_of(n * cols, 128), cols)]


def both_columns(ref, blocks, cols):
    return jnp.concatenate([column(ref, n, cols) for n in blocks], axis=1)


def far_kernel(place, *refs):
    out = refs[-1]
    cols = out.shape[-1]
    for i in range(out.shape[0]):
        a, d = refs[2 * i], refs[2 * i + 1]
        term = dot_tn(a[...], both_columns(d, corners(place)[0], cols))
        for j in range(2):
            out[i, j] = term[:, j * cols : (j + 1) * cols].astype(BF16)


def put_quadrants(x, scratch, k, i, here, outs):
    dx, dy, qx, qy, own = outs
    rows = own.shape[2]
    if here:
        own[k, i] = scratch[k, x]
        qx[k, i] = scratch[k, 1 - x].astype(BF16)
    else:
        qy[k, i] = scratch[k, x].astype(BF16)
        dx[k, i] = scratch[k, 1 - x, pl.ds(0, rows // 2)].astype(BF16)
        dy[k, i] = scratch[k, 1 - x, pl.ds(rows // 2, rows // 2)].astype(BF16)


def near_kernel(place, *refs):
    from_c, *outs, scratch = refs[-7:]
    zs, units, rows, cols = outs[-1].shape
    for i in range(units):
        a, d = refs[2 * i], refs[2 * i + 1]
        term = dot_tn(a[...], both_columns(d, corners(place)[1], cols))
        for j in range(2):
            part = term[:, j * cols : (j + 1) * cols] + from_c[i, j].astype(F32)
            scratch[...] = part.reshape(scratch.shape)
            for k in range(zs):
                put_quadrants(place[1], scratch, k, i, j == 0, outs)


def quadrant_shapes(units, ring, rows, cols):
    half, full = (ring, units, rows // 2, cols), (ring, units, rows, cols)
    return [jax.ShapeDtypeStruct(half, BF16)] * 2 + [
        jax.ShapeDtypeStruct(full, BF16), jax.ShapeDtypeStruct(full, BF16), jax.ShapeDtypeStruct(full, F32)
    ]


def quadrant_specs(units, zs, rows, cols, stepped):
    def at(s, *_):
        return (s if stepped else 0, 0, 0, 0)

    half = pl.BlockSpec((zs, units, rows // 2, cols), at)
    full = pl.BlockSpec((zs, units, rows, cols), at)
    return [half] * 2 + [full] * 3


def token_terms(grid, place, pairs, rows, cols, from_c=None, params=FULL_VMEM):
    units, tokens = len(pairs), pairs[0][0].shape[0]
    height = grid.wide * rows
    zs = max(1, 128 // (2 * rows))
    if 2 * rows >= 128 and height // (2 * rows) > 1 and rows * cols <= 128 * 256:
        zs = min(grid.ring, 2)
    tall = zs * 2 * rows
    in_specs, args = [], []
    for a, d in pairs:
        in_specs += [
            pl.BlockSpec((tokens, tall), lambda s, *_: (0, s)),
            pl.BlockSpec(d.shape, lambda s, *_: (0, 0)),
        ]
        args += [a, d]
    block = pl.BlockSpec((units, 2, tall, cols), lambda s, *_: (0, 0, s, 0))
    scratch = []
    if from_c is None:
        kernel, out_specs = far_kernel, block
        out_shape = jax.ShapeDtypeStruct((units, 2, height, cols), BF16)
    else:
        in_specs.append(block)
        args.append(from_c)
        kernel = near_kernel
        out_specs = quadrant_specs(units, zs, rows, cols, True)
        out_shape = quadrant_shapes(units, grid.ring, rows, cols)
        scratch = [pltpu.VMEM((zs, 2, rows, cols), F32)]
    return pl.pallas_call(
        kernel,
        grid_spec=pltpu.PrefetchScalarGridSpec(
            num_scalar_prefetch=1,
            grid=(height // tall,),
            in_specs=in_specs,
            out_specs=out_specs,
            scratch_shapes=scratch,
        ),
        out_shape=out_shape,
        compiler_params=params,
        cost_estimate=CHEAP,
        name="weight_terms",
    )(place, *args)


def memory_terms_kernel(near, pairs, place, mem, dk, dv, *refs):
    tokens, refs = refs[: 2 * pairs], refs[2 * pairs :]
    if near:
        from_c, dx, dy, qx, qy, own, acc = refs
    else:
        out, acc = refs
    cols = acc.shape[-1]
    m = pl.program_id(0)
    blocks = corners(place)[1 if near else 0]

    @pl.when(m == 0)
    def _():
        for i in range(pairs):
            term = dot_tn(tokens[2 * i][...], both_columns(tokens[2 * i + 1], blocks, cols))
            for j in range(2):
                acc[i, j] = term[:, j * cols : (j + 1) * cols].reshape(acc.shape[2:])
        acc[pairs:] = jnp.zeros_like(acc[pairs:])
        if near:
            acc[...] += from_c[...].astype(F32).reshape(acc.shape)

    grads = jnp.concatenate([both_columns(d.at[0], blocks, cols) for d in (dk, dv)], axis=1)
    term = dot_tn(mem[0], grads)
    for q in range(4):
        part = term[:, q * cols : (q + 1) * cols].reshape(acc.shape[2:])
        acc[pairs + q // 2, q % 2] += part

    @pl.when(m == pl.num_programs(0) - 1)
    def _():
        if near:
            x = place[1]
            for i in range(pairs + 2):
                for j in range(2):
                    for k in range(own.shape[0]):
                        put_quadrants(x, acc.at[i, j], k, i, j == 0, (dx, dy, qx, qy, own))
        else:
            out[...] = acc[...].reshape(out.shape).astype(BF16)


def memory_terms(grid, place, memory, grads, pairs, rows, cols, from_c=None):
    units, (mems, length, wide_cols) = len(pairs) + 2, memory.shape
    height = grid.wide * rows
    near = from_c is not None
    one = pl.BlockSpec((1, length, wide_cols), lambda m, *_: (m, 0, 0))
    term = pl.BlockSpec((units, 2, height, cols), lambda m, *_: (0, 0, 0, 0))
    tokens = [array for pair in pairs for array in pair]
    return pl.pallas_call(
        functools.partial(memory_terms_kernel, near, len(pairs)),
        grid_spec=pltpu.PrefetchScalarGridSpec(
            num_scalar_prefetch=1,
            grid=(mems,),
            in_specs=[one] * 3
            + [pl.BlockSpec(a.shape, lambda m, *_: (0, 0)) for a in tokens]
            + ([term] if near else []),
            out_specs=quadrant_specs(units, grid.ring, rows, cols, False) if near else term,
            scratch_shapes=[pltpu.VMEM((units, 2, grid.ring, 2, rows, cols), F32)],
        ),
        out_shape=quadrant_shapes(units, grid.ring, rows, cols)
        if near
        else jax.ShapeDtypeStruct((units, 2, height, cols), BF16),
        compiler_params=FULL_VMEM,
        cost_estimate=CHEAP,
        name="memory_terms",
    )(place, memory, *grads, *tokens, *([from_c] if near else []))


def add_corners_kernel(qx, qy, from_x, from_y, sx, sy):
    half = from_x.shape[2]
    first, second = pl.ds(0, half), pl.ds(half, half)
    sx[0, :, first] = qx[0, :, first]
    sx[0, :, second] = (qx[0, :, second].astype(F32) + from_y[0].astype(F32)).astype(BF16)
    sy[0, :, first] = (qy[0, :, first].astype(F32) + from_x[0].astype(F32)).astype(BF16)
    sy[0, :, second] = qy[0, :, second]


def add_corners(qx, qy, from_x, from_y):
    ring, units, rows, cols = qx.shape
    full = pl.BlockSpec((1, units, rows, cols), lambda k: (k, 0, 0, 0))
    half = pl.BlockSpec((1, units, rows // 2, cols), lambda k: (k, 0, 0, 0))
    return pl.pallas_call(
        add_corners_kernel,
        grid=(ring,),
        in_specs=[full, full, half, half],
        out_specs=[full, full],
        out_shape=[jax.ShapeDtypeStruct(qx.shape, BF16)] * 2,
        compiler_params=FULL_VMEM,
        cost_estimate=CHEAP,
        name="add_corners",
    )(qx, qy, from_x, from_y)


class Reduce:
    def __init__(self, grid, place, terms, rows):
        self.grid, self.place, self.terms, self.rows = grid, place, terms, rows

    def far(self):
        self.out = self.terms(None)
        return self.out

    def swap(self):
        self.from_c = self.grid.send("c", self.out)
        return self.from_c

    def near(self):
        self.dx, self.dy, self.qx, self.qy, self.own = self.terms(self.grid.clock.now(self.from_c))
        return self.dx

    def across(self):
        self.from_x, self.from_y = self.grid.send("x", self.dx), self.grid.send("y", self.dy)
        return self.from_x, self.from_y

    def add(self):
        from_x = self.grid.clock.now(self.from_x)
        self.sx, self.sy = add_corners(self.qx, self.qy, from_x, self.from_y)
        return self.sx

    def pairs(self):
        self.back_x, self.back_y = self.grid.send("x", self.sx), self.grid.send("y", self.sy)
        return self.back_x, self.back_y

    def chunk(self, step):
        index = lax.rem(self.place[0] + (self.grid.ring - step), self.grid.ring)
        parts = [
            lax.dynamic_index_in_dim(a, index, 0, keepdims=False)
            for a in self.grid.clock.now((self.own, self.back_x, self.back_y))
        ]
        return parts[0] + parts[1].astype(F32) + parts[2].astype(F32)


class RingSum:
    def __init__(self, grid, reduces):
        self.grid, self.reduces, self.done, self.came = grid, reduces, 0, None

    def step(self, *after):
        self.done += 1
        total = jnp.concatenate([r.chunk(self.done % self.grid.ring) for r in self.reduces], axis=0)
        if self.came is not None:
            total = total + tie(self.grid.clock.now(self.came), *after).astype(F32)
        if self.done == self.grid.ring:
            self.came = total
        else:
            self.came = self.grid.send("z", total.astype(BF16))
        return self.came


class SmallSum:
    def __init__(self, grid, place, terms):
        self.grid, self.place, self.done, self.came = grid, place, 0, None
        self.mine = terms.reshape(grid.ring, 2, 2, 2, -1)
        self.steps = grid.ring + 2

    def pair(self, name, axis, at):
        far = lax.dynamic_index_in_dim(self.mine, 1 - at, axis, keepdims=False)
        self.came = self.grid.send(name, far)
        self.near = lax.dynamic_index_in_dim(self.mine, at, axis, keepdims=False)

    def settle(self, *after):
        if self.came is not None:
            came = tie(self.came, *after) if after else self.came
            self.mine = self.near + came

    def step(self, *after):
        grid, place = self.grid, self.place
        if self.done == 0:
            self.pair("c", 3, place[3])
        elif self.done < grid.ring:
            if self.done == 1:
                self.settle(*after)
            index = lax.rem(place[0] + (grid.ring - self.done), grid.ring)
            total = lax.dynamic_index_in_dim(self.mine, index, 0, keepdims=False)
            if self.done > 1:
                total = total + (tie(self.came, *after) if after else self.came)
            self.came = grid.send("z", total)
            self.near = lax.dynamic_index_in_dim(self.mine, place[0], 0, keepdims=False)
        else:
            self.settle(*after)
            if self.done == grid.ring:
                self.pair("y", 1, place[2])
            else:
                self.pair("x", 0, place[1])
        self.done += 1
        return self.came

    def result(self):
        return self.near + self.came


def halves(place, own, other):
    c = place[3]
    return [(2 * y + core, y, half) for half, core in ((own, c), (other, 1 - c)) for y in range(2)]


def at_block(n, cols):
    return pl.ds(pl.multiple_of(n * cols, 128), cols)


def times_t(place, d, own, other):
    cols = own.shape[-1]
    return sum(dot_nt(d[:, at_block(n, cols)], half[y]) for n, y, half in halves(place, own, other))


def norm_parts(values):
    centre = values - jnp.mean(values, axis=-1, keepdims=True)
    scale = lax.rsqrt(jnp.mean(centre * centre, axis=-1, keepdims=True) + EPSILON)
    return centre * scale, scale


def norm_back(normed, scale, gain, grad):
    inner = grad * gain
    back = scale * (
        inner
        - jnp.mean(inner, axis=-1, keepdims=True)
        - normed * jnp.mean(inner * normed, axis=-1, keepdims=True)
    )
    return back, jnp.sum(grad * normed, axis=0, keepdims=True), jnp.sum(grad, axis=0, keepdims=True)


def column_sum(values):
    return jnp.sum(values.astype(F32), axis=0, keepdims=True)


GAIN, BIAS = 0, 3


def row(vectors, i):
    return vectors[i : i + 1, :]


def memory_kernel(place, mem, vectors, k_own, k_other, v_own, v_other, keys, values):
    cols = k_own.shape[-1]
    for n, y, half in halves(place, k_own, k_other):
        keys[0, :, at_block(n, cols)] = dot_nn(mem[0], half[y]).astype(BF16)
    for n, y, half in halves(place, v_own, v_other):
        bias = vectors[BIAS + 6 : BIAS + 7, at_block(n, cols)]
        values[0, :, at_block(n, cols)] = (dot_nn(mem[0], half[y]) + bias).astype(BF16)


def qkv_kernel(place, tokens, vectors, *refs):
    weights, (normed, q, k, v) = refs[:6], refs[6:]
    n, _ = norm_parts(tokens[...].astype(F32))
    normed[...] = (n * row(vectors, GAIN) + row(vectors, BIAS)).astype(BF16)
    cols = weights[0].shape[-1]
    for i, (out, bias_at) in enumerate(((q, 1), (k, None), (v, 2))):
        for n, y, half in halves(place, weights[2 * i], weights[2 * i + 1]):
            term = dot_nn(normed[...], half[y])
            if bias_at is not None:
                term = term + vectors[BIAS + bias_at : BIAS + bias_at + 1, at_block(n, cols)]
            out[:, at_block(n, cols)] = term.astype(BF16)


def middle_kernel(place, tokens, mixed, vectors, so_own, so_other, cq_own, cq_other, after, normed, queries):
    cols = so_own.shape[-1]
    for n, y, half in halves(place, so_own, so_other):
        at = at_block(n, cols)
        after[:, at] = tokens[:, at].astype(F32) + dot_nn(mixed[...], half[y]) + vectors[BIAS + 3 : BIAS + 4, at]
    n, _ = norm_parts(after[...])
    normed[...] = (n * row(vectors, GAIN + 1) + row(vectors, BIAS + 4)).astype(BF16)
    for n, y, half in halves(place, cq_own, cq_other):
        at = at_block(n, cols)
        queries[:, at] = (dot_nn(normed[...], half[y]) + vectors[BIAS + 5 : BIAS + 6, at]).astype(BF16)


def cross_out_kernel(place, before, mixed, vectors, own, other, after, normed):
    cols = own.shape[-1]
    for n, y, half in halves(place, own, other):
        at = at_block(n, cols)
        after[:, at] = before[:, at] + dot_nn(mixed[...], half[y]) + vectors[BIAS + 7 : BIAS + 8, at]
    n, _ = norm_parts(after[...])
    normed[...] = (n * row(vectors, GAIN + 2) + row(vectors, BIAS + 8)).astype(BF16)


def up_kernel(place, normed, bias, own, other, act, slope):
    c, cols = place[3], own.shape[-1]
    y = pl.program_id(0)
    for n, half in ((2 * y + c, own), (2 * y + 1 - c, other)):
        for j in range(4):
            at = at_block(4 * n + j, cols)
            u = dot_nn(normed[...], half[0, j * D : (j + 1) * D]) + bias[:, at]
            below = 0.5 * (1.0 + lax.erf(u * (1.0 / math.sqrt(2.0))))
            act[:, at] = (u * below).astype(BF16)
            slope[:, at] = (below + u * jnp.exp(-0.5 * u * u) * (1.0 / math.sqrt(2.0 * math.pi))).astype(BF16)


def down_kernel(place, after, act, vectors, own, other, out):
    c, y = place[3], pl.program_id(0)
    cols = own.shape[-1]
    for n, half in ((2 * y + c, own), (2 * y + 1 - c, other)):
        at = at_block(n, cols)
        total = after[:, at] + dot_nn(act[...], half[0]) + vectors[BIAS + 9 : BIAS + 10, at]
        out[:, at] = total.astype(BF16)


def down_back_kernel(place, grad, slope, normed, own, other, grad_pre, bias_grad, far):
    back = (times_t(place, grad, own, other) * slope[...].astype(F32)).astype(BF16)
    grad_pre[...] = back
    bias_grad[...] = column_sum(back)
    for i, n in enumerate(corners(place)[0]):

        @pl.when(pl.program_id(0) == n)
        def _():
            far[0, i] = dot_tn(normed[...], back).astype(BF16)


def up_back_kernel(
    place, grad_pre, grad_out, after, vectors, own, other, co_own, co_other,
    grad, branch, mixed, gain_grad, shift_grad, out_grad, last_grad, total,
):
    c, y = place[3], pl.program_id(0)
    cols = own.shape[-1]
    term = sum(
        dot_nt(grad_pre[:, at_block(4 * n + j, cols)], half[0, j * D : (j + 1) * D])
        for n, half in ((2 * y + c, own), (2 * y + 1 - c, other))
        for j in range(4)
    )

    @pl.when(y == 0)
    def _():
        total[...] = term

    @pl.when(y == 1)
    def _():
        n, scale = norm_parts(after[...])
        back, gain_grad[...], shift_grad[...] = norm_back(n, scale, row(vectors, GAIN + 2), total[...] + term)
        out = grad_out[...].astype(F32) + back
        grad[...] = out
        branch[...] = out.astype(BF16)
        out_grad[...] = column_sum(branch[...])
        last_grad[...] = column_sum(grad_out[...])
        mixed[...] = times_t(place, branch, co_own, co_other).astype(BF16)


def middle_back_kernel(
    place, grad_queries, grad_after, after, vectors, cq_own, cq_other, so_own, so_other,
    grad, branch, mixed, gain_grad, shift_grad, out_grad, query_grad,
):
    n, scale = norm_parts(after[...])
    dense = times_t(place, grad_queries, cq_own, cq_other)
    back, gain_grad[...], shift_grad[...] = norm_back(n, scale, row(vectors, GAIN + 1), dense)
    out = grad_after[...] + back
    grad[...] = out
    branch[...] = out.astype(BF16)
    out_grad[...] = column_sum(branch[...])
    query_grad[...] = column_sum(grad_queries[...])
    mixed[...] = times_t(place, branch, so_own, so_other).astype(BF16)


def first_back_kernel(place, tokens, grad_after, gq, gk, gv, vectors, *refs):
    weights, (grad, gain_grad, shift_grad, query_grad, value_grad) = refs[:6], refs[6:]
    n, scale = norm_parts(tokens[...].astype(F32))
    dense = sum(
        times_t(place, d, weights[2 * i], weights[2 * i + 1]) for i, d in enumerate((gq, gk, gv))
    )
    back, gain_grad[...], shift_grad[...] = norm_back(n, scale, row(vectors, GAIN), dense)
    grad[...] = (grad_after[...] + back).astype(BF16)
    query_grad[...] = column_sum(gq[...])
    value_grad[...] = column_sum(gv[...])


def memory_back_kernel(place, gk, gv, k_own, k_other, v_own, v_other, grad):
    total = times_t(place, gk.at[0], k_own, k_other) + times_t(place, gv.at[0], v_own, v_other)
    grad[0] = total.astype(BF16)


def in_place(array):
    return pl.pallas_call(
        lambda _, out: None,
        in_specs=anywhere(1),
        out_specs=pl.BlockSpec(memory_space=pl.ANY),
        out_shape=jax.ShapeDtypeStruct(array.shape, array.dtype),
        input_output_aliases={0: 0},
        compiler_params=BIG_VMEM,
        cost_estimate=CHEAP,
        name="in_place",
    )(array)


def dense_call(kernel, name, place, ins, outs, grid=(1,), scratch=(), params=BIG_VMEM):
    def spec(array, block, index):
        block = block or array.shape
        zeros = (0,) * len(block)
        return pl.BlockSpec(block, index or (lambda *_: zeros))

    return pl.pallas_call(
        kernel,
        grid_spec=pltpu.PrefetchScalarGridSpec(
            num_scalar_prefetch=1,
            grid=grid,
            in_specs=[spec(*one) for one in ins],
            out_specs=[spec(*one) for one in outs],
            scratch_shapes=scratch,
        ),
        out_shape=[one[0] for one in outs],
        compiler_params=params,
        cost_estimate=CHEAP,
        name=name,
    )(place, *[one[0] for one in ins])


def full(array):
    return (array, None, None)


def result(shape, dtype):
    return (jax.ShapeDtypeStruct(shape, dtype), None, None)


def matrix(gathered, i, height=D):
    block = (2, height, gathered.own.shape[-1])
    return [(half, block, lambda *_: (0, i, 0)) for half in (gathered.own, gathered.other)]


def by_y(gathered):
    block = (1,) + gathered.own.shape[1:]
    return [(half, block, lambda y, *_: (y, 0, 0)) for half in (gathered.own, gathered.other)]


def by_rows(gathered, rows):
    block = (2, rows, gathered.own.shape[-1])
    return [(half, block, lambda s, *_: (0, s, 0)) for half in (gathered.own, gathered.other)]


def local(
    shape,
    tokens,
    memory,
    segment_ids,
    page_map,
    mem_lengths,
    gains,
    biases,
    fc1_bias,
    self_qkv,
    self_out,
    cross_q,
    cross_kv,
    cross_out,
    fc1,
    fc2,
    cotangent,
):
    grid = Grid(*shape)
    wide_at, narrow_at = lax.axis_index("wide"), lax.axis_index("narrow")
    place = jnp.stack((wide_at // 2, wide_at % 2, narrow_at // 2, narrow_at % 2)).astype(jnp.int32)
    devices = grid.devices
    mem_count, token_count = memory.shape[0], tokens.shape[0]
    rows, cols = self_out.shape

    each, up_each = gains.shape[1], fc1_bias.size
    n_gain, n_bias = gains.size, biases.size
    small = jnp.pad(
        jnp.concatenate((gains, biases), axis=0), ((0, SMALL_ROWS - 13), (0, cols - each))
    )
    small = lax.dynamic_update_slice(small, fc1_bias[None], (0, 128))
    send, clock = grid.send, grid.clock
    now, tick = clock.now, clock.tick
    steps = grid.ring - 1
    gather = functools.partial(Gather, grid, place)
    ckv_height = 2 * rows + SMALL_ROWS
    fc2_rows = fc2.shape[0]
    part = fc2_rows // 2
    g_ckv = gather(2, ckv_height, cols, True)
    g_qkv = gather(3, 3 * rows, cols)
    g_mix = gather(3, 3 * rows, cols)
    g_fc1 = gather(4, 4 * rows, cols)
    g_fc2 = gather(1, fc2_rows, cols)

    start = Rearrange()
    out = start.out(1, 5 * rows, cols)
    for k, (array, i) in enumerate(((cross_kv, 0), (cross_kv, 1), (self_qkv, 0), (self_qkv, 1), (self_qkv, 2))):
        start.move(out, 0, k * rows, array, i, 0, rows)
    ring_one = start.run(clock)
    ring_one.append(send("z", ring_one[-1]))
    ring_small = [small[None]]
    ring_small.append(send("z", ring_small[-1]))
    top = Square(g_fc2, [[(fc2[None], 0, 0, part, 0)]], part)
    more = Rearrange()
    out = more.out(1, 3 * rows, cols)
    for k, array in enumerate((self_out, cross_q, cross_out)):
        more.move(out, 0, k * rows, array[None], 0, 0, rows)
    out = more.out(1, 4 * rows + part, cols)
    for k in range(4):
        more.move(out, 0, k * rows, fc1[None], 0, 0, rows, k * cols)
    more.move(out, 0, 4 * rows, fc2[None], 0, part, part)
    ring_mix, ring_up = [[array] for array in more.run(clock)]
    came = exchange(grid, None, top)
    tick(ring_one[-1], ring_small[-1], ring_mix[0], ring_up[0])
    ring_one.append(send("z", ring_one[-1]))
    ring_small.append(send("z", ring_small[-1]))
    memory = in_place(now(memory))
    tick(ring_one[-1], ring_small[-1], memory, *came)
    came = exchange(grid, top, None)
    for _ in range(steps - 2):
        ring_one.append(send("z", ring_one[-1]))
        ring_small.append(send("z", ring_small[-1]))
        tick(ring_one[-1], ring_small[-1], *came)

    def from_ring(arrays, first, count):
        return [[(array, 0, first, count, 0)] for array in arrays]

    ckv = Square(
        g_ckv, [a + b for a, b in zip(from_ring(ring_one, 0, 2 * rows), from_ring(ring_small, 0, SMALL_ROWS))],
        ckv_height,
    )
    qkv = Square(g_qkv, from_ring(ring_one, 2 * rows, 3 * rows), 3 * rows)
    ring_mix.append(send("z", ring_mix[-1]))
    ring_up.append(send("z", ring_up[-1]))
    tick(ring_mix[-1], ring_up[-1], *exchange(grid, None, ckv))

    make = Rearrange()
    out = make.out(4, part, cols)
    (_, own, own_at, _, _), (_, by_x, x_at, _, _), (_, by_y_, y_at, _, _), (_, low, _, _, _), (_, high, _, _, _) = g_fc2.parts
    g_fc2.parts = []
    for k, (array, at) in enumerate(((own, own_at), (by_x, x_at), (by_y_, y_at))):
        make.move(out, k, 0, array, 0, at, part)
    make.move(out, 3, 0, low, 0, 0, top.cut)
    make.move(out, 3, top.cut, high, 0, 0, part - top.cut)
    came = exchange(grid, ckv, qkv)
    ring_top = make.run(clock)
    ring_up.append(send("z", ring_up[-1]))
    for _ in range(steps - 1):
        ring_mix.append(send("z", ring_mix[-1]))
    tick(ring_mix[-1], ring_up[-1], ring_top[-1], *came)

    mix = Square(g_mix, from_ring(ring_mix, 0, 3 * rows), 3 * rows)
    came = exchange(grid, qkv, mix)
    for _ in range(steps - 2):
        ring_up.append(send("z", ring_up[-1]))
    ring_top.append(send("z", ring_top[-1]))
    g_ckv.half(g_mix.parts[0][1])
    g_ckv.swap()
    small_all = g_ckv.small_rows()
    vectors = unfold(small_all, 13, 0, each)
    up_bias = unfold(small_all, 1, 128, up_each)
    mem_block = (1,) + memory.shape[1:]
    mem_shape = jax.ShapeDtypeStruct(memory.shape, BF16)

    def by_memory(array):
        return (array, mem_block, lambda m, *_: (m, 0, 0))

    mem_keys, mem_values = dense_call(
        memory_kernel, "memory_keys_values", place,
        [by_memory(now(memory)), full(vectors)] + matrix(g_ckv, 0) + matrix(g_ckv, 1),
        [by_memory(mem_shape), by_memory(mem_shape)], grid=(mem_count,),
    )
    tick(ring_up[-1], ring_top[-1], mem_keys, *came)

    up = Square(g_fc1, from_ring(ring_up, 0, 4 * rows), 4 * rows)
    low = Square(g_fc2, from_ring(ring_up, 4 * rows, part), part, part)
    came = exchange(grid, mix, up)
    ring_top.append(send("z", ring_top[-1]))
    g_qkv.half(g_fc1.parts[0][1])
    g_qkv.swap()
    wide_row = (token_count, D)
    normed_one, self_queries, self_keys, self_values = dense_call(
        qkv_kernel, "self_qkv", place,
        [full(now(tokens)), full(vectors)] + matrix(g_qkv, 0) + matrix(g_qkv, 1) + matrix(g_qkv, 2),
        [result(wide_row, BF16)] * 4,
    )
    self_mixed, self_lse = self_forward(segment_ids, self_queries, self_keys, self_values)
    tick(self_mixed, ring_top[-1], *came)

    came = exchange(grid, up, low)
    g_mix.half(g_fc2.parts[0][1])
    g_mix.swap()
    for _ in range(steps - 2):
        ring_top.append(send("z", ring_top[-1]))
    after_self, normed_two, cross_queries = dense_call(
        middle_kernel, "self_out_cross_q", place,
        [full(tokens), full(now(self_mixed)), full(vectors)] + matrix(g_mix, 0) + matrix(g_mix, 1),
        [result(wide_row, F32), result(wide_row, BF16), result(wide_row, BF16)],
    )
    first_mem = lax.axis_index(AXES) * mem_count
    local_map = (page_map - first_mem).reshape(-1).astype(jnp.int32)
    picks = local_map[:, None] == jnp.arange(mem_count, dtype=jnp.int32)[None, :]
    row_lengths = jnp.sum(jnp.where(picks, mem_lengths[None, :], 0), axis=-1).astype(jnp.int32)
    cross_mixed, cross_lse = cross_forward(
        local_map, row_lengths, segment_ids, cross_queries, mem_keys, mem_values
    )
    tick(cross_mixed, ring_top[-1], *came)

    came = exchange(grid, low, None)
    g_fc1.half()
    g_fc1.swap()
    after_cross, normed_three = dense_call(
        cross_out_kernel, "cross_out", place,
        [full(after_self), full(now(cross_mixed)), full(vectors)] + matrix(g_mix, 2),
        [result(wide_row, F32), result(wide_row, BF16)],
    )
    hidden = up_bias.shape[1]
    activated, slope = dense_call(
        up_kernel, "fc1_gelu", place,
        [full(normed_three), full(up_bias)] + by_y(g_fc1),
        [result((token_count, hidden), BF16)] * 2, grid=(2,),
    )
    tick(activated, *came)
    spread = [(0, 0), (1, 0), (0, 1), (1, 1)]
    for step, array in enumerate(ring_top):
        g_fc2.put([(step, dx, dy) for dx, dy in spread], array, 0, part, 0)

    def settle(pairs, shard, params=FULL_VMEM):
        part_rows, part_cols = shard.shape
        return Reduce(
            grid, place,
            lambda from_c: token_terms(grid, place, pairs, part_rows, part_cols, from_c, params),
            part_rows,
        )

    one_row = result((1, D), F32)
    r_fc2 = settle([(now(activated), cotangent)], fc2, BIG_VMEM)
    r_fc2.far()
    r_fc2.swap()
    g_fc2.half()
    g_fc2.swap()
    tick(r_fc2.near())
    slab = hidden // 4
    some = lambda array: (array, (token_count, slab), lambda s, *_: (0, s))
    grad_pre, grad_up_bias, far_fc1 = dense_call(
        down_back_kernel, "fc2_gelu_back", place,
        [full(now(cotangent)), some(slope), full(normed_three)] + by_rows(g_fc2, slab),
        [
            some(jax.ShapeDtypeStruct((token_count, hidden), BF16)),
            (jax.ShapeDtypeStruct((1, hidden), F32), (1, slab), lambda s, *_: (0, s)),
            result((1, 2, D, slab), BF16),
        ],
        grid=(4,), params=FULL_VMEM,
    )
    r_fc1 = settle([(normed_three, grad_pre)], fc1)
    r_fc1.out = far_fc1
    tick(far_fc1, *r_fc2.across())
    r_fc2.add()
    came = list(r_fc2.pairs())
    r_fc1.swap()
    (
        grad_after_cross, grad_branch_two, grad_cross_mixed,
        grad_gain_three, grad_bias_eight, grad_bias_seven, grad_bias_nine,
    ) = dense_call(
        up_back_kernel, "fc1_norm_back", place,
        [full(tie(now(grad_pre), r_fc2.sx)), full(cotangent), full(after_cross), full(vectors)]
        + by_y(g_fc1) + matrix(g_mix, 2),
        [result(wide_row, F32), result(wide_row, BF16), result(wide_row, BF16)] + [one_row] * 4,
        grid=(2,), scratch=[pltpu.VMEM(wide_row, F32)], params=FULL_VMEM,
    )
    tick(r_fc1.near(), grad_cross_mixed)

    came += r_fc1.across()
    grad_cq, grad_ck, grad_cv, grad_bias_six = cross_backward(
        local_map, row_lengths, segment_ids, cross_queries, mem_keys, mem_values,
        now(grad_cross_mixed), cross_lse,
    )
    r_mem = Reduce(
        grid, place,
        lambda from_c: memory_terms(grid, place, memory, (grad_ck, grad_cv), [], rows, cols, from_c),
        rows,
    )
    tick(grad_cq, r_mem.far(), *came)
    ring_fc2 = RingSum(grid, [r_fc2])
    r_fc1.add()
    r_mem.swap()
    ring_fc2.step()
    grad_cq = tie(now(grad_cq), r_fc1.sx)
    (
        grad_after_self, grad_branch_one, grad_self_mixed,
        grad_gain_two, grad_bias_four, grad_bias_three, grad_bias_five,
    ) = dense_call(
        middle_back_kernel, "cross_q_norm_back", place,
        [full(grad_cq), full(grad_after_cross), full(after_self), full(vectors)]
        + matrix(g_mix, 1) + matrix(g_mix, 0),
        [result(wide_row, F32), result(wide_row, BF16), result(wide_row, BF16)] + [one_row] * 4,
        params=FULL_VMEM,
    )
    grad_sq, grad_sk, grad_sv = self_backward(
        segment_ids, self_queries, self_keys, self_values, grad_self_mixed, self_lse
    )
    r_rest = settle(
        [
            (normed_one, grad_sq), (normed_one, grad_sk), (normed_one, grad_sv),
            (self_mixed, grad_branch_one), (normed_two, grad_cq), (cross_mixed, grad_branch_two),
        ],
        cross_q,
    )
    tick(r_rest.far(), r_mem.near(), ring_fc2.came, *r_fc1.pairs())
    ring_fc1 = RingSum(grid, [r_fc1])
    came = r_mem.across()
    r_rest.swap()
    ring_fc2.step()
    ring_fc1.step()
    grad_tokens, grad_gain_one, grad_bias_zero, grad_bias_one, grad_bias_two = dense_call(
        first_back_kernel, "self_qkv_norm_back", place,
        [full(tokens), full(grad_after_self)] + [full(d) for d in now((grad_sq, grad_sk, grad_sv))]
        + [full(vectors)] + matrix(g_qkv, 0) + matrix(g_qkv, 1) + matrix(g_qkv, 2),
        [result(wide_row, BF16)] + [one_row] * 4,
        params=FULL_VMEM,
    )
    tick(r_rest.near(), grad_tokens, ring_fc2.came, ring_fc1.came, *came)

    def by_device(array):
        return array.reshape(array.shape[0], devices, -1).transpose(1, 0, 2).reshape(devices, -1)

    small_grads = jnp.concatenate(
        (
            by_device(
                jnp.concatenate(
                    (
                        grad_gain_one, grad_gain_two, grad_gain_three,
                        grad_bias_zero, grad_bias_one, grad_bias_two, grad_bias_three, grad_bias_four,
                        grad_bias_five, grad_bias_six, grad_bias_seven, grad_bias_eight, grad_bias_nine,
                    ),
                    axis=0,
                )
            ),
            by_device(grad_up_bias),
        ),
        axis=1,
    )
    small_sum = SmallSum(grid, place, now(small_grads))
    r_mem.add()
    ring_fc2.step()
    (grad_memory,) = dense_call(
        memory_back_kernel, "memory_back", place,
        [by_memory(a) for a in tie(now((grad_ck, grad_cv)), r_mem.sx)] + matrix(g_ckv, 0) + matrix(g_ckv, 1),
        [by_memory(mem_shape)], grid=(mem_count,), params=FULL_VMEM,
    )
    tick(grad_memory, ring_fc2.came, *r_mem.pairs(), *r_rest.across())
    small_sum.step()
    ring_mem = RingSum(grid, [r_mem])
    r_rest.add()
    turned_memory = in_place(tie(now(grad_memory).transpose(1, 0, 2), r_rest.sx))
    grad_memory = turned_memory.transpose(1, 0, 2)
    ring_fc1.step()
    ring_mem.step()
    for _ in range(steps):
        small_sum.step()
    (layer_out,) = dense_call(
        down_kernel, "fc2", place,
        [full(after_cross), full(tie(now(activated), turned_memory)), full(vectors)] + by_y(g_fc2),
        [result(wide_row, BF16)], grid=(2,), params=FULL_VMEM,
    )
    ring_fc1.step(turned_memory)
    ring_mem.step(turned_memory)
    tick(turned_memory, layer_out, small_sum.came, ring_fc1.came, ring_mem.came, *r_rest.pairs())
    ring_fc2.step()
    ring_rest = RingSum(grid, [r_rest])
    ring_rest.step()
    ring_fc1.step()
    ring_mem.step()
    small_sum.step()
    tick(ring_rest.came, ring_mem.came, small_sum.came)
    for _ in range(steps - 1):
        ring_mem.step() if ring_mem.done < grid.ring else None
        small_sum.step() if small_sum.done < small_sum.steps else None
        tick(ring_rest.step(), ring_mem.came, small_sum.came)
    for ring in (ring_fc2, ring_fc1, ring_mem, ring_rest):
        while ring.done < grid.ring:
            ring.step()
    while small_sum.done < small_sum.steps:
        small_sum.step()
    came_mem, came_rest = ring_mem.came, ring_rest.came
    small_shard = small_sum.result()
    return (
        layer_out,
        grad_tokens,
        grad_memory,
        small_shard[:n_gain].reshape(gains.shape),
        small_shard[n_gain : n_gain + n_bias].reshape(biases.shape),
        small_shard[n_gain + n_bias :],
        came_rest[:3],
        came_rest[3],
        came_rest[4],
        came_mem,
        came_rest[5],
        ring_fc1.came[0],
        ring_fc2.came[0],
    )


def solution(mesh):
    shape = (mesh.shape["wide"], mesh.shape["narrow"])
    in_specs = (
        P(AXES, None),
        P(AXES, None, None),
        P(AXES, None),
        P(AXES, None),
        P(AXES),
        P(None, AXES),
        P(None, AXES),
        P(AXES),
        P(None, "wide", "narrow"),
        P("wide", "narrow"),
        P("wide", "narrow"),
        P(None, "wide", "narrow"),
        P("wide", "narrow"),
        P("wide", "narrow"),
        P("wide", "narrow"),
        P(AXES, None),
    )
    out_specs = (
        P(AXES, None),
        P(AXES, None),
        P(AXES, None, None),
        P(None, AXES),
        P(None, AXES),
        P(AXES),
        P(None, "wide", "narrow"),
        P("wide", "narrow"),
        P("wide", "narrow"),
        P(None, "wide", "narrow"),
        P("wide", "narrow"),
        P("wide", "narrow"),
        P("wide", "narrow"),
    )
    return jax.shard_map(
        functools.partial(local, shape), mesh=mesh, in_specs=in_specs, out_specs=out_specs, check_vma=False
    )
```

```python
import functools
import math

import jax
import jax.numpy as jnp
from jax import lax
from jax.experimental import pallas as pl
from jax.experimental.pallas import tpu as pltpu
from jax.sharding import PartitionSpec as P

D = 1024
HEADS = 16
HEAD_DIM = 64
PAIRS = HEADS // 2

EPSILON = 1e-05
NEG_FILL = -1e30
LOG2E = math.log2(math.e)
SCALE = 1.0 / math.sqrt(HEAD_DIM)
AXES = ("wide", "narrow")

F32 = jnp.float32
BF16 = jnp.bfloat16
VMEM = 24 * 2**20
CHEAP = pl.CostEstimate(flops=10**6, bytes_accessed=10**5, transcendentals=0)
BIG_VMEM = pltpu.CompilerParams(vmem_limit_bytes=VMEM)
SMALL_VMEM = pltpu.CompilerParams(vmem_limit_bytes=16 * 2**20)
FULL_VMEM = pltpu.CompilerParams(vmem_limit_bytes=39 * 2**20)


def dot_nt(a, b):
    return lax.dot_general(a, b, (((1,), (1,)), ((), ())), preferred_element_type=F32)


def dot_nn(a, b):
    return lax.dot_general(a, b, (((1,), (0,)), ((), ())), preferred_element_type=F32)


def dot_tn(a, b):
    return lax.dot_general(a, b, (((0,), (0,)), ((), ())), preferred_element_type=F32)


def two_heads(block):
    lane = lax.broadcasted_iota(jnp.int32, block.shape, 1)
    zero = jnp.zeros_like(block)
    return jnp.concatenate(
        (jnp.where(lane < HEAD_DIM, block, zero), jnp.where(lane < HEAD_DIM, zero, block)), axis=0
    )


def own_heads(both):
    half = both.shape[1] // 2
    line = lax.broadcasted_iota(jnp.int32, (both.shape[0], half), 0)
    return jnp.transpose(jnp.where(line < HEAD_DIM, both[:, :half], both[:, half:]))


CUTS = [slice(128 * h, 128 * h + 128) for h in range(PAIRS)]


def heads_forward(q_ref, k_ref, v_ref, valid, put):
    scores = [dot_nt(k_ref(cut), two_heads(q_ref(cut))) for cut in CUTS]
    weights, lses = [], []
    for one in scores:
        one = jnp.where(valid, one * (SCALE * LOG2E), NEG_FILL)
        top = jnp.max(one, axis=0, keepdims=True)
        expo = jnp.exp2(one - top)
        total = jnp.sum(expo, axis=0, keepdims=True)
        weights.append((expo * (1.0 / total)).astype(BF16))
        lses.append(top + jnp.log2(total))
    for h, cut in enumerate(CUTS):
        put(h, own_heads(dot_tn(v_ref(cut), weights[h])).astype(BF16), lses[h])


def heads_backward(q_ref, k_ref, v_ref, do_ref, lse_of, valid, put, group=4):
    for first in range(0, PAIRS, group):
        hs = range(first, first + group)
        qs = [two_heads(q_ref(CUTS[h])) for h in hs]
        ds = [two_heads(do_ref(CUTS[h])) for h in hs]
        scores = [dot_nt(k_ref(CUTS[h]), q) for h, q in zip(hs, qs)]
        grads = [dot_nt(v_ref(CUTS[h]), d) for h, d in zip(hs, ds)]
        weights, grad_scores = [], []
        for h, one, grad in zip(hs, scores, grads):
            weight = jnp.where(valid, jnp.exp2(one * (SCALE * LOG2E) - lse_of(h)), 0.0)
            inner = jnp.sum(weight * grad, axis=0, keepdims=True)
            grad_scores.append((weight * (grad - inner)).astype(BF16))
            weights.append(weight.astype(BF16))
        for h, q, d, weight, grad in zip(hs, qs, ds, weights, grad_scores):
            grad_q = (own_heads(dot_tn(k_ref(CUTS[h]), grad)) * SCALE).astype(BF16)
            grad_k = (dot_nn(grad, q) * SCALE).astype(BF16)
            put(h, grad_q, grad_k, dot_nn(weight, d).astype(BF16))


def columns_in(ref):
    return lambda cut: ref[:, cut]


def memory_columns(ref):
    return lambda cut: ref[0, :, cut]


def self_valid(seg_row, seg_col):
    length = seg_row.shape[-1]
    key = lax.broadcasted_iota(jnp.int32, (length, length), 0)
    tok = lax.broadcasted_iota(jnp.int32, (length, length), 1)
    one = (key <= tok) & (seg_row == seg_col)
    return jnp.concatenate((one, one), axis=1)


def self_fwd_kernel(seg_row, seg_col, q_ref, k_ref, v_ref, o_ref, lse_ref):
    def put(h, mixed, lse):
        o_ref[:, CUTS[h]] = mixed
        lse_ref[0, h : h + 1, :] = lse

    heads_forward(
        columns_in(q_ref), columns_in(k_ref), columns_in(v_ref), self_valid(seg_row[0], seg_col[0]), put
    )


def self_bwd_kernel(seg_row, seg_col, q_ref, k_ref, v_ref, do_ref, lse_ref, dq_ref, dk_ref, dv_ref):
    def put(h, grad_q, grad_k, grad_v):
        dq_ref[:, CUTS[h]] = grad_q
        dk_ref[:, CUTS[h]] = grad_k
        dv_ref[:, CUTS[h]] = grad_v

    heads_backward(
        columns_in(q_ref), columns_in(k_ref), columns_in(v_ref), columns_in(do_ref),
        lambda h: lse_ref[0, h : h + 1, :], self_valid(seg_row[0], seg_col[0]), put, PAIRS,
    )


def self_specs(row_len):
    seg = [
        pl.BlockSpec((1, 1, row_len), lambda r: (r, 0, 0)),
        pl.BlockSpec((1, row_len, 1), lambda r: (r, 0, 0)),
    ]
    row = pl.BlockSpec((row_len, D), lambda r: (r, 0))
    lse = pl.BlockSpec((1, PAIRS, 2 * row_len), lambda r: (r, 0, 0))
    return seg, row, lse


def self_forward(seg, queries, keys, values):
    rows, row_len = seg.shape
    seg_specs, row, lse = self_specs(row_len)
    return pl.pallas_call(
        self_fwd_kernel,
        grid=(rows,),
        in_specs=seg_specs + [row] * 3,
        out_specs=[row, lse],
        out_shape=[
            jax.ShapeDtypeStruct(queries.shape, BF16),
            jax.ShapeDtypeStruct((rows, PAIRS, 2 * row_len), F32),
        ],
        compiler_params=BIG_VMEM,
        cost_estimate=CHEAP,
        name="self_forward",
    )(seg[:, None, :], seg[:, :, None], queries, keys, values)


def self_backward(seg, queries, keys, values, grad_mixed, lse_rows):
    rows, row_len = seg.shape
    seg_specs, row, lse = self_specs(row_len)
    return pl.pallas_call(
        self_bwd_kernel,
        grid=(rows,),
        in_specs=seg_specs + [row] * 4 + [lse],
        out_specs=[row] * 3,
        out_shape=[jax.ShapeDtypeStruct(queries.shape, BF16)] * 3,
        compiler_params=FULL_VMEM,
        cost_estimate=CHEAP,
        name="self_backward",
    )(seg[:, None, :], seg[:, :, None], queries, keys, values, grad_mixed, lse_rows)


def cross_fwd_kernel(map_ref, len_ref, seg_row, seg_col, q_ref, k_ref, v_ref, o_ref, lse_ref):
    r, page = pl.program_id(0), pl.program_id(1)
    keys, toks = k_ref.shape[1], q_ref.shape[0]
    valid = lax.broadcasted_iota(jnp.int32, (keys, 2 * toks), 0) < len_ref[r * 2 + page]
    mine_col = (seg_col[0] == page) | (page == 0)
    mine_row = (seg_row[0] == page) | (page == 0)
    mine_row = jnp.concatenate((mine_row, mine_row), axis=1)

    def put(h, mixed, lse):
        o_ref[:, CUTS[h]] = jnp.where(mine_col, mixed, o_ref[:, CUTS[h]])
        lse_ref[0, h : h + 1, :] = jnp.where(mine_row, lse, lse_ref[0, h : h + 1, :])

    heads_forward(columns_in(q_ref), memory_columns(k_ref), memory_columns(v_ref), valid, put)


def cross_bwd_kernel(
    map_ref, len_ref, seg_row, seg_col, q_ref, k_ref, v_ref, do_ref, lse_ref,
    dq_ref, dk_ref, dv_ref, sum_ref,
):
    r, page = pl.program_id(0), pl.program_id(1)
    keys, toks = k_ref.shape[1], q_ref.shape[0]
    valid = lax.broadcasted_iota(jnp.int32, (keys, 2 * toks), 0) < len_ref[r * 2 + page]
    mine_col = (seg_col[0] == page) | (page == 0)
    mine_row = seg_row[0] == page
    mine_row = jnp.concatenate((mine_row, mine_row), axis=1)

    def put(h, grad_q, grad_k, grad_v):
        cut = CUTS[h]
        dq_ref[:, cut] = jnp.where(mine_col, grad_q, dq_ref[:, cut])
        dk_ref[0, :, cut] = grad_k
        dv_ref[0, :, cut] = grad_v
        before = jnp.where(r + page == 0, jnp.zeros((1, 128), F32), sum_ref[:, cut])
        sum_ref[:, cut] = before + jnp.sum(grad_v.astype(F32), axis=0, keepdims=True)

    heads_backward(
        columns_in(q_ref), memory_columns(k_ref), memory_columns(v_ref), columns_in(do_ref),
        lambda h: jnp.where(mine_row, lse_ref[0, h : h + 1, :], -NEG_FILL), valid, put,
    )


def cross_specs(row_len, mem_len):
    seg = [
        pl.BlockSpec((1, 1, row_len), lambda r, p, *_: (r, 0, 0)),
        pl.BlockSpec((1, row_len, 1), lambda r, p, *_: (r, 0, 0)),
    ]
    row = pl.BlockSpec((row_len, D), lambda r, p, *_: (r, 0))
    mem = pl.BlockSpec((1, mem_len, D), lambda r, p, mp, ln: (mp[r * 2 + p], 0, 0))
    lse = pl.BlockSpec((1, PAIRS, 2 * row_len), lambda r, p, *_: (r, 0, 0))
    return seg, row, mem, lse


def cross_forward(local_map, lengths, seg, queries, keys, values):
    rows, row_len = seg.shape
    mem_len = keys.shape[1]
    seg_specs, row, mem, lse = cross_specs(row_len, mem_len)
    return pl.pallas_call(
        cross_fwd_kernel,
        grid_spec=pltpu.PrefetchScalarGridSpec(
            num_scalar_prefetch=2,
            grid=(rows, 2),
            in_specs=seg_specs + [row, mem, mem],
            out_specs=[row, lse],
        ),
        out_shape=[
            jax.ShapeDtypeStruct(queries.shape, BF16),
            jax.ShapeDtypeStruct((rows, PAIRS, 2 * row_len), F32),
        ],
        compiler_params=FULL_VMEM,
        cost_estimate=CHEAP,
        name="cross_forward",
    )(local_map, lengths, seg[:, None, :], seg[:, :, None], queries, keys, values)


def cross_backward(local_map, lengths, seg, queries, keys, values, grad_mixed, lse_rows):
    rows, row_len = seg.shape
    mem_len = keys.shape[1]
    seg_specs, row, mem, lse = cross_specs(row_len, mem_len)
    return pl.pallas_call(
        cross_bwd_kernel,
        grid_spec=pltpu.PrefetchScalarGridSpec(
            num_scalar_prefetch=2,
            grid=(rows, 2),
            in_specs=seg_specs + [row, mem, mem, row, lse],
            out_specs=[row, mem, mem, pl.BlockSpec((1, D), lambda r, p, *_: (0, 0))],
        ),
        out_shape=[
            jax.ShapeDtypeStruct(queries.shape, BF16),
            jax.ShapeDtypeStruct(keys.shape, BF16),
            jax.ShapeDtypeStruct(values.shape, BF16),
            jax.ShapeDtypeStruct((1, D), F32),
        ],
        compiler_params=FULL_VMEM,
        cost_estimate=CHEAP,
        name="cross_backward",
    )(local_map, lengths, seg[:, None, :], seg[:, :, None], queries, keys, values, grad_mixed, lse_rows)


SMALL_ROWS = 16


def tie(values, *after):
    return lax.optimization_barrier((values, after))[0]


class Clock:
    def __init__(self):
        self.last = ()

    def now(self, values):
        return tie(values, *self.last) if self.last else values

    def tick(self, *arrays):
        self.last = arrays


class Grid:
    def __init__(self, wide, narrow):
        self.wide, self.narrow, self.ring = wide, narrow, wide // 2
        self.devices = wide * narrow
        moves = {
            "z": lambda w, n: ((w + 2) % wide, n),
            "x": lambda w, n: (w ^ 1, n),
            "y": lambda w, n: (w, n ^ 2),
            "c": lambda w, n: (w, n ^ 1),
        }
        self.perms = {}
        for name, move in moves.items():
            pairs = []
            for w in range(wide):
                for n in range(narrow):
                    w2, n2 = move(w, n)
                    pairs.append((w * narrow + n, w2 * narrow + n2))
            self.perms[name] = pairs
        self.clock = Clock()

    def send(self, name, array):
        return lax.ppermute(self.clock.now(array), AXES, self.perms[name])


def segments(first, height, g, rows):
    out, at, end = [], first, first + height
    while at < end:
        k = min(at // rows, g)
        stop = min(end, (k + 1) * rows) if k < g else end
        out.append((k, at - k * rows, at - first, stop - at))
        at = stop
    return out


def half_kernel(parts, ring, wide, g, rows, place, *refs):
    *arrays, out = refs
    z, x, y = place[0], place[1], place[2]
    height = wide * rows
    for which, first_row, count, offset, labels in parts:
        for i, (dz, dx, dy) in enumerate(labels):
            row = 2 * lax.rem(z + (ring - dz), ring) + (x + dx - 2 * x * dx)
            col = y + dy - 2 * y * dy
            for k, matrix_row, at, n in segments(offset, count, g, rows):
                each = rows if k < g else SMALL_ROWS
                first = pl.multiple_of(k * height + row * each + matrix_row, 16)
                out[col, pl.ds(first, n)] = arrays[which][i, pl.ds(first_row + at, n)]


def anywhere(count):
    return [pl.BlockSpec(memory_space=pl.ANY)] * count


PLACE = pl.BlockSpec(memory_space=pltpu.SMEM)


def rearrange_kernel(moves, n_in, *refs):
    ins, outs = refs[:n_in], refs[n_in:]
    for i, bi, ri, ci, rows, o, bo, ro in moves:
        cols = outs[o].shape[-1]
        outs[o][bo, pl.ds(ro, rows)] = ins[i][bi, pl.ds(ri, rows), pl.ds(ci, cols)]


class Rearrange:
    def __init__(self):
        self.ins, self.shapes, self.moves = [], [], []

    def source(self, array):
        for i, known in enumerate(self.ins):
            if known is array:
                return i
        self.ins.append(array)
        return len(self.ins) - 1

    def out(self, blocks, rows, cols):
        self.shapes.append((blocks, rows, cols))
        return len(self.shapes) - 1

    def move(self, out, block, row, array, from_block, first, rows, column=0):
        self.moves.append((self.source(array), from_block, first, column, rows, out, block, row))

    def run(self, clock):
        outs = pl.pallas_call(
            functools.partial(rearrange_kernel, self.moves, len(self.ins)),
            in_specs=[pl.BlockSpec(memory_space=pltpu.VMEM)] * len(self.ins),
            out_specs=[pl.BlockSpec(memory_space=pltpu.VMEM)] * len(self.shapes),
            out_shape=[jax.ShapeDtypeStruct(shape, BF16) for shape in self.shapes],
            compiler_params=SMALL_VMEM,
            cost_estimate=CHEAP,
            name="rearrange",
        )(*clock.now(self.ins))
        return list(outs)


class Gather:
    def __init__(self, grid, place, g, height, cols, small=False):
        self.grid, self.place, self.g, self.height, self.cols = grid, place, g, height, cols
        self.rows = (height - (SMALL_ROWS if small else 0)) // g
        self.parts = []

    def put(self, labels, array, first_row, count, offset):
        self.parts.append((labels, array, first_row, count, offset))

    def half(self, *after):
        grid, arrays, parts = self.grid, [], []
        for labels, array, first_row, count, offset in self.parts:
            which = [i for i, known in enumerate(arrays) if known is array]
            if not which:
                arrays.append(array)
                which = [len(arrays) - 1]
            parts.append((which[0], first_row, count, offset, labels))
        self.own = pl.pallas_call(
            functools.partial(half_kernel, parts, grid.ring, grid.wide, self.g, self.rows),
            in_specs=[PLACE] + [pl.BlockSpec(memory_space=pltpu.VMEM)] * len(arrays),
            out_specs=pl.BlockSpec(memory_space=pltpu.VMEM),
            out_shape=jax.ShapeDtypeStruct((2, grid.wide * self.height, self.cols), BF16),
            compiler_params=SMALL_VMEM,
            cost_estimate=CHEAP,
            name="half_weights",
        )(self.place, *tie(grid.clock.now(arrays), *after))
        return self.own

    def swap(self):
        self.other = self.grid.send("c", self.own)
        return self.other

    def small_rows(self):
        first = self.g * self.grid.wide * self.rows
        own, other = self.grid.clock.now((self.own[:, first:], self.other[:, first:]))
        flip = self.place[3] == 0
        both = jnp.stack((jnp.where(flip, own, other), jnp.where(flip, other, own)))
        return both.reshape(2, 2, self.grid.wide, SMALL_ROWS, -1).astype(F32)


class Square:
    def __init__(self, gather, blocks, height, offset=0):
        self.gather, self.blocks, self.height, self.offset = gather, blocks, height, offset
        self.cut = height // 32 * 16

    def labels(self, dx, dy):
        return [(dz, dx, dy) for dz in range(len(self.blocks))]


def exchange(grid, before, after):
    make = Rearrange()
    cols = (before or after).gather.cols
    depth = len((before or after).blocks)
    heights = [0, 0]
    if before:
        heights = [before.cut, before.height - before.cut]
    total = [h + (after.height if after else 0) for h in heights]
    outs = [make.out(depth, h, cols) for h in total]
    if before:
        (near_x, x_first), (near_y, y_first) = before.near
        for k in range(depth):
            make.move(outs[0], k, 0, near_y, k, y_first, heights[0])
            make.move(outs[1], k, 0, near_x, k, x_first + before.cut, heights[1])
    if after:
        for out, first in zip(outs, heights):
            for k, pieces in enumerate(after.blocks):
                at = first
                for array, block, row, count, column in pieces:
                    make.move(out, k, at, array, block, row, count, column)
                    at += count
    send_x, send_y = make.run(grid.clock)
    from_x, from_y = grid.send("x", send_x), grid.send("y", send_y)
    if before:
        before.gather.put(before.labels(1, 1), from_x, 0, heights[0], before.offset)
        before.gather.put(before.labels(1, 1), from_y, 0, heights[1], before.offset + before.cut)
    if after:
        after.near = ((from_x, heights[0]), (from_y, heights[1]))
        put = after.gather.put
        put(after.labels(0, 0), send_x, heights[0], after.height, after.offset)
        put(after.labels(1, 0), from_x, heights[0], after.height, after.offset)
        put(after.labels(0, 1), from_y, heights[1], after.height, after.offset)
    return from_x, from_y


def unfold(small, count, start, width):
    part = small[:, :, :, :count, start : start + width]
    return part.transpose(3, 2, 1, 0, 4).reshape(count, -1)


def corners(place):
    y, c = place[2], place[3]
    return (2 * y + 1 - c, 2 * (1 - y) + 1 - c), (2 * y + c, 2 * (1 - y) + c)


def column(ref, n, cols):
    return ref[:, pl.ds(pl.multiple_of(n * cols, 128), cols)]


def both_columns(ref, blocks, cols):
    return jnp.concatenate([column(ref, n, cols) for n in blocks], axis=1)


def far_kernel(place, *refs):
    out = refs[-1]
    cols = out.shape[-1]
    for i in range(out.shape[0]):
        a, d = refs[2 * i], refs[2 * i + 1]
        term = dot_tn(a[...], both_columns(d, corners(place)[0], cols))
        for j in range(2):
            out[i, j] = term[:, j * cols : (j + 1) * cols].astype(BF16)


def put_quadrants(x, scratch, k, i, here, outs):
    dx, dy, qx, qy, own = outs
    rows = own.shape[2]
    if here:
        own[k, i] = scratch[k, x]
        qx[k, i] = scratch[k, 1 - x].astype(BF16)
    else:
        qy[k, i] = scratch[k, x].astype(BF16)
        dx[k, i] = scratch[k, 1 - x, pl.ds(0, rows // 2)].astype(BF16)
        dy[k, i] = scratch[k, 1 - x, pl.ds(rows // 2, rows // 2)].astype(BF16)


def near_kernel(place, *refs):
    from_c, *outs, scratch = refs[-7:]
    zs, units, rows, cols = outs[-1].shape
    for i in range(units):
        a, d = refs[2 * i], refs[2 * i + 1]
        term = dot_tn(a[...], both_columns(d, corners(place)[1], cols))
        for j in range(2):
            part = term[:, j * cols : (j + 1) * cols] + from_c[i, j].astype(F32)
            scratch[...] = part.reshape(scratch.shape)
            for k in range(zs):
                put_quadrants(place[1], scratch, k, i, j == 0, outs)


def quadrant_shapes(units, ring, rows, cols):
    half, full = (ring, units, rows // 2, cols), (ring, units, rows, cols)
    return [jax.ShapeDtypeStruct(half, BF16)] * 2 + [
        jax.ShapeDtypeStruct(full, BF16), jax.ShapeDtypeStruct(full, BF16), jax.ShapeDtypeStruct(full, F32)
    ]


def quadrant_specs(units, zs, rows, cols, stepped):
    def at(s, *_):
        return (s if stepped else 0, 0, 0, 0)

    half = pl.BlockSpec((zs, units, rows // 2, cols), at)
    full = pl.BlockSpec((zs, units, rows, cols), at)
    return [half] * 2 + [full] * 3


def token_terms(grid, place, pairs, rows, cols, from_c=None, params=FULL_VMEM):
    units, tokens = len(pairs), pairs[0][0].shape[0]
    height = grid.wide * rows
    zs = max(1, 128 // (2 * rows))
    if 2 * rows >= 128 and height // (2 * rows) > 1 and rows * cols <= 128 * 256:
        zs = min(grid.ring, 2)
    tall = zs * 2 * rows
    in_specs, args = [], []
    for a, d in pairs:
        in_specs += [
            pl.BlockSpec((tokens, tall), lambda s, *_: (0, s)),
            pl.BlockSpec(d.shape, lambda s, *_: (0, 0)),
        ]
        args += [a, d]
    block = pl.BlockSpec((units, 2, tall, cols), lambda s, *_: (0, 0, s, 0))
    scratch = []
    if from_c is None:
        kernel, out_specs = far_kernel, block
        out_shape = jax.ShapeDtypeStruct((units, 2, height, cols), BF16)
    else:
        in_specs.append(block)
        args.append(from_c)
        kernel = near_kernel
        out_specs = quadrant_specs(units, zs, rows, cols, True)
        out_shape = quadrant_shapes(units, grid.ring, rows, cols)
        scratch = [pltpu.VMEM((zs, 2, rows, cols), F32)]
    return pl.pallas_call(
        kernel,
        grid_spec=pltpu.PrefetchScalarGridSpec(
            num_scalar_prefetch=1,
            grid=(height // tall,),
            in_specs=in_specs,
            out_specs=out_specs,
            scratch_shapes=scratch,
        ),
        out_shape=out_shape,
        compiler_params=params,
        cost_estimate=CHEAP,
        name="weight_terms",
    )(place, *args)


def memory_terms_kernel(near, pairs, place, mem, dk, dv, *refs):
    tokens, refs = refs[: 2 * pairs], refs[2 * pairs :]
    if near:
        from_c, dx, dy, qx, qy, own, acc = refs
    else:
        out, acc = refs
    cols = acc.shape[-1]
    m = pl.program_id(0)
    blocks = corners(place)[1 if near else 0]

    @pl.when(m == 0)
    def _():
        for i in range(pairs):
            term = dot_tn(tokens[2 * i][...], both_columns(tokens[2 * i + 1], blocks, cols))
            for j in range(2):
                acc[i, j] = term[:, j * cols : (j + 1) * cols].reshape(acc.shape[2:])
        acc[pairs:] = jnp.zeros_like(acc[pairs:])
        if near:
            acc[...] += from_c[...].astype(F32).reshape(acc.shape)

    grads = jnp.concatenate([both_columns(d.at[0], blocks, cols) for d in (dk, dv)], axis=1)
    term = dot_tn(mem[0], grads)
    for q in range(4):
        part = term[:, q * cols : (q + 1) * cols].reshape(acc.shape[2:])
        acc[pairs + q // 2, q % 2] += part

    @pl.when(m == pl.num_programs(0) - 1)
    def _():
        if near:
            x = place[1]
            for i in range(pairs + 2):
                for j in range(2):
                    for k in range(own.shape[0]):
                        put_quadrants(x, acc.at[i, j], k, i, j == 0, (dx, dy, qx, qy, own))
        else:
            out[...] = acc[...].reshape(out.shape).astype(BF16)


def memory_terms(grid, place, memory, grads, pairs, rows, cols, from_c=None):
    units, (mems, length, wide_cols) = len(pairs) + 2, memory.shape
    height = grid.wide * rows
    near = from_c is not None
    one = pl.BlockSpec((1, length, wide_cols), lambda m, *_: (m, 0, 0))
    term = pl.BlockSpec((units, 2, height, cols), lambda m, *_: (0, 0, 0, 0))
    tokens = [array for pair in pairs for array in pair]
    return pl.pallas_call(
        functools.partial(memory_terms_kernel, near, len(pairs)),
        grid_spec=pltpu.PrefetchScalarGridSpec(
            num_scalar_prefetch=1,
            grid=(mems,),
            in_specs=[one] * 3
            + [pl.BlockSpec(a.shape, lambda m, *_: (0, 0)) for a in tokens]
            + ([term] if near else []),
            out_specs=quadrant_specs(units, grid.ring, rows, cols, False) if near else term,
            scratch_shapes=[pltpu.VMEM((units, 2, grid.ring, 2, rows, cols), F32)],
        ),
        out_shape=quadrant_shapes(units, grid.ring, rows, cols)
        if near
        else jax.ShapeDtypeStruct((units, 2, height, cols), BF16),
        compiler_params=FULL_VMEM,
        cost_estimate=CHEAP,
        name="memory_terms",
    )(place, memory, *grads, *tokens, *([from_c] if near else []))


def add_corners_kernel(qx, qy, from_x, from_y, sx, sy):
    half = from_x.shape[2]
    first, second = pl.ds(0, half), pl.ds(half, half)
    sx[0, :, first] = qx[0, :, first]
    sx[0, :, second] = (qx[0, :, second].astype(F32) + from_y[0].astype(F32)).astype(BF16)
    sy[0, :, first] = (qy[0, :, first].astype(F32) + from_x[0].astype(F32)).astype(BF16)
    sy[0, :, second] = qy[0, :, second]


def add_corners(qx, qy, from_x, from_y):
    ring, units, rows, cols = qx.shape
    full = pl.BlockSpec((1, units, rows, cols), lambda k: (k, 0, 0, 0))
    half = pl.BlockSpec((1, units, rows // 2, cols), lambda k: (k, 0, 0, 0))
    return pl.pallas_call(
        add_corners_kernel,
        grid=(ring,),
        in_specs=[full, full, half, half],
        out_specs=[full, full],
        out_shape=[jax.ShapeDtypeStruct(qx.shape, BF16)] * 2,
        compiler_params=FULL_VMEM,
        cost_estimate=CHEAP,
        name="add_corners",
    )(qx, qy, from_x, from_y)


class Reduce:
    def __init__(self, grid, place, terms, rows):
        self.grid, self.place, self.terms, self.rows = grid, place, terms, rows

    def far(self):
        self.out = self.terms(None)
        return self.out

    def swap(self):
        self.from_c = self.grid.send("c", self.out)
        return self.from_c

    def near(self):
        self.dx, self.dy, self.qx, self.qy, self.own = self.terms(self.grid.clock.now(self.from_c))
        return self.dx

    def across(self):
        self.from_x, self.from_y = self.grid.send("x", self.dx), self.grid.send("y", self.dy)
        return self.from_x, self.from_y

    def add(self):
        from_x = self.grid.clock.now(self.from_x)
        self.sx, self.sy = add_corners(self.qx, self.qy, from_x, self.from_y)
        return self.sx

    def pairs(self):
        self.back_x, self.back_y = self.grid.send("x", self.sx), self.grid.send("y", self.sy)
        return self.back_x, self.back_y

    def chunk(self, step):
        index = lax.rem(self.place[0] + (self.grid.ring - step), self.grid.ring)
        parts = [
            lax.dynamic_index_in_dim(a, index, 0, keepdims=False)
            for a in self.grid.clock.now((self.own, self.back_x, self.back_y))
        ]
        return parts[0] + parts[1].astype(F32) + parts[2].astype(F32)


class RingSum:
    def __init__(self, grid, reduces):
        self.grid, self.reduces, self.done, self.came = grid, reduces, 0, None

    def step(self, *after):
        self.done += 1
        total = jnp.concatenate([r.chunk(self.done % self.grid.ring) for r in self.reduces], axis=0)
        if self.came is not None:
            total = total + tie(self.grid.clock.now(self.came), *after).astype(F32)
        if self.done == self.grid.ring:
            self.came = total
        else:
            self.came = self.grid.send("z", total.astype(BF16))
        return self.came


class SmallSum:
    def __init__(self, grid, place, terms):
        self.grid, self.place, self.done, self.came = grid, place, 0, None
        self.mine = terms.reshape(grid.ring, 2, 2, 2, -1)
        self.steps = grid.ring + 2

    def pair(self, name, axis, at):
        far = lax.dynamic_index_in_dim(self.mine, 1 - at, axis, keepdims=False)
        self.came = self.grid.send(name, far)
        self.near = lax.dynamic_index_in_dim(self.mine, at, axis, keepdims=False)

    def settle(self, *after):
        if self.came is not None:
            came = tie(self.came, *after) if after else self.came
            self.mine = self.near + came

    def step(self, *after):
        grid, place = self.grid, self.place
        if self.done == 0:
            self.pair("c", 3, place[3])
        elif self.done < grid.ring:
            if self.done == 1:
                self.settle(*after)
            index = lax.rem(place[0] + (grid.ring - self.done), grid.ring)
            total = lax.dynamic_index_in_dim(self.mine, index, 0, keepdims=False)
            if self.done > 1:
                total = total + (tie(self.came, *after) if after else self.came)
            self.came = grid.send("z", total)
            self.near = lax.dynamic_index_in_dim(self.mine, place[0], 0, keepdims=False)
        else:
            self.settle(*after)
            if self.done == grid.ring:
                self.pair("y", 1, place[2])
            else:
                self.pair("x", 0, place[1])
        self.done += 1
        return self.came

    def result(self):
        return self.near + self.came


def halves(place, own, other):
    c = place[3]
    return [(2 * y + core, y, half) for half, core in ((own, c), (other, 1 - c)) for y in range(2)]


def at_block(n, cols):
    return pl.ds(pl.multiple_of(n * cols, 128), cols)


def times_t(place, d, own, other):
    cols = own.shape[-1]
    return sum(dot_nt(d[:, at_block(n, cols)], half[y]) for n, y, half in halves(place, own, other))


def norm_parts(values):
    centre = values - jnp.mean(values, axis=-1, keepdims=True)
    scale = lax.rsqrt(jnp.mean(centre * centre, axis=-1, keepdims=True) + EPSILON)
    return centre * scale, scale


def norm_back(normed, scale, gain, grad):
    inner = grad * gain
    back = scale * (
        inner
        - jnp.mean(inner, axis=-1, keepdims=True)
        - normed * jnp.mean(inner * normed, axis=-1, keepdims=True)
    )
    return back, jnp.sum(grad * normed, axis=0, keepdims=True), jnp.sum(grad, axis=0, keepdims=True)


def column_sum(values):
    return jnp.sum(values.astype(F32), axis=0, keepdims=True)


GAIN, BIAS = 0, 3


def row(vectors, i):
    return vectors[i : i + 1, :]


def memory_kernel(place, mem, vectors, k_own, k_other, v_own, v_other, keys, values):
    cols = k_own.shape[-1]
    for n, y, half in halves(place, k_own, k_other):
        keys[0, :, at_block(n, cols)] = dot_nn(mem[0], half[y]).astype(BF16)
    for n, y, half in halves(place, v_own, v_other):
        bias = vectors[BIAS + 6 : BIAS + 7, at_block(n, cols)]
        values[0, :, at_block(n, cols)] = (dot_nn(mem[0], half[y]) + bias).astype(BF16)


def qkv_kernel(place, tokens, vectors, *refs):
    weights, (normed, q, k, v) = refs[:6], refs[6:]
    n, _ = norm_parts(tokens[...].astype(F32))
    normed[...] = (n * row(vectors, GAIN) + row(vectors, BIAS)).astype(BF16)
    cols = weights[0].shape[-1]
    for i, (out, bias_at) in enumerate(((q, 1), (k, None), (v, 2))):
        for n, y, half in halves(place, weights[2 * i], weights[2 * i + 1]):
            term = dot_nn(normed[...], half[y])
            if bias_at is not None:
                term = term + vectors[BIAS + bias_at : BIAS + bias_at + 1, at_block(n, cols)]
            out[:, at_block(n, cols)] = term.astype(BF16)


def middle_kernel(place, tokens, mixed, vectors, so_own, so_other, cq_own, cq_other, after, normed, queries):
    cols = so_own.shape[-1]
    for n, y, half in halves(place, so_own, so_other):
        at = at_block(n, cols)
        after[:, at] = tokens[:, at].astype(F32) + dot_nn(mixed[...], half[y]) + vectors[BIAS + 3 : BIAS + 4, at]
    n, _ = norm_parts(after[...])
    normed[...] = (n * row(vectors, GAIN + 1) + row(vectors, BIAS + 4)).astype(BF16)
    for n, y, half in halves(place, cq_own, cq_other):
        at = at_block(n, cols)
        queries[:, at] = (dot_nn(normed[...], half[y]) + vectors[BIAS + 5 : BIAS + 6, at]).astype(BF16)


def cross_out_kernel(place, before, mixed, vectors, own, other, after, normed):
    cols = own.shape[-1]
    for n, y, half in halves(place, own, other):
        at = at_block(n, cols)
        after[:, at] = before[:, at] + dot_nn(mixed[...], half[y]) + vectors[BIAS + 7 : BIAS + 8, at]
    n, _ = norm_parts(after[...])
    normed[...] = (n * row(vectors, GAIN + 2) + row(vectors, BIAS + 8)).astype(BF16)


def up_kernel(place, normed, bias, own, other, act, slope):
    c, cols = place[3], own.shape[-1]
    y = pl.program_id(0)
    for n, half in ((2 * y + c, own), (2 * y + 1 - c, other)):
        for j in range(4):
            at = at_block(4 * n + j, cols)
            u = dot_nn(normed[...], half[0, j * D : (j + 1) * D]) + bias[:, at]
            below = 0.5 * (1.0 + lax.erf(u * (1.0 / math.sqrt(2.0))))
            act[:, at] = (u * below).astype(BF16)
            slope[:, at] = (below + u * jnp.exp(-0.5 * u * u) * (1.0 / math.sqrt(2.0 * math.pi))).astype(BF16)


def down_kernel(place, after, act, vectors, own, other, out):
    c, y = place[3], pl.program_id(0)
    cols = own.shape[-1]
    for n, half in ((2 * y + c, own), (2 * y + 1 - c, other)):
        at = at_block(n, cols)
        total = after[:, at] + dot_nn(act[...], half[0]) + vectors[BIAS + 9 : BIAS + 10, at]
        out[:, at] = total.astype(BF16)


def down_back_kernel(place, grad, slope, normed, own, other, grad_pre, bias_grad, far):
    back = (times_t(place, grad, own, other) * slope[...].astype(F32)).astype(BF16)
    grad_pre[...] = back
    bias_grad[...] = column_sum(back)
    for i, n in enumerate(corners(place)[0]):

        @pl.when(pl.program_id(0) == n)
        def _():
            far[0, i] = dot_tn(normed[...], back).astype(BF16)


def up_back_kernel(
    place, grad_pre, grad_out, after, vectors, own, other, co_own, co_other,
    grad, branch, mixed, gain_grad, shift_grad, out_grad, last_grad, total,
):
    c, y = place[3], pl.program_id(0)
    cols = own.shape[-1]
    term = sum(
        dot_nt(grad_pre[:, at_block(4 * n + j, cols)], half[0, j * D : (j + 1) * D])
        for n, half in ((2 * y + c, own), (2 * y + 1 - c, other))
        for j in range(4)
    )

    @pl.when(y == 0)
    def _():
        total[...] = term

    @pl.when(y == 1)
    def _():
        n, scale = norm_parts(after[...])
        back, gain_grad[...], shift_grad[...] = norm_back(n, scale, row(vectors, GAIN + 2), total[...] + term)
        out = grad_out[...].astype(F32) + back
        grad[...] = out
        branch[...] = out.astype(BF16)
        out_grad[...] = column_sum(branch[...])
        last_grad[...] = column_sum(grad_out[...])
        mixed[...] = times_t(place, branch, co_own, co_other).astype(BF16)


def middle_back_kernel(
    place, grad_queries, grad_after, after, vectors, cq_own, cq_other, so_own, so_other,
    grad, branch, mixed, gain_grad, shift_grad, out_grad, query_grad,
):
    n, scale = norm_parts(after[...])
    dense = times_t(place, grad_queries, cq_own, cq_other)
    back, gain_grad[...], shift_grad[...] = norm_back(n, scale, row(vectors, GAIN + 1), dense)
    out = grad_after[...] + back
    grad[...] = out
    branch[...] = out.astype(BF16)
    out_grad[...] = column_sum(branch[...])
    query_grad[...] = column_sum(grad_queries[...])
    mixed[...] = times_t(place, branch, so_own, so_other).astype(BF16)


def first_back_kernel(place, tokens, grad_after, gq, gk, gv, vectors, *refs):
    weights, (grad, gain_grad, shift_grad, query_grad, value_grad) = refs[:6], refs[6:]
    n, scale = norm_parts(tokens[...].astype(F32))
    dense = sum(
        times_t(place, d, weights[2 * i], weights[2 * i + 1]) for i, d in enumerate((gq, gk, gv))
    )
    back, gain_grad[...], shift_grad[...] = norm_back(n, scale, row(vectors, GAIN), dense)
    grad[...] = (grad_after[...] + back).astype(BF16)
    query_grad[...] = column_sum(gq[...])
    value_grad[...] = column_sum(gv[...])


def memory_back_kernel(place, gk, gv, k_own, k_other, v_own, v_other, grad):
    total = times_t(place, gk.at[0], k_own, k_other) + times_t(place, gv.at[0], v_own, v_other)
    grad[0] = total.astype(BF16)


def in_place(array):
    return pl.pallas_call(
        lambda _, out: None,
        in_specs=anywhere(1),
        out_specs=pl.BlockSpec(memory_space=pl.ANY),
        out_shape=jax.ShapeDtypeStruct(array.shape, array.dtype),
        input_output_aliases={0: 0},
        compiler_params=BIG_VMEM,
        cost_estimate=CHEAP,
        name="in_place",
    )(array)


def dense_call(kernel, name, place, ins, outs, grid=(1,), scratch=(), params=BIG_VMEM):
    def spec(array, block, index):
        block = block or array.shape
        zeros = (0,) * len(block)
        return pl.BlockSpec(block, index or (lambda *_: zeros))

    return pl.pallas_call(
        kernel,
        grid_spec=pltpu.PrefetchScalarGridSpec(
            num_scalar_prefetch=1,
            grid=grid,
            in_specs=[spec(*one) for one in ins],
            out_specs=[spec(*one) for one in outs],
            scratch_shapes=scratch,
        ),
        out_shape=[one[0] for one in outs],
        compiler_params=params,
        cost_estimate=CHEAP,
        name=name,
    )(place, *[one[0] for one in ins])


def full(array):
    return (array, None, None)


def result(shape, dtype):
    return (jax.ShapeDtypeStruct(shape, dtype), None, None)


def matrix(gathered, i, height=D):
    block = (2, height, gathered.own.shape[-1])
    return [(half, block, lambda *_: (0, i, 0)) for half in (gathered.own, gathered.other)]


def by_y(gathered):
    block = (1,) + gathered.own.shape[1:]
    return [(half, block, lambda y, *_: (y, 0, 0)) for half in (gathered.own, gathered.other)]


def by_rows(gathered, rows):
    block = (2, rows, gathered.own.shape[-1])
    return [(half, block, lambda s, *_: (0, s, 0)) for half in (gathered.own, gathered.other)]


def local(
    shape,
    tokens,
    memory,
    segment_ids,
    page_map,
    mem_lengths,
    gains,
    biases,
    fc1_bias,
    self_qkv,
    self_out,
    cross_q,
    cross_kv,
    cross_out,
    fc1,
    fc2,
    cotangent,
):
    grid = Grid(*shape)
    wide_at, narrow_at = lax.axis_index("wide"), lax.axis_index("narrow")
    place = jnp.stack((wide_at // 2, wide_at % 2, narrow_at // 2, narrow_at % 2)).astype(jnp.int32)
    devices = grid.devices
    mem_count, token_count = memory.shape[0], tokens.shape[0]
    rows, cols = self_out.shape

    each, up_each = gains.shape[1], fc1_bias.size
    n_gain, n_bias = gains.size, biases.size
    small = jnp.pad(
        jnp.concatenate((gains, biases), axis=0), ((0, SMALL_ROWS - 13), (0, cols - each))
    )
    small = lax.dynamic_update_slice(small, fc1_bias[None], (0, 128))
    send, clock = grid.send, grid.clock
    now, tick = clock.now, clock.tick
    steps = grid.ring - 1
    gather = functools.partial(Gather, grid, place)
    ckv_height = 2 * rows + SMALL_ROWS
    fc2_rows = fc2.shape[0]
    part = fc2_rows // 2
    g_ckv = gather(2, ckv_height, cols, True)
    g_qkv = gather(3, 3 * rows, cols)
    g_mix = gather(3, 3 * rows, cols)
    g_fc1 = gather(4, 4 * rows, cols)
    g_fc2 = gather(1, fc2_rows, cols)

    start = Rearrange()
    out = start.out(1, 5 * rows, cols)
    for k, (array, i) in enumerate(((cross_kv, 0), (cross_kv, 1), (self_qkv, 0), (self_qkv, 1), (self_qkv, 2))):
        start.move(out, 0, k * rows, array, i, 0, rows)
    ring_one = start.run(clock)
    ring_one.append(send("z", ring_one[-1]))
    ring_small = [small[None]]
    ring_small.append(send("z", ring_small[-1]))
    top = Square(g_fc2, [[(fc2[None], 0, 0, part, 0)]], part)
    more = Rearrange()
    out = more.out(1, 3 * rows, cols)
    for k, array in enumerate((self_out, cross_q, cross_out)):
        more.move(out, 0, k * rows, array[None], 0, 0, rows)
    out = more.out(1, 4 * rows + part, cols)
    for k in range(4):
        more.move(out, 0, k * rows, fc1[None], 0, 0, rows, k * cols)
    more.move(out, 0, 4 * rows, fc2[None], 0, part, part)
    ring_mix, ring_up = [[array] for array in more.run(clock)]
    came = exchange(grid, None, top)
    tick(ring_one[-1], ring_small[-1], ring_mix[0], ring_up[0])
    ring_one.append(send("z", ring_one[-1]))
    ring_small.append(send("z", ring_small[-1]))
    memory = in_place(now(memory))
    tick(ring_one[-1], ring_small[-1], memory, *came)
    came = exchange(grid, top, None)
    for _ in range(steps - 2):
        ring_one.append(send("z", ring_one[-1]))
        ring_small.append(send("z", ring_small[-1]))
        tick(ring_one[-1], ring_small[-1], *came)

    def from_ring(arrays, first, count):
        return [[(array, 0, first, count, 0)] for array in arrays]

    ckv = Square(
        g_ckv, [a + b for a, b in zip(from_ring(ring_one, 0, 2 * rows), from_ring(ring_small, 0, SMALL_ROWS))],
        ckv_height,
    )
    qkv = Square(g_qkv, from_ring(ring_one, 2 * rows, 3 * rows), 3 * rows)
    ring_mix.append(send("z", ring_mix[-1]))
    ring_up.append(send("z", ring_up[-1]))
    tick(ring_mix[-1], ring_up[-1], *exchange(grid, None, ckv))

    make = Rearrange()
    out = make.out(4, part, cols)
    (_, own, own_at, _, _), (_, by_x, x_at, _, _), (_, by_y_, y_at, _, _), (_, low, _, _, _), (_, high, _, _, _) = g_fc2.parts
    g_fc2.parts = []
    for k, (array, at) in enumerate(((own, own_at), (by_x, x_at), (by_y_, y_at))):
        make.move(out, k, 0, array, 0, at, part)
    make.move(out, 3, 0, low, 0, 0, top.cut)
    make.move(out, 3, top.cut, high, 0, 0, part - top.cut)
    came = exchange(grid, ckv, qkv)
    ring_top = make.run(clock)
    ring_up.append(send("z", ring_up[-1]))
    for _ in range(steps - 1):
        ring_mix.append(send("z", ring_mix[-1]))
    tick(ring_mix[-1], ring_up[-1], ring_top[-1], *came)

    mix = Square(g_mix, from_ring(ring_mix, 0, 3 * rows), 3 * rows)
    came = exchange(grid, qkv, mix)
    for _ in range(steps - 2):
        ring_up.append(send("z", ring_up[-1]))
    ring_top.append(send("z", ring_top[-1]))
    g_ckv.half(g_mix.parts[0][1])
    g_ckv.swap()
    small_all = g_ckv.small_rows()
    vectors = unfold(small_all, 13, 0, each)
    up_bias = unfold(small_all, 1, 128, up_each)
    mem_block = (1,) + memory.shape[1:]
    mem_shape = jax.ShapeDtypeStruct(memory.shape, BF16)

    def by_memory(array):
        return (array, mem_block, lambda m, *_: (m, 0, 0))

    mem_keys, mem_values = dense_call(
        memory_kernel, "memory_keys_values", place,
        [by_memory(now(memory)), full(vectors)] + matrix(g_ckv, 0) + matrix(g_ckv, 1),
        [by_memory(mem_shape), by_memory(mem_shape)], grid=(mem_count,),
    )
    tick(ring_up[-1], ring_top[-1], mem_keys, *came)

    up = Square(g_fc1, from_ring(ring_up, 0, 4 * rows), 4 * rows)
    low = Square(g_fc2, from_ring(ring_up, 4 * rows, part), part, part)
    came = exchange(grid, mix, up)
    ring_top.append(send("z", ring_top[-1]))
    g_qkv.half(g_fc1.parts[0][1])
    g_qkv.swap()
    wide_row = (token_count, D)
    normed_one, self_queries, self_keys, self_values = dense_call(
        qkv_kernel, "self_qkv", place,
        [full(now(tokens)), full(vectors)] + matrix(g_qkv, 0) + matrix(g_qkv, 1) + matrix(g_qkv, 2),
        [result(wide_row, BF16)] * 4,
    )
    self_mixed, self_lse = self_forward(segment_ids, self_queries, self_keys, self_values)
    tick(self_mixed, ring_top[-1], *came)

    came = exchange(grid, up, low)
    g_mix.half(g_fc2.parts[0][1])
    g_mix.swap()
    for _ in range(steps - 2):
        ring_top.append(send("z", ring_top[-1]))
    after_self, normed_two, cross_queries = dense_call(
        middle_kernel, "self_out_cross_q", place,
        [full(tokens), full(now(self_mixed)), full(vectors)] + matrix(g_mix, 0) + matrix(g_mix, 1),
        [result(wide_row, F32), result(wide_row, BF16), result(wide_row, BF16)],
    )
    first_mem = lax.axis_index(AXES) * mem_count
    local_map = (page_map - first_mem).reshape(-1).astype(jnp.int32)
    picks = local_map[:, None] == jnp.arange(mem_count, dtype=jnp.int32)[None, :]
    row_lengths = jnp.sum(jnp.where(picks, mem_lengths[None, :], 0), axis=-1).astype(jnp.int32)
    cross_mixed, cross_lse = cross_forward(
        local_map, row_lengths, segment_ids, cross_queries, mem_keys, mem_values
    )
    tick(cross_mixed, ring_top[-1], *came)

    came = exchange(grid, low, None)
    g_fc1.half()
    g_fc1.swap()
    after_cross, normed_three = dense_call(
        cross_out_kernel, "cross_out", place,
        [full(after_self), full(now(cross_mixed)), full(vectors)] + matrix(g_mix, 2),
        [result(wide_row, F32), result(wide_row, BF16)],
    )
    hidden = up_bias.shape[1]
    activated, slope = dense_call(
        up_kernel, "fc1_gelu", place,
        [full(normed_three), full(up_bias)] + by_y(g_fc1),
        [result((token_count, hidden), BF16)] * 2, grid=(2,),
    )
    tick(activated, *came)
    spread = [(0, 0), (1, 0), (0, 1), (1, 1)]
    for step, array in enumerate(ring_top):
        g_fc2.put([(step, dx, dy) for dx, dy in spread], array, 0, part, 0)

    def settle(pairs, shard, params=FULL_VMEM):
        part_rows, part_cols = shard.shape
        return Reduce(
            grid, place,
            lambda from_c: token_terms(grid, place, pairs, part_rows, part_cols, from_c, params),
            part_rows,
        )

    one_row = result((1, D), F32)
    r_fc2 = settle([(now(activated), cotangent)], fc2, BIG_VMEM)
    r_fc2.far()
    r_fc2.swap()
    g_fc2.half()
    g_fc2.swap()
    tick(r_fc2.near())
    slab = hidden // 4
    some = lambda array: (array, (token_count, slab), lambda s, *_: (0, s))
    grad_pre, grad_up_bias, far_fc1 = dense_call(
        down_back_kernel, "fc2_gelu_back", place,
        [full(now(cotangent)), some(slope), full(normed_three)] + by_rows(g_fc2, slab),
        [
            some(jax.ShapeDtypeStruct((token_count, hidden), BF16)),
            (jax.ShapeDtypeStruct((1, hidden), F32), (1, slab), lambda s, *_: (0, s)),
            result((1, 2, D, slab), BF16),
        ],
        grid=(4,), params=FULL_VMEM,
    )
    r_fc1 = settle([(normed_three, grad_pre)], fc1)
    r_fc1.out = far_fc1
    tick(far_fc1, *r_fc2.across())
    r_fc2.add()
    came = list(r_fc2.pairs())
    r_fc1.swap()
    (
        grad_after_cross, grad_branch_two, grad_cross_mixed,
        grad_gain_three, grad_bias_eight, grad_bias_seven, grad_bias_nine,
    ) = dense_call(
        up_back_kernel, "fc1_norm_back", place,
        [full(tie(now(grad_pre), r_fc2.sx)), full(cotangent), full(after_cross), full(vectors)]
        + by_y(g_fc1) + matrix(g_mix, 2),
        [result(wide_row, F32), result(wide_row, BF16), result(wide_row, BF16)] + [one_row] * 4,
        grid=(2,), scratch=[pltpu.VMEM(wide_row, F32)], params=FULL_VMEM,
    )
    tick(r_fc1.near(), grad_cross_mixed)

    came += r_fc1.across()
    grad_cq, grad_ck, grad_cv, grad_bias_six = cross_backward(
        local_map, row_lengths, segment_ids, cross_queries, mem_keys, mem_values,
        now(grad_cross_mixed), cross_lse,
    )
    r_mem = Reduce(
        grid, place,
        lambda from_c: memory_terms(grid, place, memory, (grad_ck, grad_cv), [], rows, cols, from_c),
        rows,
    )
    tick(grad_cq, r_mem.far(), *came)
    ring_fc2 = RingSum(grid, [r_fc2])
    r_fc1.add()
    r_mem.swap()
    ring_fc2.step()
    grad_cq = tie(now(grad_cq), r_fc1.sx)
    (
        grad_after_self, grad_branch_one, grad_self_mixed,
        grad_gain_two, grad_bias_four, grad_bias_three, grad_bias_five,
    ) = dense_call(
        middle_back_kernel, "cross_q_norm_back", place,
        [full(grad_cq), full(grad_after_cross), full(after_self), full(vectors)]
        + matrix(g_mix, 1) + matrix(g_mix, 0),
        [result(wide_row, F32), result(wide_row, BF16), result(wide_row, BF16)] + [one_row] * 4,
        params=FULL_VMEM,
    )
    grad_sq, grad_sk, grad_sv = self_backward(
        segment_ids, self_queries, self_keys, self_values, grad_self_mixed, self_lse
    )
    r_rest = settle(
        [
            (normed_one, grad_sq), (normed_one, grad_sk), (normed_one, grad_sv),
            (self_mixed, grad_branch_one), (normed_two, grad_cq), (cross_mixed, grad_branch_two),
        ],
        cross_q,
    )
    tick(r_rest.far(), r_mem.near(), ring_fc2.came, *r_fc1.pairs())
    ring_fc1 = RingSum(grid, [r_fc1])
    came = r_mem.across()
    r_rest.swap()
    ring_fc2.step()
    ring_fc1.step()
    grad_tokens, grad_gain_one, grad_bias_zero, grad_bias_one, grad_bias_two = dense_call(
        first_back_kernel, "self_qkv_norm_back", place,
        [full(tokens), full(grad_after_self)] + [full(d) for d in now((grad_sq, grad_sk, grad_sv))]
        + [full(vectors)] + matrix(g_qkv, 0) + matrix(g_qkv, 1) + matrix(g_qkv, 2),
        [result(wide_row, BF16)] + [one_row] * 4,
        params=FULL_VMEM,
    )
    tick(r_rest.near(), grad_tokens, ring_fc2.came, ring_fc1.came, *came)

    def by_device(array):
        return array.reshape(array.shape[0], devices, -1).transpose(1, 0, 2).reshape(devices, -1)

    small_grads = jnp.concatenate(
        (
            by_device(
                jnp.concatenate(
                    (
                        grad_gain_one, grad_gain_two, grad_gain_three,
                        grad_bias_zero, grad_bias_one, grad_bias_two, grad_bias_three, grad_bias_four,
                        grad_bias_five, grad_bias_six, grad_bias_seven, grad_bias_eight, grad_bias_nine,
                    ),
                    axis=0,
                )
            ),
            by_device(grad_up_bias),
        ),
        axis=1,
    )
    small_sum = SmallSum(grid, place, now(small_grads))
    r_mem.add()
    ring_fc2.step()
    (grad_memory,) = dense_call(
        memory_back_kernel, "memory_back", place,
        [by_memory(a) for a in tie(now((grad_ck, grad_cv)), r_mem.sx)] + matrix(g_ckv, 0) + matrix(g_ckv, 1),
        [by_memory(mem_shape)], grid=(mem_count,), params=FULL_VMEM,
    )
    tick(grad_memory, ring_fc2.came, *r_mem.pairs(), *r_rest.across())
    small_sum.step()
    ring_mem = RingSum(grid, [r_mem])
    r_rest.add()
    turned_memory = in_place(tie(now(grad_memory).transpose(1, 0, 2), r_rest.sx))
    grad_memory = turned_memory.transpose(1, 0, 2)
    ring_fc1.step()
    ring_mem.step()
    for _ in range(steps):
        small_sum.step()
    (layer_out,) = dense_call(
        down_kernel, "fc2", place,
        [full(after_cross), full(tie(now(activated), turned_memory)), full(vectors)] + by_y(g_fc2),
        [result(wide_row, BF16)], grid=(2,), params=FULL_VMEM,
    )
    ring_fc1.step(turned_memory)
    ring_mem.step(turned_memory)
    tick(turned_memory, layer_out, small_sum.came, ring_fc1.came, ring_mem.came, *r_rest.pairs())
    ring_fc2.step()
    ring_rest = RingSum(grid, [r_rest])
    ring_rest.step()
    ring_fc1.step()
    ring_mem.step()
    small_sum.step()
    tick(ring_rest.came, ring_mem.came, small_sum.came)
    for _ in range(steps - 1):
        ring_mem.step() if ring_mem.done < grid.ring else None
        small_sum.step() if small_sum.done < small_sum.steps else None
        tick(ring_rest.step(), ring_mem.came, small_sum.came)
    for ring in (ring_fc2, ring_fc1, ring_mem, ring_rest):
        while ring.done < grid.ring:
            ring.step()
    while small_sum.done < small_sum.steps:
        small_sum.step()
    came_mem, came_rest = ring_mem.came, ring_rest.came
    small_shard = small_sum.result()
    return (
        layer_out,
        grad_tokens,
        grad_memory,
        small_shard[:n_gain].reshape(gains.shape),
        small_shard[n_gain : n_gain + n_bias].reshape(biases.shape),
        small_shard[n_gain + n_bias :],
        came_rest[:3],
        came_rest[3],
        came_rest[4],
        came_mem,
        came_rest[5],
        ring_fc1.came[0],
        ring_fc2.came[0],
    )


def solution(mesh):
    shape = (mesh.shape["wide"], mesh.shape["narrow"])
    in_specs = (
        P(AXES, None),
        P(AXES, None, None),
        P(AXES, None),
        P(AXES, None),
        P(AXES),
        P(None, AXES),
        P(None, AXES),
        P(AXES),
        P(None, "wide", "narrow"),
        P("wide", "narrow"),
        P("wide", "narrow"),
        P(None, "wide", "narrow"),
        P("wide", "narrow"),
        P("wide", "narrow"),
        P("wide", "narrow"),
        P(AXES, None),
    )
    out_specs = (
        P(AXES, None),
        P(AXES, None),
        P(AXES, None, None),
        P(None, AXES),
        P(None, AXES),
        P(AXES),
        P(None, "wide", "narrow"),
        P("wide", "narrow"),
        P("wide", "narrow"),
        P(None, "wide", "narrow"),
        P("wide", "narrow"),
        P("wide", "narrow"),
        P("wide", "narrow"),
    )
    return jax.shard_map(
        functools.partial(local, shape), mesh=mesh, in_specs=in_specs, out_specs=out_specs, check_vma=False
    )
```
